32 devices in a mesh: section: 2 (over core), ctx: 4 (over y, x), wt: 4 (over z).
Axes of the slice: x: 2, y: 2, z: 4, core: 2. Of those that a mesh axis runs over, the one named last changes fastest.
Arguments:
- tokens: bfloat16 [2, 1024, 1536], P(None, ('ctx', 'wt')), may hold values from -6 to 6
- cotangent: bfloat16 [2, 1024, 1536], P(None, ('ctx', 'wt')), may hold values from -6 to 6
- blocks: int32 [2, 8], replicated, may hold values from 0 to 7, each once within a row
- routes: int32 [2, 2, 1024, 8], P('section', None, 'ctx'), may hold values from 0 to 15, all different within a row; in each aligned block of 256 rows (0 to 255, 256 to 511, ..., all dimensions but the last counted through in order) at most 160 rows name the same one
- norm_gain: float32 [2, 2, 1536], P('section'), may hold values from 0.5 to 1.5
- w_query: bfloat16 [2, 1536, 1536], P('section', 'ctx', 'wt'), may hold values from -1.25 to 1.25
- key_value_weight: bfloat16 [2, 1536, 8, 128], P('section', 'ctx', 'wt'), may hold values from -0.15625 to 0.15625
- w_attn_out: bfloat16 [2, 1536, 1536], P('section', 'wt', 'ctx'), may hold values from -2.5 to 2.5
- router: bfloat16 [2, 1536, 16], P('section'), may hold values from -0.078125 to 0.078125
- w_in: bfloat16 [2, 16, 1536, 1024], P('section', 'wt', 'ctx'), may hold values from -0.15625 to 0.15625
- w_down: bfloat16 [2, 16, 512, 1536], P('section', 'wt', 'ctx'), may hold values from -1 to 1
Outputs:
- layer_out: bfloat16 [2, 2, 1024, 1536], P('section', None, ('ctx', 'wt'))
- input_grads: bfloat16 [2, 2, 1024, 1536], P('section', None, ('ctx', 'wt'))
- grad_gain: float32 [2, 2, 1536], P('section', None, ('ctx', 'wt'))
- grad_query: float32 [2, 1536, 1536], P('section', 'ctx', 'wt')
- grad_kv: float32 [2, 1536, 8, 128], P('section', 'ctx', 'wt')
- grad_attn_out: float32 [2, 1536, 1536], P('section', 'wt', 'ctx')
- grad_router: float32 [2, 1536, 16], P('section', ('ctx', 'wt'))
- grad_in: float32 [2, 16, 1536, 1024], P('section', 'wt', 'ctx')
- grad_down: float32 [2, 16, 512, 1536], P('section', 'wt', 'ctx')
The draws below stay inside these ranges and needn't reach their ends.
Inputs may be any that keep to these rules, and one draw needn't show every extreme that they name: `blocks`: each row names every stored block of a micro-batch once. `routes`: each token names 8 different experts; among the 256 rows of one index of ctx in one micro-batch no expert is named by more than 160 rows, and in every draw some expert is named by exactly 160.
All inputs are finite; a program needn't handle non-finite values.
Results may differ from the reference program's by a relative error of at most 0.034.
Values may be sent and summed in bfloat16 or wider, within the bound.
A program may use at most 256 MiB of HBM per device.

```python
import math
import jax
import jax.numpy as jnp
import numpy as np
from jax import lax

MODEL_WIDTH = 1536
QUERY_HEADS = 24
KEY_VALUE_HEADS = 8
HEAD_SIZE = 64
FF = 512
TOPK = 8
E_DEV = 4
TOK_CTX = 256
MB = 2
CONT_LEN = 1024
SEQ = 1024
CAP = 160
N_CTX = 4
N_WT = 4


def level_of(own_key, shape, pieces, smallest, top_value):
    gain = 1.0
    for axis_at, parts in pieces:
        steps = jax.random.uniform(jax.random.fold_in(jax.random.fold_in(own_key, 6), axis_at), (parts,), jnp.float32, smallest / len(pieces), top_value / len(pieces))
        gain = gain * jnp.repeat(jnp.exp(steps), shape[axis_at] // parts).reshape((-1,) + (1,) * (len(shape) - 1 - axis_at))
    return gain


def assign_block(stream_key, own, number, rows, count, top, reach, skew):
    order = jax.random.permutation(stream_key, count)
    packed, usual = load_shares(count, rows * top, reach, skew, True), load_shares(count, rows * top, reach, skew, False)
    places = jnp.arange(count)

    def named(tallies, rotation):
        used = int((tallies > 0).sum())
        fixed = max(1, used // 4)
        passed = fixed + (places - fixed + rotation * (used - fixed)) % max(1, count - fixed)
        return jnp.zeros((count,), jnp.int32).at[order[jnp.where(places < fixed, places, passed)]].set(jnp.asarray(tallies, jnp.int32))

    tallies = jnp.where(number % 4 == 0, named(packed, number // 4), named(usual, number - number // 4 - 1))
    mixed = jax.random.permutation(jax.random.fold_in(own, 3), count)
    source_of, receiver = mixed[0:count // 2 * 2:2], mixed[1:count // 2 * 2:2]
    margin = jnp.minimum(tallies[source_of] - 1, reach - tallies[receiver]) // 2
    margin = jnp.where((source_of == order[0]) | (receiver == order[0]) | (tallies[receiver] == 0), 0, jnp.maximum(margin, 0))
    passed = jax.random.randint(jax.random.fold_in(own, 4), (count // 2,), 0, 1 << 20) % (margin + 1)
    tallies = tallies.at[source_of].add(-passed).at[receiver].add(passed)
    items = jnp.searchsorted(jnp.cumsum(tallies), jnp.arange(rows * top), side="right").astype(jnp.int32)
    listing = items.reshape(top, rows).T
    listing = listing[jax.random.permutation(jax.random.fold_in(own, 1), rows)]
    rotation = jax.random.randint(jax.random.fold_in(own, 2), (rows, 1), 0, top)
    return jnp.take_along_axis(listing, (jnp.arange(top)[None, :] + rotation) % top, axis=1)


def load_shares(amount, total, limit, skew, full):
    portions = [(1 << 20) // math.isqrt(rank ** skew) + 1 for rank in range(1, amount + 1)]
    largest = limit if full else min(limit, max(-(-total // amount), total * portions[0] // sum(portions)))
    least = 1 if total - largest >= amount - 1 else 0
    given, surplus = [largest] + [least] * (amount - 1), total - largest - least * (amount - 1)
    while surplus > 0:
        free = [i for i in range(1, amount) if given[i] < largest] or [i for i in range(1, amount) if given[i] < limit]
        pool, remaining = sum([portions[i] for i in free]), surplus
        for i in free:
            extra = min(limit - given[i], max(1, remaining * portions[i] // pool), surplus)
            given[i] = given[i] + extra
            surplus = surplus - extra
    return np.array(given)


def centred(key, shape, scale, most, cuts=(), kind=jnp.bfloat16):
    factor_of = level_of(key, shape, cuts, -0.22, 0.18) if cuts else 1.0
    values = jax.random.normal(key, shape, jnp.float32) * scale * factor_of
    return jnp.minimum(jnp.maximum(values, -most), most).astype(kind)


def setup_inputs(seed: int = 0) -> dict:
    key_list = jax.random.split(jax.random.key(seed), 12)
    tokens = centred(key_list[0], (MB, SEQ, MODEL_WIDTH), 1.0, 6.0, ((1, 16),))
    cotangent = centred(key_list[1], (MB, SEQ, MODEL_WIDTH), 1.0, 6.0, ((1, 16),))
    blocks = jax.vmap(lambda own: jax.random.permutation(own, 2 * N_CTX))(jax.random.split(key_list[2], MB)).reshape((MB, 2 * N_CTX)).astype(jnp.int32)
    routes_keys = jax.random.split(jax.random.fold_in(key_list[3], 1), 2 * MB * SEQ // TOK_CTX)
    routes_turns = jax.random.permutation(jax.random.fold_in(key_list[3], 3), 2 * MB * SEQ // TOK_CTX)
    routes = jax.vmap(lambda own, number: assign_block(jax.random.fold_in(key_list[3], 2), own, number, TOK_CTX, E_DEV * N_WT, TOPK, CAP, 1))(routes_keys, routes_turns).reshape((2, MB, SEQ, TOPK))
    norm_gain = jnp.clip(1.0 + 0.1 * jax.random.normal(key_list[4], (2, 2, MODEL_WIDTH), jnp.float32), 0.5, 1.5)
    w_query = centred(key_list[5], (2, MODEL_WIDTH, QUERY_HEADS * HEAD_SIZE), (MODEL_WIDTH // 64) ** -0.5, 1.25, ((0, 2), (1, 4), (2, 4)))
    key_value_weight = centred(key_list[6], (2, MODEL_WIDTH, KEY_VALUE_HEADS, 2 * HEAD_SIZE), MODEL_WIDTH ** -0.5, 0.15625, ((0, 2), (1, 4), (2, 4)))
    w_attn_out = centred(key_list[7], (2, QUERY_HEADS * HEAD_SIZE, MODEL_WIDTH), (max(QUERY_HEADS * HEAD_SIZE // 256, 1)) ** -0.5, 2.5, ((0, 2), (1, 4), (2, 4)))
    router = centred(key_list[8], (2, MODEL_WIDTH, E_DEV * N_WT), (4 * MODEL_WIDTH) ** -0.5, 0.078125, ((0, 2),))
    w_in = centred(key_list[9], (2, E_DEV * N_WT, MODEL_WIDTH, 2 * FF), MODEL_WIDTH ** -0.5, 0.15625, ((0, 2), (1, 4), (2, 4)))
    w_down = centred(key_list[10], (2, E_DEV * N_WT, FF, MODEL_WIDTH), (FF // 16) ** -0.5, 1.0, ((0, 2), (1, 4), (2, 4)))
    return {"tokens": tokens, "cotangent": cotangent, "blocks": blocks, "routes": routes, "norm_gain": norm_gain, "w_query": w_query, "key_value_weight": key_value_weight, "w_attn_out": w_attn_out, "router": router, "w_in": w_in, "w_down": w_down}


@jax.custom_vjp
def low(v):
    return lax.optimization_barrier(v.astype(jnp.bfloat16)).astype(jnp.float32)

@jax.custom_vjp
def lower_backward(v):
    return v

def low_keep(v):
    return (low(v), None)

def low_pass(kept, grad):
    return (grad,)

def back_keep(v):
    return (v, None)

def back_low(kept, grad):
    return (low(grad),)
low.defvjp(low_keep, low_pass)
lower_backward.defvjp(back_keep, back_low)
EPSILON = 1e-06
ROPE_BASE = 10000.0
MASKED = -1e+30

def matrix_product(left, right):
    return jnp.dot(left, right, precision=lax.Precision.HIGHEST, preferred_element_type=jnp.float32)

def inverse_freq(head_width):
    return jnp.power(ROPE_BASE, -jnp.arange(head_width // 2, dtype=jnp.float32) * 2.0 / head_width)

def rotate(values, angles):
    half_width = values.shape[-1] // 2
    cosine = jnp.cos(angles)[:, None, :]
    sine_part = jnp.sin(angles)[:, None, :]
    leading = values[..., :half_width]
    trailing = values[..., half_width:]
    return jnp.concatenate([leading * cosine - trailing * sine_part, trailing * cosine + leading * sine_part], -1)

def layout(blocks):
    block_len = SEQ // blocks.shape[1]
    placed = (blocks[:, :, None] * block_len + jnp.arange(block_len, dtype=jnp.int32)[None, None, :]).reshape(blocks.shape[0], SEQ)
    rpos = jnp.concatenate([placed[0], SEQ + placed[1] % CONT_LEN])
    seg = jnp.concatenate([jnp.zeros((SEQ,), jnp.int32), 1 + placed[1] // CONT_LEN])
    return (rpos, seg)

def norm_scale(stream):
    return lax.rsqrt(lax.optimization_barrier(jnp.mean(stream * stream, -1, keepdims=True)) + EPSILON)

def attend(query_rows, key_rot, value_part, rpos, seg):
    count_of_rows = query_rows.shape[0]
    block_span_width = min(512, count_of_rows)
    query_group_size = QUERY_HEADS // KEY_VALUE_HEADS
    grouped_queries = query_rows.reshape(count_of_rows // block_span_width, block_span_width, KEY_VALUE_HEADS, query_group_size, HEAD_SIZE)

    def query_block(members):
        part_q, q_pos, q_seg = members
        logit_block = lower_backward(jnp.einsum('qhgd,khd->hgqk', part_q, key_rot, precision=lax.Precision.HIGHEST) * (1.0 / HEAD_SIZE))
        allowed = ((seg[None, :] == 0) | (seg[None, :] == q_seg[:, None])) & (rpos[None, :] <= q_pos[:, None])
        logit_block = jnp.where(allowed, logit_block, MASKED)
        largest = lax.optimization_barrier(jnp.max(logit_block, -1, keepdims=True))
        expos = jnp.where(allowed, jnp.exp(logit_block - largest), 0.0)
        attn_probs = low(expos / lax.optimization_barrier(jnp.sum(expos, -1, keepdims=True)))
        return jnp.einsum('hgqk,khd->qhgd', attn_probs, value_part, precision=lax.Precision.HIGHEST)
    result = lax.map(jax.checkpoint(query_block), (grouped_queries, rpos.reshape(-1, block_span_width), seg.reshape(-1, block_span_width)))
    return result.reshape(count_of_rows, QUERY_HEADS * HEAD_SIZE)

def layer(stream, gains, query_mat, pairing_matrix, out_mat, router_table, gate_up_mat, down_mat, route_rows, angles, rpos, seg):
    count_of_rows = stream.shape[0]
    normalized_input = low(stream * norm_scale(stream) * gains[0])
    q_raw = lower_backward(matrix_product(normalized_input, query_mat)).reshape(count_of_rows, QUERY_HEADS, HEAD_SIZE)
    query_rows = low(rotate(q_raw, angles))
    unnormalized_pairs = lower_backward(matrix_product(normalized_input, pairing_matrix.reshape(MODEL_WIDTH, KEY_VALUE_HEADS * 2 * HEAD_SIZE))).reshape(count_of_rows, KEY_VALUE_HEADS, 2 * HEAD_SIZE)
    key_rot = low(rotate(unnormalized_pairs[..., :HEAD_SIZE], angles))
    value_part = low(unnormalized_pairs[..., HEAD_SIZE:])
    attended = lower_backward(low(attend(query_rows, key_rot, value_part, rpos, seg)))
    middle = stream + lower_backward(matrix_product(attended, out_mat))
    normed_mid = low(middle * norm_scale(middle) * gains[1])
    logits = matrix_product(normed_mid, router_table)
    chosen = jnp.take_along_axis(logits, route_rows, 1)
    chosen = chosen - lax.optimization_barrier(jnp.max(chosen, 1, keepdims=True))
    expos = jnp.exp(chosen)
    gates = expos / lax.optimization_barrier(jnp.sum(expos, 1, keepdims=True))

    def expert_step(summed, members):
        expert_in, expert_down, expert_index = members
        weight = lax.optimization_barrier(jnp.sum(jnp.where(route_rows == expert_index, gates, 0.0), 1))
        gate_up = lower_backward(matrix_product(normed_mid, expert_in))
        hidden = low(jax.nn.silu(gate_up[:, :FF]) * gate_up[:, FF:])
        expert_out = lower_backward(matrix_product(hidden, expert_down))
        return (summed + weight[:, None] * expert_out, None)
    mixed, unused = lax.scan(jax.checkpoint(expert_step), jnp.zeros((count_of_rows, MODEL_WIDTH), jnp.float32), (gate_up_mat, down_mat, jnp.arange(E_DEV * N_WT, dtype=jnp.int32)))
    return lower_backward(low(middle + lower_backward(mixed)))

def reference(tokens, cotangent, blocks, routes, norm_gain, w_query, key_value_weight, w_attn_out, router, w_in, w_down):
    count_of_rows = tokens.shape[0] * SEQ
    rpos, seg = layout(blocks)
    angles = rpos.astype(jnp.float32)[:, None] * inverse_freq(HEAD_SIZE)[None, :]

    def section_fn(layer_index):
        route_rows = routes[layer_index].reshape(count_of_rows, TOPK)

        def run(stream, gains, query_mat, pairing_matrix, out_mat, router_table, gate_up_mat, down_mat):
            return layer(stream, gains, query_mat, pairing_matrix, out_mat, router_table, gate_up_mat, down_mat, route_rows, angles, rpos, seg)
        return run

    def weights_of(layer_index):
        return (norm_gain[layer_index].astype(jnp.float32), w_query[layer_index].astype(jnp.float32), key_value_weight[layer_index].astype(jnp.float32), w_attn_out[layer_index].astype(jnp.float32), router[layer_index].astype(jnp.float32), w_in[layer_index].astype(jnp.float32), w_down[layer_index].astype(jnp.float32))
    start_rows = tokens.astype(jnp.float32).reshape(count_of_rows, MODEL_WIDTH)
    middle_rows, back_first = jax.vjp(section_fn(0), start_rows, *weights_of(0))
    final_rows, back_last = jax.vjp(section_fn(1), middle_rows, *weights_of(1))
    grads_last = back_last(cotangent.astype(jnp.float32).reshape(count_of_rows, MODEL_WIDTH))
    grads_first = back_first(grads_last[0])
    out_shape = (2, tokens.shape[0], SEQ, MODEL_WIDTH)
    layer_out = jnp.stack([middle_rows, final_rows]).reshape(out_shape).astype(jnp.bfloat16)
    input_grads = jnp.stack([grads_first[0], grads_last[0]]).reshape(out_shape).astype(jnp.bfloat16)

    def paired(position):
        return jnp.stack([grads_first[position], grads_last[position]])
    return (layer_out, input_grads, paired(1), paired(2), paired(3), paired(4), paired(5), paired(6), paired(7))
```

```python
import functools

import jax
import jax.numpy as jnp
from jax import lax
from jax.experimental import pallas as pl
from jax.experimental.pallas import tpu as pltpu
from jax.sharding import PartitionSpec as P

HEAD_SIZE = 64
FF = 512
CONT_LEN = 1024
EPSILON = 1e-06
ROPE_BASE = 10000.0
MASKED = -1e30
MESH = pl.DeviceIdType.MESH
F32 = jnp.float32
BF16 = jnp.bfloat16


def dot(left, right, contract):
    return lax.dot_general(left, right, (contract, ((), ())), preferred_element_type=F32)


def norm_scale(rows):
    return lax.rsqrt(jnp.mean(rows * rows, -1, keepdims=True) + EPSILON)


def place():
    return lax.axis_index("section"), lax.axis_index("ctx"), lax.axis_index("wt")


def greet(targets):
    barrier = pltpu.get_barrier_semaphore()
    for target in targets:
        pl.semaphore_signal(barrier, inc=1, device_id=target, device_id_type=MESH)
    pl.semaphore_wait(barrier, len(targets))


def remote(source, destination, send_sem, recv_sem, target):
    return pltpu.make_async_remote_copy(
        src_ref=source,
        dst_ref=destination,
        send_sem=send_sem,
        recv_sem=recv_sem,
        device_id=target,
        device_id_type=MESH,
    )


def exchange_kernel(n_wt, reduce, back, spread, rounded, *refs):
    refs = list(refs)
    section, ctx, wt = place()
    sibling = (1 - section, ctx, wt)
    peers = [(section, ctx, lax.rem(wt + k, n_wt)) for k in range(1, n_wt)]
    parts = refs.pop(0) if reduce else None
    rows_ref = refs.pop(0)
    stream_ref = refs.pop(0) if back else None
    gain_ref = refs.pop(0) if (back or spread) else None
    result_ref = refs.pop(0) if reduce else None
    gain_grad_ref = refs.pop(0) if back else None
    all_ref = refs.pop(0) if spread else None
    if reduce:
        from_sibling, from_peers, staged, rs_send, rs_recv = refs[:5]
        refs = refs[5:]
    if spread:
        ag_send, ag_recv = refs
    greet([sibling] + peers)
    own = section * n_wt + wt
    if reduce:
        sends = []
        order = [lax.rem(wt + k, n_wt) for k in range(1, n_wt)] + [wt]
        swaps = []
        for k, block in enumerate(order):
            copy = remote(
                parts.at[(1 - section) * n_wt + block], from_sibling.at[block], rs_send.at[k], rs_recv.at[k], sibling
            )
            copy.start()
            swaps.append(copy)
        for k, block in enumerate(order[:-1]):
            swaps[k].wait_recv()
            staged[k] = (parts[section * n_wt + block].astype(F32) + from_sibling[block].astype(F32)).astype(BF16)
            copy = remote(
                staged.at[k], from_peers.at[k], rs_send.at[n_wt + k], rs_recv.at[n_wt + k], peers[k]
            )
            copy.start()
            sends.append(copy)
        swaps[-1].wait_recv()
        total = parts[own].astype(F32) + from_sibling[wt].astype(F32)
        for k in range(n_wt - 1):
            sends[k].wait_recv()
            total = total + from_peers[k].astype(F32)
        if back:
            stream = stream_ref[...]
            scale = norm_scale(stream)
            weighted = gain_ref[...] * total
            gain_grad_ref[...] = jnp.sum(total * stream * scale, 0, keepdims=True)
            total = scale * weighted - stream * (scale * scale * scale) * jnp.mean(
                weighted * stream, -1, keepdims=True
            )
        total = rows_ref[...].astype(F32) + total
        if rounded:
            total = total.astype(BF16).astype(F32)
        result_ref[...] = total
    else:
        total = rows_ref[...].astype(F32)
    if spread:
        if spread == "norm":
            total = total * norm_scale(total) * gain_ref[...]
        all_ref[own] = total.astype(BF16)
        copies = []
        for k in range(1, n_wt):
            copy = remote(all_ref.at[own], all_ref.at[own], ag_send.at[k], ag_recv.at[k], peers[k - 1])
            copy.start()
            copies.append(copy)
        copy = remote(all_ref.at[own], all_ref.at[own], ag_send.at[0], ag_recv.at[0], sibling)
        copy.start()
        swaps_out = [copy]
        for k in range(1, n_wt):
            copies[k - 1].wait_recv()
            block = section * n_wt + lax.rem(wt + n_wt - k, n_wt)
            copy = remote(all_ref.at[block], all_ref.at[block], ag_send.at[n_wt + k], ag_recv.at[n_wt + k], sibling)
            copy.start()
            swaps_out.append(copy)
        for copy in swaps_out:
            copy.wait()
        for copy in copies:
            copy.wait_send()
    if reduce:
        for copy in swaps + sends:
            copy.wait_send()


VMEM = pl.BlockSpec(memory_space=pltpu.VMEM)


def exchange(number, parts, rows, stream=None, gain=None, spread=None, rounded=False):
    n_wt = lax.axis_size("wt")
    shape = rows.shape
    reduce, back = parts is not None, stream is not None
    operands = [
        member
        for member, wanted in ((parts, reduce), (rows, True), (stream, back), (gain, back or spread))
        if wanted
    ]
    outs = []
    scratch = []
    if reduce:
        outs.append(jax.ShapeDtypeStruct(shape, F32))
        scratch += [
            pltpu.VMEM((n_wt,) + shape, BF16),
            pltpu.VMEM((n_wt - 1,) + shape, BF16),
            pltpu.VMEM((n_wt - 1,) + shape, BF16),
            pltpu.SemaphoreType.DMA((2 * n_wt,)),
            pltpu.SemaphoreType.DMA((2 * n_wt,)),
        ]
    if back:
        outs.append(jax.ShapeDtypeStruct((1, shape[1]), F32))
    if spread:
        outs.append(jax.ShapeDtypeStruct((2 * n_wt,) + shape, BF16))
        scratch += [pltpu.SemaphoreType.DMA((2 * n_wt,)), pltpu.SemaphoreType.DMA((2 * n_wt,))]
    return pl.pallas_call(
        functools.partial(exchange_kernel, n_wt, reduce, back, spread, rounded),
        out_shape=outs,
        in_specs=[VMEM] * len(operands),
        out_specs=[VMEM] * len(outs),
        scratch_shapes=scratch,
        compiler_params=pltpu.CompilerParams(
            collective_id=number, has_side_effects=True, vmem_limit_bytes=40 << 20
        ),
    )(*operands)


def ctx_gather_kernel(n_ctx, own_ref, all_ref, send, recv, local):
    section, ctx, wt = place()
    peers = [(section, lax.rem(ctx + k, n_ctx), wt) for k in range(1, n_ctx)]
    greet(peers)
    keep = pltpu.make_async_copy(own_ref, all_ref.at[ctx], local)
    keep.start()
    copies = [
        remote(own_ref, all_ref.at[ctx], send.at[k], recv.at[k], peers[k]) for k in range(n_ctx - 1)
    ]
    for copy in copies:
        copy.start()
    keep.wait()
    for copy in copies:
        copy.wait()


def ctx_gather(number, own):
    n_ctx = lax.axis_size("ctx")
    return pl.pallas_call(
        functools.partial(ctx_gather_kernel, n_ctx),
        out_shape=jax.ShapeDtypeStruct((n_ctx,) + own.shape, own.dtype),
        in_specs=[VMEM],
        out_specs=VMEM,
        scratch_shapes=[
            pltpu.SemaphoreType.DMA((n_ctx - 1,)),
            pltpu.SemaphoreType.DMA((n_ctx - 1,)),
            pltpu.SemaphoreType.DMA,
        ],
        compiler_params=pltpu.CompilerParams(collective_id=number, has_side_effects=True),
    )(own)


def ctx_sum_kernel(n_ctx, parts_ref, total_ref, landed, send, recv):
    section, ctx, wt = place()
    peers = [(section, lax.rem(ctx + k, n_ctx), wt) for k in range(1, n_ctx)]
    greet(peers)
    copies = [
        remote(parts_ref.at[lax.rem(ctx + k, n_ctx)], landed.at[k - 1], send.at[k - 1], recv.at[k - 1], peers[k - 1])
        for k in range(1, n_ctx)
    ]
    for copy in copies:
        copy.start()
    total = parts_ref[ctx].astype(F32)
    for k, copy in enumerate(copies):
        copy.wait_recv()
        total = total + landed[k].astype(F32)
    total_ref[...] = total
    for copy in copies:
        copy.wait_send()


def ctx_sum(number, parts):
    n_ctx = lax.axis_size("ctx")
    return pl.pallas_call(
        functools.partial(ctx_sum_kernel, n_ctx),
        out_shape=jax.ShapeDtypeStruct(parts.shape[1:], F32),
        in_specs=[VMEM],
        out_specs=VMEM,
        scratch_shapes=[
            pltpu.VMEM((n_ctx - 1,) + parts.shape[1:], BF16),
            pltpu.SemaphoreType.DMA((n_ctx - 1,)),
            pltpu.SemaphoreType.DMA((n_ctx - 1,)),
        ],
        compiler_params=pltpu.CompilerParams(
            collective_id=number, has_side_effects=True, vmem_limit_bytes=40 << 20
        ),
    )(parts)


def turn(values, cosine, sine, heads):
    pieces = []
    for head in range(heads):
        a = values[:, head * 64 : head * 64 + 32]
        b = values[:, head * 64 + 32 : head * 64 + 64]
        pieces += [a * cosine - b * sine, b * cosine + a * sine]
    return jnp.concatenate(pieces, -1)


def allowed_pairs(q_pos, q_seg, k_pos, k_seg):
    return ((k_seg[None, :] == 0) | (k_seg[None, :] == q_seg[:, None])) & (k_pos[None, :] <= q_pos[:, None])


def attend(query, pairs, q_pos, q_seg, k_pos, k_seg):
    logits = jnp.einsum("hqd,kd->hqk", query, pairs[:, :64], preferred_element_type=F32) * (1.0 / HEAD_SIZE)
    allowed = allowed_pairs(q_pos, q_seg, k_pos, k_seg)[None]
    logits = jnp.where(allowed, logits, MASKED)
    largest = jnp.max(logits, -1, keepdims=True)
    expos = jnp.exp(logits - largest)
    total = jnp.sum(expos, -1, keepdims=True)
    probs = (expos / total).astype(BF16)
    out = jnp.einsum("hqk,kd->hqd", probs, pairs[:, 64:], preferred_element_type=F32)
    return out, largest + jnp.log(total)


def attend_back(query, pairs, q_pos, q_seg, k_pos, k_seg, log_total, out, d_out):
    logits = jnp.einsum("hqd,kd->hqk", query, pairs[:, :64], preferred_element_type=F32) * (1.0 / HEAD_SIZE)
    allowed = allowed_pairs(q_pos, q_seg, k_pos, k_seg)[None]
    probs = jnp.where(allowed, jnp.exp(logits - log_total), 0.0)
    delta = jnp.sum(d_out.astype(F32) * out, -1, keepdims=True)
    d_probs = jnp.einsum("hqd,kd->hqk", d_out, pairs[:, 64:], preferred_element_type=F32)
    d_scores = (probs * (d_probs - delta)).astype(BF16)
    d_query = jnp.einsum("hqk,kd->hqd", d_scores, pairs[:, :64], preferred_element_type=F32) * (1.0 / HEAD_SIZE)
    d_keys = jnp.einsum("hqk,hqd->kd", d_scores, query, preferred_element_type=F32) * (1.0 / HEAD_SIZE)
    d_values = jnp.einsum("hqk,hqd->kd", probs.astype(BF16), d_out, preferred_element_type=F32)
    return d_query, jnp.concatenate([d_keys, d_values], -1)


def heads_first(rows, micro_count):
    count = rows.shape[0] // micro_count
    return jnp.transpose(rows.reshape(micro_count, count, -1, HEAD_SIZE), (0, 2, 1, 3))


def rows_first(heads):
    micro_count, h, q, d = heads.shape
    return jnp.transpose(heads, (0, 2, 1, 3)).reshape(micro_count * q, h * d)


def shards(tokens, cotangent, blocks, routes, norm_gain, w_query, key_value_weight, w_attn_out, router, w_in, w_down):
    section, ctx, wt = place()
    n_ctx, n_wt, layers = lax.axis_size("ctx"), lax.axis_size("wt"), lax.axis_size("section")
    micro_count, share, width = tokens.shape
    per_ctx = routes.shape[2]
    seq_len = per_ctx * n_ctx
    experts = w_in.shape[1] // 2
    n_experts = router.shape[2]
    q_cols = w_query.shape[2] // 2
    heads = q_cols // HEAD_SIZE
    depth = w_query.shape[1]

    block_len = seq_len // blocks.shape[1]
    placed = (blocks[:, :, None] * block_len + jnp.arange(block_len, dtype=jnp.int32)[None, None, :]).reshape(
        micro_count, seq_len
    )
    later = (jnp.arange(micro_count) > 0)[:, None]
    k_pos = jnp.where(later, seq_len + placed % CONT_LEN, placed)
    k_seg = jnp.where(later, 1 + placed // CONT_LEN, 0)
    q_pos = lax.dynamic_slice_in_dim(k_pos, ctx * per_ctx, per_ctx, 1)
    q_seg = lax.dynamic_slice_in_dim(k_seg, ctx * per_ctx, per_ctx, 1)
    inverse = jnp.power(ROPE_BASE, -jnp.arange(HEAD_SIZE // 2, dtype=F32) * 2.0 / HEAD_SIZE)
    angles = q_pos.reshape(-1).astype(F32)[:, None] * inverse[None, :]
    cosine, sine = jnp.cos(angles), jnp.sin(angles)

    def swap(values):
        return lax.ppermute(values, "section", [(0, 1), (1, 0)])

    def by_layer(halves):
        mine = lax.dynamic_index_in_dim(halves, section, 0, False)
        other = swap(lax.dynamic_index_in_dim(halves, 1 - section, 0, False))
        return [jnp.where(section == layer, mine, other) for layer in range(2)]

    def to_owner(first, second):
        mine = jnp.where(section == 0, first, second)
        other = swap(jnp.where(section == 0, second, first))
        return jnp.where(section == 0, mine, other), jnp.where(section == 0, other, mine)

    attn_pack = jnp.concatenate(
        [
            jnp.transpose(w_query[0].reshape(depth, 2, q_cols), (1, 0, 2)),
            jnp.transpose(key_value_weight[0], (1, 0, 2)),
            jnp.transpose(w_attn_out[0].reshape(2, q_cols, depth), (0, 2, 1)),
        ],
        -1,
    )
    attn_pack = by_layer(attn_pack)
    in_pack = by_layer(w_in[0].reshape((2, experts) + w_in.shape[2:]))
    down_pack = by_layer(w_down[0].reshape((2, experts) + w_down.shape[2:]))
    route_pack = lax.all_gather(routes[0], "section", axis=0)
    gain_pack = lax.all_gather(norm_gain[0], "section", axis=0)
    router_pack = lax.all_gather(router[0], "section", axis=0)

    attn_full = [lax.all_gather(member, "ctx", axis=0, tiled=True) for member in attn_pack]
    in_full = [lax.all_gather(member, "ctx", axis=1, tiled=True) for member in in_pack]
    down_full = [lax.all_gather(member, "ctx", axis=1, tiled=True) for member in down_pack]

    my_first = wt * 2 * experts + section * experts
    n_rows = micro_count * per_ctx

    def routed(layer):
        names = route_pack[layer].reshape(n_rows, -1)
        return jnp.any(names[:, :, None] == jnp.arange(n_experts, dtype=jnp.int32)[None, None, :], 1)

    def full_rows(values):
        return values.reshape(n_rows, width)

    def blocked(values):
        return values.reshape(2 * n_wt, share, width).astype(BF16)

    stream = lax.dynamic_index_in_dim(tokens, section, 0, False).astype(F32)
    top = lax.dynamic_index_in_dim(cotangent, section, 0, False).astype(F32)

    (normed_in,) = exchange(0, None, stream, gain=gain_pack[0, 0:1], spread="norm")
    (d_mixed,) = exchange(1, None, top, gain=gain_pack[0, 0:1], spread="plain")
    saved = []
    outputs = []
    for layer in range(2):
        rows_in = full_rows(normed_in)
        weights = attn_full[layer]
        mixed_heads = dot(rows_in, weights[:, : q_cols + 2 * HEAD_SIZE], ((1,), (0,)))
        turned = turn(mixed_heads[:, : q_cols + HEAD_SIZE], cosine, sine, heads + 1)
        queries = turned[:, :q_cols].astype(BF16)
        own_pairs = jnp.concatenate([turned[:, q_cols:], mixed_heads[:, q_cols + HEAD_SIZE :]], -1).astype(BF16)
        pairs = ctx_gather(2 + layer, own_pairs)
        pairs = jnp.transpose(
            pairs.reshape(n_ctx, micro_count, per_ctx, 2 * HEAD_SIZE), (1, 0, 2, 3)
        ).reshape(micro_count * seq_len, 2 * HEAD_SIZE)
        by_head = heads_first(queries, micro_count)
        outs = [
            attend(
                by_head[m],
                pairs[: (m + 1) * seq_len],
                q_pos[m],
                q_seg[m],
                k_pos.reshape(-1)[: (m + 1) * seq_len],
                k_seg.reshape(-1)[: (m + 1) * seq_len],
            )
            for m in range(micro_count)
        ]
        out_full = jnp.stack([member[0] for member in outs])
        log_total = [member[1] for member in outs]
        attended = rows_first(out_full).astype(BF16)
        partial = dot(attended, weights[:, q_cols + 2 * HEAD_SIZE :], ((1,), (1,)))
        middle, normed_mid = exchange(
            4 + layer, blocked(partial), stream, gain=gain_pack[layer, 1:2], spread="norm"
        )
        rows_mid = full_rows(normed_mid)
        logits = dot(rows_mid, router_pack[layer], ((1,), (0,)))
        hit = routed(layer)
        masked = jnp.where(hit, logits, MASKED)
        expos = jnp.where(hit, jnp.exp(masked - jnp.max(masked, 1, keepdims=True)), 0.0)
        gates = expos / jnp.sum(expos, 1, keepdims=True)
        my_gates = lax.dynamic_slice_in_dim(gates, my_first, experts, 1)
        gate_up = jnp.einsum("td,edf->etf", rows_mid, in_full[layer], preferred_element_type=F32)
        hidden = jax.nn.silu(gate_up[..., :FF]) * gate_up[..., FF:]
        weighted_hidden = (hidden * jnp.transpose(my_gates)[:, :, None]).astype(BF16)
        partial = jnp.einsum("etf,efd->td", weighted_hidden, down_full[layer], preferred_element_type=F32)
        saved.append(
            dict(
                stream=stream,
                middle=middle,
                rows_in=rows_in,
                rows_mid=rows_mid,
                queries=by_head,
                pairs=pairs,
                out_full=out_full,
                attended=attended,
                log_total=log_total,
                gates=gates,
                my_gates=my_gates,
                gate_up=gate_up,
                weighted_hidden=weighted_hidden,
            )
        )
        if layer == 0:
            stream, normed_in = exchange(
                6, blocked(partial), middle, gain=gain_pack[1, 0:1], spread="norm", rounded=True
            )
        else:
            (stream,) = exchange(7, blocked(partial), middle, rounded=True)
        outputs.append(stream.astype(BF16))

    upstream = top
    grads_in = [None, None]
    attn_grads = [None, None]
    in_grads = [None, None]
    down_grads = [None, None]
    small = [None, None]
    for layer in (1, 0):
        kept = saved[layer]
        rows_d = full_rows(d_mixed)
        d_weighted = jnp.einsum("td,efd->etf", rows_d, down_full[layer], preferred_element_type=F32)
        gate_part, up_part = kept["gate_up"][..., :FF], kept["gate_up"][..., FF:]
        sigmoid = jax.nn.sigmoid(gate_part)
        activated = gate_part * sigmoid
        d_weight = jnp.sum((activated * up_part).astype(BF16).astype(F32) * d_weighted, -1)
        d_hidden = d_weighted * jnp.transpose(kept["my_gates"])[:, :, None]
        d_gate_up = jnp.concatenate(
            [d_hidden * up_part * (sigmoid * (1.0 + gate_part * (1.0 - sigmoid))), d_hidden * activated], -1
        ).astype(BF16)
        down_grad = jnp.einsum("etf,td->efd", kept["weighted_hidden"], rows_d, preferred_element_type=F32)
        in_grad = jnp.einsum("td,etf->edf", kept["rows_mid"], d_gate_up, preferred_element_type=F32)
        down_grads[layer] = lax.psum_scatter(down_grad.astype(BF16), "ctx", scatter_dimension=1, tiled=True)
        in_grads[layer] = lax.psum_scatter(in_grad.astype(BF16), "ctx", scatter_dimension=1, tiled=True)
        partial = jnp.einsum("etf,edf->td", d_gate_up, in_full[layer], preferred_element_type=F32)
        terms = kept["my_gates"] * jnp.transpose(d_weight)
        placed_terms = lax.dynamic_update_slice_in_dim(jnp.zeros_like(kept["gates"]), terms, my_first, 1)
        d_logits = placed_terms - kept["gates"] * jnp.sum(terms, 1, keepdims=True)
        partial = partial + lax.dot_general(
            d_logits,
            router_pack[layer].astype(F32),
            (((1,), (1,)), ((), ())),
            precision=lax.Precision.HIGHEST,
            preferred_element_type=F32,
        )
        router_grad = lax.dot_general(
            d_logits,
            kept["rows_mid"].astype(F32),
            (((0,), (0,)), ((), ())),
            precision=lax.Precision.HIGHEST,
            preferred_element_type=F32,
        )
        d_middle, gain_grad_mid, d_attn = exchange(
            8 + layer, blocked(partial), upstream, kept["middle"], gain_pack[layer, 1:2], spread="plain"
        )
        rows_a = full_rows(d_attn)
        weights = attn_full[layer]
        d_attended = dot(rows_a, weights[:, q_cols + 2 * HEAD_SIZE :], ((1,), (0,))).astype(BF16)
        out_grad = dot(rows_a, kept["attended"], ((0,), (0,)))
        d_heads = heads_first(d_attended, micro_count)
        d_queries = []
        d_pairs = 0.0
        for m in range(micro_count):
            d_query, d_pair = attend_back(
                kept["queries"][m],
                kept["pairs"][: (m + 1) * seq_len],
                q_pos[m],
                q_seg[m],
                k_pos.reshape(-1)[: (m + 1) * seq_len],
                k_seg.reshape(-1)[: (m + 1) * seq_len],
                kept["log_total"][m],
                kept["out_full"][m],
                d_heads[m],
            )
            d_queries.append(d_query)
            d_pairs = d_pairs + jnp.pad(d_pair, ((0, (micro_count - 1 - m) * seq_len), (0, 0)))
        d_pairs = jnp.transpose(
            d_pairs.reshape(micro_count, n_ctx, per_ctx, 2 * HEAD_SIZE), (1, 0, 2, 3)
        ).reshape(n_ctx, n_rows, 2 * HEAD_SIZE)
        d_own = ctx_sum(10 + layer, d_pairs.astype(BF16))
        raw = jnp.concatenate([rows_first(jnp.stack(d_queries)), d_own[:, :HEAD_SIZE]], -1)
        raw = jnp.concatenate([turn(raw, cosine, -sine, heads + 1), d_own[:, HEAD_SIZE:]], -1).astype(BF16)
        heads_grad = dot(kept["rows_in"], raw, ((0,), (0,)))
        attn_grads[layer] = lax.psum_scatter(
            jnp.concatenate([heads_grad, out_grad], -1).astype(BF16), "ctx", scatter_dimension=0, tiled=True
        )
        partial = dot(raw, weights[:, : q_cols + 2 * HEAD_SIZE], ((1,), (1,)))
        if layer == 1:
            upstream, gain_grad_in, d_mixed = exchange(
                12, blocked(partial), d_middle, kept["stream"], gain_pack[1, 0:1], spread="plain", rounded=True
            )
        else:
            upstream, gain_grad_in = exchange(
                13, blocked(partial), d_middle, kept["stream"], gain_pack[0, 0:1], rounded=True
            )
        grads_in[layer] = upstream.astype(BF16)
        small[layer] = jnp.concatenate([gain_grad_in, gain_grad_mid, router_grad], 0)

    small_sum = lax.psum_scatter(
        jnp.transpose(
            jnp.concatenate(small, 0).reshape(-1, n_ctx * n_wt, width // (n_ctx * n_wt)), (1, 0, 2)
        ),
        ("ctx", "wt"),
        scatter_dimension=0,
        tiled=False,
    )
    small_first, small_second = jnp.split(small_sum, 2, 0)
    mine, other = to_owner(small_first, small_second)
    small_total = mine + other
    out_pair = jnp.stack(to_owner(outputs[0], outputs[1]))
    grad_pair = jnp.stack(to_owner(grads_in[0], grads_in[1]))
    attn_first, attn_second = [member.astype(F32) for member in to_owner(attn_grads[0], attn_grads[1])]
    kv_at = q_cols
    out_at = q_cols + 2 * HEAD_SIZE
    grad_query = jnp.concatenate([attn_first[:, :kv_at], attn_second[:, :kv_at]], -1)
    grad_kv = jnp.stack([attn_first[:, kv_at:out_at], attn_second[:, kv_at:out_at]], 1)
    grad_out = jnp.concatenate([jnp.transpose(attn_first[:, out_at:]), jnp.transpose(attn_second[:, out_at:])], 0)
    grad_in = jnp.concatenate(to_owner(in_grads[0], in_grads[1]), 0).astype(F32)
    grad_down = jnp.concatenate(to_owner(down_grads[0], down_grads[1]), 0).astype(F32)
    return (
        out_pair[None],
        grad_pair[None],
        small_total[:2][None],
        grad_query[None],
        grad_kv[None],
        grad_out[None],
        jnp.transpose(small_total[2:])[None],
        grad_in[None],
        grad_down[None],
    )


def solution(mesh):
    return jax.shard_map(
        shards,
        mesh=mesh,
        in_specs=(
            P(None, ("ctx", "wt"), None),
            P(None, ("ctx", "wt"), None),
            P(),
            P("section", None, "ctx", None),
            P("section", None, None),
            P("section", "ctx", "wt"),
            P("section", "ctx", "wt", None),
            P("section", "wt", "ctx"),
            P("section", None, None),
            P("section", "wt", "ctx", None),
            P("section", "wt", "ctx", None),
        ),
        out_specs=(
            P("section", None, ("ctx", "wt"), None),
            P("section", None, ("ctx", "wt"), None),
            P("section", None, ("ctx", "wt")),
            P("section", "ctx", "wt"),
            P("section", "ctx", "wt", None),
            P("section", "wt", "ctx"),
            P("section", ("ctx", "wt"), None),
            P("section", "wt", "ctx", None),
            P("section", "wt", "ctx", None),
        ),
        check_vma=False,
    )
```

```python
import functools

import jax
import jax.numpy as jnp
from jax import lax
from jax.experimental import pallas as pl
from jax.experimental.pallas import tpu as pltpu
from jax.sharding import PartitionSpec as P

HEAD_SIZE = 64
FF = 512
CONT_LEN = 1024
EPSILON = 1e-06
ROPE_BASE = 10000.0
MASKED = -1e30
MESH = pl.DeviceIdType.MESH
F32 = jnp.float32
BF16 = jnp.bfloat16


def dot(left, right, contract):
    return lax.dot_general(left, right, (contract, ((), ())), preferred_element_type=F32)


def norm_scale(rows):
    return lax.rsqrt(jnp.mean(rows * rows, -1, keepdims=True) + EPSILON)


def place():
    return lax.axis_index("section"), lax.axis_index("ctx"), lax.axis_index("wt")


def greet(targets):
    barrier = pltpu.get_barrier_semaphore()
    for target in targets:
        pl.semaphore_signal(barrier, inc=1, device_id=target, device_id_type=MESH)
    pl.semaphore_wait(barrier, len(targets))


def remote(source, destination, send_sem, recv_sem, target):
    return pltpu.make_async_remote_copy(
        src_ref=source,
        dst_ref=destination,
        send_sem=send_sem,
        recv_sem=recv_sem,
        device_id=target,
        device_id_type=MESH,
    )


def exchange_kernel(n_wt, reduce, back, spread, rounded, *refs):
    refs = list(refs)
    section, ctx, wt = place()
    sibling = (1 - section, ctx, wt)
    peers = [(section, ctx, lax.rem(wt + k, n_wt)) for k in range(1, n_wt)]
    parts = refs.pop(0) if reduce else None
    rows_ref = refs.pop(0)
    stream_ref = refs.pop(0) if back else None
    gain_ref = refs.pop(0) if (back or spread) else None
    result_ref = refs.pop(0) if reduce else None
    gain_grad_ref = refs.pop(0) if back else None
    all_ref = refs.pop(0) if spread else None
    if reduce:
        from_sibling, from_peers, staged, rs_send, rs_recv = refs[:5]
        refs = refs[5:]
    if spread:
        ag_send, ag_recv = refs
    greet([sibling] + peers)
    own = section * n_wt + wt
    if reduce:
        sends = []
        order = [lax.rem(wt + k, n_wt) for k in range(1, n_wt)] + [wt]
        swaps = []
        for k, block in enumerate(order):
            copy = remote(
                parts.at[(1 - section) * n_wt + block], from_sibling.at[block], rs_send.at[k], rs_recv.at[k], sibling
            )
            copy.start()
            swaps.append(copy)
        for k, block in enumerate(order[:-1]):
            swaps[k].wait_recv()
            staged[k] = (parts[section * n_wt + block].astype(F32) + from_sibling[block].astype(F32)).astype(BF16)
            copy = remote(
                staged.at[k], from_peers.at[k], rs_send.at[n_wt + k], rs_recv.at[n_wt + k], peers[k]
            )
            copy.start()
            sends.append(copy)
        swaps[-1].wait_recv()
        total = parts[own].astype(F32) + from_sibling[wt].astype(F32)
        for k in range(n_wt - 1):
            sends[k].wait_recv()
            total = total + from_peers[k].astype(F32)
        if back:
            stream = stream_ref[...]
            scale = norm_scale(stream)
            weighted = gain_ref[...] * total
            gain_grad_ref[...] = jnp.sum(total * stream * scale, 0, keepdims=True)
            total = scale * weighted - stream * (scale * scale * scale) * jnp.mean(
                weighted * stream, -1, keepdims=True
            )
        total = rows_ref[...].astype(F32) + total
        if rounded:
            total = total.astype(BF16).astype(F32)
        result_ref[...] = total
    else:
        total = rows_ref[...].astype(F32)
    if spread:
        if spread == "norm":
            total = total * norm_scale(total) * gain_ref[...]
        all_ref[own] = total.astype(BF16)
        copies = []
        for k in range(1, n_wt):
            copy = remote(all_ref.at[own], all_ref.at[own], ag_send.at[k], ag_recv.at[k], peers[k - 1])
            copy.start()
            copies.append(copy)
        copy = remote(all_ref.at[own], all_ref.at[own], ag_send.at[0], ag_recv.at[0], sibling)
        copy.start()
        swaps_out = [copy]
        for k in range(1, n_wt):
            copies[k - 1].wait_recv()
            block = section * n_wt + lax.rem(wt + n_wt - k, n_wt)
            copy = remote(all_ref.at[block], all_ref.at[block], ag_send.at[n_wt + k], ag_recv.at[n_wt + k], sibling)
            copy.start()
            swaps_out.append(copy)
        for copy in swaps_out:
            copy.wait()
        for copy in copies:
            copy.wait_send()
    if reduce:
        for copy in swaps + sends:
            copy.wait_send()


VMEM = pl.BlockSpec(memory_space=pltpu.VMEM)


def exchange(number, parts, rows, stream=None, gain=None, spread=None, rounded=False):
    n_wt = lax.axis_size("wt")
    shape = rows.shape
    reduce, back = parts is not None, stream is not None
    operands = [
        member
        for member, wanted in ((parts, reduce), (rows, True), (stream, back), (gain, back or spread))
        if wanted
    ]
    outs = []
    scratch = []
    if reduce:
        outs.append(jax.ShapeDtypeStruct(shape, F32))
        scratch += [
            pltpu.VMEM((n_wt,) + shape, BF16),
            pltpu.VMEM((n_wt - 1,) + shape, BF16),
            pltpu.VMEM((n_wt - 1,) + shape, BF16),
            pltpu.SemaphoreType.DMA((2 * n_wt,)),
            pltpu.SemaphoreType.DMA((2 * n_wt,)),
        ]
    if back:
        outs.append(jax.ShapeDtypeStruct((1, shape[1]), F32))
    if spread:
        outs.append(jax.ShapeDtypeStruct((2 * n_wt,) + shape, BF16))
        scratch += [pltpu.SemaphoreType.DMA((2 * n_wt,)), pltpu.SemaphoreType.DMA((2 * n_wt,))]
    return pl.pallas_call(
        functools.partial(exchange_kernel, n_wt, reduce, back, spread, rounded),
        out_shape=outs,
        in_specs=[VMEM] * len(operands),
        out_specs=[VMEM] * len(outs),
        scratch_shapes=scratch,
        compiler_params=pltpu.CompilerParams(
            collective_id=number, has_side_effects=True, vmem_limit_bytes=40 << 20
        ),
        cost_estimate=pl.CostEstimate(flops=0, bytes_accessed=120 << 20, transcendentals=0),
    )(*operands)


def ctx_gather_kernel(n_ctx, own_ref, all_ref, send, recv, local):
    section, ctx, wt = place()
    peers = [(section, lax.rem(ctx + k, n_ctx), wt) for k in range(1, n_ctx)]
    greet(peers)
    keep = pltpu.make_async_copy(own_ref, all_ref.at[ctx], local)
    keep.start()
    copies = [
        remote(own_ref, all_ref.at[ctx], send.at[k], recv.at[k], peers[k]) for k in range(n_ctx - 1)
    ]
    for copy in copies:
        copy.start()
    keep.wait()
    for copy in copies:
        copy.wait()


def ctx_gather(number, own):
    n_ctx = lax.axis_size("ctx")
    return pl.pallas_call(
        functools.partial(ctx_gather_kernel, n_ctx),
        out_shape=jax.ShapeDtypeStruct((n_ctx,) + own.shape, own.dtype),
        in_specs=[VMEM],
        out_specs=VMEM,
        scratch_shapes=[
            pltpu.SemaphoreType.DMA((n_ctx - 1,)),
            pltpu.SemaphoreType.DMA((n_ctx - 1,)),
            pltpu.SemaphoreType.DMA,
        ],
        compiler_params=pltpu.CompilerParams(collective_id=number, has_side_effects=True),
    )(own)


def ctx_sum_kernel(n_ctx, parts_ref, total_ref, landed, send, recv):
    section, ctx, wt = place()
    peers = [(section, lax.rem(ctx + k, n_ctx), wt) for k in range(1, n_ctx)]
    greet(peers)
    copies = [
        remote(parts_ref.at[lax.rem(ctx + k, n_ctx)], landed.at[k - 1], send.at[k - 1], recv.at[k - 1], peers[k - 1])
        for k in range(1, n_ctx)
    ]
    for copy in copies:
        copy.start()
    total = parts_ref[ctx].astype(F32)
    for k, copy in enumerate(copies):
        copy.wait_recv()
        total = total + landed[k].astype(F32)
    total_ref[...] = total
    for copy in copies:
        copy.wait_send()


def ctx_sum(number, parts):
    n_ctx = lax.axis_size("ctx")
    return pl.pallas_call(
        functools.partial(ctx_sum_kernel, n_ctx),
        out_shape=jax.ShapeDtypeStruct(parts.shape[1:], F32),
        in_specs=[VMEM],
        out_specs=VMEM,
        scratch_shapes=[
            pltpu.VMEM((n_ctx - 1,) + parts.shape[1:], BF16),
            pltpu.SemaphoreType.DMA((n_ctx - 1,)),
            pltpu.SemaphoreType.DMA((n_ctx - 1,)),
        ],
        compiler_params=pltpu.CompilerParams(
            collective_id=number, has_side_effects=True, vmem_limit_bytes=40 << 20
        ),
    )(parts)


def small_sum_kernel(n_ctx, n_wt, parts_ref, total_ref, landed, summed, from_sibling, send, recv):
    section, ctx, wt = place()
    count = n_ctx * n_wt
    own = ctx * n_wt + wt
    blocks = [lax.rem(own + k, count) for k in range(1, count)]
    peers = [(section, block // n_wt, lax.rem(block, n_wt)) for block in blocks]
    sibling = (1 - section, ctx, wt)
    greet([sibling] + peers)
    copies = [
        remote(parts_ref.at[blocks[k]], landed.at[k], send.at[k], recv.at[k], peers[k]) for k in range(count - 1)
    ]
    for copy in copies:
        copy.start()
    total = parts_ref[own]
    for k, copy in enumerate(copies):
        copy.wait_recv()
        total = total + landed[k]
    summed[...] = total
    swap = remote(
        summed.at[1 - section], from_sibling, send.at[count - 1], recv.at[count - 1], sibling
    )
    swap.start()
    swap.wait()
    total_ref[...] = summed[section] + from_sibling[...]
    for copy in copies:
        copy.wait_send()


def small_sum(number, parts):
    n_ctx, n_wt = lax.axis_size("ctx"), lax.axis_size("wt")
    count = n_ctx * n_wt
    return pl.pallas_call(
        functools.partial(small_sum_kernel, n_ctx, n_wt),
        out_shape=jax.ShapeDtypeStruct(parts.shape[2:], F32),
        in_specs=[VMEM],
        out_specs=VMEM,
        scratch_shapes=[
            pltpu.VMEM((count - 1,) + parts.shape[1:], F32),
            pltpu.VMEM(parts.shape[1:], F32),
            pltpu.VMEM(parts.shape[2:], F32),
            pltpu.SemaphoreType.DMA((count,)),
            pltpu.SemaphoreType.DMA((count,)),
        ],
        compiler_params=pltpu.CompilerParams(
            collective_id=number, has_side_effects=True, vmem_limit_bytes=40 << 20
        ),
    )(parts)


def turn(values, cosine, sine, heads):
    pieces = []
    for head in range(heads):
        a = values[:, head * 64 : head * 64 + 32]
        b = values[:, head * 64 + 32 : head * 64 + 64]
        pieces += [a * cosine - b * sine, b * cosine + a * sine]
    return jnp.concatenate(pieces, -1)


def allowed_pairs(q_pos, q_seg, k_pos, k_seg):
    return ((k_seg[None, :] == 0) | (k_seg[None, :] == q_seg[:, None])) & (k_pos[None, :] <= q_pos[:, None])


def attend(query, pairs, q_pos, q_seg, k_pos, k_seg):
    logits = jnp.einsum("hqd,kd->hqk", query, pairs[:, :64], preferred_element_type=F32) * (1.0 / HEAD_SIZE)
    allowed = allowed_pairs(q_pos, q_seg, k_pos, k_seg)[None]
    logits = jnp.where(allowed, logits, MASKED)
    largest = jnp.max(logits, -1, keepdims=True)
    expos = jnp.exp(logits - largest)
    total = jnp.sum(expos, -1, keepdims=True)
    probs = (expos / total).astype(BF16)
    out = jnp.einsum("hqk,kd->hqd", probs, pairs[:, 64:], preferred_element_type=F32)
    return out, largest + jnp.log(total)


def attend_back(query, pairs, q_pos, q_seg, k_pos, k_seg, log_total, out, d_out):
    logits = jnp.einsum("hqd,kd->hqk", query, pairs[:, :64], preferred_element_type=F32) * (1.0 / HEAD_SIZE)
    allowed = allowed_pairs(q_pos, q_seg, k_pos, k_seg)[None]
    probs = jnp.where(allowed, jnp.exp(logits - log_total), 0.0)
    delta = jnp.sum(d_out.astype(F32) * out, -1, keepdims=True)
    d_probs = jnp.einsum("hqd,kd->hqk", d_out, pairs[:, 64:], preferred_element_type=F32)
    d_scores = (probs * (d_probs - delta)).astype(BF16)
    d_query = jnp.einsum("hqk,kd->hqd", d_scores, pairs[:, :64], preferred_element_type=F32) * (1.0 / HEAD_SIZE)
    d_keys = jnp.einsum("hqk,hqd->kd", d_scores, query, preferred_element_type=F32) * (1.0 / HEAD_SIZE)
    d_values = jnp.einsum("hqk,hqd->kd", probs.astype(BF16), d_out, preferred_element_type=F32)
    return d_query, jnp.concatenate([d_keys, d_values], -1)


def heads_first(rows, micro_count):
    count = rows.shape[0] // micro_count
    return jnp.transpose(rows.reshape(micro_count, count, -1, HEAD_SIZE), (0, 2, 1, 3))


def rows_first(heads):
    micro_count, h, q, d = heads.shape
    return jnp.transpose(heads, (0, 2, 1, 3)).reshape(micro_count * q, h * d)


def shards(tokens, cotangent, blocks, routes, norm_gain, w_query, key_value_weight, w_attn_out, router, w_in, w_down):
    section, ctx, wt = place()
    n_ctx, n_wt, layers = lax.axis_size("ctx"), lax.axis_size("wt"), lax.axis_size("section")
    micro_count, share, width = tokens.shape
    per_ctx = routes.shape[2]
    seq_len = per_ctx * n_ctx
    experts = w_in.shape[1] // 2
    n_experts = router.shape[2]
    q_cols = w_query.shape[2] // 2
    heads = q_cols // HEAD_SIZE
    depth = w_query.shape[1]

    block_len = seq_len // blocks.shape[1]
    placed = (blocks[:, :, None] * block_len + jnp.arange(block_len, dtype=jnp.int32)[None, None, :]).reshape(
        micro_count, seq_len
    )
    later = (jnp.arange(micro_count) > 0)[:, None]
    k_pos = jnp.where(later, seq_len + placed % CONT_LEN, placed)
    k_seg = jnp.where(later, 1 + placed // CONT_LEN, 0)
    q_pos = lax.dynamic_slice_in_dim(k_pos, ctx * per_ctx, per_ctx, 1)
    q_seg = lax.dynamic_slice_in_dim(k_seg, ctx * per_ctx, per_ctx, 1)
    inverse = jnp.power(ROPE_BASE, -jnp.arange(HEAD_SIZE // 2, dtype=F32) * 2.0 / HEAD_SIZE)
    angles = q_pos.reshape(-1).astype(F32)[:, None] * inverse[None, :]
    cosine, sine = jnp.cos(angles), jnp.sin(angles)

    def swap(values):
        return lax.ppermute(values, "section", [(0, 1), (1, 0)])

    def by_layer(halves):
        mine = lax.dynamic_index_in_dim(halves, section, 0, False)
        other = swap(lax.dynamic_index_in_dim(halves, 1 - section, 0, False))
        return [jnp.where(section == layer, mine, other) for layer in range(2)]

    def side_by_side(values):
        halves = values.reshape((2, experts) + values.shape[1:])
        return jnp.concatenate([halves[:, e] for e in range(experts)], -1)

    def to_owner(first, second):
        mine = jnp.where(section == 0, first, second)
        other = swap(jnp.where(section == 0, second, first))
        return jnp.where(section == 0, mine, other), jnp.where(section == 0, other, mine)

    attn_pack = jnp.concatenate(
        [
            jnp.transpose(w_query[0].reshape(depth, 2, q_cols), (1, 0, 2)),
            jnp.transpose(key_value_weight[0], (1, 0, 2)),
            jnp.transpose(w_attn_out[0].reshape(2, q_cols, depth), (0, 2, 1)),
        ],
        -1,
    )
    attn_pack = by_layer(attn_pack)
    in_pack = by_layer(side_by_side(w_in[0]))
    down_pack = by_layer(side_by_side(w_down[0]))
    route_pack = lax.all_gather(routes[0], "section", axis=0)
    gain_pack = lax.all_gather(norm_gain[0], "section", axis=0)
    router_pack = lax.all_gather(router[0], "section", axis=0)

    def packed(in_part, down_part):
        wide = in_part.shape[1]
        rest = down_part[:, wide:]
        half = rest.shape[0] // 2
        return jnp.concatenate(
            [in_part, down_part[:, :wide], jnp.concatenate([rest[:half], rest[half:]], 1)], 0
        )

    def unpacked(values, in_rows, down_rows):
        wide = values.shape[-1]
        n = values.shape[0]
        rest = values[:, in_rows + down_rows :]
        rest = jnp.concatenate([rest[..., : wide // 2], rest[..., wide // 2 :]], 1)
        down_part = jnp.concatenate([values[:, in_rows : in_rows + down_rows], rest], 2)
        return values[:, :in_rows].reshape(n * in_rows, wide), down_part.reshape(n * down_rows, -1)

    def after(value, earlier):
        return value if earlier is None else lax.optimization_barrier((value, earlier))[0]

    in_rows, down_rows = w_in.shape[2], w_down.shape[2]
    attn_full, in_full, down_full = [], [], []
    last = None

    def gather_experts(pack):
        full = lax.all_gather(pack, "ctx", axis=0, tiled=True)
        one, two = unpacked(full.reshape(n_ctx, -1, full.shape[1]), in_rows, down_rows)
        in_full.append(one)
        down_full.append(two)

    moe_pack = [packed(in_pack[layer], down_pack[layer]) for layer in range(2)]
    attn_full = [lax.all_gather(member, "ctx", axis=0, tiled=True) for member in attn_pack]
    gather_experts(moe_pack[0])

    my_first = wt * 2 * experts + section * experts
    n_rows = micro_count * per_ctx

    def routed(layer):
        names = route_pack[layer].reshape(n_rows, -1)
        return jnp.any(names[:, :, None] == jnp.arange(n_experts, dtype=jnp.int32)[None, None, :], 1)

    def full_rows(values):
        return values.reshape(n_rows, width)

    def blocked(values):
        return values.reshape(2 * n_wt, share, width).astype(BF16)

    stream = lax.dynamic_index_in_dim(tokens, section, 0, False).astype(F32)
    top = lax.dynamic_index_in_dim(cotangent, section, 0, False).astype(F32)

    (normed_in,) = exchange(0, None, stream, gain=gain_pack[0, 0:1], spread="norm")
    (d_mixed,) = exchange(1, None, top, gain=gain_pack[0, 0:1], spread="plain")
    saved = []
    outputs = []
    for layer in range(2):
        rows_in = full_rows(normed_in)
        weights = attn_full[layer]
        mixed_heads = dot(rows_in, weights[:, : q_cols + 2 * HEAD_SIZE], ((1,), (0,)))
        turned = turn(mixed_heads[:, : q_cols + HEAD_SIZE], cosine, sine, heads + 1)
        queries = turned[:, :q_cols].astype(BF16)
        own_pairs = jnp.concatenate([turned[:, q_cols:], mixed_heads[:, q_cols + HEAD_SIZE :]], -1).astype(BF16)
        pairs = ctx_gather(2 + layer, own_pairs)
        pairs = jnp.transpose(
            pairs.reshape(n_ctx, micro_count, per_ctx, 2 * HEAD_SIZE), (1, 0, 2, 3)
        ).reshape(micro_count * seq_len, 2 * HEAD_SIZE)
        by_head = heads_first(queries, micro_count)
        outs = [
            attend(
                by_head[m],
                pairs[: (m + 1) * seq_len],
                q_pos[m],
                q_seg[m],
                k_pos.reshape(-1)[: (m + 1) * seq_len],
                k_seg.reshape(-1)[: (m + 1) * seq_len],
            )
            for m in range(micro_count)
        ]
        out_full = jnp.stack([member[0] for member in outs])
        log_total = [member[1] for member in outs]
        attended = rows_first(out_full).astype(BF16)
        partial = dot(attended, weights[:, q_cols + 2 * HEAD_SIZE :], ((1,), (1,)))
        middle, normed_mid = exchange(
            4 + layer, blocked(partial), stream, gain=gain_pack[layer, 1:2], spread="norm"
        )
        if layer == 0:
            normed_mid, second = lax.optimization_barrier((normed_mid, moe_pack[1]))
            gather_experts(second)
        rows_mid = full_rows(normed_mid)
        logits = dot(rows_mid, router_pack[layer], ((1,), (0,)))
        hit = routed(layer)
        masked = jnp.where(hit, logits, MASKED)
        expos = jnp.where(hit, jnp.exp(masked - jnp.max(masked, 1, keepdims=True)), 0.0)
        gates = expos / jnp.sum(expos, 1, keepdims=True)
        my_gates = lax.dynamic_slice_in_dim(gates, my_first, experts, 1)
        gate_up = dot(rows_mid, in_full[layer], ((1,), (0,)))
        weighted_hidden = []
        partial = 0.0
        for e in range(experts):
            gate_part = gate_up[:, 2 * e * FF : (2 * e + 1) * FF]
            up_part = gate_up[:, (2 * e + 1) * FF : (2 * e + 2) * FF]
            weighted_hidden.append((jax.nn.silu(gate_part) * up_part * my_gates[:, e : e + 1]).astype(BF16))
            partial = partial + dot(
                weighted_hidden[e], down_full[layer][:, e * width : (e + 1) * width], ((1,), (0,))
            )
        saved.append(
            dict(
                stream=stream,
                middle=middle,
                rows_in=rows_in,
                rows_mid=rows_mid,
                queries=by_head,
                pairs=pairs,
                out_full=out_full,
                attended=attended,
                log_total=log_total,
                gates=gates,
                my_gates=my_gates,
                gate_up=gate_up,
                weighted_hidden=weighted_hidden,
            )
        )
        if layer == 0:
            stream, normed_in = exchange(
                6, blocked(partial), middle, gain=gain_pack[1, 0:1], spread="norm", rounded=True
            )
        else:
            (stream,) = exchange(7, blocked(partial), middle, rounded=True)
        outputs.append(stream.astype(BF16))

    upstream = top
    last = None
    grads_in = [None, None]
    attn_grads = [None, None]
    moe_grads = [None, None]
    small = [None, None]
    for layer in (1, 0):
        kept = saved[layer]
        rows_d = full_rows(d_mixed)
        gate_up = kept["gate_up"]
        d_gate_up = []
        down_grad = []
        d_weight = []
        for e in range(experts):
            d_weighted = dot(rows_d, down_full[layer][:, e * width : (e + 1) * width], ((1,), (1,)))
            gate_part = gate_up[:, 2 * e * FF : (2 * e + 1) * FF]
            up_part = gate_up[:, (2 * e + 1) * FF : (2 * e + 2) * FF]
            sigmoid = jax.nn.sigmoid(gate_part)
            activated = gate_part * sigmoid
            d_weight.append(jnp.sum((activated * up_part).astype(BF16).astype(F32) * d_weighted, -1, keepdims=True))
            d_hidden = d_weighted * kept["my_gates"][:, e : e + 1]
            d_gate_up.append(
                (d_hidden * up_part * (sigmoid * (1.0 + gate_part * (1.0 - sigmoid)))).astype(BF16)
            )
            d_gate_up.append((d_hidden * activated).astype(BF16))
            down_grad.append(dot(kept["weighted_hidden"][e], rows_d, ((0,), (0,))).astype(BF16))
        d_gate_up = jnp.concatenate(d_gate_up, -1)
        d_weight = jnp.concatenate(d_weight, -1)
        down_grad = jnp.concatenate(down_grad, -1)
        in_grad = dot(kept["rows_mid"], d_gate_up, ((0,), (0,))).astype(BF16)
        partial = dot(d_gate_up, in_full[layer], ((1,), (1,)))
        packed_grad = jax.vmap(packed)(
            in_grad.reshape(n_ctx, in_rows, -1), down_grad.reshape(n_ctx, down_rows, -1)
        )
        if layer == 0:
            partial, packed_grad, moe_grads[1], attn_grads[1] = lax.optimization_barrier(
                (partial, packed_grad, moe_grads[1], attn_grads[1])
            )
        else:
            partial, packed_grad = lax.optimization_barrier((partial, packed_grad))
        last = lax.psum_scatter(after(packed_grad, last), "ctx", scatter_dimension=0, tiled=False)
        moe_grads[layer] = last
        terms = kept["my_gates"] * d_weight
        placed_terms = lax.dynamic_update_slice_in_dim(jnp.zeros_like(kept["gates"]), terms, my_first, 1)
        d_logits = placed_terms - kept["gates"] * jnp.sum(terms, 1, keepdims=True)
        partial = partial + lax.dot_general(
            d_logits,
            router_pack[layer].astype(F32),
            (((1,), (1,)), ((), ())),
            precision=lax.Precision.HIGHEST,
            preferred_element_type=F32,
        )
        router_grad = lax.dot_general(
            d_logits,
            kept["rows_mid"].astype(F32),
            (((0,), (0,)), ((), ())),
            precision=lax.Precision.HIGHEST,
            preferred_element_type=F32,
        )
        d_middle, gain_grad_mid, d_attn = exchange(
            8 + layer, blocked(partial), upstream, kept["middle"], gain_pack[layer, 1:2], spread="plain"
        )
        rows_a = full_rows(d_attn)
        weights = attn_full[layer]
        d_attended = dot(rows_a, weights[:, q_cols + 2 * HEAD_SIZE :], ((1,), (0,))).astype(BF16)
        out_grad = dot(rows_a, kept["attended"], ((0,), (0,)))
        d_heads = heads_first(d_attended, micro_count)
        d_queries = []
        d_pairs = 0.0
        for m in range(micro_count):
            d_query, d_pair = attend_back(
                kept["queries"][m],
                kept["pairs"][: (m + 1) * seq_len],
                q_pos[m],
                q_seg[m],
                k_pos.reshape(-1)[: (m + 1) * seq_len],
                k_seg.reshape(-1)[: (m + 1) * seq_len],
                kept["log_total"][m],
                kept["out_full"][m],
                d_heads[m],
            )
            d_queries.append(d_query)
            d_pairs = d_pairs + jnp.pad(d_pair, ((0, (micro_count - 1 - m) * seq_len), (0, 0)))
        d_pairs = jnp.transpose(
            d_pairs.reshape(micro_count, n_ctx, per_ctx, 2 * HEAD_SIZE), (1, 0, 2, 3)
        ).reshape(n_ctx, n_rows, 2 * HEAD_SIZE)
        d_own = ctx_sum(10 + layer, d_pairs.astype(BF16))
        raw = jnp.concatenate([rows_first(jnp.stack(d_queries)), d_own[:, :HEAD_SIZE]], -1)
        raw = jnp.concatenate([turn(raw, cosine, -sine, heads + 1), d_own[:, HEAD_SIZE:]], -1).astype(BF16)
        heads_grad = dot(kept["rows_in"], raw, ((0,), (0,)))
        last = lax.psum_scatter(
            after(jnp.concatenate([heads_grad, out_grad], -1).astype(BF16), last),
            "ctx",
            scatter_dimension=0,
            tiled=True,
        )
        attn_grads[layer] = last
        partial = dot(raw, weights[:, : q_cols + 2 * HEAD_SIZE], ((1,), (1,)))
        if layer == 0:
            partial, moe_grads[0] = lax.optimization_barrier((partial, moe_grads[0]))
        if layer == 1:
            upstream, gain_grad_in, d_mixed = exchange(
                12, blocked(partial), d_middle, kept["stream"], gain_pack[1, 0:1], spread="plain", rounded=True
            )
        else:
            upstream, gain_grad_in = exchange(
                13, blocked(partial), d_middle, kept["stream"], gain_pack[0, 0:1], rounded=True
            )
        grads_in[layer] = upstream.astype(BF16)
        small[layer] = jnp.concatenate([gain_grad_in, gain_grad_mid, router_grad], 0)

    piece = width // (n_ctx * n_wt)
    small_parts = jnp.transpose(
        jnp.stack(small).reshape(2, small[0].shape[0], n_ctx * n_wt, piece), (2, 0, 1, 3)
    )
    small_parts = jnp.pad(small_parts, ((0, 0), (0, 0), (0, -small[0].shape[0] % 8), (0, -piece % 128)))
    small_total = small_sum(14, small_parts)[: small[0].shape[0], :piece]
    out_pair = jnp.stack(to_owner(outputs[0], outputs[1]))
    grad_pair = jnp.stack(to_owner(grads_in[0], grads_in[1]))
    attn_first, attn_second = [member.astype(F32) for member in to_owner(attn_grads[0], attn_grads[1])]
    kv_at = q_cols
    out_at = q_cols + 2 * HEAD_SIZE
    grad_query = jnp.concatenate([attn_first[:, :kv_at], attn_second[:, :kv_at]], -1)
    grad_kv = jnp.stack([attn_first[:, kv_at:out_at], attn_second[:, kv_at:out_at]], 1)
    grad_out = jnp.concatenate([jnp.transpose(attn_first[:, out_at:]), jnp.transpose(attn_second[:, out_at:])], 0)

    def stacked(halves):
        columns = halves[0].shape[1] // experts
        return jnp.stack(
            [half[:, e * columns : (e + 1) * columns] for half in halves for e in range(experts)]
        ).astype(F32)

    moe_pair = [unpacked(member[None], in_rows, down_rows) for member in to_owner(moe_grads[0], moe_grads[1])]
    grad_in = stacked([member[0] for member in moe_pair])
    grad_down = stacked([member[1] for member in moe_pair])
    return (
        out_pair[None],
        grad_pair[None],
        small_total[:2][None],
        grad_query[None],
        grad_kv[None],
        grad_out[None],
        jnp.transpose(small_total[2:])[None],
        grad_in[None],
        grad_down[None],
    )


def solution(mesh):
    return jax.shard_map(
        shards,
        mesh=mesh,
        in_specs=(
            P(None, ("ctx", "wt"), None),
            P(None, ("ctx", "wt"), None),
            P(),
            P("section", None, "ctx", None),
            P("section", None, None),
            P("section", "ctx", "wt"),
            P("section", "ctx", "wt", None),
            P("section", "wt", "ctx"),
            P("section", None, None),
            P("section", "wt", "ctx", None),
            P("section", "wt", "ctx", None),
        ),
        out_specs=(
            P("section", None, ("ctx", "wt"), None),
            P("section", None, ("ctx", "wt"), None),
            P("section", None, ("ctx", "wt")),
            P("section", "ctx", "wt"),
            P("section", "ctx", "wt", None),
            P("section", "wt", "ctx"),
            P("section", ("ctx", "wt"), None),
            P("section", "wt", "ctx", None),
            P("section", "wt", "ctx", None),
        ),
        check_vma=False,
    )
```

```python
import functools

import jax
import jax.numpy as jnp
from jax import lax
from jax.experimental import pallas as pl
from jax.experimental.pallas import tpu as pltpu
from jax.sharding import PartitionSpec as P

HEAD_SIZE = 64
FF = 512
CONT_LEN = 1024
EPSILON = 1e-06
ROPE_BASE = 10000.0
MASKED = -1e30
MESH = pl.DeviceIdType.MESH
F32 = jnp.float32
BF16 = jnp.bfloat16


def dot(left, right, contract):
    return lax.dot_general(left, right, (contract, ((), ())), preferred_element_type=F32)


def norm_scale(rows):
    return lax.rsqrt(jnp.mean(rows * rows, -1, keepdims=True) + EPSILON)


def place():
    return lax.axis_index("section"), lax.axis_index("ctx"), lax.axis_index("wt")


def greet(targets):
    barrier = pltpu.get_barrier_semaphore()
    for target in targets:
        pl.semaphore_signal(barrier, inc=1, device_id=target, device_id_type=MESH)
    pl.semaphore_wait(barrier, len(targets))


def remote(source, destination, send_sem, recv_sem, target):
    return pltpu.make_async_remote_copy(
        src_ref=source,
        dst_ref=destination,
        send_sem=send_sem,
        recv_sem=recv_sem,
        device_id=target,
        device_id_type=MESH,
    )


def exchange_kernel(n_ctx, n_wt, reduce, back, spread, rounded, ride, *refs):
    refs = list(refs)
    section, ctx, wt = place()
    sibling = (1 - section, ctx, wt)
    right = (section, ctx, jnp.minimum(wt + 1, n_wt - 1))
    left = (section, ctx, jnp.maximum(wt - 1, 0))
    has_right, has_left = wt < n_wt - 1, wt > 0
    peers = [(section, lax.rem(ctx + k, n_ctx), wt) for k in range(1, n_ctx)]
    parts = refs.pop(0) if reduce else None
    rows_ref = refs.pop(0)
    stream_ref = refs.pop(0) if back else None
    gain_ref = refs.pop(0) if (back or spread) else None
    ride_ref = refs.pop(0) if ride else None
    result_ref = refs.pop(0) if reduce else None
    gain_grad_ref = refs.pop(0) if back else None
    all_ref = refs.pop(0) if spread else None
    rode_ref = refs.pop(0) if ride else None
    if reduce:
        from_sibling, in_right, in_left, out_right, out_left, swap_send, swap_recv, rs_send, rs_recv = refs[:9]
        refs = refs[9:]
    if spread:
        ag_send, ag_recv, pass_send, pass_recv = refs[:4]
        refs = refs[4:]
    if ride:
        landed, ride_send, ride_recv, ride_local = refs

    barrier = pltpu.get_barrier_semaphore()

    def hail(target):
        pl.semaphore_signal(barrier, inc=1, device_id=target, device_id_type=MESH)

    hail(sibling)
    pl.when(has_right)(lambda: hail(right))
    pl.when(has_left)(lambda: hail(left))
    if ride:
        for peer in peers:
            hail(peer)
    met = 1 + (n_ctx - 1 if ride else 0)
    pl.semaphore_wait(barrier, met + has_right.astype(jnp.int32) + has_left.astype(jnp.int32))

    finish = []

    def launch(condition, copy):
        pl.when(condition)(copy.start)
        finish.append((condition, copy))

    if reduce:
        order = []
        for step in range(n_wt - 1):
            order += [n_wt - 1 - step, step]
        order = list(dict.fromkeys(order))
        swaps = {}
        for block in order:
            swaps[block] = remote(
                parts.at[(1 - section) * n_wt + block],
                from_sibling.at[block],
                swap_send.at[block],
                swap_recv.at[block],
                sibling,
            )
            swaps[block].start()
    if ride == "gather":
        keep = pltpu.make_async_copy(ride_ref, rode_ref.at[ctx], ride_local)
        keep.start()
        riders = [
            remote(ride_ref, rode_ref.at[ctx], ride_send.at[k], ride_recv.at[k], peers[k]) for k in range(n_ctx - 1)
        ]
    elif ride == "sum":
        riders = [
            remote(
                ride_ref.at[lax.rem(ctx + 1 + k, n_ctx)], landed.at[k], ride_send.at[k], ride_recv.at[k], peers[k]
            )
            for k in range(n_ctx - 1)
        ]
    if ride:
        for copy in riders:
            copy.start()

    if reduce:

        def chip_sum(block):
            return parts[section * n_wt + block].astype(F32) + from_sibling[block].astype(F32)

        def send_on(block, inward, outward, first, target, number):
            swaps[block].wait_recv()
            outward[block] = chip_sum(block).astype(BF16)

            @pl.when(first)
            def _():
                remote(outward.at[block], inward.at[block], rs_send.at[number], rs_recv.at[number], target).wait_recv()
                outward[block] = (chip_sum(block) + inward[block].astype(F32)).astype(BF16)

            remote(outward.at[block], inward.at[block], rs_send.at[number], rs_recv.at[number], target).start()

        for step in range(n_wt - 1):
            far, near = n_wt - 1 - step, step
            pl.when(wt < far)(functools.partial(send_on, far, in_right, out_right, has_left, right, far))
            pl.when(wt > near)(functools.partial(send_on, near, in_left, out_left, has_right, left, n_wt + near))
        swap = remote(
            parts.at[(1 - section) * n_wt + wt], from_sibling.at[wt], swap_send.at[wt], swap_recv.at[wt], sibling
        )
        swap.wait_recv()
        result_ref[...] = chip_sum(wt)

        @pl.when(has_left)
        def _():
            remote(out_right.at[wt], in_right.at[wt], rs_send.at[wt], rs_recv.at[wt], right).wait_recv()
            result_ref[...] += in_right[wt].astype(F32)

        @pl.when(has_right)
        def _():
            remote(out_left.at[wt], in_left.at[wt], rs_send.at[n_wt + wt], rs_recv.at[n_wt + wt], left).wait_recv()
            result_ref[...] += in_left[wt].astype(F32)

        total = result_ref[...]
        if back:
            stream = stream_ref[...]
            scale = norm_scale(stream)
            weighted = gain_ref[...] * total
            gain_grad_ref[...] = jnp.sum(total * stream * scale, 0, keepdims=True)
            total = scale * weighted - stream * (scale * scale * scale) * jnp.mean(
                weighted * stream, -1, keepdims=True
            )
        total = rows_ref[...].astype(F32) + total
        if rounded:
            total = total.astype(BF16).astype(F32)
        result_ref[...] = total
    else:
        total = rows_ref[...].astype(F32)
    if spread:
        if spread == "norm":
            total = total * norm_scale(total) * gain_ref[...]
        own = section * n_wt + wt
        all_ref[own] = total.astype(BF16)

        def along(block, number, target):
            return remote(all_ref.at[block], all_ref.at[block], ag_send.at[number], ag_recv.at[number], target)

        def across(block, number):
            return remote(all_ref.at[block], all_ref.at[block], pass_send.at[number], pass_recv.at[number], sibling)

        always = wt >= 0
        launch(has_right, along(own, 1, right))
        launch(has_left, along(own, n_wt + 1, left))
        launch(always, across(own, 0))
        arrivals = [(always, across(own, 0))]
        for hop in range(1, n_wt):
            came_right = wt >= hop
            block = jnp.maximum(own - hop, 0)
            pl.when(came_right)(along(block, hop, right).wait_recv)
            if hop + 1 < n_wt:
                launch(came_right & has_right, along(block, hop + 1, right))
            launch(came_right, across(block, hop))
            arrivals.append((came_right, across(block, hop)))
            came_left = wt + hop < n_wt
            block = jnp.minimum(own + hop, 2 * n_wt - 1)
            pl.when(came_left)(along(block, n_wt + hop, left).wait_recv)
            if hop + 1 < n_wt:
                launch(came_left & has_left, along(block, n_wt + hop + 1, left))
            launch(came_left, across(block, n_wt + hop))
            arrivals.append((came_left, across(block, n_wt + hop)))
        for condition, copy in arrivals:
            pl.when(condition)(copy.wait_recv)
    if ride == "gather":
        keep.wait()
        for copy in riders:
            copy.wait()
    elif ride == "sum":
        total = ride_ref[ctx].astype(F32)
        for k, copy in enumerate(riders):
            copy.wait()
            total = total + landed[k].astype(F32)
        rode_ref[...] = total
    for condition, copy in finish:
        pl.when(condition)(copy.wait_send)
    if reduce:
        for block in order:
            swaps[block].wait_send()
        for block in range(n_wt):
            if block > 0:
                pl.when(wt < block)(
                    remote(out_right.at[block], in_right.at[block], rs_send.at[block], rs_recv.at[block], right).wait_send
                )
            if block < n_wt - 1:
                pl.when(wt > block)(
                    remote(
                        out_left.at[block], in_left.at[block], rs_send.at[n_wt + block], rs_recv.at[n_wt + block], left
                    ).wait_send
                )


VMEM = pl.BlockSpec(memory_space=pltpu.VMEM)


def exchange(number, parts, rows, stream=None, gain=None, spread=None, rounded=False, gather=None, add=None):
    n_ctx, n_wt = lax.axis_size("ctx"), lax.axis_size("wt")
    shape = rows.shape
    reduce, back = parts is not None, stream is not None
    ride = "gather" if gather is not None else "sum" if add is not None else None
    rider = gather if gather is not None else add
    operands = [
        member
        for member, wanted in (
            (parts, reduce),
            (rows, True),
            (stream, back),
            (gain, back or spread),
            (rider, ride),
        )
        if wanted
    ]
    outs = []
    scratch = []
    dma = pltpu.SemaphoreType.DMA
    if reduce:
        outs.append(jax.ShapeDtypeStruct(shape, F32))
        scratch += [pltpu.VMEM((n_wt,) + shape, BF16)] * 5
        scratch += [dma((n_wt,)), dma((n_wt,)), dma((2 * n_wt,)), dma((2 * n_wt,))]
    if back:
        outs.append(jax.ShapeDtypeStruct((1, shape[1]), F32))
    if spread:
        outs.append(jax.ShapeDtypeStruct((2 * n_wt,) + shape, BF16))
        scratch += [dma((2 * n_wt,))] * 4
    if ride == "gather":
        outs.append(jax.ShapeDtypeStruct((n_ctx,) + rider.shape, BF16))
        scratch += [pltpu.VMEM((8, 128), BF16), dma((n_ctx - 1,)), dma((n_ctx - 1,)), dma]
    elif ride == "sum":
        outs.append(jax.ShapeDtypeStruct(rider.shape[1:], F32))
        scratch += [pltpu.VMEM((n_ctx - 1,) + rider.shape[1:], BF16), dma((n_ctx - 1,)), dma((n_ctx - 1,)), dma]
    return pl.pallas_call(
        functools.partial(exchange_kernel, n_ctx, n_wt, reduce, back, spread, rounded, ride),
        out_shape=outs,
        in_specs=[VMEM] * len(operands),
        out_specs=[VMEM] * len(outs),
        scratch_shapes=scratch,
        compiler_params=pltpu.CompilerParams(
            collective_id=number, has_side_effects=True, vmem_limit_bytes=40 << 20
        ),
        cost_estimate=pl.CostEstimate(flops=0, bytes_accessed=110 << 20, transcendentals=0),
    )(*operands)


def ctx_gather_kernel(n_ctx, own_ref, all_ref, send, recv, local):
    section, ctx, wt = place()
    peers = [(section, lax.rem(ctx + k, n_ctx), wt) for k in range(1, n_ctx)]
    greet(peers)
    keep = pltpu.make_async_copy(own_ref, all_ref.at[ctx], local)
    keep.start()
    copies = [
        remote(own_ref, all_ref.at[ctx], send.at[k], recv.at[k], peers[k]) for k in range(n_ctx - 1)
    ]
    for copy in copies:
        copy.start()
    keep.wait()
    for copy in copies:
        copy.wait()


def ctx_gather(number, own):
    n_ctx = lax.axis_size("ctx")
    return pl.pallas_call(
        functools.partial(ctx_gather_kernel, n_ctx),
        out_shape=jax.ShapeDtypeStruct((n_ctx,) + own.shape, own.dtype),
        in_specs=[VMEM],
        out_specs=VMEM,
        scratch_shapes=[
            pltpu.SemaphoreType.DMA((n_ctx - 1,)),
            pltpu.SemaphoreType.DMA((n_ctx - 1,)),
            pltpu.SemaphoreType.DMA,
        ],
        compiler_params=pltpu.CompilerParams(collective_id=number, has_side_effects=True),
    )(own)


def ctx_sum_kernel(n_ctx, parts_ref, total_ref, landed, send, recv):
    section, ctx, wt = place()
    peers = [(section, lax.rem(ctx + k, n_ctx), wt) for k in range(1, n_ctx)]
    greet(peers)
    copies = [
        remote(parts_ref.at[lax.rem(ctx + k, n_ctx)], landed.at[k - 1], send.at[k - 1], recv.at[k - 1], peers[k - 1])
        for k in range(1, n_ctx)
    ]
    for copy in copies:
        copy.start()
    total = parts_ref[ctx].astype(F32)
    for k, copy in enumerate(copies):
        copy.wait_recv()
        total = total + landed[k].astype(F32)
    total_ref[...] = total
    for copy in copies:
        copy.wait_send()


def ctx_sum(number, parts):
    n_ctx = lax.axis_size("ctx")
    return pl.pallas_call(
        functools.partial(ctx_sum_kernel, n_ctx),
        out_shape=jax.ShapeDtypeStruct(parts.shape[1:], F32),
        in_specs=[VMEM],
        out_specs=VMEM,
        scratch_shapes=[
            pltpu.VMEM((n_ctx - 1,) + parts.shape[1:], BF16),
            pltpu.SemaphoreType.DMA((n_ctx - 1,)),
            pltpu.SemaphoreType.DMA((n_ctx - 1,)),
        ],
        compiler_params=pltpu.CompilerParams(
            collective_id=number, has_side_effects=True, vmem_limit_bytes=40 << 20
        ),
    )(parts)


def small_sum_kernel(n_ctx, n_wt, parts_ref, total_ref, landed, summed, from_sibling, send, recv):
    section, ctx, wt = place()
    count = n_ctx * n_wt
    own = ctx * n_wt + wt
    blocks = [lax.rem(own + k, count) for k in range(1, count)]
    peers = [(section, block // n_wt, lax.rem(block, n_wt)) for block in blocks]
    sibling = (1 - section, ctx, wt)
    greet([sibling] + peers)
    copies = [
        remote(parts_ref.at[blocks[k]], landed.at[k], send.at[k], recv.at[k], peers[k]) for k in range(count - 1)
    ]
    for copy in copies:
        copy.start()
    total = parts_ref[own]
    for k, copy in enumerate(copies):
        copy.wait_recv()
        total = total + landed[k]
    summed[...] = total
    swap = remote(
        summed.at[1 - section], from_sibling, send.at[count - 1], recv.at[count - 1], sibling
    )
    swap.start()
    swap.wait()
    total_ref[...] = summed[section] + from_sibling[...]
    for copy in copies:
        copy.wait_send()


def small_sum(number, parts):
    n_ctx, n_wt = lax.axis_size("ctx"), lax.axis_size("wt")
    count = n_ctx * n_wt
    return pl.pallas_call(
        functools.partial(small_sum_kernel, n_ctx, n_wt),
        out_shape=jax.ShapeDtypeStruct(parts.shape[2:], F32),
        in_specs=[VMEM],
        out_specs=VMEM,
        scratch_shapes=[
            pltpu.VMEM((count - 1,) + parts.shape[1:], F32),
            pltpu.VMEM(parts.shape[1:], F32),
            pltpu.VMEM(parts.shape[2:], F32),
            pltpu.SemaphoreType.DMA((count,)),
            pltpu.SemaphoreType.DMA((count,)),
        ],
        compiler_params=pltpu.CompilerParams(
            collective_id=number, has_side_effects=True, vmem_limit_bytes=40 << 20
        ),
    )(parts)


LANES = 2 * HEAD_SIZE
HEADS = 3


def roll(values, by):
    return pltpu.roll(values, by, 1)


def lower_half(shape):
    return lax.broadcasted_iota(jnp.int32, shape, 1) < HEAD_SIZE


def turned(values, cosine, sine):
    first = lax.rem(lax.broadcasted_iota(jnp.int32, values.shape, 1), HEAD_SIZE) < HEAD_SIZE // 2
    half = HEAD_SIZE // 2
    return values * cosine + jnp.where(first, roll(values, LANES - half), roll(values, half)) * sine


def visible(key_place, query_place, query_start):
    return (key_place <= query_place) & (key_place >= query_start)


def attend_kernel(
    n_ctx,
    x_ref,
    w_ref,
    cos_ref,
    sin_ref,
    key_place,
    query_place,
    query_start,
    part_ref,
    q_ref,
    pairs_ref,
    out_ref,
    lse_ref,
    att_ref,
    top_ref,
    sum_ref,
    acc_ref,
    send,
    recv,
):
    section, ctx, wt = place()
    peers = [(section, lax.rem(ctx + k, n_ctx), wt) for k in range(1, n_ctx)]
    greet(peers)
    rows = x_ref.shape[0] // 2
    low = lower_half((2 * rows, LANES))
    mixed = dot(x_ref[...], w_ref[:, : 3 * LANES], ((1,), (0,)))
    cosine, sine = cos_ref[...], sin_ref[...]
    first = turned(mixed[:, :LANES], cosine, sine)
    second = turned(mixed[:, LANES : 2 * LANES], cosine, sine)
    pairs_ref[ctx] = jnp.where(low, roll(second, HEAD_SIZE), roll(mixed[:, 2 * LANES :], HEAD_SIZE)).astype(BF16)

    def passing(k):
        return remote(
            pairs_ref.at[ctx], pairs_ref.at[ctx], send.at[k], recv.at[k], (section, lax.rem(ctx + k, n_ctx), wt)
        )

    for k in range(1, n_ctx):
        passing(k).start()
    for h, part in enumerate((first, roll(first, HEAD_SIZE), second)):
        scaled = jnp.where(low, part * (1.0 / HEAD_SIZE), 0.0).astype(BF16)
        q_ref[0, h] = scaled[:rows]
        q_ref[1, h] = scaled[rows:]
    top_ref[...] = jnp.full(top_ref.shape, MASKED, F32)
    sum_ref[...] = jnp.zeros(sum_ref.shape, F32)
    acc_ref[...] = jnp.zeros(acc_ref.shape, F32)

    def block(c, m, j):
        keys = pairs_ref[c, j * rows : (j + 1) * rows, :]
        if m == j:
            seen = visible(key_place[c, j * rows : (j + 1) * rows, :], query_place[m], query_start[m])
        for h in range(HEADS):
            logits = dot(keys, q_ref[m, h], ((1,), (1,)))
            if m == j:
                logits = jnp.where(seen, logits, MASKED)
            before = top_ref[m, h]
            top = jnp.maximum(before, jnp.max(logits, 0, keepdims=True))
            expos = jnp.exp(logits - top)
            shrink = jnp.exp(before - top)
            top_ref[m, h] = top
            sum_ref[m, h] = sum_ref[m, h] * shrink + jnp.sum(expos, 0, keepdims=True)
            acc_ref[m, h] = acc_ref[m, h] * shrink + dot(keys, expos.astype(BF16), ((0,), (0,)))

    def blocks_of(c):
        block(c, 0, 0)
        block(c, 1, 1)
        block(c, 1, 0)

    blocks_of(ctx)

    @pl.loop(1, n_ctx)
    def _(k):
        passing(k).wait_recv()
        blocks_of(lax.rem(ctx + n_ctx - k, n_ctx))

    low = lower_half((rows, LANES))
    for m in range(2):
        outs = []
        for h in range(HEADS):
            lse_ref[m, h] = top_ref[m, h] + jnp.log(sum_ref[m, h])
            outs.append(jnp.transpose(acc_ref[m, h] / sum_ref[m, h]))
            out_ref[m, h] = outs[h]
        att_ref[m * rows : (m + 1) * rows, :LANES] = jnp.where(low, 0.0, outs[0]).astype(BF16)
        att_ref[m * rows : (m + 1) * rows, LANES:] = jnp.where(low, roll(outs[1], HEAD_SIZE), outs[2]).astype(BF16)
    part_ref[...] = dot(att_ref[...], w_ref[:, 2 * LANES :], ((1,), (1,))).astype(BF16)
    for k in range(1, n_ctx):
        passing(k).wait_send()


def attend(number, rows_in, weights, tables):
    n_ctx = lax.axis_size("ctx")
    n_rows, width = rows_in.shape
    rows = n_rows // 2
    dma = pltpu.SemaphoreType.DMA
    return pl.pallas_call(
        functools.partial(attend_kernel, n_ctx),
        out_shape=[
            jax.ShapeDtypeStruct((n_rows, width), BF16),
            jax.ShapeDtypeStruct((2, HEADS, rows, LANES), BF16),
            jax.ShapeDtypeStruct((n_ctx, n_rows, LANES), BF16),
            jax.ShapeDtypeStruct((2, HEADS, rows, LANES), F32),
            jax.ShapeDtypeStruct((2, HEADS, 1, rows), F32),
            jax.ShapeDtypeStruct((n_rows, 2 * LANES), BF16),
        ],
        in_specs=[VMEM] * 7,
        out_specs=[VMEM] * 6,
        scratch_shapes=[
            pltpu.VMEM((2, HEADS, 1, rows), F32),
            pltpu.VMEM((2, HEADS, 1, rows), F32),
            pltpu.VMEM((2, HEADS, LANES, rows), F32),
            dma((n_ctx,)),
            dma((n_ctx,)),
        ],
        compiler_params=pltpu.CompilerParams(
            collective_id=number, has_side_effects=True, vmem_limit_bytes=40 << 20
        ),
        cost_estimate=pl.CostEstimate(flops=0, bytes_accessed=70 << 20, transcendentals=0),
    )(rows_in, weights, *tables)


def attend_back_kernel(
    n_ctx,
    a_ref,
    w_ref,
    cos_ref,
    sin_ref,
    key_place,
    query_place,
    query_start,
    q_ref,
    pairs_ref,
    out_ref,
    lse_ref,
    part_ref,
    raw_ref,
    do_ref,
    delta_ref,
    dq_ref,
    dkv_ref,
    own_ref,
    landed,
    send,
    recv,
):
    section, ctx, wt = place()
    peers = [(section, lax.rem(ctx + k, n_ctx), wt) for k in range(1, n_ctx)]
    greet(peers)
    rows = a_ref.shape[0] // 2
    low = lower_half((2 * rows, LANES))
    d_att = dot(a_ref[...], w_ref[:, 2 * LANES :], ((1,), (0,)))
    for h, part in enumerate((d_att[:, :LANES], roll(d_att[:, LANES:], HEAD_SIZE), d_att[:, LANES:])):
        d_out = jnp.where(low, 0.0, part).astype(BF16)
        for m in range(2):
            do_ref[m, h] = d_out[m * rows : (m + 1) * rows]
            product = do_ref[m, h].astype(F32) * out_ref[m, h]
            delta_ref[m, h] = jnp.sum(jnp.transpose(product), 0, keepdims=True)
    dq_ref[...] = jnp.zeros(dq_ref.shape, F32)

    def block(c, j):
        keys = pairs_ref[c, j * rows : (j + 1) * rows, :]
        total = jnp.zeros((rows, LANES), F32)
        for m in range(j, 2):
            if m == j:
                seen = visible(key_place[c, j * rows : (j + 1) * rows, :], query_place[m], query_start[m])
            for h in range(HEADS):
                probs = jnp.exp(dot(keys, q_ref[m, h], ((1,), (1,))) - lse_ref[m, h])
                if m == j:
                    probs = jnp.where(seen, probs, 0.0)
                d_probs = dot(keys, do_ref[m, h], ((1,), (1,)))
                d_scores = (probs * (d_probs - delta_ref[m, h])).astype(BF16)
                total = total + dot(d_scores, q_ref[m, h], ((1,), (0,)))
                total = total + dot(probs.astype(BF16), do_ref[m, h], ((1,), (0,)))
                dq_ref[m, h] += dot(keys, d_scores, ((0,), (0,)))
        return total

    def passing(k):
        target = lax.rem(ctx + k, n_ctx)
        return remote(dkv_ref.at[target], landed.at[k - 1], send.at[k], recv.at[k], (section, target, wt))

    @pl.loop(1, n_ctx)
    def _(k):
        c = lax.rem(ctx + k, n_ctx)
        for j in range(2):
            dkv_ref[c, j * rows : (j + 1) * rows, :] = block(c, j).astype(BF16)
        passing(k).start()

    for j in range(2):
        own_ref[j * rows : (j + 1) * rows, :] = block(ctx, j)

    @pl.loop(1, n_ctx)
    def _(k):
        passing(k).wait_recv()
        own_ref[...] += landed[k - 1].astype(F32)

    cosine, sine = cos_ref[...], sin_ref[...]
    d_own = own_ref[...]
    over = roll(d_own, HEAD_SIZE)
    d_query = [
        jnp.concatenate([jnp.transpose(dq_ref[m, h]) for m in range(2)], 0) * (1.0 / HEAD_SIZE) for h in range(HEADS)
    ]
    first = jnp.where(low, d_query[0], roll(d_query[1], HEAD_SIZE))
    second = jnp.where(low, d_query[2], over)
    raw_ref[:, :LANES] = turned(first, cosine, -sine).astype(BF16)
    raw_ref[:, LANES : 2 * LANES] = turned(second, cosine, -sine).astype(BF16)
    raw_ref[:, 2 * LANES :] = jnp.where(low, over, 0.0).astype(BF16)
    part_ref[...] = dot(raw_ref[...], w_ref[:, : 3 * LANES], ((1,), (1,))).astype(BF16)
    for k in range(1, n_ctx):
        passing(k).wait_send()


def attend_back(number, rows_a, weights, tables, kept):
    n_ctx = lax.axis_size("ctx")
    n_rows, width = rows_a.shape
    rows = n_rows // 2
    dma = pltpu.SemaphoreType.DMA
    return pl.pallas_call(
        functools.partial(attend_back_kernel, n_ctx),
        out_shape=[
            jax.ShapeDtypeStruct((n_rows, width), BF16),
            jax.ShapeDtypeStruct((n_rows, 3 * LANES), BF16),
        ],
        in_specs=[VMEM] * 11,
        out_specs=[VMEM] * 2,
        scratch_shapes=[
            pltpu.VMEM((2, HEADS, rows, LANES), BF16),
            pltpu.VMEM((2, HEADS, 1, rows), F32),
            pltpu.VMEM((2, HEADS, LANES, rows), F32),
            pltpu.VMEM((n_ctx, n_rows, LANES), BF16),
            pltpu.VMEM((n_rows, LANES), F32),
            pltpu.VMEM((n_ctx - 1, n_rows, LANES), BF16),
            dma((n_ctx,)),
            dma((n_ctx,)),
        ],
        compiler_params=pltpu.CompilerParams(
            collective_id=number, has_side_effects=True, vmem_limit_bytes=40 << 20
        ),
        cost_estimate=pl.CostEstimate(flops=0, bytes_accessed=100 << 20, transcendentals=0),
    )(rows_a, weights, *tables, *kept)


def shards(tokens, cotangent, blocks, routes, norm_gain, w_query, key_value_weight, w_attn_out, router, w_in, w_down):
    section, ctx, wt = place()
    n_ctx, n_wt, layers = lax.axis_size("ctx"), lax.axis_size("wt"), lax.axis_size("section")
    micro_count, share, width = tokens.shape
    per_ctx = routes.shape[2]
    seq_len = per_ctx * n_ctx
    experts = w_in.shape[1] // 2
    n_experts = router.shape[2]
    q_cols = w_query.shape[2] // 2
    depth = w_query.shape[1]

    block_len = seq_len // blocks.shape[1]
    placed = (blocks[:, :, None] * block_len + jnp.arange(block_len, dtype=jnp.int32)[None, None, :]).reshape(
        micro_count, seq_len
    )
    query_place = lax.dynamic_slice_in_dim(placed, ctx * per_ctx, per_ctx, 1)
    later = (jnp.arange(micro_count) > 0)[:, None]
    query_start = jnp.where(later, query_place - query_place % CONT_LEN, 0)
    query_pos = jnp.where(later, seq_len + query_place % CONT_LEN, query_place)
    inverse = jnp.power(ROPE_BASE, -jnp.arange(HEAD_SIZE // 2, dtype=F32) * 2.0 / HEAD_SIZE)
    angles = query_pos.reshape(-1).astype(F32)[:, None] * inverse[None, :]
    cosine, sine = jnp.cos(angles), jnp.sin(angles)
    tables = (
        jnp.tile(cosine, (1, 4)),
        jnp.concatenate([-sine, sine, -sine, sine], 1),
        jnp.transpose(placed.reshape(micro_count, n_ctx, per_ctx), (1, 0, 2)).reshape(n_ctx, -1, 1),
        query_place[:, None, :],
        query_start[:, None, :],
    )

    def swap(values):
        return lax.ppermute(values, "section", [(0, 1), (1, 0)])

    def by_layer(halves):
        mine = lax.dynamic_index_in_dim(halves, section, 0, False)
        other = swap(lax.dynamic_index_in_dim(halves, 1 - section, 0, False))
        return [jnp.where(section == layer, mine, other) for layer in range(2)]

    def side_by_side(values):
        halves = values.reshape((2, experts) + values.shape[1:])
        return jnp.concatenate([halves[:, e] for e in range(experts)], -1)

    def to_owner(first, second):
        mine = jnp.where(section == 0, first, second)
        other = swap(jnp.where(section == 0, second, first))
        return jnp.where(section == 0, mine, other), jnp.where(section == 0, other, mine)

    attn_pack = jnp.concatenate(
        [
            jnp.transpose(w_query[0].reshape(depth, 2, q_cols), (1, 0, 2)),
            jnp.transpose(key_value_weight[0], (1, 0, 2)),
            jnp.transpose(w_attn_out[0].reshape(2, q_cols, depth), (0, 2, 1)),
        ],
        -1,
    )
    attn_pack = by_layer(attn_pack)
    in_pack = by_layer(side_by_side(w_in[0]))
    down_pack = by_layer(side_by_side(w_down[0]))
    route_pack = lax.all_gather(routes[0], "section", axis=0)
    gain_pack = lax.all_gather(norm_gain[0], "section", axis=0)
    router_pack = lax.all_gather(router[0], "section", axis=0)

    def packed(in_part, down_part):
        wide = in_part.shape[1]
        rest = down_part[:, wide:]
        half = rest.shape[0] // 2
        return jnp.concatenate(
            [in_part, down_part[:, :wide], jnp.concatenate([rest[:half], rest[half:]], 1)], 0
        )

    def unpacked(values, in_rows, down_rows):
        wide = values.shape[-1]
        n = values.shape[0]
        rest = values[:, in_rows + down_rows :]
        rest = jnp.concatenate([rest[..., : wide // 2], rest[..., wide // 2 :]], 1)
        down_part = jnp.concatenate([values[:, in_rows : in_rows + down_rows], rest], 2)
        return values[:, :in_rows].reshape(n * in_rows, wide), down_part.reshape(n * down_rows, -1)

    def after(value, earlier):
        return value if earlier is None else lax.optimization_barrier((value, earlier))[0]

    in_rows, down_rows = w_in.shape[2], w_down.shape[2]
    attn_full, in_full, down_full = [], [], []
    last = None

    def unpack_experts(full):
        one, two = unpacked(full.reshape(n_ctx, -1, full.shape[1]), in_rows, down_rows)
        in_full.append(one)
        down_full.append(two)

    def gather_experts(pack):
        return lax.all_gather(pack, "ctx", axis=0, tiled=True)

    moe_pack = [packed(in_pack[layer], down_pack[layer]) for layer in range(2)]
    attn_full = [None, None]

    my_first = wt * 2 * experts + section * experts
    n_rows = micro_count * per_ctx

    def routed(layer):
        names = route_pack[layer].reshape(n_rows, -1)
        return jnp.any(names[:, :, None] == jnp.arange(n_experts, dtype=jnp.int32)[None, None, :], 1)

    def full_rows(values):
        return values.reshape(n_rows, width)

    def blocked(values):
        return values.reshape(2 * n_wt, share, width).astype(BF16)

    stream = lax.dynamic_index_in_dim(tokens, section, 0, False).astype(F32)
    top = lax.dynamic_index_in_dim(cotangent, section, 0, False).astype(F32)

    normed_in, full = exchange(0, None, stream, gain=gain_pack[0, 0:1], spread="norm", gather=attn_pack[0])
    attn_full[0] = full.reshape(-1, full.shape[2])
    normed_in, first = lax.optimization_barrier((normed_in, moe_pack[0]))
    moe_full = [gather_experts(first), None]
    (d_mixed,) = exchange(1, None, top, gain=gain_pack[0, 0:1], spread="plain")
    saved = []
    outputs = []
    for layer in range(2):
        rows_in = full_rows(normed_in)
        weights = attn_full[layer]
        partial, queries, pairs, out_full, log_total, attended = attend(2 + layer, rows_in, weights, tables)
        middle, normed_mid = exchange(
            4 + layer, blocked(partial), stream, gain=gain_pack[layer, 1:2], spread="norm"
        )
        if layer == 0:
            normed_mid, second = lax.optimization_barrier((normed_mid, moe_pack[1]))
            moe_full[1] = gather_experts(second)
        normed_mid, full = lax.optimization_barrier((normed_mid, moe_full[layer]))
        unpack_experts(full)
        rows_mid = full_rows(normed_mid)
        logits = dot(rows_mid, router_pack[layer], ((1,), (0,)))
        hit = routed(layer)
        masked = jnp.where(hit, logits, MASKED)
        expos = jnp.where(hit, jnp.exp(masked - jnp.max(masked, 1, keepdims=True)), 0.0)
        gates = expos / jnp.sum(expos, 1, keepdims=True)
        my_gates = lax.dynamic_slice_in_dim(gates, my_first, experts, 1)
        gate_up = dot(rows_mid, in_full[layer], ((1,), (0,)))
        weighted_hidden = []
        partial = 0.0
        for e in range(experts):
            gate_part = gate_up[:, 2 * e * FF : (2 * e + 1) * FF]
            up_part = gate_up[:, (2 * e + 1) * FF : (2 * e + 2) * FF]
            weighted_hidden.append((jax.nn.silu(gate_part) * up_part * my_gates[:, e : e + 1]).astype(BF16))
            partial = partial + dot(
                weighted_hidden[e], down_full[layer][:, e * width : (e + 1) * width], ((1,), (0,))
            )
        saved.append(
            dict(
                stream=stream,
                middle=middle,
                rows_in=rows_in,
                rows_mid=rows_mid,
                heads=(queries, pairs, out_full, log_total),
                attended=attended,
                gates=gates,
                my_gates=my_gates,
                gate_up=gate_up,
                weighted_hidden=weighted_hidden,
            )
        )
        if layer == 0:
            stream, normed_in, full = exchange(
                6, blocked(partial), middle, gain=gain_pack[1, 0:1], spread="norm", rounded=True, gather=attn_pack[1]
            )
            attn_full[1] = full.reshape(-1, full.shape[2])
        else:
            (stream,) = exchange(7, blocked(partial), middle, rounded=True)
        outputs.append(stream.astype(BF16))

    upstream = top
    last = None
    grads_in = [None, None]
    attn_grads = [None, None]
    moe_grads = [None, None]
    small = [None, None]
    for layer in (1, 0):
        kept = saved[layer]
        rows_d = full_rows(d_mixed)
        gate_up = kept["gate_up"]
        d_gate_up = []
        down_grad = []
        d_weight = []
        for e in range(experts):
            d_weighted = dot(rows_d, down_full[layer][:, e * width : (e + 1) * width], ((1,), (1,)))
            gate_part = gate_up[:, 2 * e * FF : (2 * e + 1) * FF]
            up_part = gate_up[:, (2 * e + 1) * FF : (2 * e + 2) * FF]
            sigmoid = jax.nn.sigmoid(gate_part)
            activated = gate_part * sigmoid
            d_weight.append(jnp.sum((activated * up_part).astype(BF16).astype(F32) * d_weighted, -1, keepdims=True))
            d_hidden = d_weighted * kept["my_gates"][:, e : e + 1]
            d_gate_up.append(
                (d_hidden * up_part * (sigmoid * (1.0 + gate_part * (1.0 - sigmoid)))).astype(BF16)
            )
            d_gate_up.append((d_hidden * activated).astype(BF16))
            down_grad.append(dot(kept["weighted_hidden"][e], rows_d, ((0,), (0,))).astype(BF16))
        d_gate_up = jnp.concatenate(d_gate_up, -1)
        d_weight = jnp.concatenate(d_weight, -1)
        down_grad = jnp.concatenate(down_grad, -1)
        in_grad = dot(kept["rows_mid"], d_gate_up, ((0,), (0,))).astype(BF16)
        partial = dot(d_gate_up, in_full[layer], ((1,), (1,)))
        packed_grad = jax.vmap(packed)(
            in_grad.reshape(n_ctx, in_rows, -1), down_grad.reshape(n_ctx, down_rows, -1)
        )
        if layer == 0:
            partial, packed_grad, moe_grads[1] = lax.optimization_barrier((partial, packed_grad, moe_grads[1]))
        else:
            partial, packed_grad = lax.optimization_barrier((partial, packed_grad))
        last = lax.psum_scatter(after(packed_grad, last), "ctx", scatter_dimension=0, tiled=False)
        moe_grads[layer] = last
        terms = kept["my_gates"] * d_weight
        placed_terms = lax.dynamic_update_slice_in_dim(jnp.zeros_like(kept["gates"]), terms, my_first, 1)
        d_logits = placed_terms - kept["gates"] * jnp.sum(terms, 1, keepdims=True)
        partial = partial + lax.dot_general(
            d_logits,
            router_pack[layer].astype(F32),
            (((1,), (1,)), ((), ())),
            precision=lax.Precision.HIGHEST,
            preferred_element_type=F32,
        )
        router_grad = lax.dot_general(
            d_logits,
            kept["rows_mid"].astype(F32),
            (((0,), (0,)), ((), ())),
            precision=lax.Precision.HIGHEST,
            preferred_element_type=F32,
        )
        d_middle, gain_grad_mid, d_attn = exchange(
            8 + layer, blocked(partial), upstream, kept["middle"], gain_pack[layer, 1:2], spread="plain"
        )
        rows_a = full_rows(d_attn)
        weights = attn_full[layer]
        partial, raw = attend_back(10 + layer, rows_a, weights, tables, kept["heads"])
        attn_parts = dot(kept["rows_in"], jnp.pad(raw, ((0, 0), (0, weights.shape[1] - raw.shape[1]))), ((0,), (0,)))
        attn_parts = attn_parts + dot(
            rows_a, jnp.pad(kept["attended"], ((0, 0), (weights.shape[1] - kept["attended"].shape[1], 0))), ((0,), (0,))
        )
        attn_parts = attn_parts.astype(BF16).reshape(n_ctx, depth, -1)
        if layer == 0:
            partial, moe_grads[0] = lax.optimization_barrier((partial, moe_grads[0]))
        if layer == 1:
            upstream, gain_grad_in, d_mixed, attn_grads[1] = exchange(
                12,
                blocked(partial),
                d_middle,
                kept["stream"],
                gain_pack[1, 0:1],
                spread="plain",
                rounded=True,
                add=attn_parts,
            )
        else:
            upstream, gain_grad_in, attn_grads[0] = exchange(
                13, blocked(partial), d_middle, kept["stream"], gain_pack[0, 0:1], rounded=True, add=attn_parts
            )
        grads_in[layer] = upstream.astype(BF16)
        small[layer] = jnp.concatenate([gain_grad_in, gain_grad_mid, router_grad], 0)

    piece = width // (n_ctx * n_wt)
    small_parts = jnp.transpose(
        jnp.stack(small).reshape(2, small[0].shape[0], n_ctx * n_wt, piece), (2, 0, 1, 3)
    )
    small_parts = jnp.pad(small_parts, ((0, 0), (0, 0), (0, -small[0].shape[0] % 8), (0, -piece % 128)))
    small_total = small_sum(14, small_parts)[: small[0].shape[0], :piece]
    out_pair = jnp.stack(to_owner(outputs[0], outputs[1]))
    grad_pair = jnp.stack(to_owner(grads_in[0], grads_in[1]))
    attn_first, attn_second = [member.astype(F32) for member in to_owner(attn_grads[0], attn_grads[1])]
    kv_at = q_cols
    out_at = q_cols + 2 * HEAD_SIZE
    grad_query = jnp.concatenate([attn_first[:, :kv_at], attn_second[:, :kv_at]], -1)
    grad_kv = jnp.stack([attn_first[:, kv_at:out_at], attn_second[:, kv_at:out_at]], 1)
    grad_out = jnp.concatenate([jnp.transpose(attn_first[:, out_at:]), jnp.transpose(attn_second[:, out_at:])], 0)

    def stacked(halves):
        columns = halves[0].shape[1] // experts
        return jnp.stack(
            [half[:, e * columns : (e + 1) * columns] for half in halves for e in range(experts)]
        ).astype(F32)

    moe_pair = [unpacked(member[None], in_rows, down_rows) for member in to_owner(moe_grads[0], moe_grads[1])]
    grad_in = stacked([member[0] for member in moe_pair])
    grad_down = stacked([member[1] for member in moe_pair])
    return (
        out_pair[None],
        grad_pair[None],
        small_total[:2][None],
        grad_query[None],
        grad_kv[None],
        grad_out[None],
        jnp.transpose(small_total[2:])[None],
        grad_in[None],
        grad_down[None],
    )


def solution(mesh):
    return jax.shard_map(
        shards,
        mesh=mesh,
        in_specs=(
            P(None, ("ctx", "wt"), None),
            P(None, ("ctx", "wt"), None),
            P(),
            P("section", None, "ctx", None),
            P("section", None, None),
            P("section", "ctx", "wt"),
            P("section", "ctx", "wt", None),
            P("section", "wt", "ctx"),
            P("section", None, None),
            P("section", "wt", "ctx", None),
            P("section", "wt", "ctx", None),
        ),
        out_specs=(
            P("section", None, ("ctx", "wt"), None),
            P("section", None, ("ctx", "wt"), None),
            P("section", None, ("ctx", "wt")),
            P("section", "ctx", "wt"),
            P("section", "ctx", "wt", None),
            P("section", "wt", "ctx"),
            P("section", ("ctx", "wt"), None),
            P("section", "wt", "ctx", None),
            P("section", "wt", "ctx", None),
        ),
        check_vma=False,
    )
```

```python
import functools

import jax
import jax.numpy as jnp
from jax import lax
from jax.experimental import pallas as pl
from jax.experimental.pallas import tpu as pltpu
from jax.sharding import PartitionSpec as P

HEAD_SIZE = 64
FF = 512
CONT_LEN = 1024
EPSILON = 1e-06
ROPE_BASE = 10000.0
MASKED = -1e30
CHUNKS = 2
LANES = 2 * HEAD_SIZE
MESH = pl.DeviceIdType.MESH
F32 = jnp.float32
BF16 = jnp.bfloat16


def dot(left, right, contract):
    return lax.dot_general(left, right, (contract, ((), ())), preferred_element_type=F32)


def norm_scale(rows):
    return lax.rsqrt(jnp.mean(rows * rows, -1, keepdims=True) + EPSILON)


def place():
    return lax.axis_index("section"), lax.axis_index("ctx"), lax.axis_index("wt")


def greet(targets):
    barrier = pltpu.get_barrier_semaphore()
    for target in targets:
        pl.semaphore_signal(barrier, inc=1, device_id=target, device_id_type=MESH)
    pl.semaphore_wait(barrier, len(targets))


def remote(source, destination, send_sem, recv_sem, target):
    return pltpu.make_async_remote_copy(
        src_ref=source,
        dst_ref=destination,
        send_sem=send_sem,
        recv_sem=recv_sem,
        device_id=target,
        device_id_type=MESH,
    )


class Near:
    def __init__(self, n_wt):
        self.section, self.ctx, self.wt = place()
        self.n_wt = n_wt
        self.sibling = (1 - self.section, self.ctx, self.wt)
        self.right = (self.section, self.ctx, jnp.minimum(self.wt + 1, n_wt - 1))
        self.left = (self.section, self.ctx, jnp.maximum(self.wt - 1, 0))
        self.has_right, self.has_left = self.wt < n_wt - 1, self.wt > 0
        self.own = self.section * n_wt + self.wt

    def greet(self, others=()):
        barrier = pltpu.get_barrier_semaphore()

        def hail(target):
            pl.semaphore_signal(barrier, inc=1, device_id=target, device_id_type=MESH)

        hail(self.sibling)
        pl.when(self.has_right)(lambda: hail(self.right))
        pl.when(self.has_left)(lambda: hail(self.left))
        for other in others:
            hail(other)
        pl.semaphore_wait(
            barrier, 1 + len(others) + self.has_right.astype(jnp.int32) + self.has_left.astype(jnp.int32)
        )


def rows_of(chunk, rows):
    return slice(chunk * rows, (chunk + 1) * rows)


class RowSum:
    def __init__(self, near, chunks, parts, scratch):
        self.near, self.chunks, self.parts = near, chunks, parts
        self.rows = parts.shape[1] // chunks
        self.from_sibling, self.in_right, self.in_left, self.out_right, self.out_left = scratch[:5]
        self.swap_send, self.swap_recv, self.send, self.recv = scratch[5:]

    @staticmethod
    def scratch(n_wt, shape, chunks):
        dma = pltpu.SemaphoreType.DMA
        return [pltpu.VMEM((n_wt,) + shape, BF16)] * 5 + [dma((chunks * n_wt,))] * 2 + [dma((2 * chunks * n_wt,))] * 2

    def swap(self, chunk, block):
        at = rows_of(chunk, self.rows)
        number = chunk * self.near.n_wt + block
        return remote(
            self.parts.at[(1 - self.near.section) * self.near.n_wt + block, at],
            self.from_sibling.at[block, at],
            self.swap_send.at[number],
            self.swap_recv.at[number],
            self.near.sibling,
        )

    def begin(self):
        n_wt = self.near.n_wt
        order = []
        for step in range(n_wt - 1):
            order += [n_wt - 1 - step, step]
        for chunk in range(self.chunks):
            for block in dict.fromkeys(order):
                self.swap(chunk, block).start()

    def chip_sum(self, chunk, block):
        at = rows_of(chunk, self.rows)
        mine = self.parts[self.near.section * self.near.n_wt + block, at, :]
        return mine.astype(F32) + self.from_sibling[block, at, :].astype(F32)

    def toward(self, chunk, block, rightward):
        at = rows_of(chunk, self.rows)
        number = (2 * chunk + (0 if rightward else 1)) * self.near.n_wt + block
        source, target = (self.out_right, self.in_right) if rightward else (self.out_left, self.in_left)
        return remote(
            source.at[block, at],
            target.at[block, at],
            self.send.at[number],
            self.recv.at[number],
            self.near.right if rightward else self.near.left,
        )

    def send_on(self, chunk, block, rightward):
        at = rows_of(chunk, self.rows)
        self.swap(chunk, block).wait_recv()
        outward, inward = (self.out_right, self.in_right) if rightward else (self.out_left, self.in_left)
        behind = self.near.has_left if rightward else self.near.has_right

        @pl.when(jnp.logical_not(behind))
        def _():
            outward[block, at, :] = self.chip_sum(chunk, block).astype(BF16)

        @pl.when(behind)
        def _():
            self.toward(chunk, block, rightward).wait_recv()
            outward[block, at, :] = (self.chip_sum(chunk, block) + inward[block, at, :].astype(F32)).astype(BF16)

        self.toward(chunk, block, rightward).start()

    def step(self, chunk, step):
        wt, n_wt = self.near.wt, self.near.n_wt
        far, near = n_wt - 1 - step, step
        lower = 2 * wt < n_wt
        pl.when((wt < far) & lower)(lambda: self.send_on(chunk, far, True))
        pl.when(wt > near)(lambda: self.send_on(chunk, near, False))
        pl.when((wt < far) & jnp.logical_not(lower))(lambda: self.send_on(chunk, far, True))

    def collect(self, chunk, result):
        at, wt = rows_of(chunk, self.rows), self.near.wt
        self.swap(chunk, wt).wait_recv()
        result[at, :] = self.chip_sum(chunk, wt)

        @pl.when(self.near.has_left)
        def _():
            self.toward(chunk, wt, True).wait_recv()
            result[at, :] += self.in_right[wt, at, :].astype(F32)

        @pl.when(self.near.has_right)
        def _():
            self.toward(chunk, wt, False).wait_recv()
            result[at, :] += self.in_left[wt, at, :].astype(F32)

    def end(self):
        wt, n_wt = self.near.wt, self.near.n_wt
        for chunk in range(self.chunks):
            for block in range(n_wt):
                self.swap(chunk, block).wait_send()
                if block > 0:
                    pl.when(wt < block)(self.toward(chunk, block, True).wait_send)
                if block < n_wt - 1:
                    pl.when(wt > block)(self.toward(chunk, block, False).wait_send)


class RowGather:
    def __init__(self, near, chunks, all_ref, scratch):
        self.near, self.chunks, self.all = near, chunks, all_ref
        self.rows = all_ref.shape[1] // chunks
        self.send, self.recv, self.pass_send, self.pass_recv = scratch
        self.sent, self.arrivals = [], []

    @staticmethod
    def scratch(n_wt, chunks):
        return [pltpu.SemaphoreType.DMA((2 * chunks * n_wt,))] * 4

    def along(self, chunk, block, hop, rightward):
        at = rows_of(chunk, self.rows)
        number = (2 * chunk + (0 if rightward else 1)) * self.near.n_wt + hop
        return remote(
            self.all.at[block, at],
            self.all.at[block, at],
            self.send.at[number],
            self.recv.at[number],
            self.near.right if rightward else self.near.left,
        )

    def across(self, chunk, block, number):
        at = rows_of(chunk, self.rows)
        number = 2 * chunk * self.near.n_wt + number
        return remote(
            self.all.at[block, at],
            self.all.at[block, at],
            self.pass_send.at[number],
            self.pass_recv.at[number],
            self.near.sibling,
        )

    def launch(self, condition, copy):
        pl.when(condition)(copy.start)
        self.sent.append((condition, copy))

    def first(self, chunk):
        near = self.near
        always = near.wt >= 0
        self.launch(near.has_right, self.along(chunk, near.own, 1, True))
        self.launch(near.has_left, self.along(chunk, near.own, 1, False))
        self.launch(always, self.across(chunk, near.own, 0))
        self.arrivals.append((always, self.across(chunk, near.own, 0)))

    def hop(self, chunk, hop):
        near, n_wt = self.near, self.near.n_wt
        for rightward, came, more, block, number in (
            (True, near.wt >= hop, near.has_right, jnp.maximum(near.own - hop, 0), hop),
            (False, near.wt + hop < n_wt, near.has_left, jnp.minimum(near.own + hop, 2 * n_wt - 1), n_wt + hop),
        ):
            pl.when(came)(self.along(chunk, block, hop, rightward).wait_recv)
            if hop + 1 < n_wt:
                self.launch(came & more, self.along(chunk, block, hop + 1, rightward))
            self.launch(came, self.across(chunk, block, number))
            self.arrivals.append((came, self.across(chunk, block, number)))

    def arrive(self):
        for condition, copy in self.arrivals:
            pl.when(condition)(copy.wait_recv)

    def end(self):
        for condition, copy in self.sent:
            pl.when(condition)(copy.wait_send)


def exchange_kernel(n_ctx, n_wt, reduce, back, spread, rounded, ride, *refs):
    refs = list(refs)
    near = Near(n_wt)
    section, ctx, wt = near.section, near.ctx, near.wt
    peers = [(section, lax.rem(ctx + k, n_ctx), wt) for k in range(1, n_ctx)]
    parts = refs.pop(0) if reduce else None
    rows_ref = refs.pop(0)
    stream_ref = refs.pop(0) if back else None
    gain_ref = refs.pop(0) if (back or spread) else None
    ride_ref = refs.pop(0) if ride else None
    result_ref = refs.pop(0) if reduce else None
    gain_grad_ref = refs.pop(0) if back else None
    all_ref = refs.pop(0) if spread else None
    rode_ref = refs.pop(0) if ride else None
    if reduce:
        sums = RowSum(near, CHUNKS, parts, refs[:9])
        refs = refs[9:]
    if spread:
        gathers = RowGather(near, CHUNKS, all_ref, refs[:4])
        refs = refs[4:]
    if ride:
        landed, ride_send, ride_recv, ride_local = refs
    chunk_rows = rows_ref.shape[0] // CHUNKS
    near.greet(peers if ride else ())
    if reduce:
        sums.begin()
    if ride == "gather":
        keep = pltpu.make_async_copy(ride_ref, rode_ref.at[ctx], ride_local)
        keep.start()
        riders = [
            remote(ride_ref, rode_ref.at[ctx], ride_send.at[k], ride_recv.at[k], peers[k]) for k in range(n_ctx - 1)
        ]
    elif ride == "sum":
        riders = [
            remote(
                ride_ref.at[lax.rem(ctx + 1 + k, n_ctx)], landed.at[k], ride_send.at[k], ride_recv.at[k], peers[k]
            )
            for k in range(n_ctx - 1)
        ]
    if ride:
        for copy in riders:
            copy.start()

    def settle(chunk):
        at = rows_of(chunk, chunk_rows)
        if reduce:
            sums.collect(chunk, result_ref)
            total = result_ref[at, :]
            if back:
                stream = stream_ref[at, :]
                scale = norm_scale(stream)
                weighted = gain_ref[...] * total
                gain_part = jnp.sum(total * stream * scale, 0, keepdims=True)
                gain_grad_ref[...] = gain_part if chunk == 0 else gain_grad_ref[...] + gain_part
                total = scale * weighted - stream * (scale * scale * scale) * jnp.mean(
                    weighted * stream, -1, keepdims=True
                )
            total = rows_ref[at, :].astype(F32) + total
            if rounded:
                total = total.astype(BF16).astype(F32)
            result_ref[at, :] = total
        else:
            total = rows_ref[at, :].astype(F32)
        if spread:
            if spread == "norm":
                total = total * norm_scale(total) * gain_ref[...]
            all_ref[near.own, at, :] = total.astype(BF16)
            gathers.first(chunk)

    stages = []
    if reduce:
        stages += [functools.partial(sums.step, step=step) for step in range(n_wt - 1)]
    stages.append(settle)
    if spread:
        stages += [functools.partial(gathers.hop, hop=hop) for hop in range(1, n_wt)]
    for slot in range(CHUNKS + len(stages) - 1):
        for chunk in reversed(range(CHUNKS)):
            if 0 <= slot - chunk < len(stages):
                stages[slot - chunk](chunk)

    if spread:
        gathers.arrive()
    if ride == "gather":
        keep.wait()
        for copy in riders:
            copy.wait()
    elif ride == "sum":
        total = ride_ref[ctx].astype(F32)
        for k, copy in enumerate(riders):
            copy.wait()
            total = total + landed[k].astype(F32)
        rode_ref[...] = total
    if spread:
        gathers.end()
    if reduce:
        sums.end()


VMEM = pl.BlockSpec(memory_space=pltpu.VMEM)


def exchange(number, parts, rows, stream=None, gain=None, spread=None, rounded=False, gather=None, add=None):
    n_ctx, n_wt = lax.axis_size("ctx"), lax.axis_size("wt")
    shape = rows.shape
    reduce, back = parts is not None, stream is not None
    ride = "gather" if gather is not None else "sum" if add is not None else None
    rider = gather if gather is not None else add
    operands = [
        member
        for member, wanted in (
            (parts, reduce),
            (rows, True),
            (stream, back),
            (gain, back or spread),
            (rider, ride),
        )
        if wanted
    ]
    outs = []
    scratch = []
    dma = pltpu.SemaphoreType.DMA
    if reduce:
        outs.append(jax.ShapeDtypeStruct(shape, F32))
        scratch += RowSum.scratch(n_wt, shape, CHUNKS)
    if back:
        outs.append(jax.ShapeDtypeStruct((1, shape[1]), F32))
    if spread:
        outs.append(jax.ShapeDtypeStruct((2 * n_wt,) + shape, BF16))
        scratch += RowGather.scratch(n_wt, CHUNKS)
    if ride == "gather":
        outs.append(jax.ShapeDtypeStruct((n_ctx,) + rider.shape, BF16))
        scratch += [pltpu.VMEM((8, 128), BF16), dma((n_ctx - 1,)), dma((n_ctx - 1,)), dma]
    elif ride == "sum":
        outs.append(jax.ShapeDtypeStruct(rider.shape[1:], F32))
        scratch += [pltpu.VMEM((n_ctx - 1,) + rider.shape[1:], BF16), dma((n_ctx - 1,)), dma((n_ctx - 1,)), dma]
    return pl.pallas_call(
        functools.partial(exchange_kernel, n_ctx, n_wt, reduce, back, spread, rounded, ride),
        out_shape=outs,
        in_specs=[VMEM] * len(operands),
        out_specs=[VMEM] * len(outs),
        scratch_shapes=scratch,
        compiler_params=pltpu.CompilerParams(
            collective_id=number, has_side_effects=True, vmem_limit_bytes=40 << 20
        ),
        cost_estimate=pl.CostEstimate(flops=0, bytes_accessed=110 << 20, transcendentals=0),
    )(*operands)


def small_sum_kernel(n_ctx, n_wt, *refs):
    small, kept = refs[:6], refs[6:12]
    total_ref, attn_ref, out_ref, grad_ref = refs[12:16]
    parts, landed, summed, from_sibling, send, recv, swap_send, swap_recv = refs[16:]
    section, ctx, wt = place()
    count = n_ctx * n_wt
    own = ctx * n_wt + wt
    blocks = [lax.rem(own + k, count) for k in range(1, count)]
    peers = [(section, block // n_wt, lax.rem(block, n_wt)) for block in blocks]
    sibling = (1 - section, ctx, wt)
    greet([sibling] + peers)
    members = list(zip(kept[0::2], kept[1::2], (attn_ref, out_ref, grad_ref)))
    swaps = swap_copies(section, sibling, members, swap_send, swap_recv)
    start_swaps(section, swaps)
    piece = small[0].shape[1] // count
    parts[...] = jnp.zeros(parts.shape, F32)
    for block in range(count):
        for layer in range(2):
            at = 0
            for ref in small[3 * layer : 3 * layer + 3]:
                end = at + ref.shape[0]
                parts[block, layer, at:end, :piece] = ref[:, block * piece : (block + 1) * piece]
                at = end
    copies = [
        remote(parts.at[blocks[k]], landed.at[k], send.at[k], recv.at[k], peers[k]) for k in range(count - 1)
    ]
    for copy in copies:
        copy.start()
    total = parts[own]
    for k, copy in enumerate(copies):
        copy.wait_recv()
        total = total + landed[k]
    summed[...] = total
    swap = remote(summed.at[1 - section], from_sibling, send.at[count - 1], recv.at[count - 1], sibling)
    swap.start()
    swap.wait()
    total_ref[...] = summed[section] + from_sibling[...]
    for copy in copies:
        copy.wait_send()
    wait_swaps(section, swaps)


def swap_copies(section, sibling, members, send, recv):
    return [
        [remote(pair[1 - layer], pair[2], send.at[k], recv.at[k], sibling) for k, pair in enumerate(members)]
        for layer in range(2)
    ]


def start_swaps(section, swaps):
    for layer in range(2):

        @pl.when(section == layer)
        def _():
            for copy in swaps[layer]:
                copy.start()


def wait_swaps(section, swaps):
    for layer in range(2):

        @pl.when(section == layer)
        def _():
            for copy in swaps[layer]:
                copy.wait()


def small_sum(number, small, kept):
    n_ctx, n_wt = lax.axis_size("ctx"), lax.axis_size("wt")
    count = n_ctx * n_wt
    rows = sum(member.shape[0] for member in small[:3])
    shape = (2, rows + -rows % 8, LANES)
    dma = pltpu.SemaphoreType.DMA
    any_place = pl.BlockSpec(memory_space=pl.ANY)
    return pl.pallas_call(
        functools.partial(small_sum_kernel, n_ctx, n_wt),
        out_shape=[jax.ShapeDtypeStruct(shape[1:], F32)]
        + [jax.ShapeDtypeStruct(member.shape, member.dtype) for member in kept[0::2]],
        in_specs=[VMEM] * 6 + [any_place] * 6,
        out_specs=[VMEM] + [any_place] * 3,
        scratch_shapes=[
            pltpu.VMEM((count,) + shape, F32),
            pltpu.VMEM((count - 1,) + shape, F32),
            pltpu.VMEM(shape, F32),
            pltpu.VMEM(shape[1:], F32),
            dma((count,)),
            dma((count,)),
            dma((3,)),
            dma((3,)),
        ],
        compiler_params=pltpu.CompilerParams(
            collective_id=number, has_side_effects=True, vmem_limit_bytes=40 << 20
        ),
        cost_estimate=pl.CostEstimate(flops=0, bytes_accessed=40 << 20, transcendentals=0),
    )(*small, *kept)


def hand_over_kernel(first, second, result, send, recv):
    section, ctx, wt = place()
    sibling = (1 - section, ctx, wt)
    greet([sibling])
    swaps = swap_copies(section, sibling, [(first, second, result)], send, recv)
    start_swaps(section, swaps)
    wait_swaps(section, swaps)


def hand_over(number, first, second):
    any_place = pl.BlockSpec(memory_space=pl.ANY)
    return pl.pallas_call(
        hand_over_kernel,
        out_shape=jax.ShapeDtypeStruct(first.shape, first.dtype),
        in_specs=[any_place] * 2,
        out_specs=any_place,
        scratch_shapes=[pltpu.SemaphoreType.DMA((1,))] * 2,
        compiler_params=pltpu.CompilerParams(collective_id=number, has_side_effects=True),
    )(first, second)


HEADS = 3


def roll(values, by):
    return pltpu.roll(values, by, 1)


def lower_half(shape):
    return lax.broadcasted_iota(jnp.int32, shape, 1) < HEAD_SIZE


def turned(values, cosine, sine):
    first = lax.rem(lax.broadcasted_iota(jnp.int32, values.shape, 1), HEAD_SIZE) < HEAD_SIZE // 2
    half = HEAD_SIZE // 2
    return values * cosine + jnp.where(first, roll(values, LANES - half), roll(values, half)) * sine


def visible(key_place, query_place, query_start):
    return (key_place <= query_place) & (key_place >= query_start)


def attend_kernel(
    n_ctx,
    n_wt,
    ride,
    x_ref,
    w_ref,
    cos_ref,
    sin_ref,
    key_place,
    query_place,
    query_start,
    *refs,
):
    refs = list(refs)
    ride_ref = refs.pop(0) if ride else None
    part_ref, q_ref, pairs_ref, out_ref, lse_ref, att_ref = [refs.pop(0) for _ in range(6)]
    all_ref = refs.pop(0) if ride else None
    top_ref, sum_ref, acc_ref, send, recv = refs[:5]
    near = Near(n_wt)
    section, ctx, wt = near.section, near.ctx, near.wt
    peers = [(section, lax.rem(ctx + k, n_ctx), wt) for k in range(1, n_ctx)]
    waiting = []
    if ride:
        gathers = RowGather(near, 1, all_ref, refs[5:])
        waiting = [functools.partial(gathers.hop, 0, hop) for hop in range(1, n_wt)]
        all_ref[near.own] = ride_ref[...]
        near.greet(peers)
        gathers.first(0)
    else:
        greet(peers)

    def ride_on():
        if waiting:
            waiting.pop(0)()

    rows = x_ref.shape[0] // 2
    low = lower_half((2 * rows, LANES))
    mixed = dot(x_ref[...], w_ref[:, : 3 * LANES], ((1,), (0,)))
    cosine, sine = cos_ref[...], sin_ref[...]
    first = turned(mixed[:, :LANES], cosine, sine)
    second = turned(mixed[:, LANES : 2 * LANES], cosine, sine)
    pairs_ref[ctx] = jnp.where(low, roll(second, HEAD_SIZE), roll(mixed[:, 2 * LANES :], HEAD_SIZE)).astype(BF16)

    def passing(k):
        return remote(
            pairs_ref.at[ctx], pairs_ref.at[ctx], send.at[k], recv.at[k], (section, lax.rem(ctx + k, n_ctx), wt)
        )

    for k in range(1, n_ctx):
        passing(k).start()
    for h, part in enumerate((first, roll(first, HEAD_SIZE), second)):
        scaled = jnp.where(low, part * (1.0 / HEAD_SIZE), 0.0).astype(BF16)
        q_ref[0, h] = scaled[:rows]
        q_ref[1, h] = scaled[rows:]
    ride_on()
    top_ref[...] = jnp.full(top_ref.shape, MASKED, F32)
    sum_ref[...] = jnp.zeros(sum_ref.shape, F32)
    acc_ref[...] = jnp.zeros(acc_ref.shape, F32)

    def block(c, m, j):
        keys = pairs_ref[c, j * rows : (j + 1) * rows, :]
        if m == j:
            seen = visible(key_place[c, j * rows : (j + 1) * rows, :], query_place[m], query_start[m])
        for h in range(HEADS):
            logits = dot(keys, q_ref[m, h], ((1,), (1,)))
            if m == j:
                logits = jnp.where(seen, logits, MASKED)
            before = top_ref[m, h]
            top = jnp.maximum(before, jnp.max(logits, 0, keepdims=True))
            expos = jnp.exp(logits - top)
            shrink = jnp.exp(before - top)
            top_ref[m, h] = top
            sum_ref[m, h] = sum_ref[m, h] * shrink + jnp.sum(expos, 0, keepdims=True)
            acc_ref[m, h] = acc_ref[m, h] * shrink + dot(keys, expos.astype(BF16), ((0,), (0,)))

    def blocks_of(c):
        block(c, 0, 0)
        block(c, 1, 1)
        block(c, 1, 0)

    blocks_of(ctx)
    ride_on()

    def arrived(k):
        passing(k).wait_recv()
        blocks_of(lax.rem(ctx + n_ctx - k, n_ctx))

    arrived(1)
    ride_on()
    pl.loop(2, n_ctx)(arrived)
    while waiting:
        ride_on()
    low = lower_half((rows, LANES))
    for m in range(2):
        outs = []
        for h in range(HEADS):
            lse_ref[m, h] = top_ref[m, h] + jnp.log(sum_ref[m, h])
            outs.append(jnp.transpose(acc_ref[m, h] / sum_ref[m, h]))
            out_ref[m, h] = outs[h]
        att_ref[m * rows : (m + 1) * rows, :LANES] = jnp.where(low, 0.0, outs[0]).astype(BF16)
        att_ref[m * rows : (m + 1) * rows, LANES:] = jnp.where(low, roll(outs[1], HEAD_SIZE), outs[2]).astype(BF16)
    part_ref[...] = dot(att_ref[...], w_ref[:, 2 * LANES :], ((1,), (1,))).astype(BF16)
    if ride:
        gathers.arrive()
        gathers.end()
    for k in range(1, n_ctx):
        passing(k).wait_send()


def attend(number, rows_in, weights, tables, ride=None):
    n_ctx, n_wt = lax.axis_size("ctx"), lax.axis_size("wt")
    riders = [] if ride is None else [ride]
    n_rows, width = rows_in.shape
    rows = n_rows // 2
    dma = pltpu.SemaphoreType.DMA
    return pl.pallas_call(
        functools.partial(attend_kernel, n_ctx, n_wt, bool(riders)),
        out_shape=[
            jax.ShapeDtypeStruct((n_rows, width), BF16),
            jax.ShapeDtypeStruct((2, HEADS, rows, LANES), BF16),
            jax.ShapeDtypeStruct((n_ctx, n_rows, LANES), BF16),
            jax.ShapeDtypeStruct((2, HEADS, rows, LANES), F32),
            jax.ShapeDtypeStruct((2, HEADS, 1, rows), F32),
            jax.ShapeDtypeStruct((n_rows, 2 * LANES), BF16),
        ]
        + [jax.ShapeDtypeStruct((2 * n_wt,) + member.shape, BF16) for member in riders],
        in_specs=[VMEM] * (7 + len(riders)),
        out_specs=[VMEM] * (6 + len(riders)),
        scratch_shapes=[
            pltpu.VMEM((2, HEADS, 1, rows), F32),
            pltpu.VMEM((2, HEADS, 1, rows), F32),
            pltpu.VMEM((2, HEADS, LANES, rows), F32),
            dma((n_ctx,)),
            dma((n_ctx,)),
        ]
        + (RowGather.scratch(n_wt, 1) if riders else []),
        compiler_params=pltpu.CompilerParams(
            collective_id=number, has_side_effects=True, vmem_limit_bytes=40 << 20
        ),
        cost_estimate=pl.CostEstimate(flops=0, bytes_accessed=70 << 20, transcendentals=0),
    )(rows_in, weights, *tables, *riders)


def attend_back_kernel(
    n_ctx,
    n_wt,
    ride,
    a_ref,
    w_ref,
    cos_ref,
    sin_ref,
    key_place,
    query_place,
    query_start,
    q_ref,
    pairs_ref,
    out_ref,
    lse_ref,
    *refs,
):
    refs = list(refs)
    ride_refs = [refs.pop(0), refs.pop(0)] if ride else None
    part_ref, raw_ref = refs.pop(0), refs.pop(0)
    rode_ref = refs.pop(0) if ride else None
    do_ref, delta_ref, dq_ref, dkv_ref, own_ref, landed, send, recv = refs[:8]
    near = Near(n_wt)
    section, ctx, wt = near.section, near.ctx, near.wt
    peers = [(section, lax.rem(ctx + k, n_ctx), wt) for k in range(1, n_ctx)]
    waiting = []
    if ride:
        sums = RowSum(near, 1, ride_refs[0], refs[8:])
        waiting = [functools.partial(sums.step, 0, step) for step in range(n_wt - 1)]
        near.greet(peers)
        sums.begin()
    else:
        greet(peers)

    def ride_on():
        if waiting:
            waiting.pop(0)()

    rows = a_ref.shape[0] // 2
    low = lower_half((2 * rows, LANES))
    d_att = dot(a_ref[...], w_ref[:, 2 * LANES :], ((1,), (0,)))
    for h, part in enumerate((d_att[:, :LANES], roll(d_att[:, LANES:], HEAD_SIZE), d_att[:, LANES:])):
        d_out = jnp.where(low, 0.0, part).astype(BF16)
        for m in range(2):
            do_ref[m, h] = d_out[m * rows : (m + 1) * rows]
            product = do_ref[m, h].astype(F32) * out_ref[m, h]
            delta_ref[m, h] = jnp.sum(jnp.transpose(product), 0, keepdims=True)
    dq_ref[...] = jnp.zeros(dq_ref.shape, F32)
    ride_on()

    def block(c, j):
        keys = pairs_ref[c, j * rows : (j + 1) * rows, :]
        total = jnp.zeros((rows, LANES), F32)
        for m in range(j, 2):
            if m == j:
                seen = visible(key_place[c, j * rows : (j + 1) * rows, :], query_place[m], query_start[m])
            for h in range(HEADS):
                probs = jnp.exp(dot(keys, q_ref[m, h], ((1,), (1,))) - lse_ref[m, h])
                if m == j:
                    probs = jnp.where(seen, probs, 0.0)
                d_probs = dot(keys, do_ref[m, h], ((1,), (1,)))
                d_scores = (probs * (d_probs - delta_ref[m, h])).astype(BF16)
                total = total + dot(d_scores, q_ref[m, h], ((1,), (0,)))
                total = total + dot(probs.astype(BF16), do_ref[m, h], ((1,), (0,)))
                dq_ref[m, h] += dot(keys, d_scores, ((0,), (0,)))
        return total

    def passing(k):
        target = lax.rem(ctx + k, n_ctx)
        return remote(dkv_ref.at[target], landed.at[k - 1], send.at[k], recv.at[k], (section, target, wt))

    def sent(k):
        c = lax.rem(ctx + k, n_ctx)
        for j in range(2):
            dkv_ref[c, j * rows : (j + 1) * rows, :] = block(c, j).astype(BF16)
        passing(k).start()

    sent(1)
    ride_on()
    pl.loop(2, n_ctx)(sent)
    ride_on()

    for j in range(2):
        own_ref[j * rows : (j + 1) * rows, :] = block(ctx, j)

    while waiting:
        ride_on()
    if ride:
        sums.collect(0, rode_ref)
        rode_ref[...] += ride_refs[1][...]

    @pl.loop(1, n_ctx)
    def _(k):
        passing(k).wait_recv()
        own_ref[...] += landed[k - 1].astype(F32)

    cosine, sine = cos_ref[...], sin_ref[...]
    d_own = own_ref[...]
    over = roll(d_own, HEAD_SIZE)
    d_query = [
        jnp.concatenate([jnp.transpose(dq_ref[m, h]) for m in range(2)], 0) * (1.0 / HEAD_SIZE) for h in range(HEADS)
    ]
    first = jnp.where(low, d_query[0], roll(d_query[1], HEAD_SIZE))
    second = jnp.where(low, d_query[2], over)
    raw_ref[:, :LANES] = turned(first, cosine, -sine).astype(BF16)
    raw_ref[:, LANES : 2 * LANES] = turned(second, cosine, -sine).astype(BF16)
    raw_ref[:, 2 * LANES :] = jnp.where(low, over, 0.0).astype(BF16)
    part_ref[...] = dot(raw_ref[...], w_ref[:, : 3 * LANES], ((1,), (1,))).astype(BF16)
    if ride:
        sums.end()
    for k in range(1, n_ctx):
        passing(k).wait_send()


def attend_back(number, rows_a, weights, tables, kept, ride=()):
    n_ctx, n_wt = lax.axis_size("ctx"), lax.axis_size("wt")
    n_rows, width = rows_a.shape
    rows = n_rows // 2
    dma = pltpu.SemaphoreType.DMA
    return pl.pallas_call(
        functools.partial(attend_back_kernel, n_ctx, n_wt, bool(ride)),
        out_shape=[
            jax.ShapeDtypeStruct((n_rows, width), BF16),
            jax.ShapeDtypeStruct((n_rows, 3 * LANES), BF16),
        ]
        + [jax.ShapeDtypeStruct(member.shape, F32) for member in ride[1:]],
        in_specs=[VMEM] * (11 + len(ride)),
        out_specs=[VMEM] * (2 + len(ride) // 2),
        scratch_shapes=[
            pltpu.VMEM((2, HEADS, rows, LANES), BF16),
            pltpu.VMEM((2, HEADS, 1, rows), F32),
            pltpu.VMEM((2, HEADS, LANES, rows), F32),
            pltpu.VMEM((n_ctx, n_rows, LANES), BF16),
            pltpu.VMEM((n_rows, LANES), F32),
            pltpu.VMEM((n_ctx - 1, n_rows, LANES), BF16),
            dma((n_ctx,)),
            dma((n_ctx,)),
        ]
        + (RowSum.scratch(n_wt, ride[1].shape, 1) if ride else []),
        compiler_params=pltpu.CompilerParams(
            collective_id=number, has_side_effects=True, vmem_limit_bytes=40 << 20
        ),
        cost_estimate=pl.CostEstimate(flops=0, bytes_accessed=100 << 20, transcendentals=0),
    )(rows_a, weights, *tables, *kept, *ride)


def expert_halves(inward, down, packed, half, per_core):
    depth, down_rows = inward.shape[1], down.shape[1]
    wide, width = packed.shape[1], down.shape[2]
    column, second = inward.shape[2], depth + down_rows
    first, middle = wide - width, down_rows // 2
    a, b = half * per_core, half * per_core + 1
    return [
        (inward.at[a], packed.at[:depth, :column]),
        (inward.at[b], packed.at[:depth, column:]),
        (down.at[a], packed.at[depth:second, :width]),
        (down.at[b, :, :first], packed.at[depth:second, width:]),
        (down.at[b, :middle, first:], packed.at[second:, : wide // 2]),
        (down.at[b, middle:, first:], packed.at[second:, wide // 2 :]),
    ]


def prepare_kernel(query, pair, out, inward, down, routes, gains, router, *refs):
    attn, moe = refs[:2], refs[2:4]
    all_routes, all_gains, all_router, halves, keep_sem, send, recv = refs[4:]
    section, ctx, wt = place()
    sibling = (1 - section, ctx, wt)
    greet([sibling])
    per_core = inward.shape[0] // 2
    q_cols = query.shape[1] // 2
    outward = jnp.transpose(out[...].astype(F32))
    for half in range(2):
        halves[half] = jnp.concatenate(
            [
                query[:, half * q_cols : (half + 1) * q_cols].astype(F32),
                pair[:, half * LANES : (half + 1) * LANES].astype(F32),
                outward[:, half * q_cols : (half + 1) * q_cols],
            ],
            1,
        ).astype(BF16)
    for layer in range(2):

        @pl.when(section == layer)
        def _():
            own = expert_halves(inward, down, moe[layer], layer, per_core)
            other = expert_halves(inward, down, moe[layer], 1 - layer, per_core)
            own += [
                (halves.at[layer], attn[layer]),
                (routes, all_routes.at[layer]),
                (gains, all_gains.at[layer]),
                (router, all_router.at[layer]),
            ]
            other += [
                (halves.at[1 - layer], attn[layer]),
                (routes, all_routes.at[layer]),
                (gains, all_gains.at[layer]),
                (router, all_router.at[layer]),
            ]
            copies = [pltpu.make_async_copy(a, b, keep_sem.at[k]) for k, (a, b) in enumerate(own)]
            moves = [remote(a, b, send.at[k], recv.at[k], sibling) for k, (a, b) in enumerate(other)]
            for copy in moves + copies:
                copy.start()
            for copy in moves:
                copy.wait_send()
            for copy in copies:
                copy.wait()
            arrive = expert_halves(inward, down, moe[1 - layer], layer, per_core)
            arrive += [
                (halves.at[layer], attn[1 - layer]),
                (routes, all_routes.at[1 - layer]),
                (gains, all_gains.at[1 - layer]),
                (router, all_router.at[1 - layer]),
            ]
            for k, (a, b) in enumerate(arrive):
                remote(a, b, send.at[k], recv.at[k], sibling).wait_recv()


def prepare(number, query, pair, out, inward, down, routes, gains, router):
    depth, down_rows = inward.shape[1], down.shape[1]
    any_place = pl.BlockSpec(memory_space=pl.ANY)
    columns = query.shape[1] + LANES
    wide = inward.shape[0] // 2 * inward.shape[2]
    packed = jax.ShapeDtypeStruct((depth + down_rows + down_rows // 2, wide), BF16)
    attn = jax.ShapeDtypeStruct((depth, columns), BF16)
    both = [jax.ShapeDtypeStruct((2,) + member.shape, member.dtype) for member in (routes, gains, router)]
    dma = pltpu.SemaphoreType.DMA
    return pl.pallas_call(
        prepare_kernel,
        out_shape=[attn, attn, packed, packed] + both,
        in_specs=[VMEM] * 3 + [any_place] * 5,
        out_specs=[any_place] * 7,
        scratch_shapes=[pltpu.VMEM((2, depth, columns), BF16), dma((10,)), dma((10,)), dma((10,))],
        compiler_params=pltpu.CompilerParams(
            collective_id=number, has_side_effects=True, vmem_limit_bytes=40 << 20
        ),
    )(query, pair, out, inward, down, routes, gains, router)


TILE = 256


def expert_pieces(packed, inward, down, depth, down_rows):
    n, wide, width = packed.shape[0], packed.shape[2], down.shape[2]
    half = down_rows // 2
    first = wide - width
    pairs = []
    for c in range(n):
        at = c * down_rows
        second = depth + down_rows
        pairs += [
            (packed.at[c, depth:second, :width], down.at[0, at : at + down_rows, :]),
            (packed.at[c, depth:second, width:], down.at[1, at : at + down_rows, :first]),
            (packed.at[c, second:, : wide // 2], down.at[1, at : at + half, first:]),
            (packed.at[c, second:, wide // 2 :], down.at[1, at + half : at + down_rows, first:]),
        ]
    for c in range(n):
        pairs.append((packed.at[c, :depth, :], inward.at[c * depth : (c + 1) * depth, :]))
    return pairs


def gate_rows(x, router, routes):
    lane = lax.broadcasted_iota(jnp.int32, (x.shape[0], LANES), 1)
    named = routes[:, 0:1] == lane
    for t in range(1, routes.shape[1]):
        named = named | (routes[:, t : t + 1] == lane)
    logits = jnp.where(named, dot(x, router, ((1,), (0,))), MASKED)
    expos = jnp.where(named, jnp.exp(logits - jnp.max(logits, 1, keepdims=True)), 0.0)
    return expos / jnp.sum(expos, 1, keepdims=True)


def experts_kernel(forward, backward, depth, down_rows, *refs):
    refs = list(refs)
    x_ref, packed_ref, router_ref, pick_ref = [refs.pop(0) for _ in range(4)]
    if forward:
        hit_ref = refs.pop(0)
    else:
        gates_ref, gate_up_ref = refs.pop(0), refs.pop(0)
    d_ref = refs.pop(0) if backward else None
    part_ref = refs.pop(0) if forward else None
    if forward and not backward:
        gates_ref, gate_up_ref = refs.pop(0), refs.pop(0)
    if backward:
        back_ref, grads_ref, router_grad_ref = [refs.pop(0) for _ in range(3)]
    inward, down, weighted, load = [refs.pop(0) for _ in range(4)]
    if forward and backward:
        gates_ref, gate_up_ref = refs.pop(0), refs.pop(0)
    if backward:
        d_gate_up, x_turned, in_grad, down_grad, store = refs

    pieces = expert_pieces(packed_ref, inward, down, depth, down_rows)
    loads = [pltpu.make_async_copy(source, target, load.at[k]) for k, (source, target) in enumerate(pieces)]
    n_down = 4 * packed_ref.shape[0]
    for copy in (loads[n_down:] + loads[:n_down]) if forward else loads:
        copy.start()
    columns = [slice(t * TILE, (t + 1) * TILE) for t in range(2 * FF // TILE)]
    per_expert = FF // TILE
    width = x_ref.shape[1]

    def gate_at(t):
        return slice(2 * FF * (t // per_expert) + TILE * (t % per_expert), 2 * FF * (t // per_expert) + TILE * (t % per_expert + 1))

    def up_at(t):
        return slice(gate_at(t).start + FF, gate_at(t).stop + FF)

    def weight_of(e):
        return jnp.sum(gates_ref[...] * pick_ref[e : e + 1, :], 1, keepdims=True)

    if forward:
        gates_ref[...] = gate_rows(x_ref[...], router_ref[...], hit_ref[...])
        for copy in loads[n_down:]:
            copy.wait()
        for t, place_of in enumerate(columns):
            gate = dot(x_ref[...], inward[:, gate_at(t)], ((1,), (0,)))
            up = dot(x_ref[...], inward[:, up_at(t)], ((1,), (0,)))
            gate_up_ref[:, gate_at(t)] = gate.astype(BF16)
            gate_up_ref[:, up_at(t)] = up.astype(BF16)
            weighted[:, place_of] = (gate / (1.0 + jnp.exp(-gate)) * up * weight_of(t // per_expert)).astype(BF16)
        for copy in loads[:n_down]:
            copy.wait()
        for n in range(width // TILE):
            at = slice(n * TILE, (n + 1) * TILE)
            part_ref[:, at] = (
                dot(weighted[:, :FF], down[0, :, at], ((1,), (0,)))
                + dot(weighted[:, FF:], down[1, :, at], ((1,), (0,)))
            ).astype(BF16)
    else:
        for copy in loads[:n_down]:
            copy.wait()
    if backward:
        d_weight = [0.0, 0.0]
        for t, place_of in enumerate(columns):
            e = t // per_expert
            rows_of = slice(TILE * (t % per_expert), TILE * (t % per_expert + 1))
            weight = weight_of(e)
            d_weighted = dot(d_ref[...], down[e, rows_of, :], ((1,), (1,)))
            gate = gate_up_ref[:, gate_at(t)].astype(F32)
            up = gate_up_ref[:, up_at(t)].astype(F32)
            sigmoid = 1.0 / (1.0 + jnp.exp(-gate))
            activated = gate * sigmoid
            hidden = activated * up
            d_weight[e] = d_weight[e] + jnp.sum(hidden * d_weighted, 1, keepdims=True)
            weighted[:, place_of] = (hidden * weight).astype(BF16)
            d_hidden = d_weighted * weight
            d_gate_up[:, gate_at(t)] = (d_hidden * up * (sigmoid * (1.0 + gate * (1.0 - sigmoid)))).astype(BF16)
            d_gate_up[:, up_at(t)] = (d_hidden * activated).astype(BF16)
        gates = gates_ref[...]
        terms = gates * (pick_ref[0:1, :] * d_weight[0] + pick_ref[1:2, :] * d_weight[1])
        d_logits = terms - gates * jnp.sum(terms, 1, keepdims=True)
        high = d_logits.astype(BF16)
        low = (d_logits - high.astype(F32)).astype(BF16)
        both = jnp.concatenate([high, low], 1)
        if not forward:
            for copy in loads[n_down:]:
                copy.wait()
        for n in range(width // TILE):
            at = slice(n * TILE, (n + 1) * TILE)
            table = router_ref[at, :]
            back_ref[:, at] = (
                dot(d_gate_up[...], inward[at, :], ((1,), (1,)))
                + dot(both, jnp.concatenate([table, table], 1), ((1,), (1,)))
            ).astype(BF16)
        x_turned[...] = jnp.transpose(x_ref[...])
        router_grad = dot(both, x_ref[...], ((0,), (0,)))
        named = router_grad_ref.shape[0]
        router_grad_ref[...] = router_grad[:named] + router_grad[LANES : LANES + named]
        for n in range(2 * 2 * FF // TILE):
            at = slice(n * TILE, (n + 1) * TILE)
            in_grad[:, at] = dot(x_turned[...], d_gate_up[:, at], ((1,), (0,))).astype(BF16)
        for e in range(2):
            turned_hidden = jnp.transpose(weighted[:, e * FF : (e + 1) * FF])
            for n in range(width // TILE):
                at = slice(n * TILE, (n + 1) * TILE)
                down_grad[e, :, at] = dot(turned_hidden, d_ref[:, at], ((1,), (0,))).astype(BF16)
        stores = [
            pltpu.make_async_copy(source, target, store.at[k])
            for k, (target, source) in enumerate(expert_pieces(grads_ref, in_grad, down_grad, depth, down_rows))
        ]
        for copy in stores:
            copy.start()
        for copy in stores:
            copy.wait()


def experts(x, packed, router, pick, n_experts, depth, down_rows, hit=None, kept=None, d_rows=None):
    forward, backward = hit is not None, d_rows is not None
    n_rows, width = x.shape
    any_place = pl.BlockSpec(memory_space=pl.ANY)
    operands = [x, packed, router, pick]
    operands += [hit] if forward else list(kept)
    operands += [d_rows] if backward else []
    in_specs = [VMEM, any_place] + [VMEM] * (len(operands) - 2)
    rows_out = jax.ShapeDtypeStruct((n_rows, width), BF16)
    inner = [jax.ShapeDtypeStruct((n_rows, LANES), F32), jax.ShapeDtypeStruct((n_rows, 4 * FF), BF16)]
    n_pieces = 5 * packed.shape[0]
    scratch = [
        pltpu.VMEM((width, 4 * FF), BF16),
        pltpu.VMEM((2, FF, width), BF16),
        pltpu.VMEM((n_rows, 2 * FF), BF16),
        pltpu.SemaphoreType.DMA((n_pieces,)),
    ]
    outs = []
    out_specs = []
    if forward:
        outs += [rows_out]
        out_specs += [VMEM]
    if forward and not backward:
        outs += inner
        out_specs += [VMEM] * 2
    if backward:
        outs += [rows_out, jax.ShapeDtypeStruct(packed.shape, BF16), jax.ShapeDtypeStruct((n_experts, width), F32)]
        out_specs += [VMEM, any_place, VMEM]
        if forward:
            scratch += [pltpu.VMEM(member.shape, member.dtype) for member in inner]
        scratch += [
            pltpu.VMEM((n_rows, 4 * FF), BF16),
            pltpu.VMEM((width, n_rows), BF16),
            pltpu.VMEM((width, 4 * FF), BF16),
            pltpu.VMEM((2, FF, width), BF16),
            pltpu.SemaphoreType.DMA((n_pieces,)),
        ]
    work = n_rows * 6 * width * FF * 2 * ((1 if forward else 0) + (2 if backward else 0))
    return pl.pallas_call(
        functools.partial(experts_kernel, forward, backward, depth, down_rows),
        out_shape=outs,
        in_specs=in_specs,
        out_specs=out_specs,
        scratch_shapes=scratch,
        compiler_params=pltpu.CompilerParams(vmem_limit_bytes=56 << 20),
        cost_estimate=pl.CostEstimate(flops=2 * work, bytes_accessed=40 << 20, transcendentals=0),
    )(*operands)


def shards(tokens, cotangent, blocks, routes, norm_gain, w_query, key_value_weight, w_attn_out, router, w_in, w_down):
    section, ctx, wt = place()
    n_ctx, n_wt, layers = lax.axis_size("ctx"), lax.axis_size("wt"), lax.axis_size("section")
    micro_count, share, width = tokens.shape
    per_ctx = routes.shape[2]
    seq_len = per_ctx * n_ctx
    per_core = w_in.shape[1] // 2
    n_experts = router.shape[2]
    q_cols = w_query.shape[2] // 2
    depth = w_query.shape[1]

    block_len = seq_len // blocks.shape[1]
    placed = (blocks[:, :, None] * block_len + jnp.arange(block_len, dtype=jnp.int32)[None, None, :]).reshape(
        micro_count, seq_len
    )
    query_place = lax.dynamic_slice_in_dim(placed, ctx * per_ctx, per_ctx, 1)
    later = (jnp.arange(micro_count) > 0)[:, None]
    query_start = jnp.where(later, query_place - query_place % CONT_LEN, 0)
    query_pos = jnp.where(later, seq_len + query_place % CONT_LEN, query_place)
    inverse = jnp.power(ROPE_BASE, -jnp.arange(HEAD_SIZE // 2, dtype=F32) * 2.0 / HEAD_SIZE)
    angles = query_pos.reshape(-1).astype(F32)[:, None] * inverse[None, :]
    cosine, sine = jnp.cos(angles), jnp.sin(angles)
    tables = (
        jnp.tile(cosine, (1, 4)),
        jnp.concatenate([-sine, sine, -sine, sine], 1),
        jnp.transpose(placed.reshape(micro_count, n_ctx, per_ctx), (1, 0, 2)).reshape(n_ctx, -1, 1),
        query_place[:, None, :],
        query_start[:, None, :],
    )

    prepared = prepare(
        15,
        w_query[0],
        key_value_weight[0].reshape(depth, -1),
        w_attn_out[0],
        w_in[0],
        w_down[0],
        routes[0],
        norm_gain[0],
        router[0],
    )
    attn_pack, moe_pack = prepared[:2], prepared[2:4]
    route_pack, gain_pack, router_pack = prepared[4:]

    def unpacked(values, in_rows, down_rows):
        wide = values.shape[-1]
        n = values.shape[0]
        rest = values[:, in_rows + down_rows :]
        rest = jnp.concatenate([rest[..., : wide // 2], rest[..., wide // 2 :]], 1)
        down_part = jnp.concatenate([values[:, in_rows : in_rows + down_rows], rest], 2)
        return values[:, :in_rows].reshape(n * in_rows, wide), down_part.reshape(n * down_rows, -1)

    in_rows, down_rows = w_in.shape[2], w_down.shape[2]

    def gather_experts(pack):
        return lax.all_gather(pack, "ctx", axis=0, tiled=True).reshape((n_ctx,) + pack.shape)

    attn_full = [None, None]

    my_first = wt * 2 * per_core + section * per_core
    n_rows = micro_count * per_ctx

    hits = [route_pack[layer].reshape(n_rows, -1) for layer in range(2)]
    pick = (jnp.arange(LANES)[None, :] == my_first + jnp.arange(8)[:, None]).astype(F32)
    router_wide = [jnp.pad(router_pack[layer], ((0, 0), (0, LANES - n_experts))) for layer in range(2)]

    def full_rows(values):
        return values.reshape(n_rows, width)

    def blocked(values):
        return values.reshape(2 * n_wt, share, width).astype(BF16)

    stream = lax.dynamic_index_in_dim(tokens, section, 0, False).astype(F32)
    top = lax.dynamic_index_in_dim(cotangent, section, 0, False).astype(F32)

    normed_in, full = exchange(0, None, stream, gain=gain_pack[0, 0:1], spread="norm", gather=attn_pack[0])
    attn_full[0] = full.reshape(-1, full.shape[2])
    moe_full = [gather_experts(moe_pack[0]), None]
    saved = []
    outputs = []
    for layer in range(2):
        rows_in = full_rows(normed_in)
        weights = attn_full[layer]
        if layer == 0:
            top_low = lax.dynamic_index_in_dim(cotangent, section, 0, False)
            partial, *heads, attended, d_mixed = attend(2, rows_in, weights, tables, top_low)
        else:
            partial, *heads, attended = attend(3, rows_in, weights, tables)
        middle, normed_mid = exchange(
            4 + layer, blocked(partial), stream, gain=gain_pack[layer, 1:2], spread="norm"
        )
        if layer == 0:
            normed_mid, second = lax.optimization_barrier((normed_mid, moe_pack[1]))
            moe_full[1] = gather_experts(second)
        normed_mid, moe_full[layer] = lax.optimization_barrier((normed_mid, moe_full[layer]))
        rows_mid = full_rows(normed_mid)
        if layer == 0:
            partial, gates, gate_up = experts(
                rows_mid, moe_full[0], router_wide[0], pick, n_experts, in_rows, down_rows, hit=hits[0]
            )
            inner = (gates, gate_up)
        else:
            partial, *back_parts = experts(
                rows_mid, moe_full[1], router_wide[1], pick, n_experts, in_rows, down_rows, hit=hits[1], d_rows=full_rows(d_mixed)
            )
            inner = None
        saved.append(
            dict(
                stream=stream,
                middle=middle,
                rows_in=rows_in,
                rows_mid=rows_mid,
                heads=heads,
                attended=attended,
                inner=inner,
            )
        )
        if layer == 0:
            stream, normed_in, full = exchange(
                6, blocked(partial), middle, gain=gain_pack[1, 0:1], spread="norm", rounded=True, gather=attn_pack[1]
            )
            attn_full[1] = full.reshape(-1, full.shape[2])
            outputs.append(stream.astype(BF16))
        else:
            last_rows = (blocked(partial), middle)
    upstream = top
    grads_in = [None, None]
    attn_grads = [None, None]
    moe_grads = [None, None]
    small = [None, None]
    for layer in (1, 0):
        kept = saved[layer]
        if layer == 0:
            back_parts = experts(
                kept["rows_mid"],
                moe_full[0],
                router_wide[0],
                pick,
                n_experts,
                in_rows,
                down_rows,
                kept=kept["inner"],
                d_rows=full_rows(d_mixed),
            )
        partial, packed_grad, router_grad = back_parts
        if layer == 0:
            partial, packed_grad, moe_grads[1] = lax.optimization_barrier((partial, packed_grad, moe_grads[1]))
        else:
            partial, packed_grad = lax.optimization_barrier((partial, packed_grad))
        moe_grads[layer] = lax.psum_scatter(packed_grad, "ctx", scatter_dimension=0, tiled=False)
        d_middle, gain_grad_mid, d_attn = exchange(
            8 + layer, blocked(partial), upstream, kept["middle"], gain_pack[layer, 1:2], spread="plain"
        )
        rows_a = full_rows(d_attn)
        weights = attn_full[layer]
        if layer == 1:
            partial, raw, last = attend_back(11, rows_a, weights, tables, kept["heads"], last_rows)
            outputs.append(last.astype(BF16))
        else:
            partial, raw = attend_back(10, rows_a, weights, tables, kept["heads"])
        attn_parts = dot(kept["rows_in"], jnp.pad(raw, ((0, 0), (0, weights.shape[1] - raw.shape[1]))), ((0,), (0,)))
        attn_parts = attn_parts + dot(
            rows_a, jnp.pad(kept["attended"], ((0, 0), (weights.shape[1] - kept["attended"].shape[1], 0))), ((0,), (0,))
        )
        attn_parts = attn_parts.astype(BF16).reshape(n_ctx, depth, -1)
        if layer == 1:
            upstream, gain_grad_in, d_mixed, attn_grads[1] = exchange(
                12,
                blocked(partial),
                d_middle,
                kept["stream"],
                gain_pack[1, 0:1],
                spread="plain",
                rounded=True,
                add=attn_parts,
            )
        else:
            upstream, gain_grad_in, attn_grads[0] = exchange(
                1, blocked(partial), d_middle, kept["stream"], gain_pack[0, 0:1], rounded=True, add=attn_parts
            )
        grads_in[layer] = upstream.astype(BF16)
        small[layer] = [router_grad, gain_grad_in, gain_grad_mid]

    def by_core(parts, received):
        return jnp.where(section == 0, parts[0], received), jnp.where(section == 0, received, parts[1])

    small_total, *received = small_sum(14, small[0] + small[1], attn_grads + outputs + grads_in)
    out_pair = jnp.stack(by_core(outputs, received[1]))
    grad_pair = jnp.stack(by_core(grads_in, received[2]))
    piece = width // (n_ctx * n_wt)
    router_total = small_total[:n_experts, :piece]
    gain_total = small_total[n_experts : n_experts + 2, :piece]
    attn_first, attn_second = by_core(attn_grads, received[0])
    kv_at = q_cols
    out_at = q_cols + 2 * HEAD_SIZE
    grad_query = jnp.concatenate([attn_first[:, :kv_at], attn_second[:, :kv_at]], -1)
    grad_kv = jnp.stack([attn_first[:, kv_at:out_at], attn_second[:, kv_at:out_at]], 1)
    grad_out = jnp.concatenate([jnp.transpose(attn_first[:, out_at:]), jnp.transpose(attn_second[:, out_at:])], 0)

    def stacked(halves):
        columns = halves[0].shape[1] // per_core
        return jnp.stack(
            [half[:, e * columns : (e + 1) * columns] for half in halves for e in range(per_core)]
        ).astype(F32)

    moe_grads = [member.reshape(member.shape[-2:]) for member in moe_grads]
    moe_pair = by_core(moe_grads, hand_over(13, moe_grads[0], moe_grads[1]))
    moe_pair = [unpacked(member[None], in_rows, down_rows) for member in moe_pair]
    grad_in = stacked([member[0] for member in moe_pair])
    grad_down = stacked([member[1] for member in moe_pair])
    return (
        out_pair[None],
        grad_pair[None],
        gain_total[None],
        grad_query[None],
        grad_kv[None],
        grad_out[None],
        jnp.transpose(router_total)[None],
        grad_in[None],
        grad_down[None],
    )


def solution(mesh):
    return jax.shard_map(
        shards,
        mesh=mesh,
        in_specs=(
            P(None, ("ctx", "wt"), None),
            P(None, ("ctx", "wt"), None),
            P(),
            P("section", None, "ctx", None),
            P("section", None, None),
            P("section", "ctx", "wt"),
            P("section", "ctx", "wt", None),
            P("section", "wt", "ctx"),
            P("section", None, None),
            P("section", "wt", "ctx", None),
            P("section", "wt", "ctx", None),
        ),
        out_specs=(
            P("section", None, ("ctx", "wt"), None),
            P("section", None, ("ctx", "wt"), None),
            P("section", None, ("ctx", "wt")),
            P("section", "ctx", "wt"),
            P("section", "ctx", "wt", None),
            P("section", "wt", "ctx"),
            P("section", ("ctx", "wt"), None),
            P("section", "wt", "ctx", None),
            P("section", "wt", "ctx", None),
        ),
        check_vma=False,
    )
```

```python
import functools

import jax
import jax.numpy as jnp
from jax import lax
from jax.experimental import pallas as pl
from jax.experimental.pallas import tpu as pltpu
from jax.sharding import PartitionSpec as P

HEAD_SIZE = 64
FF = 512
CONT_LEN = 1024
EPSILON = 1e-06
ROPE_BASE = 10000.0
MASKED = -1e30
CHUNKS = 2
LANES = 2 * HEAD_SIZE
MESH = pl.DeviceIdType.MESH
F32 = jnp.float32
BF16 = jnp.bfloat16


def dot(left, right, contract):
    return lax.dot_general(left, right, (contract, ((), ())), preferred_element_type=F32)


def norm_scale(rows):
    return lax.rsqrt(jnp.mean(rows * rows, -1, keepdims=True) + EPSILON)


def place():
    return lax.axis_index("section"), lax.axis_index("ctx"), lax.axis_index("wt")


def greet(targets):
    barrier = pltpu.get_barrier_semaphore()
    for target in targets:
        pl.semaphore_signal(barrier, inc=1, device_id=target, device_id_type=MESH)
    pl.semaphore_wait(barrier, len(targets))


def remote(source, destination, send_sem, recv_sem, target):
    return pltpu.make_async_remote_copy(
        src_ref=source,
        dst_ref=destination,
        send_sem=send_sem,
        recv_sem=recv_sem,
        device_id=target,
        device_id_type=MESH,
    )


class Near:
    def __init__(self, n_wt):
        self.section, self.ctx, self.wt = place()
        self.n_wt = n_wt
        self.sibling = (1 - self.section, self.ctx, self.wt)
        self.right = (self.section, self.ctx, jnp.minimum(self.wt + 1, n_wt - 1))
        self.left = (self.section, self.ctx, jnp.maximum(self.wt - 1, 0))
        self.has_right, self.has_left = self.wt < n_wt - 1, self.wt > 0
        self.own = self.section * n_wt + self.wt

    def greet(self, others=()):
        barrier = pltpu.get_barrier_semaphore()

        def hail(target):
            pl.semaphore_signal(barrier, inc=1, device_id=target, device_id_type=MESH)

        hail(self.sibling)
        pl.when(self.has_right)(lambda: hail(self.right))
        pl.when(self.has_left)(lambda: hail(self.left))
        for other in others:
            hail(other)
        pl.semaphore_wait(
            barrier, 1 + len(others) + self.has_right.astype(jnp.int32) + self.has_left.astype(jnp.int32)
        )


def rows_of(chunk, rows):
    return slice(chunk * rows, (chunk + 1) * rows)


def block_at(last, block, rightward):
    return last + 1 - block if rightward else block - 1


class RowSum:
    def __init__(self, near, chunks, parts, scratch):
        self.near, self.chunks, self.parts = near, chunks, parts
        self.rows = parts.shape[1] // chunks
        self.from_sibling, self.in_right, self.in_left, self.out_right, self.out_left = scratch[:5]
        self.swap_send, self.swap_recv, self.send, self.recv = scratch[5:]

    @staticmethod
    def scratch(n_wt, shape, chunks):
        dma = pltpu.SemaphoreType.DMA
        return [pltpu.VMEM((n_wt,) + shape, BF16)] * 5 + [dma((chunks * n_wt,))] * 2 + [dma((2 * chunks * n_wt,))] * 2

    def swap(self, chunk, block):
        at = rows_of(chunk, self.rows)
        number = chunk * self.near.n_wt + block
        return remote(
            self.parts.at[(1 - self.near.section) * self.near.n_wt + block, at],
            self.from_sibling.at[block, at],
            self.swap_send.at[number],
            self.swap_recv.at[number],
            self.near.sibling,
        )

    def begin(self):
        n_wt = self.near.n_wt
        order = []
        for step in range(n_wt - 1):
            order += [n_wt - 1 - step, step]
        for chunk in range(self.chunks):
            for block in dict.fromkeys(order):
                self.swap(chunk, block).start()

    def chip_sum(self, chunk, block):
        at = rows_of(chunk, self.rows)
        mine = self.parts[self.near.section * self.near.n_wt + block, at, :]
        return mine.astype(F32) + self.from_sibling[block, at, :].astype(F32)

    def toward(self, chunk, block, rightward):
        at = rows_of(chunk, self.rows)
        number = (2 * chunk + (0 if rightward else 1)) * self.near.n_wt + block
        source, target = (self.out_right, self.in_right) if rightward else (self.out_left, self.in_left)
        return remote(
            source.at[block, at],
            target.at[block, at],
            self.send.at[number],
            self.recv.at[number],
            self.near.right if rightward else self.near.left,
        )

    def send_on(self, chunk, block, rightward):
        at = rows_of(chunk, self.rows)
        self.swap(chunk, block).wait_recv()
        outward, inward = (self.out_right, self.in_right) if rightward else (self.out_left, self.in_left)
        behind = self.near.has_left if rightward else self.near.has_right

        @pl.when(jnp.logical_not(behind))
        def _():
            outward[block, at, :] = self.chip_sum(chunk, block).astype(BF16)

        @pl.when(behind)
        def _():
            self.toward(chunk, block, rightward).wait_recv()
            outward[block, at, :] = (self.chip_sum(chunk, block) + inward[block, at, :].astype(F32)).astype(BF16)

        self.toward(chunk, block, rightward).start()

    def step(self, chunk, step):
        wt, n_wt = self.near.wt, self.near.n_wt
        far, near = n_wt - 1 - step, step
        lower = 2 * wt < n_wt
        pl.when((wt < far) & lower)(lambda: self.send_on(chunk, far, True))
        pl.when(wt > near)(lambda: self.send_on(chunk, near, False))
        pl.when((wt < far) & jnp.logical_not(lower))(lambda: self.send_on(chunk, far, True))

    def point(self, chunk, number):
        wt, last = self.near.wt, self.near.n_wt - 1
        for block in range(1, last + 1):
            turn = last - block
            if number == 0:
                pl.when(wt == 0)(functools.partial(self.send_on, chunk, block_at(last, block, True), True))
                pl.when(wt == last)(functools.partial(self.send_on, chunk, block_at(last, block, False), False))
            elif 1 <= number - turn < block:
                pl.when(wt == number - turn)(functools.partial(self.send_on, chunk, block, True))
                pl.when(wt == last - (number - turn))(functools.partial(self.send_on, chunk, last - block, False))

    def collect(self, chunk, result):
        at, wt = rows_of(chunk, self.rows), self.near.wt
        self.swap(chunk, wt).wait_recv()
        result[at, :] = self.chip_sum(chunk, wt)

        @pl.when(self.near.has_left)
        def _():
            self.toward(chunk, wt, True).wait_recv()
            result[at, :] += self.in_right[wt, at, :].astype(F32)

        @pl.when(self.near.has_right)
        def _():
            self.toward(chunk, wt, False).wait_recv()
            result[at, :] += self.in_left[wt, at, :].astype(F32)

    def end(self):
        wt, n_wt = self.near.wt, self.near.n_wt
        for chunk in range(self.chunks):
            for block in range(n_wt):
                self.swap(chunk, block).wait_send()
                if block > 0:
                    pl.when(wt < block)(self.toward(chunk, block, True).wait_send)
                if block < n_wt - 1:
                    pl.when(wt > block)(self.toward(chunk, block, False).wait_send)


class RowGather:
    def __init__(self, near, chunks, all_ref, scratch):
        self.near, self.chunks, self.all = near, chunks, all_ref
        self.rows = all_ref.shape[1] // chunks
        self.send, self.recv, self.pass_send, self.pass_recv = scratch
        self.sent, self.arrivals = [], []

    @staticmethod
    def scratch(n_wt, chunks):
        return [pltpu.SemaphoreType.DMA((2 * chunks * n_wt,))] * 4

    def along(self, chunk, block, hop, rightward):
        at = rows_of(chunk, self.rows)
        number = (2 * chunk + (0 if rightward else 1)) * self.near.n_wt + hop
        return remote(
            self.all.at[block, at],
            self.all.at[block, at],
            self.send.at[number],
            self.recv.at[number],
            self.near.right if rightward else self.near.left,
        )

    def across(self, chunk, block, number):
        at = rows_of(chunk, self.rows)
        number = 2 * chunk * self.near.n_wt + number
        return remote(
            self.all.at[block, at],
            self.all.at[block, at],
            self.pass_send.at[number],
            self.pass_recv.at[number],
            self.near.sibling,
        )

    def launch(self, condition, copy):
        pl.when(condition)(copy.start)
        self.sent.append((condition, copy))

    def first(self, chunk):
        near = self.near
        always = near.wt >= 0
        self.launch(near.has_right, self.along(chunk, near.own, 1, True))
        self.launch(near.has_left, self.along(chunk, near.own, 1, False))
        self.launch(always, self.across(chunk, near.own, 0))
        self.arrivals.append((always, self.across(chunk, near.own, 0)))

    def hop(self, chunk, hop):
        near, n_wt = self.near, self.near.n_wt
        for rightward, came, more, block, number in (
            (True, near.wt >= hop, near.has_right, jnp.maximum(near.own - hop, 0), hop),
            (False, near.wt + hop < n_wt, near.has_left, jnp.minimum(near.own + hop, 2 * n_wt - 1), n_wt + hop),
        ):
            pl.when(came)(self.along(chunk, block, hop, rightward).wait_recv)
            if hop + 1 < n_wt:
                self.launch(came & more, self.along(chunk, block, hop + 1, rightward))
            self.launch(came, self.across(chunk, block, number))
            self.arrivals.append((came, self.across(chunk, block, number)))

    def arrive(self):
        for condition, copy in self.arrivals:
            pl.when(condition)(copy.wait_recv)

    def end(self):
        for condition, copy in self.sent:
            pl.when(condition)(copy.wait_send)


def exchange_kernel(n_ctx, n_wt, reduce, back, spread, rounded, ride, *refs):
    refs = list(refs)
    near = Near(n_wt)
    section, ctx, wt = near.section, near.ctx, near.wt
    peers = [(section, lax.rem(ctx + k, n_ctx), wt) for k in range(1, n_ctx)]
    parts = refs.pop(0) if reduce else None
    rows_ref = refs.pop(0)
    stream_ref = refs.pop(0) if back else None
    gain_ref = refs.pop(0) if (back or spread) else None
    ride_ref = refs.pop(0) if ride else None
    result_ref = refs.pop(0) if reduce else None
    gain_grad_ref = refs.pop(0) if back else None
    all_ref = refs.pop(0) if spread else None
    rode_ref = refs.pop(0) if ride else None
    token_ref = refs.pop(0)
    token_ref[...] = jnp.zeros(token_ref.shape, F32)
    if reduce:
        sums = RowSum(near, CHUNKS, parts, refs[:9])
        refs = refs[9:]
        sum_ref = refs.pop(0) if rounded else result_ref
    if spread:
        gathers = RowGather(near, CHUNKS, all_ref, refs[:4])
        refs = refs[4:]
    if ride:
        landed, ride_send, ride_recv, ride_local = refs
    chunk_rows = rows_ref.shape[0] // CHUNKS
    near.greet(peers if ride else ())
    if reduce:
        sums.begin()
    if ride == "gather":
        keep = pltpu.make_async_copy(ride_ref, rode_ref.at[ctx], ride_local)
        keep.start()
        riders = [
            remote(ride_ref, rode_ref.at[ctx], ride_send.at[k], ride_recv.at[k], peers[k]) for k in range(n_ctx - 1)
        ]
    elif ride == "sum":
        riders = [
            remote(
                ride_ref.at[lax.rem(ctx + 1 + k, n_ctx)], landed.at[k], ride_send.at[k], ride_recv.at[k], peers[k]
            )
            for k in range(n_ctx - 1)
        ]
    if ride:
        for copy in riders:
            copy.start()

    def settle(chunk):
        at = rows_of(chunk, chunk_rows)
        if reduce:
            sums.collect(chunk, sum_ref)
            total = sum_ref[at, :]
            if back:
                stream = stream_ref[at, :].astype(F32)
                scale = norm_scale(stream)
                weighted = gain_ref[...] * total
                gain_part = jnp.sum(total * stream * scale, 0, keepdims=True)
                gain_grad_ref[...] = gain_part if chunk == 0 else gain_grad_ref[...] + gain_part
                total = scale * weighted - stream * (scale * scale * scale) * jnp.mean(
                    weighted * stream, -1, keepdims=True
                )
            total = rows_ref[at, :].astype(F32) + total
            if rounded:
                total = total.astype(BF16)
            result_ref[at, :] = total
            total = total.astype(F32)
        else:
            total = rows_ref[at, :].astype(F32)
        if spread:
            if spread == "norm":
                total = total * norm_scale(total) * gain_ref[...]
            all_ref[near.own, at, :] = total.astype(BF16)
            gathers.first(chunk)

    stages = []
    if reduce:
        stages += [functools.partial(sums.step, step=step) for step in range(n_wt - 1)]
    stages.append(settle)
    if spread:
        stages += [functools.partial(gathers.hop, hop=hop) for hop in range(1, n_wt)]
    for slot in range(CHUNKS + len(stages) - 1):
        for chunk in reversed(range(CHUNKS)):
            if 0 <= slot - chunk < len(stages):
                stages[slot - chunk](chunk)

    if spread:
        gathers.arrive()
    if ride == "gather":
        keep.wait()
        for copy in riders:
            copy.wait()
    elif ride == "sum":
        total = ride_ref[ctx].astype(F32)
        for k, copy in enumerate(riders):
            copy.wait()
            total = total + landed[k].astype(F32)
        rode_ref[...] = total
    if spread:
        gathers.end()
    if reduce:
        sums.end()


VMEM = pl.BlockSpec(memory_space=pltpu.VMEM)


def exchange(number, parts, rows, stream=None, gain=None, spread=None, rounded=False, gather=None, add=None):
    n_ctx, n_wt = lax.axis_size("ctx"), lax.axis_size("wt")
    shape = rows.shape
    reduce, back = parts is not None, stream is not None
    ride = "gather" if gather is not None else "sum" if add is not None else None
    rider = gather if gather is not None else add
    operands = [
        member
        for member, wanted in (
            (parts, reduce),
            (rows, True),
            (stream, back),
            (gain, back or spread),
            (rider, ride),
        )
        if wanted
    ]
    outs = []
    scratch = []
    dma = pltpu.SemaphoreType.DMA
    if reduce:
        outs.append(jax.ShapeDtypeStruct(shape, BF16 if rounded else F32))
        scratch += RowSum.scratch(n_wt, shape, CHUNKS)
        scratch += [pltpu.VMEM(shape, F32)] if rounded else []
    if back:
        outs.append(jax.ShapeDtypeStruct((1, shape[1]), F32))
    if spread:
        outs.append(jax.ShapeDtypeStruct((2 * n_wt,) + shape, BF16))
        scratch += RowGather.scratch(n_wt, CHUNKS)
    if ride == "gather":
        outs.append(jax.ShapeDtypeStruct((n_ctx,) + rider.shape, BF16))
        scratch += [pltpu.VMEM((8, 128), BF16), dma((n_ctx - 1,)), dma((n_ctx - 1,)), dma]
    elif ride == "sum":
        outs.append(jax.ShapeDtypeStruct(rider.shape[1:], F32))
        scratch += [pltpu.VMEM((n_ctx - 1,) + rider.shape[1:], BF16), dma((n_ctx - 1,)), dma((n_ctx - 1,)), dma]
    outs.append(jax.ShapeDtypeStruct((8, LANES), F32))
    return pl.pallas_call(
        functools.partial(exchange_kernel, n_ctx, n_wt, reduce, back, spread, rounded, ride),
        out_shape=outs,
        in_specs=[VMEM] * len(operands),
        out_specs=[VMEM] * len(outs),
        scratch_shapes=scratch,
        compiler_params=pltpu.CompilerParams(
            collective_id=number, has_side_effects=True, vmem_limit_bytes=16 << 20
        ),
        cost_estimate=pl.CostEstimate(flops=0, bytes_accessed=110 << 20, transcendentals=0),
    )(*operands)


def finish_kernel(n_ctx, n_wt, *refs):
    small, attn, rows = refs[:6], refs[6:8], refs[8:12]
    gain_ref, router_ref, query_ref, pair_ref, out_ref, rows_ref, grads_ref = refs[12:19]
    parts, landed, summed, from_sibling, received, send, recv, swap_send, swap_recv = refs[19:]
    section, ctx, wt = place()
    count = n_ctx * n_wt
    own = ctx * n_wt + wt
    blocks = [lax.rem(own + k, count) for k in range(1, count)]
    peers = [(section, block // n_wt, lax.rem(block, n_wt)) for block in blocks]
    sibling = (1 - section, ctx, wt)
    greet([sibling] + peers)
    members = [(attn[0], attn[1], received)]
    members += [(rows[0], rows[1], rows_ref.at[section]), (rows[2], rows[3], grads_ref.at[section])]
    swaps = [
        [remote(member[1 - layer], member[2], swap_send.at[k], swap_recv.at[k], sibling) for k, member in enumerate(members)]
        for layer in range(2)
    ]
    for layer in range(2):

        @pl.when(section == layer)
        def _():
            for copy in swaps[layer]:
                copy.start()

    piece = small[0].shape[1] // count
    parts[...] = jnp.zeros(parts.shape, F32)
    for block in range(count):
        for layer in range(2):
            at = 0
            for ref in small[3 * layer : 3 * layer + 3]:
                end = at + ref.shape[0]
                parts[block, layer, at:end, :piece] = ref[:, block * piece : (block + 1) * piece]
                at = end
    copies = [
        remote(parts.at[blocks[k]], landed.at[k], send.at[k], recv.at[k], peers[k]) for k in range(count - 1)
    ]
    for copy in copies:
        copy.start()
    mine = section == 0
    rows_ref[section] = jnp.where(mine, rows[0][...], rows[1][...])
    grads_ref[section] = jnp.where(mine, rows[2][...], rows[3][...])
    for copy in swaps[0]:
        copy.wait_recv()
    held = jnp.where(mine, attn[0][...], attn[1][...])
    came = received[...]
    first, second = jnp.where(mine, held, came), jnp.where(mine, came, held)
    q_cols = query_ref.shape[1] // 2
    at = q_cols + LANES
    query_ref[...] = jnp.concatenate([first[:, :q_cols], second[:, :q_cols]], 1)
    pair_ref[...] = jnp.concatenate([first[:, q_cols:at], second[:, q_cols:at]], 1)
    out_ref[...] = jnp.transpose(jnp.concatenate([first[:, at:], second[:, at:]], 1))
    total = parts[own]
    for k, copy in enumerate(copies):
        copy.wait_recv()
        total = total + landed[k]
    summed[...] = total
    swap = remote(summed.at[1 - section], from_sibling, send.at[count - 1], recv.at[count - 1], sibling)
    swap.start()
    swap.wait()
    total = summed[section] + from_sibling[...]
    named = small[0].shape[0]
    gain_ref[...] = total[named : named + 2, :]
    router_ref[...] = total[:named, :]
    for copy in copies:
        copy.wait_send()
    for copy in swaps[0]:
        copy.wait_send()


def finish(number, small, attn, rows, q_cols):
    n_ctx, n_wt = lax.axis_size("ctx"), lax.axis_size("wt")
    count = n_ctx * n_wt
    named = small[0].shape[0]
    shape = (2, named + 2 + -(named + 2) % 8, LANES)
    dma = pltpu.SemaphoreType.DMA
    depth = attn[0].shape[0]
    pair = jax.ShapeDtypeStruct((2,) + rows[0].shape, BF16)
    return pl.pallas_call(
        functools.partial(finish_kernel, n_ctx, n_wt),
        out_shape=[
            jax.ShapeDtypeStruct((2, LANES), F32),
            jax.ShapeDtypeStruct((named, LANES), F32),
            jax.ShapeDtypeStruct((depth, 2 * q_cols), F32),
            jax.ShapeDtypeStruct((depth, 2 * LANES), F32),
            jax.ShapeDtypeStruct((2 * q_cols, depth), F32),
            pair,
            pair,
        ],
        in_specs=[VMEM] * 12,
        out_specs=[VMEM] * 7,
        scratch_shapes=[
            pltpu.VMEM((count,) + shape, F32),
            pltpu.VMEM((count - 1,) + shape, F32),
            pltpu.VMEM(shape, F32),
            pltpu.VMEM(shape[1:], F32),
            pltpu.VMEM(attn[0].shape, F32),
            dma((count,)),
            dma((count,)),
            dma((3,)),
            dma((3,)),
        ],
        compiler_params=pltpu.CompilerParams(
            collective_id=number, has_side_effects=True, vmem_limit_bytes=16 << 20
        ),
        cost_estimate=pl.CostEstimate(flops=0, bytes_accessed=40 << 20, transcendentals=0),
    )(*small, *attn, *rows)


def hand_over_kernel(per_core, first, second, after, inward, down, held, send, recv, load, keep):
    section, ctx, wt = place()
    sibling = (1 - section, ctx, wt)
    for layer, own in enumerate((first, second)):

        @pl.when(section == layer)
        def _():
            pltpu.make_async_copy(own, held, load).start()

    def moves(source):
        pieces = expert_halves(inward, down, source, section, per_core)
        return [remote(piece, target, send.at[k], recv.at[k], sibling) for k, (target, piece) in enumerate(pieces)]

    greet([sibling])
    for layer, other in enumerate((second, first)):

        @pl.when(section == layer)
        def _():
            for copy in moves(other):
                copy.start()

    pltpu.make_async_copy(first, held, load).wait()
    pieces = expert_halves(inward, down, held, section, per_core)
    copies = [pltpu.make_async_copy(piece, target, keep.at[k]) for k, (target, piece) in enumerate(pieces)]
    for copy in copies:
        copy.start()
    for copy in copies:
        copy.wait()
    for copy in moves(first):
        copy.wait()


def hand_over(number, first, second, after, depth, down_rows, per_core, width):
    any_place = pl.BlockSpec(memory_space=pl.ANY)
    dma = pltpu.SemaphoreType.DMA
    return pl.pallas_call(
        functools.partial(hand_over_kernel, per_core),
        out_shape=[
            jax.ShapeDtypeStruct((2 * per_core, depth, first.shape[1] // per_core), first.dtype),
            jax.ShapeDtypeStruct((2 * per_core, down_rows, width), first.dtype),
        ],
        in_specs=[any_place] * 3,
        out_specs=[any_place] * 2,
        scratch_shapes=[pltpu.VMEM(first.shape, first.dtype), dma((6,)), dma((6,)), dma, dma((6,))],
        compiler_params=pltpu.CompilerParams(
            collective_id=number, has_side_effects=True, vmem_limit_bytes=60 << 20
        ),
    )(first, second, after)


HEADS = 3


def roll(values, by):
    return pltpu.roll(values, by, 1)


def lower_half(shape):
    return lax.broadcasted_iota(jnp.int32, shape, 1) < HEAD_SIZE


def turned(values, cosine, sine):
    first = lax.rem(lax.broadcasted_iota(jnp.int32, values.shape, 1), HEAD_SIZE) < HEAD_SIZE // 2
    half = HEAD_SIZE // 2
    return values * cosine + jnp.where(first, roll(values, LANES - half), roll(values, half)) * sine


def visible(key_place, query_place, query_start):
    return (key_place <= query_place) & (key_place >= query_start)


def attend_kernel(
    n_ctx,
    n_wt,
    ride,
    x_ref,
    w_ref,
    cos_ref,
    sin_ref,
    key_place,
    query_place,
    query_start,
    *refs,
):
    refs = list(refs)
    ride_ref = refs.pop(0) if ride else None
    part_ref, q_ref, pairs_ref, out_ref, lse_ref, att_ref = [refs.pop(0) for _ in range(6)]
    all_ref = refs.pop(0) if ride else None
    top_ref, sum_ref, acc_ref, send, recv = refs[:5]
    near = Near(n_wt)
    section, ctx, wt = near.section, near.ctx, near.wt
    peers = [(section, lax.rem(ctx + k, n_ctx), wt) for k in range(1, n_ctx)]
    waiting = []
    if ride:
        gathers = RowGather(near, 1, all_ref, refs[5:])
        waiting = [functools.partial(gathers.hop, 0, hop) for hop in range(1, n_wt)]
        all_ref[near.own] = ride_ref[...]
        near.greet(peers)
        gathers.first(0)
    else:
        greet(peers)

    def ride_on():
        if waiting:
            waiting.pop(0)()

    rows = x_ref.shape[0] // 2
    low = lower_half((2 * rows, LANES))
    mixed = dot(x_ref[...], w_ref[:, : 3 * LANES], ((1,), (0,)))
    cosine, sine = cos_ref[...], sin_ref[...]
    first = turned(mixed[:, :LANES], cosine, sine)
    second = turned(mixed[:, LANES : 2 * LANES], cosine, sine)
    pairs_ref[ctx] = jnp.where(low, roll(second, HEAD_SIZE), roll(mixed[:, 2 * LANES :], HEAD_SIZE)).astype(BF16)

    def passing(k):
        return remote(
            pairs_ref.at[ctx], pairs_ref.at[ctx], send.at[k], recv.at[k], (section, lax.rem(ctx + k, n_ctx), wt)
        )

    for k in range(1, n_ctx):
        passing(k).start()
    for h, part in enumerate((first, roll(first, HEAD_SIZE), second)):
        scaled = jnp.where(low, part * (1.0 / HEAD_SIZE), 0.0).astype(BF16)
        q_ref[0, h] = scaled[:rows]
        q_ref[1, h] = scaled[rows:]
    ride_on()
    top_ref[...] = jnp.full(top_ref.shape, MASKED, F32)
    sum_ref[...] = jnp.zeros(sum_ref.shape, F32)
    acc_ref[...] = jnp.zeros(acc_ref.shape, F32)

    def block(c, m, j):
        keys = pairs_ref[c, j * rows : (j + 1) * rows, :]
        if m == j:
            seen = visible(key_place[c, j * rows : (j + 1) * rows, :], query_place[m], query_start[m])
        for h in range(HEADS):
            logits = dot(keys, q_ref[m, h], ((1,), (1,)))
            if m == j:
                logits = jnp.where(seen, logits, MASKED)
            before = top_ref[m, h]
            top = jnp.maximum(before, jnp.max(logits, 0, keepdims=True))
            expos = jnp.exp(logits - top)
            shrink = jnp.exp(before - top)
            top_ref[m, h] = top
            sum_ref[m, h] = sum_ref[m, h] * shrink + jnp.sum(expos, 0, keepdims=True)
            acc_ref[m, h] = acc_ref[m, h] * shrink + dot(keys, expos.astype(BF16), ((0,), (0,)))

    def blocks_of(c):
        block(c, 0, 0)
        block(c, 1, 1)
        block(c, 1, 0)

    blocks_of(ctx)
    ride_on()

    def arrived(k):
        passing(k).wait_recv()
        blocks_of(lax.rem(ctx + n_ctx - k, n_ctx))

    arrived(1)
    ride_on()
    pl.loop(2, n_ctx)(arrived)
    while waiting:
        ride_on()
    low = lower_half((rows, LANES))
    for m in range(2):
        outs = []
        for h in range(HEADS):
            lse_ref[m, h] = top_ref[m, h] + jnp.log(sum_ref[m, h])
            outs.append(jnp.transpose(acc_ref[m, h] / sum_ref[m, h]))
            out_ref[m, h] = outs[h]
        att_ref[m * rows : (m + 1) * rows, :LANES] = jnp.where(low, 0.0, outs[0]).astype(BF16)
        att_ref[m * rows : (m + 1) * rows, LANES:] = jnp.where(low, roll(outs[1], HEAD_SIZE), outs[2]).astype(BF16)
    part_ref[...] = dot(att_ref[...], w_ref[:, 2 * LANES :], ((1,), (1,))).astype(BF16)
    if ride:
        gathers.arrive()
        gathers.end()
    for k in range(1, n_ctx):
        passing(k).wait_send()


def attend(number, rows_in, weights, tables, ride=None):
    n_ctx, n_wt = lax.axis_size("ctx"), lax.axis_size("wt")
    riders = [] if ride is None else [ride]
    n_rows, width = rows_in.shape
    rows = n_rows // 2
    dma = pltpu.SemaphoreType.DMA
    return pl.pallas_call(
        functools.partial(attend_kernel, n_ctx, n_wt, bool(riders)),
        out_shape=[
            jax.ShapeDtypeStruct((n_rows, width), BF16),
            jax.ShapeDtypeStruct((2, HEADS, rows, LANES), BF16),
            jax.ShapeDtypeStruct((n_ctx, n_rows, LANES), BF16),
            jax.ShapeDtypeStruct((2, HEADS, rows, LANES), F32),
            jax.ShapeDtypeStruct((2, HEADS, 1, rows), F32),
            jax.ShapeDtypeStruct((n_rows, 2 * LANES), BF16),
        ]
        + [jax.ShapeDtypeStruct((2 * n_wt,) + member.shape, BF16) for member in riders],
        in_specs=[VMEM] * (7 + len(riders)),
        out_specs=[VMEM] * (6 + len(riders)),
        scratch_shapes=[
            pltpu.VMEM((2, HEADS, 1, rows), F32),
            pltpu.VMEM((2, HEADS, 1, rows), F32),
            pltpu.VMEM((2, HEADS, LANES, rows), F32),
            dma((n_ctx,)),
            dma((n_ctx,)),
        ]
        + (RowGather.scratch(n_wt, 1) if riders else []),
        compiler_params=pltpu.CompilerParams(
            collective_id=number, has_side_effects=True, vmem_limit_bytes=20 << 20
        ),
        cost_estimate=pl.CostEstimate(flops=0, bytes_accessed=70 << 20, transcendentals=0),
    )(rows_in, weights, *tables, *riders)


def attend_back_kernel(
    n_ctx,
    n_wt,
    ride,
    a_ref,
    w_ref,
    cos_ref,
    sin_ref,
    key_place,
    query_place,
    query_start,
    q_ref,
    pairs_ref,
    out_ref,
    lse_ref,
    *refs,
):
    refs = list(refs)
    ride_refs = [refs.pop(0), refs.pop(0)] if ride else None
    part_ref, raw_ref = refs.pop(0), refs.pop(0)
    rode_ref = refs.pop(0) if ride else None
    do_ref, delta_ref, dq_ref, dkv_ref, own_ref, landed, send, recv = refs[:8]
    near = Near(n_wt)
    section, ctx, wt = near.section, near.ctx, near.wt
    peers = [(section, lax.rem(ctx + k, n_ctx), wt) for k in range(1, n_ctx)]
    waiting = []
    if ride:
        sums = RowSum(near, 1, ride_refs[0], refs[8:17])
        rode_sum = refs[17]
        waiting = [functools.partial(sums.point, 0, number) for number in range(n_wt - 1)]
        near.greet(peers)
        sums.begin()
    else:
        greet(peers)

    def ride_on():
        if waiting:
            waiting.pop(0)()

    rows = a_ref.shape[0] // 2
    low = lower_half((2 * rows, LANES))
    d_att = dot(a_ref[...], w_ref[:, 2 * LANES :], ((1,), (0,)))
    for h, part in enumerate((d_att[:, :LANES], roll(d_att[:, LANES:], HEAD_SIZE), d_att[:, LANES:])):
        d_out = jnp.where(low, 0.0, part).astype(BF16)
        for m in range(2):
            do_ref[m, h] = d_out[m * rows : (m + 1) * rows]
            product = do_ref[m, h].astype(F32) * out_ref[m, h]
            delta_ref[m, h] = jnp.sum(jnp.transpose(product), 0, keepdims=True)
    dq_ref[...] = jnp.zeros(dq_ref.shape, F32)
    ride_on()

    def block(c, j):
        keys = pairs_ref[c, j * rows : (j + 1) * rows, :]
        total = jnp.zeros((rows, LANES), F32)
        for m in range(j, 2):
            if m == j:
                seen = visible(key_place[c, j * rows : (j + 1) * rows, :], query_place[m], query_start[m])
            for h in range(HEADS):
                probs = jnp.exp(dot(keys, q_ref[m, h], ((1,), (1,))) - lse_ref[m, h])
                if m == j:
                    probs = jnp.where(seen, probs, 0.0)
                d_probs = dot(keys, do_ref[m, h], ((1,), (1,)))
                d_scores = (probs * (d_probs - delta_ref[m, h])).astype(BF16)
                total = total + dot(d_scores, q_ref[m, h], ((1,), (0,)))
                total = total + dot(probs.astype(BF16), do_ref[m, h], ((1,), (0,)))
                dq_ref[m, h] += dot(keys, d_scores, ((0,), (0,)))
        return total

    def passing(k):
        target = lax.rem(ctx + k, n_ctx)
        return remote(dkv_ref.at[target], landed.at[k - 1], send.at[k], recv.at[k], (section, target, wt))

    def sent(k):
        c = lax.rem(ctx + k, n_ctx)
        for j in range(2):
            dkv_ref[c, j * rows : (j + 1) * rows, :] = block(c, j).astype(BF16)
        passing(k).start()

    sent(1)
    sent(2)
    ride_on()
    pl.loop(3, n_ctx)(sent)

    for j in range(2):
        own_ref[j * rows : (j + 1) * rows, :] = block(ctx, j)

    while waiting:
        ride_on()

    @pl.loop(1, n_ctx)
    def _(k):
        passing(k).wait_recv()
        own_ref[...] += landed[k - 1].astype(F32)

    cosine, sine = cos_ref[...], sin_ref[...]
    d_own = own_ref[...]
    over = roll(d_own, HEAD_SIZE)
    d_query = [
        jnp.concatenate([jnp.transpose(dq_ref[m, h]) for m in range(2)], 0) * (1.0 / HEAD_SIZE) for h in range(HEADS)
    ]
    first = jnp.where(low, d_query[0], roll(d_query[1], HEAD_SIZE))
    second = jnp.where(low, d_query[2], over)
    raw_ref[:, :LANES] = turned(first, cosine, -sine).astype(BF16)
    raw_ref[:, LANES : 2 * LANES] = turned(second, cosine, -sine).astype(BF16)
    raw_ref[:, 2 * LANES :] = jnp.where(low, over, 0.0).astype(BF16)
    part_ref[...] = dot(raw_ref[...], w_ref[:, : 3 * LANES], ((1,), (1,))).astype(BF16)
    if ride:
        sums.collect(0, rode_sum)
        rode_ref[...] = (rode_sum[...] + ride_refs[1][...]).astype(BF16)
        sums.end()
    for k in range(1, n_ctx):
        passing(k).wait_send()


def attend_back(number, rows_a, weights, tables, kept, ride=()):
    n_ctx, n_wt = lax.axis_size("ctx"), lax.axis_size("wt")
    n_rows, width = rows_a.shape
    rows = n_rows // 2
    dma = pltpu.SemaphoreType.DMA
    return pl.pallas_call(
        functools.partial(attend_back_kernel, n_ctx, n_wt, bool(ride)),
        out_shape=[
            jax.ShapeDtypeStruct((n_rows, width), BF16),
            jax.ShapeDtypeStruct((n_rows, 3 * LANES), BF16),
        ]
        + [jax.ShapeDtypeStruct(member.shape, BF16) for member in ride[1:]],
        in_specs=[VMEM] * (11 + len(ride)),
        out_specs=[VMEM] * (2 + len(ride) // 2),
        scratch_shapes=[
            pltpu.VMEM((2, HEADS, rows, LANES), BF16),
            pltpu.VMEM((2, HEADS, 1, rows), F32),
            pltpu.VMEM((2, HEADS, LANES, rows), F32),
            pltpu.VMEM((n_ctx, n_rows, LANES), BF16),
            pltpu.VMEM((n_rows, LANES), F32),
            pltpu.VMEM((n_ctx - 1, n_rows, LANES), BF16),
            dma((n_ctx,)),
            dma((n_ctx,)),
        ]
        + (RowSum.scratch(n_wt, ride[1].shape, 1) + [pltpu.VMEM(ride[1].shape, F32)] if ride else []),
        compiler_params=pltpu.CompilerParams(
            collective_id=number, has_side_effects=True, vmem_limit_bytes=24 << 20
        ),
        cost_estimate=pl.CostEstimate(flops=0, bytes_accessed=100 << 20, transcendentals=0),
    )(rows_a, weights, *tables, *kept, *ride)


def expert_halves(inward, down, packed, half, per_core):
    depth, down_rows = inward.shape[1], down.shape[1]
    wide, width = packed.shape[1], down.shape[2]
    column, second = inward.shape[2], depth + down_rows
    first, middle = wide - width, down_rows // 2
    a, b = half * per_core, half * per_core + 1
    return [
        (inward.at[a], packed.at[:depth, :column]),
        (inward.at[b], packed.at[:depth, column:]),
        (down.at[a], packed.at[depth:second, :width]),
        (down.at[b, :, :first], packed.at[depth:second, width:]),
        (down.at[b, :middle, first:], packed.at[second:, : wide // 2]),
        (down.at[b, middle:, first:], packed.at[second:, wide // 2 :]),
    ]


def prepare_kernel(inward, down, first, second, halves, load, send, recv, keep):
    packed = (first, second)
    section, ctx, wt = place()
    sibling = (1 - section, ctx, wt)
    per_core = inward.shape[0] // 2
    loads = []
    for half in range(2):
        for source, target in expert_halves(inward, down, halves.at[half], half, per_core):
            loads.append(pltpu.make_async_copy(source, target, load.at[len(loads)]))
    for copy in loads:
        copy.start()
    greet([sibling])
    for copy in loads:
        copy.wait()
    for layer in range(2):

        @pl.when(section == layer)
        def _():
            move = remote(halves.at[1 - layer], packed[layer], send, recv, sibling)
            move.start()
            own = pltpu.make_async_copy(halves.at[layer], packed[layer], keep)
            own.start()
            own.wait()
            move.wait_send()
            remote(halves.at[layer], packed[1 - layer], send, recv, sibling).wait_recv()


def prepare(number, inward, down):
    depth, down_rows = inward.shape[1], down.shape[1]
    in_place = pl.BlockSpec(memory_space=pltpu.HBM)
    shape = (depth + down_rows + down_rows // 2, inward.shape[0] // 2 * inward.shape[2])
    packed = jax.ShapeDtypeStruct(shape, BF16)
    dma = pltpu.SemaphoreType.DMA
    return pl.pallas_call(
        prepare_kernel,
        out_shape=[packed, packed],
        in_specs=[in_place] * 2,
        out_specs=[in_place] * 2,
        scratch_shapes=[pltpu.VMEM((2,) + shape, BF16), dma((12,)), dma, dma, dma],
        compiler_params=pltpu.CompilerParams(
            collective_id=number, has_side_effects=True, vmem_limit_bytes=12 << 20
        ),
    )(inward, down)


def begin_kernel(n_ctx, n_wt, *refs):
    given = refs[:7]
    all_ref, rode_ref, pack, all_gains, all_router, all_routes = refs[7:13]
    tokens, query, pair, out, gains, router, routes = refs[13:20]
    halves, first_pack, load, keep, send, recv, ride_send, ride_recv = refs[20:28]
    near = Near(n_wt)
    loads = [
        pltpu.make_async_copy(source.at[near.section] if k == 0 else source, target, load.at[k])
        for k, (source, target) in enumerate(zip(given, refs[13:20]))
    ]
    for copy in loads:
        copy.start()
    section, ctx, wt = near.section, near.ctx, near.wt
    peers = [(section, lax.rem(ctx + k, n_ctx), wt) for k in range(1, n_ctx)]
    gathers = RowGather(near, CHUNKS, all_ref, refs[28:])
    near.greet(peers)
    for copy in loads:
        copy.wait()
    named = router.shape[0]
    all_gains[section] = gains[...]
    all_routes[section] = routes[...]
    all_router[section] = jnp.zeros(all_router.shape[1:], BF16)
    all_router[section, :named, :] = router[...]
    shared = [
        remote(ref.at[section], ref.at[section], send.at[k], recv.at[k], near.sibling)
        for k, ref in enumerate((all_gains, all_router, all_routes))
    ]
    for copy in shared:
        copy.start()
    q_cols = query.shape[1] // 2
    outward = jnp.transpose(out[...].astype(F32))
    for half in range(2):
        halves[half] = jnp.concatenate(
            [
                query[:, half * q_cols : (half + 1) * q_cols].astype(F32),
                pair[:, half * LANES : (half + 1) * LANES].astype(F32),
                outward[:, half * q_cols : (half + 1) * q_cols],
            ],
            1,
        ).astype(BF16)
    packs = (first_pack, pack)
    for layer in range(2):

        @pl.when(section == layer)
        def _():
            remote(halves.at[1 - layer], packs[layer], send.at[3], recv.at[3], near.sibling).start()
            packs[layer][...] = halves[layer]

    rows = tokens[...].astype(F32)
    scaled = rows * norm_scale(rows)
    shared[0].wait_recv()
    all_ref[near.own] = (scaled * all_gains[0, 0:1, :]).astype(BF16)
    for chunk in range(CHUNKS):
        gathers.first(chunk)
    for layer in range(2):

        @pl.when(section == layer)
        def _():
            remote(halves.at[layer], packs[1 - layer], send.at[3], recv.at[3], near.sibling).wait_recv()

    own = pltpu.make_async_copy(first_pack, rode_ref.at[ctx], keep)
    riders = [
        remote(first_pack, rode_ref.at[ctx], ride_send.at[k], ride_recv.at[k], peers[k]) for k in range(n_ctx - 1)
    ]
    for copy in riders + [own]:
        copy.start()
    for hop in range(1, n_wt):
        for chunk in range(CHUNKS):
            gathers.hop(chunk, hop)
    gathers.arrive()
    own.wait()
    for copy in riders:
        copy.wait()
    gathers.end()
    shared[0].wait_send()
    for copy in shared[1:]:
        copy.wait()
    remote(halves.at[0], first_pack, send.at[3], recv.at[3], near.sibling).wait_send()


def begin(number, tokens, query, pair, out, gains, router, routes):
    n_ctx, n_wt = lax.axis_size("ctx"), lax.axis_size("wt")
    depth, columns = query.shape[0], query.shape[1] + LANES
    dma = pltpu.SemaphoreType.DMA
    pack = (depth, columns)
    return pl.pallas_call(
        functools.partial(begin_kernel, n_ctx, n_wt),
        out_shape=[
            jax.ShapeDtypeStruct((2 * n_wt,) + tokens.shape[1:], BF16),
            jax.ShapeDtypeStruct((n_ctx,) + pack, BF16),
            jax.ShapeDtypeStruct(pack, BF16),
            jax.ShapeDtypeStruct((2,) + gains.shape, gains.dtype),
            jax.ShapeDtypeStruct((2, LANES, router.shape[1]), BF16),
            jax.ShapeDtypeStruct((2,) + routes.shape, routes.dtype),
        ],
        in_specs=[pl.BlockSpec(memory_space=pltpu.HBM)] * 7,
        out_specs=[VMEM] * 6,
        scratch_shapes=[pltpu.VMEM(tokens.shape[1:], BF16)]
        + [pltpu.VMEM(member.shape, member.dtype) for member in (query, pair, out, gains, router, routes)]
        + [
            pltpu.VMEM((2,) + pack, BF16),
            pltpu.VMEM(pack, BF16),
            dma((7,)),
            dma,
            dma((4,)),
            dma((4,)),
            dma((n_ctx - 1,)),
            dma((n_ctx - 1,)),
        ]
        + RowGather.scratch(n_wt, CHUNKS),
        compiler_params=pltpu.CompilerParams(
            collective_id=number, has_side_effects=True, vmem_limit_bytes=16 << 20
        ),
        cost_estimate=pl.CostEstimate(flops=0, bytes_accessed=90 << 20, transcendentals=0),
    )(tokens, query, pair, out, gains, router, routes)


TILE = 256


def expert_pieces(packed, inward, down, depth, down_rows):
    n, wide, width = packed.shape[0], packed.shape[2], down.shape[2]
    half = down_rows // 2
    first = wide - width
    pairs = []
    for c in range(n):
        at = c * down_rows
        second = depth + down_rows
        pairs += [
            (packed.at[c, depth:second, :width], down.at[0, at : at + down_rows, :]),
            (packed.at[c, depth:second, width:], down.at[1, at : at + down_rows, :first]),
            (packed.at[c, second:, : wide // 2], down.at[1, at : at + half, first:]),
            (packed.at[c, second:, wide // 2 :], down.at[1, at + half : at + down_rows, first:]),
        ]
    for c in range(n):
        pairs.append((packed.at[c, :depth, :], inward.at[c * depth : (c + 1) * depth, :]))
    return pairs


def gate_rows(x, router, routes):
    lane = lax.broadcasted_iota(jnp.int32, (x.shape[0], LANES), 1)
    named = routes[:, 0:1] == lane
    for t in range(1, routes.shape[1]):
        named = named | (routes[:, t : t + 1] == lane)
    logits = jnp.where(named, dot(x, router, ((1,), (1,))), MASKED)
    expos = jnp.where(named, jnp.exp(logits - jnp.max(logits, 1, keepdims=True)), 0.0)
    return expos / jnp.sum(expos, 1, keepdims=True)


def experts_kernel(n_ctx, layer, forward, backward, depth, down_rows, ride, *refs):
    refs = list(refs)
    x_ref, packed_ref, router_ref, pick_ref = [refs.pop(0) for _ in range(4)]
    if forward:
        hit_ref = refs.pop(0)
    else:
        gates_ref, gate_up_ref = refs.pop(0), refs.pop(0)
    d_ref = refs.pop(0) if backward else None
    ride_ref = refs.pop(0) if ride else None
    part_ref = refs.pop(0) if forward else None
    if forward and not backward:
        gates_ref, gate_up_ref = refs.pop(0), refs.pop(0)
    if backward:
        back_ref, grads_ref, router_grad_ref = [refs.pop(0) for _ in range(3)]
    rode_ref = refs.pop(0) if ride else None
    inward, down, weighted, load = [refs.pop(0) for _ in range(4)]
    if forward and backward:
        gates_ref, gate_up_ref = refs.pop(0), refs.pop(0)
    if backward:
        d_gate_up, x_turned, in_grad, down_grad, store = refs[:5]
        refs = refs[5:]

    pieces = expert_pieces(packed_ref, inward, down, depth, down_rows)
    loads = [pltpu.make_async_copy(source, target, load.at[k]) for k, (source, target) in enumerate(pieces)]
    n_down = 4 * packed_ref.shape[0]
    for copy in (loads[n_down:] + loads[:n_down]) if forward else loads:
        copy.start()
    if ride:
        landed, ride_send, ride_recv = refs
        section, ctx, wt = place()
        peers = [(section, lax.rem(ctx + k, n_ctx), wt) for k in range(1, n_ctx)]
        greet(peers)
        riders = [
            remote(
                ride_ref.at[lax.rem(ctx + 1 + k, n_ctx)], landed.at[k], ride_send.at[k], ride_recv.at[k], peers[k]
            )
            for k in range(n_ctx - 1)
        ]
        for copy in riders:
            copy.start()
    columns = [slice(t * TILE, (t + 1) * TILE) for t in range(2 * FF // TILE)]
    per_expert = FF // TILE
    width = x_ref.shape[1]

    def gate_at(t):
        return slice(2 * FF * (t // per_expert) + TILE * (t % per_expert), 2 * FF * (t // per_expert) + TILE * (t % per_expert + 1))

    def up_at(t):
        return slice(gate_at(t).start + FF, gate_at(t).stop + FF)

    def weight_of(e):
        return jnp.sum(gates_ref[...] * pick_ref[e : e + 1, :], 1, keepdims=True)

    if forward:
        routes = hit_ref[layer]
        routes = routes.reshape(routes.shape[0] * routes.shape[1], routes.shape[2])
        gates_ref[...] = gate_rows(x_ref[...], router_ref[layer], routes)
        for copy in loads[n_down:]:
            copy.wait()
        for t, place_of in enumerate(columns):
            gate = dot(x_ref[...], inward[:, gate_at(t)], ((1,), (0,)))
            up = dot(x_ref[...], inward[:, up_at(t)], ((1,), (0,)))
            gate_up_ref[:, gate_at(t)] = gate.astype(BF16)
            gate_up_ref[:, up_at(t)] = up.astype(BF16)
            weighted[:, place_of] = (gate / (1.0 + jnp.exp(-gate)) * up * weight_of(t // per_expert)).astype(BF16)
        for copy in loads[:n_down]:
            copy.wait()
        for n in range(width // TILE):
            at = slice(n * TILE, (n + 1) * TILE)
            part_ref[:, at] = (
                dot(weighted[:, :FF], down[0, :, at], ((1,), (0,)))
                + dot(weighted[:, FF:], down[1, :, at], ((1,), (0,)))
            ).astype(BF16)
    else:
        for copy in loads[:n_down]:
            copy.wait()
    if backward:
        d_weight = [0.0, 0.0]
        for t, place_of in enumerate(columns):
            e = t // per_expert
            rows_of = slice(TILE * (t % per_expert), TILE * (t % per_expert + 1))
            weight = weight_of(e)
            d_weighted = dot(d_ref[...], down[e, rows_of, :], ((1,), (1,)))
            gate = gate_up_ref[:, gate_at(t)].astype(F32)
            up = gate_up_ref[:, up_at(t)].astype(F32)
            sigmoid = 1.0 / (1.0 + jnp.exp(-gate))
            activated = gate * sigmoid
            hidden = activated * up
            d_weight[e] = d_weight[e] + jnp.sum(hidden * d_weighted, 1, keepdims=True)
            weighted[:, place_of] = (hidden * weight).astype(BF16)
            d_hidden = d_weighted * weight
            d_gate_up[:, gate_at(t)] = (d_hidden * up * (sigmoid * (1.0 + gate * (1.0 - sigmoid)))).astype(BF16)
            d_gate_up[:, up_at(t)] = (d_hidden * activated).astype(BF16)
        gates = gates_ref[...]
        terms = gates * (pick_ref[0:1, :] * d_weight[0] + pick_ref[1:2, :] * d_weight[1])
        d_logits = terms - gates * jnp.sum(terms, 1, keepdims=True)
        high = d_logits.astype(BF16)
        low = (d_logits - high.astype(F32)).astype(BF16)
        both = jnp.concatenate([high, low], 1)
        if not forward:
            for copy in loads[n_down:]:
                copy.wait()
        for n in range(width // TILE):
            at = slice(n * TILE, (n + 1) * TILE)
            table = router_ref[layer, :, at]
            back_ref[:, at] = (
                dot(d_gate_up[...], inward[at, :], ((1,), (1,)))
                + dot(both, jnp.concatenate([table, table], 0), ((1,), (0,)))
            ).astype(BF16)
        x_turned[...] = jnp.transpose(x_ref[...])
        router_grad = dot(both, x_ref[...], ((0,), (0,)))
        named = router_grad_ref.shape[0]
        router_grad_ref[...] = router_grad[:named] + router_grad[LANES : LANES + named]
        pieces = expert_pieces(grads_ref, in_grad, down_grad, depth, down_rows)
        stores = [
            pltpu.make_async_copy(source, target, store.at[k]) for k, (target, source) in enumerate(pieces)
        ]
        for e in range(2):
            turned_hidden = jnp.transpose(weighted[:, e * FF : (e + 1) * FF])
            for n in range(width // TILE):
                at = slice(n * TILE, (n + 1) * TILE)
                down_grad[e, :, at] = dot(turned_hidden, d_ref[:, at], ((1,), (0,))).astype(BF16)
        for copy in stores[:n_down]:
            copy.start()
        for c in range(n_ctx):
            at = slice(c * depth, (c + 1) * depth)
            for n in range(2):
                wide = slice(n * 2 * FF, (n + 1) * 2 * FF)
                in_grad[at, wide] = dot(x_turned[at, :], d_gate_up[:, wide], ((1,), (0,))).astype(BF16)
            stores[n_down + c].start()
        for copy in stores:
            copy.wait()
    if ride:
        total = ride_ref[ctx].astype(F32)
        for k, copy in enumerate(riders):
            copy.wait()
            total = total + landed[k].astype(F32)
        rode_ref[...] = total


def experts(
    layer, x, packed, router, pick, n_experts, depth, down_rows, hit=None, kept=None, d_rows=None, number=None, add=None
):
    n_ctx = lax.axis_size("ctx")
    forward, backward = hit is not None, d_rows is not None
    n_rows, width = x.shape
    any_place = pl.BlockSpec(memory_space=pl.ANY)
    operands = [x, packed, router, pick]
    operands += [hit] if forward else list(kept)
    operands += [d_rows] if backward else []
    operands += [add] if add is not None else []
    in_specs = [VMEM, any_place] + [VMEM] * (len(operands) - 2)
    rows_out = jax.ShapeDtypeStruct((n_rows, width), BF16)
    inner = [jax.ShapeDtypeStruct((n_rows, LANES), F32), jax.ShapeDtypeStruct((n_rows, 4 * FF), BF16)]
    n_pieces = 5 * packed.shape[0]
    scratch = [
        pltpu.VMEM((width, 4 * FF), BF16),
        pltpu.VMEM((2, FF, width), BF16),
        pltpu.VMEM((n_rows, 2 * FF), BF16),
        pltpu.SemaphoreType.DMA((n_pieces,)),
    ]
    outs = []
    out_specs = []
    if forward:
        outs += [rows_out]
        out_specs += [VMEM]
    if forward and not backward:
        outs += inner
        out_specs += [VMEM] * 2
    if backward:
        outs += [rows_out, jax.ShapeDtypeStruct(packed.shape, BF16), jax.ShapeDtypeStruct((n_experts, width), F32)]
        out_specs += [VMEM, any_place, VMEM]
        if forward:
            scratch += [pltpu.VMEM(member.shape, member.dtype) for member in inner]
        scratch += [
            pltpu.VMEM((n_rows, 4 * FF), BF16),
            pltpu.VMEM((width, n_rows), BF16),
            pltpu.VMEM((width, 4 * FF), BF16),
            pltpu.VMEM((2, FF, width), BF16),
            pltpu.SemaphoreType.DMA((n_pieces,)),
        ]
    params = {}
    if add is not None:
        outs.append(jax.ShapeDtypeStruct(add.shape[1:], F32))
        out_specs.append(VMEM)
        scratch += [
            pltpu.VMEM((n_ctx - 1,) + add.shape[1:], BF16),
            pltpu.SemaphoreType.DMA((n_ctx - 1,)),
            pltpu.SemaphoreType.DMA((n_ctx - 1,)),
        ]
        params = dict(collective_id=number, has_side_effects=True)
    work = n_rows * 6 * width * FF * 2 * ((1 if forward else 0) + (2 if backward else 0))
    return pl.pallas_call(
        functools.partial(experts_kernel, n_ctx, layer, forward, backward, depth, down_rows, add is not None),
        out_shape=outs,
        in_specs=in_specs,
        out_specs=out_specs,
        scratch_shapes=scratch,
        compiler_params=pltpu.CompilerParams(vmem_limit_bytes=(44 if backward else 28) << 20, **params),
        cost_estimate=pl.CostEstimate(flops=2 * work, bytes_accessed=40 << 20, transcendentals=0),
    )(*operands)


def shards(tokens, cotangent, blocks, routes, norm_gain, w_query, key_value_weight, w_attn_out, router, w_in, w_down):
    section, ctx, wt = place()
    n_ctx, n_wt, layers = lax.axis_size("ctx"), lax.axis_size("wt"), lax.axis_size("section")
    micro_count, share, width = tokens.shape
    per_ctx = routes.shape[2]
    seq_len = per_ctx * n_ctx
    per_core = w_in.shape[1] // 2
    n_experts = router.shape[2]
    q_cols = w_query.shape[2] // 2
    depth = w_query.shape[1]

    block_len = seq_len // blocks.shape[1]
    placed = (blocks[:, :, None] * block_len + jnp.arange(block_len, dtype=jnp.int32)[None, None, :]).reshape(
        micro_count, seq_len
    )
    query_place = lax.dynamic_slice_in_dim(placed, ctx * per_ctx, per_ctx, 1)
    later = (jnp.arange(micro_count) > 0)[:, None]
    query_start = jnp.where(later, query_place - query_place % CONT_LEN, 0)
    query_pos = jnp.where(later, seq_len + query_place % CONT_LEN, query_place)
    half = HEAD_SIZE // 2
    inverse = jnp.power(ROPE_BASE, -(jnp.arange(LANES, dtype=jnp.int32) % half).astype(F32) * 2.0 / HEAD_SIZE)
    angles = query_pos.reshape(-1).astype(F32)[:, None] * inverse[None, :]
    sign = jnp.where(jnp.arange(LANES) % HEAD_SIZE < half, -1.0, 1.0)
    tables = (
        jnp.cos(angles),
        jnp.sin(angles) * sign[None, :],
        jnp.transpose(placed.reshape(micro_count, n_ctx, per_ctx), (1, 0, 2)).reshape(n_ctx, -1, 1),
        query_place[:, None, :],
        query_start[:, None, :],
    )

    moe_pack = prepare(15, w_in[0], w_down[0])
    normed_in, full, attn_pack, gain_pack, router_pack, route_pack = begin(
        0,
        tokens,
        w_query[0],
        key_value_weight[0].reshape(depth, -1),
        w_attn_out[0],
        norm_gain[0],
        jnp.transpose(router[0]),
        routes[0],
    )

    in_rows, down_rows = w_in.shape[2], w_down.shape[2]

    def gather_experts(pack):
        return lax.all_gather(pack, "ctx", axis=0, tiled=True).reshape((n_ctx,) + pack.shape)

    attn_full = [None, None]

    my_first = wt * 2 * per_core + section * per_core
    n_rows = micro_count * per_ctx

    pick = (jnp.arange(LANES)[None, :] == my_first + jnp.arange(8)[:, None]).astype(F32)
    def full_rows(values):
        return values.reshape(n_rows, width)

    def blocked(values):
        return values.reshape(2 * n_wt, share, width).astype(BF16)

    stream = lax.dynamic_index_in_dim(tokens, section, 0, False)
    top = lax.dynamic_index_in_dim(cotangent, section, 0, False)

    attn_full[0] = full.reshape(-1, full.shape[2])
    moe_full = [gather_experts(moe_pack[0]), None]
    saved = []
    outputs = []
    for layer in range(2):
        rows_in = full_rows(normed_in)
        weights = attn_full[layer]
        if layer == 0:
            partial, *heads, attended, d_mixed = attend(2, rows_in, weights, tables, top)
        else:
            partial, *heads, attended = attend(3, rows_in, weights, tables)
        middle, normed_mid, token = exchange(
            4 + layer, blocked(partial), stream, gain=gain_pack[layer, 1:2], spread="norm"
        )
        if layer == 0:
            token, second = lax.optimization_barrier((token, moe_pack[1]))
            moe_full[1] = gather_experts(second)
        token, moe_full[layer] = lax.optimization_barrier((token, moe_full[layer]))
        pick_now = pick + token
        rows_mid = full_rows(normed_mid)
        if layer == 0:
            partial, gates, gate_up = experts(
                0, rows_mid, moe_full[0], router_pack, pick_now, n_experts, in_rows, down_rows, hit=route_pack
            )
            inner = (gates, gate_up)
        else:
            partial, *back_parts = experts(
                1,
                rows_mid,
                moe_full[1],
                router_pack,
                pick_now,
                n_experts,
                in_rows,
                down_rows,
                hit=route_pack,
                d_rows=full_rows(d_mixed),
            )
            inner = None
        saved.append(
            dict(
                stream=stream,
                middle=middle,
                rows_in=rows_in,
                rows_mid=rows_mid,
                heads=heads,
                attended=attended,
                inner=inner,
            )
        )
        if layer == 0:
            stream, normed_in, full, token = exchange(
                6, blocked(partial), middle, gain=gain_pack[1, 0:1], spread="norm", rounded=True, gather=attn_pack
            )
            attn_full[1] = full.reshape(-1, full.shape[2])
            outputs.append(stream)
        else:
            last_rows = (blocked(partial), middle)
    upstream = top
    grads_in = [None, None]
    attn_grads = [None, None]
    moe_grads = [None, None]
    small = [None, None]
    for layer in (1, 0):
        kept = saved[layer]
        if layer == 0:
            back_parts = experts(
                0,
                kept["rows_mid"],
                moe_full[0],
                router_pack,
                pick,
                n_experts,
                in_rows,
                down_rows,
                kept=kept["inner"],
                d_rows=full_rows(d_mixed),
                number=7,
                add=attn_parts,
            )
            *back_parts, attn_grads[1] = back_parts
        partial, packed_grad, router_grad = back_parts
        gain = gain_pack[layer, 1:2]
        if layer == 0:
            gain, moe_grads[1] = lax.optimization_barrier((gain, moe_grads[1]))
        moe_grads[layer] = lax.psum_scatter(packed_grad, "ctx", scatter_dimension=0, tiled=False)
        d_middle, gain_grad_mid, d_attn, token = exchange(
            8 + layer, blocked(partial), upstream, kept["middle"], gain, spread="plain"
        )
        rows_a = full_rows(d_attn)
        weights = attn_full[layer]
        if layer == 1:
            partial, raw, last = attend_back(11, rows_a, weights, tables, kept["heads"], last_rows)
            outputs.append(last)
        else:
            partial, raw = attend_back(10, rows_a, weights, tables, kept["heads"])
        attn_parts = dot(kept["rows_in"], jnp.pad(raw, ((0, 0), (0, weights.shape[1] - raw.shape[1]))), ((0,), (0,)))
        attn_parts = attn_parts + dot(
            rows_a, jnp.pad(kept["attended"], ((0, 0), (weights.shape[1] - kept["attended"].shape[1], 0))), ((0,), (0,))
        )
        attn_parts = attn_parts.astype(BF16).reshape(n_ctx, depth, -1)
        if layer == 1:
            upstream, gain_grad_in, d_mixed, token = exchange(
                12,
                blocked(partial),
                d_middle,
                kept["stream"],
                gain_pack[1, 0:1],
                spread="plain",
                rounded=True,
            )
        else:
            upstream, gain_grad_in, attn_grads[0], token = exchange(
                1, blocked(partial), d_middle, kept["stream"], gain_pack[0, 0:1], rounded=True, add=attn_parts
            )
        grads_in[layer] = upstream
        small[layer] = [router_grad, gain_grad_in, gain_grad_mid]

    gain_total, router_total, grad_query, grad_kv, grad_out, out_pair, grad_pair = finish(
        14, small[0] + small[1], attn_grads, outputs + grads_in, q_cols
    )
    piece = width // (n_ctx * n_wt)
    moe_grads = [member.reshape(member.shape[-2:]) for member in moe_grads]
    grad_in, grad_down = hand_over(13, moe_grads[0], moe_grads[1], gain_total, in_rows, down_rows, per_core, width)
    return (
        out_pair[None],
        grad_pair[None],
        gain_total[None, :, :piece],
        grad_query[None],
        grad_kv.reshape(depth, 2, LANES)[None],
        grad_out[None],
        jnp.transpose(router_total[:, :piece])[None],
        grad_in.astype(F32)[None],
        grad_down.astype(F32)[None],
    )


def solution(mesh):
    return jax.shard_map(
        shards,
        mesh=mesh,
        in_specs=(
            P(None, ("ctx", "wt"), None),
            P(None, ("ctx", "wt"), None),
            P(),
            P("section", None, "ctx", None),
            P("section", None, None),
            P("section", "ctx", "wt"),
            P("section", "ctx", "wt", None),
            P("section", "wt", "ctx"),
            P("section", None, None),
            P("section", "wt", "ctx", None),
            P("section", "wt", "ctx", None),
        ),
        out_specs=(
            P("section", None, ("ctx", "wt"), None),
            P("section", None, ("ctx", "wt"), None),
            P("section", None, ("ctx", "wt")),
            P("section", "ctx", "wt"),
            P("section", "ctx", "wt", None),
            P("section", "wt", "ctx"),
            P("section", ("ctx", "wt"), None),
            P("section", "wt", "ctx", None),
            P("section", "wt", "ctx", None),
        ),
        check_vma=False,
    )
```

```python
import functools

import jax
import jax.numpy as jnp
from jax import lax
from jax.experimental import pallas as pl
from jax.experimental.pallas import tpu as pltpu
from jax.sharding import PartitionSpec as P

HEAD_SIZE = 64
FF = 512
CONT_LEN = 1024
EPSILON = 1e-06
ROPE_BASE = 10000.0
MASKED = -1e30
CHUNKS = 2
LANES = 2 * HEAD_SIZE
MESH = pl.DeviceIdType.MESH
F32 = jnp.float32
BF16 = jnp.bfloat16


def dot(left, right, contract):
    return lax.dot_general(left, right, (contract, ((), ())), preferred_element_type=F32)


def norm_scale(rows):
    return lax.rsqrt(jnp.mean(rows * rows, -1, keepdims=True) + EPSILON)


def place():
    return lax.axis_index("section"), lax.axis_index("ctx"), lax.axis_index("wt")


def greet(targets):
    barrier = pltpu.get_barrier_semaphore()
    for target in targets:
        pl.semaphore_signal(barrier, inc=1, device_id=target, device_id_type=MESH)
    pl.semaphore_wait(barrier, len(targets))


def remote(source, destination, send_sem, recv_sem, target):
    return pltpu.make_async_remote_copy(
        src_ref=source,
        dst_ref=destination,
        send_sem=send_sem,
        recv_sem=recv_sem,
        device_id=target,
        device_id_type=MESH,
    )


def loaded(kernel, operands, whole, **call):
    n = len(operands)

    def body(*refs):
        held, sems = refs[-n - 1 : -1], refs[-1]
        copies = [pltpu.make_async_copy(refs[k], held[k], sems.at[k]) for k in range(n)]
        for copy in copies:
            copy.start()

        def ready():
            for copy in copies:
                copy.wait()

        kernel(ready, *held, *refs[n : -n - 1])

    call["scratch_shapes"] = (
        list(call["scratch_shapes"])
        + [pltpu.VMEM(member.shape, member.dtype) for member in operands]
        + [pltpu.SemaphoreType.DMA((n,))]
    )
    call["in_specs"] = [pl.BlockSpec(memory_space=pl.ANY)] * (n + len(whole))
    return pl.pallas_call(body, **call)(*operands, *whole)


class Near:
    def __init__(self, n_wt):
        self.section, self.ctx, self.wt = place()
        self.n_wt = n_wt
        self.sibling = (1 - self.section, self.ctx, self.wt)
        self.right = (self.section, self.ctx, jnp.minimum(self.wt + 1, n_wt - 1))
        self.left = (self.section, self.ctx, jnp.maximum(self.wt - 1, 0))
        self.has_right, self.has_left = self.wt < n_wt - 1, self.wt > 0
        self.own = self.section * n_wt + self.wt

    def greet(self, others=()):
        barrier = pltpu.get_barrier_semaphore()

        def hail(target):
            pl.semaphore_signal(barrier, inc=1, device_id=target, device_id_type=MESH)

        hail(self.sibling)
        pl.when(self.has_right)(lambda: hail(self.right))
        pl.when(self.has_left)(lambda: hail(self.left))
        for other in others:
            hail(other)
        pl.semaphore_wait(
            barrier, 1 + len(others) + self.has_right.astype(jnp.int32) + self.has_left.astype(jnp.int32)
        )


def rows_of(chunk, rows):
    return slice(chunk * rows, (chunk + 1) * rows)


def block_at(last, block, rightward):
    return last + 1 - block if rightward else block - 1


class RowSum:
    def __init__(self, near, chunks, parts, scratch):
        self.near, self.chunks, self.parts = near, chunks, parts
        self.rows = parts.shape[1] // chunks
        self.from_sibling, self.in_right, self.in_left, self.out_right, self.out_left = scratch[:5]
        self.swap_send, self.swap_recv, self.send, self.recv = scratch[5:]

    @staticmethod
    def scratch(n_wt, shape, chunks):
        dma = pltpu.SemaphoreType.DMA
        return [pltpu.VMEM((n_wt,) + shape, BF16)] * 5 + [dma((chunks * n_wt,))] * 2 + [dma((2 * chunks * n_wt,))] * 2

    def swap(self, chunk, block):
        at = rows_of(chunk, self.rows)
        number = chunk * self.near.n_wt + block
        return remote(
            self.parts.at[(1 - self.near.section) * self.near.n_wt + block, at],
            self.from_sibling.at[block, at],
            self.swap_send.at[number],
            self.swap_recv.at[number],
            self.near.sibling,
        )

    def begin(self):
        n_wt = self.near.n_wt
        order = []
        for step in range(n_wt - 1):
            order += [n_wt - 1 - step, step]
        for chunk in range(self.chunks):
            for block in dict.fromkeys(order):
                self.swap(chunk, block).start()

    def chip_sum(self, chunk, block):
        at = rows_of(chunk, self.rows)
        mine = self.parts[self.near.section * self.near.n_wt + block, at, :]
        return mine.astype(F32) + self.from_sibling[block, at, :].astype(F32)

    def toward(self, chunk, block, rightward):
        at = rows_of(chunk, self.rows)
        number = (2 * chunk + (0 if rightward else 1)) * self.near.n_wt + block
        source, target = (self.out_right, self.in_right) if rightward else (self.out_left, self.in_left)
        return remote(
            source.at[block, at],
            target.at[block, at],
            self.send.at[number],
            self.recv.at[number],
            self.near.right if rightward else self.near.left,
        )

    def send_on(self, chunk, block, rightward):
        at = rows_of(chunk, self.rows)
        self.swap(chunk, block).wait_recv()
        outward, inward = (self.out_right, self.in_right) if rightward else (self.out_left, self.in_left)
        behind = self.near.has_left if rightward else self.near.has_right

        @pl.when(jnp.logical_not(behind))
        def _():
            outward[block, at, :] = self.chip_sum(chunk, block).astype(BF16)

        @pl.when(behind)
        def _():
            self.toward(chunk, block, rightward).wait_recv()
            outward[block, at, :] = (self.chip_sum(chunk, block) + inward[block, at, :].astype(F32)).astype(BF16)

        self.toward(chunk, block, rightward).start()

    def step(self, chunk, step):
        wt, n_wt = self.near.wt, self.near.n_wt
        far, near = n_wt - 1 - step, step
        lower = 2 * wt < n_wt
        pl.when((wt < far) & lower)(lambda: self.send_on(chunk, far, True))
        pl.when(wt > near)(lambda: self.send_on(chunk, near, False))
        pl.when((wt < far) & jnp.logical_not(lower))(lambda: self.send_on(chunk, far, True))

    def point(self, chunk, number):
        wt, last = self.near.wt, self.near.n_wt - 1
        for block in range(1, last + 1):
            turn = last - block
            if number == 0:
                pl.when(wt == 0)(functools.partial(self.send_on, chunk, block_at(last, block, True), True))
                pl.when(wt == last)(functools.partial(self.send_on, chunk, block_at(last, block, False), False))
            elif 1 <= number - turn < block:
                pl.when(wt == number - turn)(functools.partial(self.send_on, chunk, block, True))
                pl.when(wt == last - (number - turn))(functools.partial(self.send_on, chunk, last - block, False))

    def collect(self, chunk, result):
        at, wt = rows_of(chunk, self.rows), self.near.wt
        self.swap(chunk, wt).wait_recv()
        result[at, :] = self.chip_sum(chunk, wt)

        @pl.when(self.near.has_left)
        def _():
            self.toward(chunk, wt, True).wait_recv()
            result[at, :] += self.in_right[wt, at, :].astype(F32)

        @pl.when(self.near.has_right)
        def _():
            self.toward(chunk, wt, False).wait_recv()
            result[at, :] += self.in_left[wt, at, :].astype(F32)

    def end(self):
        wt, n_wt = self.near.wt, self.near.n_wt
        for chunk in range(self.chunks):
            for block in range(n_wt):
                self.swap(chunk, block).wait_send()
                if block > 0:
                    pl.when(wt < block)(self.toward(chunk, block, True).wait_send)
                if block < n_wt - 1:
                    pl.when(wt > block)(self.toward(chunk, block, False).wait_send)


class RowGather:
    def __init__(self, near, chunks, all_ref, scratch):
        self.near, self.chunks, self.all = near, chunks, all_ref
        self.rows = all_ref.shape[1] // chunks
        self.send, self.recv, self.pass_send, self.pass_recv = scratch
        self.sent, self.arrivals = [], []

    @staticmethod
    def scratch(n_wt, chunks):
        return [pltpu.SemaphoreType.DMA((2 * chunks * n_wt,))] * 4

    def along(self, chunk, block, hop, rightward):
        at = rows_of(chunk, self.rows)
        number = (2 * chunk + (0 if rightward else 1)) * self.near.n_wt + hop
        return remote(
            self.all.at[block, at],
            self.all.at[block, at],
            self.send.at[number],
            self.recv.at[number],
            self.near.right if rightward else self.near.left,
        )

    def across(self, chunk, block, number):
        at = rows_of(chunk, self.rows)
        number = 2 * chunk * self.near.n_wt + number
        return remote(
            self.all.at[block, at],
            self.all.at[block, at],
            self.pass_send.at[number],
            self.pass_recv.at[number],
            self.near.sibling,
        )

    def launch(self, condition, copy):
        pl.when(condition)(copy.start)
        self.sent.append((condition, copy))

    def first(self, chunk):
        near = self.near
        always = near.wt >= 0
        self.launch(near.has_right, self.along(chunk, near.own, 1, True))
        self.launch(near.has_left, self.along(chunk, near.own, 1, False))
        self.launch(always, self.across(chunk, near.own, 0))
        self.arrivals.append((always, self.across(chunk, near.own, 0)))

    def hop(self, chunk, hop):
        near, n_wt = self.near, self.near.n_wt
        for rightward, came, more, block, number in (
            (True, near.wt >= hop, near.has_right, jnp.maximum(near.own - hop, 0), hop),
            (False, near.wt + hop < n_wt, near.has_left, jnp.minimum(near.own + hop, 2 * n_wt - 1), n_wt + hop),
        ):
            pl.when(came)(self.along(chunk, block, hop, rightward).wait_recv)
            if hop + 1 < n_wt:
                self.launch(came & more, self.along(chunk, block, hop + 1, rightward))
            self.launch(came, self.across(chunk, block, number))
            self.arrivals.append((came, self.across(chunk, block, number)))

    def arrive(self):
        for condition, copy in self.arrivals:
            pl.when(condition)(copy.wait_recv)

    def end(self):
        for condition, copy in self.sent:
            pl.when(condition)(copy.wait_send)


class CtxGather:
    def __init__(self, near, n_ctx, source, target, sems):
        self.n_ctx, self.source, self.target = n_ctx, source, target
        self.send, self.recv, self.local = sems
        self.ctx = near.ctx
        x, y = lax.rem(near.ctx, 2), near.ctx // 2
        self.at_x, self.at_y = 2 * y + 1 - x, 2 * (1 - y) + x
        self.device = lambda index: (near.section, index, near.wt)
        self.half = source.shape[0] // 2

    @staticmethod
    def scratch(n_ctx):
        dma = pltpu.SemaphoreType.DMA
        return [dma((max(4, n_ctx - 1),)), dma((max(4, n_ctx - 1),)), dma]

    def copy(self, source, target, number, index):
        return remote(source, target, self.send.at[number], self.recv.at[number], self.device(index))

    def near_copies(self):
        if self.n_ctx != 4:
            return [
                self.copy(self.source, self.target.at[self.ctx], k, lax.rem(self.ctx + 1 + k, self.n_ctx))
                for k in range(self.n_ctx - 1)
            ]
        return [
            self.copy(self.source, self.target.at[self.ctx], k, index)
            for k, index in enumerate((self.at_x, self.at_y))
        ]

    def far_copies(self):
        if self.n_ctx != 4:
            return []
        parts = []
        for number, block, at, index in (
            (2, self.at_x, slice(0, self.half), self.at_y),
            (3, self.at_y, slice(self.half, 2 * self.half), self.at_x),
        ):
            ref = self.target.at[block, at]
            parts.append(self.copy(ref, ref, number, index))
        return parts

    def start(self):
        pltpu.make_async_copy(self.source, self.target.at[self.ctx], self.local).start()
        for copy in self.near_copies():
            copy.start()

    def hand_on(self):
        for copy in self.near_copies():
            copy.wait_recv()
        for copy in self.far_copies():
            copy.start()

    def finish(self):
        pltpu.make_async_copy(self.source, self.target.at[self.ctx], self.local).wait()
        for copy in self.far_copies():
            copy.wait()
        for copy in self.near_copies():
            copy.wait_send()


def exchange_steps(
    near,
    n_ctx,
    parts,
    rows_ref,
    stream_ref,
    gain_ref,
    result_ref,
    gain_grad_ref,
    all_ref,
    spread,
    rounded,
    scratch,
    ride=None,
    ride_refs=None,
    between=(),
):
    section, ctx, wt, n_wt = near.section, near.ctx, near.wt, near.n_wt
    peers = [(section, lax.rem(ctx + k, n_ctx), wt) for k in range(1, n_ctx)]
    scratch = list(scratch)
    sums = RowSum(near, CHUNKS, parts, scratch[:9])
    scratch = scratch[9:]
    sum_ref = scratch.pop(0) if rounded else result_ref
    if spread:
        gathers = RowGather(near, CHUNKS, all_ref, scratch[:4])
        scratch = scratch[4:]
    chunk_rows = rows_ref.shape[0] // CHUNKS
    sums.begin()
    if ride:
        ride_ref, rode_ref = ride_refs
        if ride == "gather":
            blocks = CtxGather(near, n_ctx, ride_ref, rode_ref, scratch)
        else:
            landed, ride_send, ride_recv = scratch
            riders = [
                remote(
                    ride_ref.at[lax.rem(ctx + 1 + k, n_ctx)], landed.at[k], ride_send.at[k], ride_recv.at[k], peers[k]
                )
                for k in range(n_ctx - 1)
            ]

    def set_off():
        if ride == "gather":
            blocks.start()
        elif ride:
            for copy in riders:
                copy.start()

    between = list(between)
    if not between:
        set_off()

    def settle(chunk):
        at = rows_of(chunk, chunk_rows)
        sums.collect(chunk, sum_ref)
        total = sum_ref[at, :]
        if stream_ref is not None:
            stream = stream_ref[at, :].astype(F32)
            scale = norm_scale(stream)
            weighted = gain_ref[...] * total
            gain_part = jnp.sum(total * stream * scale, 0, keepdims=True)
            gain_grad_ref[...] = gain_part if chunk == 0 else gain_grad_ref[...] + gain_part
            total = scale * weighted - stream * (scale * scale * scale) * jnp.mean(
                weighted * stream, -1, keepdims=True
            )
        total = rows_ref[at, :].astype(F32) + total
        if rounded:
            total = total.astype(BF16)
        result_ref[at, :] = total
        total = total.astype(F32)
        if spread:
            if spread == "norm":
                total = total * norm_scale(total) * gain_ref[...]
            all_ref[near.own, at, :] = total.astype(BF16)
            gathers.first(chunk)

    stages = [functools.partial(sums.step, step=step) for step in range(n_wt - 1)]
    stages.append(settle)
    if spread:
        stages += [functools.partial(gathers.hop, hop=hop) for hop in range(1, n_wt)]
    for slot in range(CHUNKS + len(stages) - 1):
        for chunk in reversed(range(CHUNKS)):
            if 0 <= slot - chunk < len(stages):
                stages[slot - chunk](chunk)
        if between:
            between.pop(0)()
            if not between:
                set_off()

        if ride == "gather" and slot == n_wt + 1:
            blocks.hand_on()

    if spread:
        gathers.arrive()
    if ride == "gather":
        blocks.finish()
    elif ride == "sum":
        total = ride_ref[ctx].astype(F32)
        for k, copy in enumerate(riders):
            copy.wait()
            total = total + landed[k].astype(F32)
        rode_ref[...] = total
    if spread:
        gathers.end()
    sums.end()


def exchange_scratch(n_ctx, n_wt, shape, spread, rounded, ride=None, rider=None):
    dma = pltpu.SemaphoreType.DMA
    scratch = RowSum.scratch(n_wt, shape, CHUNKS)
    scratch += [pltpu.VMEM(shape, F32)] if rounded else []
    scratch += RowGather.scratch(n_wt, CHUNKS) if spread else []
    if ride == "gather":
        scratch += CtxGather.scratch(n_ctx)
    elif ride:
        scratch += [pltpu.VMEM((n_ctx - 1,) + tuple(rider[1:]), BF16), dma((n_ctx - 1,)), dma((n_ctx - 1,))]
    return scratch


def exchange_kernel(n_ctx, n_wt, back, spread, rounded, ride, ready, *refs):
    refs = list(refs)
    near = Near(n_wt)
    peers = [(near.section, lax.rem(near.ctx + k, n_ctx), near.wt) for k in range(1, n_ctx)]
    parts, rows_ref = refs.pop(0), refs.pop(0)
    stream_ref = refs.pop(0) if back else None
    gain_ref = refs.pop(0) if (back or spread) else None
    ride_ref = refs.pop(0) if ride else None
    result_ref = refs.pop(0)
    gain_grad_ref = refs.pop(0) if back else None
    all_ref = refs.pop(0) if spread else None
    rode_ref = refs.pop(0) if ride else None
    token_ref = refs.pop(0)
    token_ref[...] = jnp.zeros(token_ref.shape, F32)
    near.greet(peers if ride else ())
    if ready:
        ready()
    exchange_steps(
        near,
        n_ctx,
        parts,
        rows_ref,
        stream_ref,
        gain_ref,
        result_ref,
        gain_grad_ref,
        all_ref,
        spread,
        rounded,
        refs,
        ride,
        (ride_ref, rode_ref),
    )


VMEM = pl.BlockSpec(memory_space=pltpu.VMEM)


def exchange(number, parts, rows, stream=None, gain=None, spread=None, rounded=False, gather=None, add=None, load=False):
    n_ctx, n_wt = lax.axis_size("ctx"), lax.axis_size("wt")
    shape = rows.shape
    back = stream is not None
    ride = "gather" if gather is not None else "sum" if add is not None else None
    rider = add if gather is None else gather
    wanted = ((parts, True), (rows, True), (stream, back), (gain, back or spread), (rider, ride))
    operands = [member for member, taken in wanted if taken]
    outs = [jax.ShapeDtypeStruct(shape, BF16 if rounded else F32)]
    if back:
        outs.append(jax.ShapeDtypeStruct((1, shape[1]), F32))
    if spread:
        outs.append(jax.ShapeDtypeStruct((2 * n_wt,) + shape, BF16))
    if ride == "gather":
        outs.append(jax.ShapeDtypeStruct((n_ctx,) + gather.shape, BF16))
    elif ride == "sum":
        outs.append(jax.ShapeDtypeStruct(add.shape[1:], F32))
    outs.append(jax.ShapeDtypeStruct((8, LANES), F32))
    kernel = functools.partial(exchange_kernel, n_ctx, n_wt, back, spread, rounded, ride)
    call = dict(
        out_shape=outs,
        out_specs=[VMEM] * len(outs),
        scratch_shapes=exchange_scratch(n_ctx, n_wt, shape, spread, rounded, ride, rider.shape if ride else None),
        compiler_params=pltpu.CompilerParams(
            collective_id=number, has_side_effects=True, vmem_limit_bytes=(60 if load else 16) << 20
        ),
        cost_estimate=pl.CostEstimate(flops=0, bytes_accessed=110 << 20, transcendentals=0),
    )
    if load:
        return loaded(kernel, operands, [], **call)
    return pl.pallas_call(functools.partial(kernel, None), in_specs=[VMEM] * len(operands), **call)(*operands)


def finish_kernel(n_ctx, n_wt, *refs):
    small, attn, rows = refs[:6], refs[6:8], refs[8:12]
    gain_ref, router_ref, query_ref, pair_ref, out_ref, rows_ref, grads_ref = refs[12:19]
    parts, landed, summed, from_sibling, received, send, recv, swap_send, swap_recv = refs[19:]
    section, ctx, wt = place()
    count = n_ctx * n_wt
    own = ctx * n_wt + wt
    blocks = [lax.rem(own + k, count) for k in range(1, count)]
    peers = [(section, block // n_wt, lax.rem(block, n_wt)) for block in blocks]
    sibling = (1 - section, ctx, wt)
    greet([sibling] + peers)
    members = [(attn[0], attn[1], received)]
    members += [(rows[0], rows[1], rows_ref.at[section]), (rows[2], rows[3], grads_ref.at[section])]
    swaps = [
        [remote(member[1 - layer], member[2], swap_send.at[k], swap_recv.at[k], sibling) for k, member in enumerate(members)]
        for layer in range(2)
    ]
    for layer in range(2):

        @pl.when(section == layer)
        def _():
            for copy in swaps[layer]:
                copy.start()

    piece = small[0].shape[1] // count
    parts[...] = jnp.zeros(parts.shape, F32)
    for block in range(count):
        for layer in range(2):
            at = 0
            for ref in small[3 * layer : 3 * layer + 3]:
                end = at + ref.shape[0]
                parts[block, layer, at:end, :piece] = ref[:, block * piece : (block + 1) * piece]
                at = end
    copies = [
        remote(parts.at[blocks[k]], landed.at[k], send.at[k], recv.at[k], peers[k]) for k in range(count - 1)
    ]
    for copy in copies:
        copy.start()
    mine = section == 0
    rows_ref[section] = jnp.where(mine, rows[0][...], rows[1][...])
    grads_ref[section] = jnp.where(mine, rows[2][...], rows[3][...])
    for copy in swaps[0]:
        copy.wait_recv()
    held = jnp.where(mine, attn[0][...], attn[1][...])
    came = received[...]
    first, second = jnp.where(mine, held, came), jnp.where(mine, came, held)
    q_cols = query_ref.shape[1] // 2
    at = q_cols + LANES
    query_ref[...] = jnp.concatenate([first[:, :q_cols], second[:, :q_cols]], 1)
    pair_ref[...] = jnp.concatenate([first[:, q_cols:at], second[:, q_cols:at]], 1)
    out_ref[...] = jnp.transpose(jnp.concatenate([first[:, at:], second[:, at:]], 1))
    total = parts[own]
    for k, copy in enumerate(copies):
        copy.wait_recv()
        total = total + landed[k]
    summed[...] = total
    swap = remote(summed.at[1 - section], from_sibling, send.at[count - 1], recv.at[count - 1], sibling)
    swap.start()
    swap.wait()
    total = summed[section] + from_sibling[...]
    named = small[0].shape[0]
    gain_ref[...] = total[named : named + 2, :]
    router_ref[...] = total[:named, :]
    for copy in copies:
        copy.wait_send()
    for copy in swaps[0]:
        copy.wait_send()


def finish(number, small, attn, rows, q_cols):
    n_ctx, n_wt = lax.axis_size("ctx"), lax.axis_size("wt")
    count = n_ctx * n_wt
    named = small[0].shape[0]
    shape = (2, named + 2 + -(named + 2) % 8, LANES)
    dma = pltpu.SemaphoreType.DMA
    depth = attn[0].shape[0]
    pair = jax.ShapeDtypeStruct((2,) + rows[0].shape, BF16)
    return pl.pallas_call(
        functools.partial(finish_kernel, n_ctx, n_wt),
        out_shape=[
            jax.ShapeDtypeStruct((2, LANES), F32),
            jax.ShapeDtypeStruct((named, LANES), F32),
            jax.ShapeDtypeStruct((depth, 2 * q_cols), F32),
            jax.ShapeDtypeStruct((depth, 2 * LANES), F32),
            jax.ShapeDtypeStruct((2 * q_cols, depth), F32),
            pair,
            pair,
        ],
        in_specs=[VMEM] * 12,
        out_specs=[VMEM] * 7,
        scratch_shapes=[
            pltpu.VMEM((count,) + shape, F32),
            pltpu.VMEM((count - 1,) + shape, F32),
            pltpu.VMEM(shape, F32),
            pltpu.VMEM(shape[1:], F32),
            pltpu.VMEM(attn[0].shape, F32),
            dma((count,)),
            dma((count,)),
            dma((3,)),
            dma((3,)),
        ],
        compiler_params=pltpu.CompilerParams(
            collective_id=number, has_side_effects=True, vmem_limit_bytes=16 << 20
        ),
        cost_estimate=pl.CostEstimate(flops=0, bytes_accessed=40 << 20, transcendentals=0),
    )(*small, *attn, *rows)


def hand_over_kernel(per_core, first, second, after, inward, down, held, send, recv, load, keep):
    section, ctx, wt = place()
    sibling = (1 - section, ctx, wt)
    for layer, own in enumerate((first, second)):

        @pl.when(section == layer)
        def _():
            pltpu.make_async_copy(own, held, load).start()

    def moves(source):
        pieces = expert_halves(inward, down, source, section, per_core)
        return [remote(piece, target, send.at[k], recv.at[k], sibling) for k, (target, piece) in enumerate(pieces)]

    greet([sibling])
    for layer, other in enumerate((second, first)):

        @pl.when(section == layer)
        def _():
            for copy in moves(other):
                copy.start()

    pltpu.make_async_copy(first, held, load).wait()
    pieces = expert_halves(inward, down, held, section, per_core)
    copies = [pltpu.make_async_copy(piece, target, keep.at[k]) for k, (target, piece) in enumerate(pieces)]
    for copy in copies:
        copy.start()
    for copy in copies:
        copy.wait()
    for copy in moves(first):
        copy.wait()


def hand_over(number, first, second, after, depth, down_rows, per_core, width):
    any_place = pl.BlockSpec(memory_space=pl.ANY)
    dma = pltpu.SemaphoreType.DMA
    return pl.pallas_call(
        functools.partial(hand_over_kernel, per_core),
        out_shape=[
            jax.ShapeDtypeStruct((2 * per_core, depth, first.shape[1] // per_core), first.dtype),
            jax.ShapeDtypeStruct((2 * per_core, down_rows, width), first.dtype),
        ],
        in_specs=[any_place] * 3,
        out_specs=[any_place] * 2,
        scratch_shapes=[pltpu.VMEM(first.shape, first.dtype), dma((6,)), dma((6,)), dma, dma((6,))],
        compiler_params=pltpu.CompilerParams(
            collective_id=number, has_side_effects=True, vmem_limit_bytes=60 << 20
        ),
    )(first, second, after)


HEADS = 3


def roll(values, by):
    return pltpu.roll(values, by, 1)


def lower_half(shape):
    return lax.broadcasted_iota(jnp.int32, shape, 1) < HEAD_SIZE


def turned(values, cosine, sine):
    first = lax.rem(lax.broadcasted_iota(jnp.int32, values.shape, 1), HEAD_SIZE) < HEAD_SIZE // 2
    half = HEAD_SIZE // 2
    return values * cosine + jnp.where(first, roll(values, LANES - half), roll(values, half)) * sine


def visible(key_place, query_place, query_start):
    return (key_place <= query_place) & (key_place >= query_start)


def attend_kernel(
    n_ctx,
    n_wt,
    ride,
    x_ref,
    w_ref,
    cos_ref,
    sin_ref,
    key_place,
    query_place,
    query_start,
    *refs,
):
    refs = list(refs)
    ride_ref = refs.pop(0) if ride else None
    part_ref, q_ref, pairs_ref, out_ref, lse_ref, att_ref = [refs.pop(0) for _ in range(6)]
    all_ref = refs.pop(0) if ride else None
    top_ref, sum_ref, acc_ref, send, recv = refs[:5]
    near = Near(n_wt)
    section, ctx, wt = near.section, near.ctx, near.wt
    peers = [(section, lax.rem(ctx + k, n_ctx), wt) for k in range(1, n_ctx)]
    waiting = []
    if ride:
        gathers = RowGather(near, 1, all_ref, refs[5:])
        waiting = [functools.partial(gathers.hop, 0, hop) for hop in range(1, n_wt)]
        all_ref[near.own] = ride_ref[...]
        near.greet(peers)
        gathers.first(0)
    else:
        greet(peers)

    def ride_on():
        if waiting:
            waiting.pop(0)()

    rows = x_ref.shape[0] // 2
    low = lower_half((2 * rows, LANES))
    mixed = dot(x_ref[...], w_ref[:, : 3 * LANES], ((1,), (0,)))
    cosine, sine = cos_ref[...], sin_ref[...]
    first = turned(mixed[:, :LANES], cosine, sine)
    second = turned(mixed[:, LANES : 2 * LANES], cosine, sine)
    pairs_ref[ctx] = jnp.where(low, roll(second, HEAD_SIZE), roll(mixed[:, 2 * LANES :], HEAD_SIZE)).astype(BF16)

    def passing(k):
        return remote(
            pairs_ref.at[ctx], pairs_ref.at[ctx], send.at[k], recv.at[k], (section, lax.rem(ctx + k, n_ctx), wt)
        )

    for k in range(1, n_ctx):
        passing(k).start()
    for h, part in enumerate((first, roll(first, HEAD_SIZE), second)):
        scaled = jnp.where(low, part * (1.0 / HEAD_SIZE), 0.0).astype(BF16)
        q_ref[0, h] = scaled[:rows]
        q_ref[1, h] = scaled[rows:]
    top_ref[...] = jnp.full(top_ref.shape, MASKED, F32)
    sum_ref[...] = jnp.zeros(sum_ref.shape, F32)
    acc_ref[...] = jnp.zeros(acc_ref.shape, F32)

    def block(c, m, j):
        keys = pairs_ref[c, j * rows : (j + 1) * rows, :]
        if m == j:
            seen = visible(key_place[c, j * rows : (j + 1) * rows, :], query_place[m], query_start[m])
        for h in range(HEADS):
            logits = dot(keys, q_ref[m, h], ((1,), (1,)))
            if m == j:
                logits = jnp.where(seen, logits, MASKED)
            before = top_ref[m, h]
            top = jnp.maximum(before, jnp.max(logits, 0, keepdims=True))
            expos = jnp.exp(logits - top)
            shrink = jnp.exp(before - top)
            top_ref[m, h] = top
            sum_ref[m, h] = sum_ref[m, h] * shrink + jnp.sum(expos, 0, keepdims=True)
            acc_ref[m, h] = acc_ref[m, h] * shrink + dot(keys, expos.astype(BF16), ((0,), (0,)))

    def blocks_of(c):
        block(c, 0, 0)
        block(c, 1, 1)
        block(c, 1, 0)

    blocks_of(ctx)
    ride_on()

    def arrived(k):
        passing(k).wait_recv()
        blocks_of(lax.rem(ctx + n_ctx - k, n_ctx))

    arrived(1)
    arrived(2)
    ride_on()
    pl.loop(3, n_ctx)(arrived)
    while waiting:
        ride_on()
    low = lower_half((rows, LANES))
    for m in range(2):
        outs = []
        for h in range(HEADS):
            lse_ref[m, h] = top_ref[m, h] + jnp.log(sum_ref[m, h])
            outs.append(jnp.transpose(acc_ref[m, h] / sum_ref[m, h]))
            out_ref[m, h] = outs[h]
        att_ref[m * rows : (m + 1) * rows, :LANES] = jnp.where(low, 0.0, outs[0]).astype(BF16)
        att_ref[m * rows : (m + 1) * rows, LANES:] = jnp.where(low, roll(outs[1], HEAD_SIZE), outs[2]).astype(BF16)
    part_ref[...] = dot(att_ref[...], w_ref[:, 2 * LANES :], ((1,), (1,))).astype(BF16)
    if ride:
        gathers.arrive()
        gathers.end()
    for k in range(1, n_ctx):
        passing(k).wait_send()


def attend(number, rows_in, weights, tables, ride=None):
    n_ctx, n_wt = lax.axis_size("ctx"), lax.axis_size("wt")
    riders = [] if ride is None else [ride]
    n_rows, width = rows_in.shape
    rows = n_rows // 2
    dma = pltpu.SemaphoreType.DMA
    return pl.pallas_call(
        functools.partial(attend_kernel, n_ctx, n_wt, bool(riders)),
        out_shape=[
            jax.ShapeDtypeStruct((n_rows, width), BF16),
            jax.ShapeDtypeStruct((2, HEADS, rows, LANES), BF16),
            jax.ShapeDtypeStruct((n_ctx, n_rows, LANES), BF16),
            jax.ShapeDtypeStruct((2, HEADS, rows, LANES), F32),
            jax.ShapeDtypeStruct((2, HEADS, 1, rows), F32),
            jax.ShapeDtypeStruct((n_rows, 2 * LANES), BF16),
        ]
        + [jax.ShapeDtypeStruct((2 * n_wt,) + member.shape, BF16) for member in riders],
        in_specs=[VMEM] * (7 + len(riders)),
        out_specs=[VMEM] * (6 + len(riders)),
        scratch_shapes=[
            pltpu.VMEM((2, HEADS, 1, rows), F32),
            pltpu.VMEM((2, HEADS, 1, rows), F32),
            pltpu.VMEM((2, HEADS, LANES, rows), F32),
            dma((n_ctx,)),
            dma((n_ctx,)),
        ]
        + (RowGather.scratch(n_wt, 1) if riders else []),
        compiler_params=pltpu.CompilerParams(
            collective_id=number, has_side_effects=True, vmem_limit_bytes=20 << 20
        ),
        cost_estimate=pl.CostEstimate(flops=0, bytes_accessed=70 << 20, transcendentals=0),
    )(rows_in, weights, *tables, *riders)


def attend_back_kernel(
    n_ctx,
    n_wt,
    ride,
    ready,
    a_ref,
    w_ref,
    cos_ref,
    sin_ref,
    key_place,
    query_place,
    query_start,
    q_ref,
    pairs_ref,
    out_ref,
    lse_ref,
    *refs,
):
    refs = list(refs)
    if ride:
        rows_ref, stream_ref, gain_ref = [refs.pop(0) for _ in range(3)]
        ride_refs = [refs.pop(0), refs.pop(0)]
        raw_ref, result_ref, gain_grad_ref, all_ref, rode_ref = [refs.pop(0) for _ in range(5)]
    else:
        raw_ref, part_ref = refs.pop(0), refs.pop(0)
    do_ref, delta_ref, dq_ref, dkv_ref, own_ref, landed, send, recv = refs[:8]
    refs = refs[8:]
    near = Near(n_wt)
    section, ctx, wt = near.section, near.ctx, near.wt
    peers = [(section, lax.rem(ctx + k, n_ctx), wt) for k in range(1, n_ctx)]
    waiting = []
    if ride:
        near.greet(peers)
    else:
        greet(peers)
    if ready:
        ready()
    if ride:
        part_ref = refs.pop(0)
        sums = RowSum(near, 1, ride_refs[0], refs[:9])
        rode_sum = refs[9]
        refs = refs[10:]
        waiting = [functools.partial(sums.point, 0, number) for number in range(n_wt - 1)]
        sums.begin()

    def ride_on():
        if waiting:
            waiting.pop(0)()

    rows = a_ref.shape[0] // 2
    low = lower_half((2 * rows, LANES))
    d_att = dot(a_ref[...], w_ref[:, 2 * LANES :], ((1,), (0,)))
    for h, part in enumerate((d_att[:, :LANES], roll(d_att[:, LANES:], HEAD_SIZE), d_att[:, LANES:])):
        d_out = jnp.where(low, 0.0, part).astype(BF16)
        for m in range(2):
            do_ref[m, h] = d_out[m * rows : (m + 1) * rows]
            product = do_ref[m, h].astype(F32) * out_ref[m, h]
            delta_ref[m, h] = jnp.sum(jnp.transpose(product), 0, keepdims=True)
    dq_ref[...] = jnp.zeros(dq_ref.shape, F32)
    ride_on()

    def block(c, j):
        keys = pairs_ref[c, j * rows : (j + 1) * rows, :]
        total = jnp.zeros((rows, LANES), F32)
        for m in range(j, 2):
            if m == j:
                seen = visible(key_place[c, j * rows : (j + 1) * rows, :], query_place[m], query_start[m])
            for h in range(HEADS):
                probs = jnp.exp(dot(keys, q_ref[m, h], ((1,), (1,))) - lse_ref[m, h])
                if m == j:
                    probs = jnp.where(seen, probs, 0.0)
                d_probs = dot(keys, do_ref[m, h], ((1,), (1,)))
                d_scores = (probs * (d_probs - delta_ref[m, h])).astype(BF16)
                total = total + dot(d_scores, q_ref[m, h], ((1,), (0,)))
                total = total + dot(probs.astype(BF16), do_ref[m, h], ((1,), (0,)))
                dq_ref[m, h] += dot(keys, d_scores, ((0,), (0,)))
        return total

    def passing(k):
        target = lax.rem(ctx + k, n_ctx)
        return remote(dkv_ref.at[target], landed.at[k - 1], send.at[k], recv.at[k], (section, target, wt))

    def sent(k):
        c = lax.rem(ctx + k, n_ctx)
        for j in range(2):
            dkv_ref[c, j * rows : (j + 1) * rows, :] = block(c, j).astype(BF16)
        passing(k).start()

    sent(1)
    sent(2)
    ride_on()
    pl.loop(3, n_ctx)(sent)

    for j in range(2):
        own_ref[j * rows : (j + 1) * rows, :] = block(ctx, j)

    while waiting:
        ride_on()

    @pl.loop(1, n_ctx)
    def _(k):
        passing(k).wait_recv()
        own_ref[...] += landed[k - 1].astype(F32)

    cosine, sine = cos_ref[...], sin_ref[...]
    d_own = own_ref[...]
    over = roll(d_own, HEAD_SIZE)
    d_query = [
        jnp.concatenate([jnp.transpose(dq_ref[m, h]) for m in range(2)], 0) * (1.0 / HEAD_SIZE) for h in range(HEADS)
    ]
    first = jnp.where(low, d_query[0], roll(d_query[1], HEAD_SIZE))
    second = jnp.where(low, d_query[2], over)
    raw_ref[:, :LANES] = turned(first, cosine, -sine).astype(BF16)
    raw_ref[:, LANES : 2 * LANES] = turned(second, cosine, -sine).astype(BF16)
    raw_ref[:, 2 * LANES :] = jnp.where(low, over, 0.0).astype(BF16)
    partial = dot(raw_ref[...], w_ref[:, : 3 * LANES], ((1,), (1,))).astype(BF16)
    part_ref[...] = partial.reshape(part_ref.shape)
    if ride:
        sums.collect(0, rode_sum)
        rode_ref[...] = (rode_sum[...] + ride_refs[1][...]).astype(BF16)

    if ride:
        exchange_steps(
            near,
            n_ctx,
            part_ref,
            rows_ref,
            stream_ref,
            gain_ref,
            result_ref,
            gain_grad_ref,
            all_ref,
            "plain",
            True,
            refs,
        )
    if ride:
        sums.end()
    for k in range(1, n_ctx):
        passing(k).wait_send()


def attend_back(number, rows_a, weights, tables, kept, then=()):
    n_ctx, n_wt = lax.axis_size("ctx"), lax.axis_size("wt")
    n_rows, width = rows_a.shape
    half = n_rows // 2
    share = n_rows // (2 * n_wt)
    dma = pltpu.SemaphoreType.DMA
    shape = (share, width)
    blocks = jax.ShapeDtypeStruct((2 * n_wt,) + shape, BF16)
    outs = [jax.ShapeDtypeStruct((n_rows, 3 * LANES), BF16)]
    scratch = [
        pltpu.VMEM((2, HEADS, half, LANES), BF16),
        pltpu.VMEM((2, HEADS, 1, half), F32),
        pltpu.VMEM((2, HEADS, LANES, half), F32),
        pltpu.VMEM((n_ctx, n_rows, LANES), BF16),
        pltpu.VMEM((n_rows, LANES), F32),
        pltpu.VMEM((n_ctx - 1, n_rows, LANES), BF16),
        dma((n_ctx,)),
        dma((n_ctx,)),
    ]
    if then:
        row = jax.ShapeDtypeStruct(shape, BF16)
        outs += [row, jax.ShapeDtypeStruct((1, width), F32), blocks, row]
        scratch += [pltpu.VMEM(blocks.shape, BF16)] + RowSum.scratch(n_wt, shape, 1) + [pltpu.VMEM(shape, F32)]
        scratch += exchange_scratch(n_ctx, n_wt, shape, "plain", True)
    else:
        outs.append(blocks)
    operands = [rows_a, weights, *tables, *kept, *then]
    kernel = functools.partial(attend_back_kernel, n_ctx, n_wt, bool(then))
    call = dict(
        out_shape=outs,
        out_specs=[VMEM] * len(outs),
        scratch_shapes=scratch,
        compiler_params=pltpu.CompilerParams(
            collective_id=number, has_side_effects=True, vmem_limit_bytes=(60 if then else 24) << 20
        ),
        cost_estimate=pl.CostEstimate(flops=0, bytes_accessed=(200 if then else 100) << 20, transcendentals=0),
    )
    if then:
        return loaded(kernel, operands, [], **call)
    return pl.pallas_call(functools.partial(kernel, None), in_specs=[VMEM] * len(operands), **call)(*operands)


def expert_halves(inward, down, packed, half, per_core):
    depth, down_rows = inward.shape[1], down.shape[1]
    wide, width = packed.shape[1], down.shape[2]
    column, second = inward.shape[2], depth + down_rows
    first, middle = wide - width, down_rows // 2
    a, b = half * per_core, half * per_core + 1
    return [
        (inward.at[a], packed.at[:depth, :column]),
        (inward.at[b], packed.at[:depth, column:]),
        (down.at[a], packed.at[depth:second, :width]),
        (down.at[b, :, :first], packed.at[depth:second, width:]),
        (down.at[b, :middle, first:], packed.at[second:, : wide // 2]),
        (down.at[b, middle:, first:], packed.at[second:, wide // 2 :]),
    ]


def prepare_kernel(inward, down, first, second, halves, load, send, recv, keep):
    packed = (first, second)
    section, ctx, wt = place()
    sibling = (1 - section, ctx, wt)
    per_core = inward.shape[0] // 2
    loads = []
    for half in range(2):
        for source, target in expert_halves(inward, down, halves.at[half], half, per_core):
            loads.append(pltpu.make_async_copy(source, target, load.at[len(loads)]))
    for copy in loads:
        copy.start()
    greet([sibling])
    for copy in loads:
        copy.wait()
    for layer in range(2):

        @pl.when(section == layer)
        def _():
            move = remote(halves.at[1 - layer], packed[layer], send, recv, sibling)
            move.start()
            own = pltpu.make_async_copy(halves.at[layer], packed[layer], keep)
            own.start()
            own.wait()
            move.wait_send()
            remote(halves.at[layer], packed[1 - layer], send, recv, sibling).wait_recv()


def prepare(number, inward, down):
    depth, down_rows = inward.shape[1], down.shape[1]
    in_place = pl.BlockSpec(memory_space=pltpu.HBM)
    shape = (depth + down_rows + down_rows // 2, inward.shape[0] // 2 * inward.shape[2])
    packed = jax.ShapeDtypeStruct(shape, BF16)
    dma = pltpu.SemaphoreType.DMA
    return pl.pallas_call(
        prepare_kernel,
        out_shape=[packed, packed],
        in_specs=[in_place] * 2,
        out_specs=[in_place] * 2,
        scratch_shapes=[pltpu.VMEM((2,) + shape, BF16), dma((12,)), dma, dma, dma],
        compiler_params=pltpu.CompilerParams(
            collective_id=number, has_side_effects=True, vmem_limit_bytes=12 << 20
        ),
    )(inward, down)


def begin_kernel(n_ctx, n_wt, *refs):
    given = refs[:7]
    all_ref, rode_ref, pack, all_gains, all_router, all_routes = refs[7:13]
    tokens, query, pair, out, gains, router, routes = refs[13:20]
    halves, first_pack, load, send, recv = refs[20:25]
    near = Near(n_wt)
    loads = [
        pltpu.make_async_copy(source.at[near.section] if k == 0 else source, target, load.at[k])
        for k, (source, target) in enumerate(zip(given, refs[13:20]))
    ]
    for copy in loads:
        copy.start()
    section, ctx, wt = near.section, near.ctx, near.wt
    peers = [(section, lax.rem(ctx + k, n_ctx), wt) for k in range(1, n_ctx)]
    blocks = CtxGather(near, n_ctx, first_pack, rode_ref, refs[25:28])
    gathers = RowGather(near, CHUNKS, all_ref, refs[28:])
    near.greet(peers)
    for copy in loads:
        copy.wait()
    named = router.shape[0]
    all_gains[section] = gains[...]
    all_routes[section] = routes[...]
    all_router[section] = jnp.zeros(all_router.shape[1:], BF16)
    all_router[section, :named, :] = router[...]
    shared = [
        remote(ref.at[section], ref.at[section], send.at[k], recv.at[k], near.sibling)
        for k, ref in enumerate((all_gains, all_router, all_routes))
    ]
    for copy in shared:
        copy.start()
    q_cols = query.shape[1] // 2
    outward = jnp.transpose(out[...].astype(F32))
    for half in range(2):
        halves[half] = jnp.concatenate(
            [
                query[:, half * q_cols : (half + 1) * q_cols].astype(F32),
                pair[:, half * LANES : (half + 1) * LANES].astype(F32),
                outward[:, half * q_cols : (half + 1) * q_cols],
            ],
            1,
        ).astype(BF16)
    packs = (first_pack, pack)
    for layer in range(2):

        @pl.when(section == layer)
        def _():
            remote(halves.at[1 - layer], packs[layer], send.at[3], recv.at[3], near.sibling).start()
            packs[layer][...] = halves[layer]

    rows = tokens[...].astype(F32)
    scaled = rows * norm_scale(rows)
    shared[0].wait_recv()
    all_ref[near.own] = (scaled * all_gains[0, 0:1, :]).astype(BF16)
    for chunk in range(CHUNKS):
        gathers.first(chunk)
    for layer in range(2):

        @pl.when(section == layer)
        def _():
            remote(halves.at[layer], packs[1 - layer], send.at[3], recv.at[3], near.sibling).wait_recv()

    blocks.start()
    for hop in range(1, n_wt):
        for chunk in range(CHUNKS):
            gathers.hop(chunk, hop)
    blocks.hand_on()
    gathers.arrive()
    blocks.finish()
    gathers.end()
    shared[0].wait_send()
    for copy in shared[1:]:
        copy.wait()
    remote(halves.at[0], first_pack, send.at[3], recv.at[3], near.sibling).wait_send()


def begin(number, tokens, query, pair, out, gains, router, routes):
    n_ctx, n_wt = lax.axis_size("ctx"), lax.axis_size("wt")
    depth, columns = query.shape[0], query.shape[1] + LANES
    dma = pltpu.SemaphoreType.DMA
    pack = (depth, columns)
    return pl.pallas_call(
        functools.partial(begin_kernel, n_ctx, n_wt),
        out_shape=[
            jax.ShapeDtypeStruct((2 * n_wt,) + tokens.shape[1:], BF16),
            jax.ShapeDtypeStruct((n_ctx,) + pack, BF16),
            jax.ShapeDtypeStruct(pack, BF16),
            jax.ShapeDtypeStruct((2,) + gains.shape, gains.dtype),
            jax.ShapeDtypeStruct((2, LANES, router.shape[1]), BF16),
            jax.ShapeDtypeStruct((2,) + routes.shape, routes.dtype),
        ],
        in_specs=[pl.BlockSpec(memory_space=pltpu.HBM)] * 7,
        out_specs=[VMEM] * 6,
        scratch_shapes=[pltpu.VMEM(tokens.shape[1:], BF16)]
        + [pltpu.VMEM(member.shape, member.dtype) for member in (query, pair, out, gains, router, routes)]
        + [
            pltpu.VMEM((2,) + pack, BF16),
            pltpu.VMEM(pack, BF16),
            dma((7,)),
            dma((4,)),
            dma((4,)),
        ]
        + CtxGather.scratch(n_ctx)
        + RowGather.scratch(n_wt, CHUNKS),
        compiler_params=pltpu.CompilerParams(
            collective_id=number, has_side_effects=True, vmem_limit_bytes=16 << 20
        ),
        cost_estimate=pl.CostEstimate(flops=0, bytes_accessed=90 << 20, transcendentals=0),
    )(tokens, query, pair, out, gains, router, routes)


TILE = 256


def expert_pieces(packed, inward, down, depth, down_rows):
    n, wide, width = packed.shape[0], packed.shape[2], down.shape[2]
    half = down_rows // 2
    first = wide - width
    pairs = []
    for c in range(n):
        at = c * down_rows
        second = depth + down_rows
        pairs += [
            (packed.at[c, depth:second, :width], down.at[0, at : at + down_rows, :]),
            (packed.at[c, depth:second, width:], down.at[1, at : at + down_rows, :first]),
            (packed.at[c, second:, : wide // 2], down.at[1, at : at + half, first:]),
            (packed.at[c, second:, wide // 2 :], down.at[1, at + half : at + down_rows, first:]),
        ]
    for c in range(n):
        pairs.append((packed.at[c, :depth, :], inward.at[c * depth : (c + 1) * depth, :]))
    return pairs


def gate_rows(x, router, routes):
    lane = lax.broadcasted_iota(jnp.int32, (x.shape[0], LANES), 1)
    named = routes[:, 0:1] == lane
    for t in range(1, routes.shape[1]):
        named = named | (routes[:, t : t + 1] == lane)
    logits = jnp.where(named, dot(x, router, ((1,), (1,))), MASKED)
    expos = jnp.where(named, jnp.exp(logits - jnp.max(logits, 1, keepdims=True)), 0.0)
    return expos / jnp.sum(expos, 1, keepdims=True)


def experts_kernel(n_ctx, layer, forward, backward, depth, down_rows, ride, ready, *refs):
    refs = list(refs)
    x_ref, router_ref, pick_ref = [refs.pop(0) for _ in range(3)]
    if forward:
        hit_ref = refs.pop(0)
    else:
        gates_ref, gate_up_ref = refs.pop(0), refs.pop(0)
    d_ref = refs.pop(0) if backward else None
    ride_ref = refs.pop(0) if ride else None
    packed_ref = refs.pop(0)
    part_ref = refs.pop(0) if forward else None
    if forward and not backward:
        gates_ref, gate_up_ref = refs.pop(0), refs.pop(0)
    if backward:
        back_out, grads_ref, router_grad_ref = [refs.pop(0) for _ in range(3)]
    rode_ref = refs.pop(0) if ride else None
    inward, down, weighted, load = [refs.pop(0) for _ in range(4)]
    if forward and backward:
        gates_ref, gate_up_ref = refs.pop(0), refs.pop(0)
    if backward:
        d_gate_up, x_turned, in_grad, down_grad, store, back_ref, leave = refs[:7]
        refs = refs[7:]
        if forward:
            part_out, part_ref = part_ref, refs.pop(0)
            part_leave = pltpu.make_async_copy(part_ref, part_out, leave.at[1])
        back_leave = pltpu.make_async_copy(back_ref, back_out, leave.at[0])

    pieces = expert_pieces(packed_ref, inward, down, depth, down_rows)
    loads = [pltpu.make_async_copy(source, target, load.at[k]) for k, (source, target) in enumerate(pieces)]
    n_down = 4 * packed_ref.shape[0]
    for copy in (loads[n_down:] + loads[:n_down]) if forward else loads:
        copy.start()
    if ride:
        landed, ride_send, ride_recv = refs
        section, ctx, wt = place()
        peers = [(section, lax.rem(ctx + k, n_ctx), wt) for k in range(1, n_ctx)]
        greet(peers)
        riders = [
            remote(
                ride_ref.at[lax.rem(ctx + 1 + k, n_ctx)], landed.at[k], ride_send.at[k], ride_recv.at[k], peers[k]
            )
            for k in range(n_ctx - 1)
        ]
        for copy in riders:
            copy.start()
    if ready:
        ready()
    columns = [slice(t * TILE, (t + 1) * TILE) for t in range(2 * FF // TILE)]
    per_expert = FF // TILE
    width = x_ref.shape[1]

    def gate_at(t):
        return slice(2 * FF * (t // per_expert) + TILE * (t % per_expert), 2 * FF * (t // per_expert) + TILE * (t % per_expert + 1))

    def up_at(t):
        return slice(gate_at(t).start + FF, gate_at(t).stop + FF)

    def weight_of(e):
        return jnp.sum(gates_ref[...] * pick_ref[e : e + 1, :], 1, keepdims=True)

    if forward:
        routes = hit_ref[layer]
        routes = routes.reshape(routes.shape[0] * routes.shape[1], routes.shape[2])
        gates_ref[...] = gate_rows(x_ref[...], router_ref[layer], routes)
        for copy in loads[n_down:]:
            copy.wait()
        for t, place_of in enumerate(columns):
            gate = dot(x_ref[...], inward[:, gate_at(t)], ((1,), (0,)))
            up = dot(x_ref[...], inward[:, up_at(t)], ((1,), (0,)))
            gate_up_ref[:, gate_at(t)] = gate.astype(BF16)
            gate_up_ref[:, up_at(t)] = up.astype(BF16)
            weighted[:, place_of] = (gate / (1.0 + jnp.exp(-gate)) * up * weight_of(t // per_expert)).astype(BF16)
        for copy in loads[:n_down]:
            copy.wait()
        for n in range(width // TILE):
            at = slice(n * TILE, (n + 1) * TILE)
            part_ref[:, at] = (
                dot(weighted[:, :FF], down[0, :, at], ((1,), (0,)))
                + dot(weighted[:, FF:], down[1, :, at], ((1,), (0,)))
            ).astype(BF16)
        if backward:
            part_leave.start()
    else:
        for copy in loads[:n_down]:
            copy.wait()
    if backward:
        d_weight = [0.0, 0.0]
        for t, place_of in enumerate(columns):
            e = t // per_expert
            rows_of = slice(TILE * (t % per_expert), TILE * (t % per_expert + 1))
            weight = weight_of(e)
            d_weighted = dot(d_ref[...], down[e, rows_of, :], ((1,), (1,)))
            gate = gate_up_ref[:, gate_at(t)].astype(F32)
            up = gate_up_ref[:, up_at(t)].astype(F32)
            sigmoid = 1.0 / (1.0 + jnp.exp(-gate))
            activated = gate * sigmoid
            hidden = activated * up
            d_weight[e] = d_weight[e] + jnp.sum(hidden * d_weighted, 1, keepdims=True)
            weighted[:, place_of] = (hidden * weight).astype(BF16)
            d_hidden = d_weighted * weight
            d_gate_up[:, gate_at(t)] = (d_hidden * up * (sigmoid * (1.0 + gate * (1.0 - sigmoid)))).astype(BF16)
            d_gate_up[:, up_at(t)] = (d_hidden * activated).astype(BF16)
        gates = gates_ref[...]
        terms = gates * (pick_ref[0:1, :] * d_weight[0] + pick_ref[1:2, :] * d_weight[1])
        d_logits = terms - gates * jnp.sum(terms, 1, keepdims=True)
        high = d_logits.astype(BF16)
        low = (d_logits - high.astype(F32)).astype(BF16)
        both = jnp.concatenate([high, low], 1)
        if not forward:
            for copy in loads[n_down:]:
                copy.wait()
        for n in range(width // TILE):
            at = slice(n * TILE, (n + 1) * TILE)
            table = router_ref[layer, :, at]
            back_ref[:, at] = (
                dot(d_gate_up[...], inward[at, :], ((1,), (1,)))
                + dot(both, jnp.concatenate([table, table], 0), ((1,), (0,)))
            ).astype(BF16)
        back_leave.start()
        x_turned[...] = jnp.transpose(x_ref[...])
        router_grad = dot(both, x_ref[...], ((0,), (0,)))
        named = router_grad_ref.shape[0]
        router_grad_ref[...] = router_grad[:named] + router_grad[LANES : LANES + named]
        pieces = expert_pieces(grads_ref, in_grad, down_grad, depth, down_rows)
        stores = [
            pltpu.make_async_copy(source, target, store.at[k]) for k, (target, source) in enumerate(pieces)
        ]
        for e in range(2):
            turned_hidden = jnp.transpose(weighted[:, e * FF : (e + 1) * FF])
            for n in range(width // TILE):
                at = slice(n * TILE, (n + 1) * TILE)
                down_grad[e, :, at] = dot(turned_hidden, d_ref[:, at], ((1,), (0,))).astype(BF16)
        for copy in stores[:n_down]:
            copy.start()
        for c in range(n_ctx):
            at = slice(c * depth, (c + 1) * depth)
            for n in range(2):
                wide = slice(n * 2 * FF, (n + 1) * 2 * FF)
                in_grad[at, wide] = dot(x_turned[at, :], d_gate_up[:, wide], ((1,), (0,))).astype(BF16)
            stores[n_down + c].start()
        for copy in stores:
            copy.wait()
        back_leave.wait()
        if forward:
            part_leave.wait()
    if ride:
        total = ride_ref[ctx].astype(F32)
        for k, copy in enumerate(riders):
            copy.wait()
            total = total + landed[k].astype(F32)
        rode_ref[...] = total


def experts(
    layer, x, packed, router, pick, n_experts, depth, down_rows, hit=None, kept=None, d_rows=None, number=None, add=None
):
    n_ctx = lax.axis_size("ctx")
    forward, backward = hit is not None, d_rows is not None
    n_rows, width = x.shape
    any_place = pl.BlockSpec(memory_space=pl.ANY)
    operands = [x, router, pick]
    operands += [hit] if forward else list(kept)
    operands += [d_rows] if backward else []
    operands += [add] if add is not None else []
    rows_out = jax.ShapeDtypeStruct((n_rows, width), BF16)
    inner = [jax.ShapeDtypeStruct((n_rows, LANES), F32), jax.ShapeDtypeStruct((n_rows, 4 * FF), BF16)]
    n_pieces = 5 * packed.shape[0]
    scratch = [
        pltpu.VMEM((width, 4 * FF), BF16),
        pltpu.VMEM((2, FF, width), BF16),
        pltpu.VMEM((n_rows, 2 * FF), BF16),
        pltpu.SemaphoreType.DMA((n_pieces,)),
    ]
    outs = []
    out_specs = []
    if forward:
        outs += [rows_out]
        out_specs += [any_place if backward else VMEM]
    if forward and not backward:
        outs += inner
        out_specs += [VMEM] * 2
    if backward:
        outs += [rows_out, jax.ShapeDtypeStruct(packed.shape, BF16), jax.ShapeDtypeStruct((n_experts, width), F32)]
        out_specs += [any_place, any_place, VMEM]
        if forward:
            scratch += [pltpu.VMEM(member.shape, member.dtype) for member in inner]
        scratch += [
            pltpu.VMEM((n_rows, 4 * FF), BF16),
            pltpu.VMEM((width, n_rows), BF16),
            pltpu.VMEM((width, 4 * FF), BF16),
            pltpu.VMEM((2, FF, width), BF16),
            pltpu.SemaphoreType.DMA((n_pieces,)),
            pltpu.VMEM((n_rows, width), BF16),
            pltpu.SemaphoreType.DMA((2,)),
        ]
        scratch += [pltpu.VMEM((n_rows, width), BF16)] if forward else []
    params = {}
    if add is not None:
        outs.append(jax.ShapeDtypeStruct(add.shape[1:], F32))
        out_specs.append(VMEM)
        scratch += [
            pltpu.VMEM((n_ctx - 1,) + add.shape[1:], BF16),
            pltpu.SemaphoreType.DMA((n_ctx - 1,)),
            pltpu.SemaphoreType.DMA((n_ctx - 1,)),
        ]
        params = dict(collective_id=number, has_side_effects=True)
    work = n_rows * 6 * width * FF * 2 * ((1 if forward else 0) + (2 if backward else 0))
    load = forward and backward
    kernel = functools.partial(experts_kernel, n_ctx, layer, forward, backward, depth, down_rows, add is not None)
    call = dict(
        out_shape=outs,
        out_specs=out_specs,
        scratch_shapes=scratch,
        compiler_params=pltpu.CompilerParams(vmem_limit_bytes=(60 if load else 44 if backward else 28) << 20, **params),
        cost_estimate=pl.CostEstimate(flops=2 * work, bytes_accessed=40 << 20, transcendentals=0),
    )
    if load:
        return loaded(kernel, operands, [packed], **call)
    in_specs = [VMEM] * len(operands) + [any_place]
    return pl.pallas_call(functools.partial(kernel, None), in_specs=in_specs, **call)(*operands, packed)


def shards(tokens, cotangent, blocks, routes, norm_gain, w_query, key_value_weight, w_attn_out, router, w_in, w_down):
    section, ctx, wt = place()
    n_ctx, n_wt, layers = lax.axis_size("ctx"), lax.axis_size("wt"), lax.axis_size("section")
    micro_count, share, width = tokens.shape
    per_ctx = routes.shape[2]
    seq_len = per_ctx * n_ctx
    per_core = w_in.shape[1] // 2
    n_experts = router.shape[2]
    q_cols = w_query.shape[2] // 2
    depth = w_query.shape[1]

    block_len = seq_len // blocks.shape[1]
    placed = (blocks[:, :, None] * block_len + jnp.arange(block_len, dtype=jnp.int32)[None, None, :]).reshape(
        micro_count, seq_len
    )
    query_place = lax.dynamic_slice_in_dim(placed, ctx * per_ctx, per_ctx, 1)
    later = (jnp.arange(micro_count) > 0)[:, None]
    query_start = jnp.where(later, query_place - query_place % CONT_LEN, 0)
    query_pos = jnp.where(later, seq_len + query_place % CONT_LEN, query_place)
    half = HEAD_SIZE // 2
    inverse = jnp.power(ROPE_BASE, -(jnp.arange(LANES, dtype=jnp.int32) % half).astype(F32) * 2.0 / HEAD_SIZE)
    angles = query_pos.reshape(-1).astype(F32)[:, None] * inverse[None, :]
    sign = jnp.where(jnp.arange(LANES) % HEAD_SIZE < half, -1.0, 1.0)
    tables = (
        jnp.cos(angles),
        jnp.sin(angles) * sign[None, :],
        jnp.transpose(placed.reshape(micro_count, n_ctx, per_ctx), (1, 0, 2)).reshape(n_ctx, -1, 1),
        query_place[:, None, :],
        query_start[:, None, :],
    )

    moe_pack = prepare(15, w_in[0], w_down[0])
    normed_in, full, attn_pack, gain_pack, router_pack, route_pack = begin(
        0,
        tokens,
        w_query[0],
        key_value_weight[0].reshape(depth, -1),
        w_attn_out[0],
        norm_gain[0],
        jnp.transpose(router[0]),
        routes[0],
    )

    in_rows, down_rows = w_in.shape[2], w_down.shape[2]

    def gather_experts(pack):
        return lax.all_gather(pack, "ctx", axis=0, tiled=True).reshape((n_ctx,) + pack.shape)

    attn_full = [None, None]

    my_first = wt * 2 * per_core + section * per_core
    n_rows = micro_count * per_ctx

    pick = (jnp.arange(LANES)[None, :] == my_first + jnp.arange(8)[:, None]).astype(F32)
    def full_rows(values):
        return values.reshape(n_rows, width)

    def blocked(values):
        return values.reshape(2 * n_wt, share, width).astype(BF16)

    stream = lax.dynamic_index_in_dim(tokens, section, 0, False)
    top = lax.dynamic_index_in_dim(cotangent, section, 0, False)

    attn_full[0] = full.reshape(-1, full.shape[2])
    moe_full = [gather_experts(member) for member in moe_pack]
    saved = []
    outputs = []
    for layer in range(2):
        rows_in = full_rows(normed_in)
        weights = attn_full[layer]
        if layer == 0:
            partial, *heads, attended, d_mixed = attend(2, rows_in, weights, tables, top)
        else:
            partial, *heads, attended = attend(3, rows_in, weights, tables)
        middle, normed_mid, token = exchange(
            4 + layer, blocked(partial), stream, gain=gain_pack[layer, 1:2], spread="norm"
        )
        token, moe_full[layer] = lax.optimization_barrier((token, moe_full[layer]))
        pick_now = pick + token
        rows_mid = full_rows(normed_mid)
        if layer == 0:
            partial, gates, gate_up = experts(
                0, rows_mid, moe_full[0], router_pack, pick_now, n_experts, in_rows, down_rows, hit=route_pack
            )
            inner = (gates, gate_up)
        else:
            partial, *back_parts = experts(
                1,
                rows_mid,
                moe_full[1],
                router_pack,
                pick_now,
                n_experts,
                in_rows,
                down_rows,
                hit=route_pack,
                d_rows=full_rows(d_mixed),
            )
            inner = None
        saved.append(
            dict(
                stream=stream,
                middle=middle,
                rows_in=rows_in,
                rows_mid=rows_mid,
                heads=heads,
                attended=attended,
                inner=inner,
            )
        )
        if layer == 0:
            stream, normed_in, full, token = exchange(
                6, blocked(partial), middle, gain=gain_pack[1, 0:1], spread="norm", rounded=True, gather=attn_pack
            )
            attn_full[1] = full.reshape(-1, full.shape[2])
            outputs.append(stream)
        else:
            last_rows = (blocked(partial), middle)
    upstream = top
    grads_in = [None, None]
    attn_grads = [None, None]
    moe_grads = [None, None]
    small = [None, None]
    for layer in (1, 0):
        kept = saved[layer]
        if layer == 0:
            back_parts = experts(
                0,
                kept["rows_mid"],
                moe_full[0],
                router_pack,
                pick,
                n_experts,
                in_rows,
                down_rows,
                kept=kept["inner"],
                d_rows=full_rows(d_mixed),
                number=7,
                add=attn_parts,
            )
            *back_parts, attn_grads[1] = back_parts
        partial, packed_grad, router_grad = back_parts
        gain = gain_pack[layer, 1:2]
        if layer == 0:
            gain, moe_grads[1] = lax.optimization_barrier((gain, moe_grads[1]))
        moe_grads[layer] = lax.psum_scatter(packed_grad, "ctx", scatter_dimension=0, tiled=False)
        d_middle, gain_grad_mid, d_attn, token = exchange(
            8 + layer, blocked(partial), upstream, kept["middle"], gain, spread="plain", load=layer == 1
        )
        rows_a = full_rows(d_attn)
        weights = attn_full[layer]
        if layer == 1:
            then = (d_middle, kept["stream"], gain_pack[1, 0:1], *last_rows)
            raw, upstream, gain_grad_in, d_mixed, last = attend_back(11, rows_a, weights, tables, kept["heads"], then)
            outputs.append(last)
        else:
            raw, partial = attend_back(10, rows_a, weights, tables, kept["heads"])
        attn_parts = dot(kept["rows_in"], jnp.pad(raw, ((0, 0), (0, LANES))), ((0,), (0,)))
        attn_parts = attn_parts + dot(rows_a, jnp.pad(kept["attended"], ((0, 0), (2 * LANES, 0))), ((0,), (0,)))
        attn_parts = attn_parts.astype(BF16).reshape(n_ctx, depth, -1)
        if layer == 0:
            upstream, gain_grad_in, attn_grads[0], token = exchange(
                1, partial, d_middle, kept["stream"], gain_pack[0, 0:1], rounded=True, add=attn_parts
            )
        grads_in[layer] = upstream
        small[layer] = [router_grad, gain_grad_in, gain_grad_mid]

    gain_total, router_total, grad_query, grad_kv, grad_out, out_pair, grad_pair = finish(
        14, small[0] + small[1], attn_grads, outputs + grads_in, q_cols
    )
    piece = width // (n_ctx * n_wt)
    moe_grads = [member.reshape(member.shape[-2:]) for member in moe_grads]
    grad_in, grad_down = hand_over(13, moe_grads[0], moe_grads[1], gain_total, in_rows, down_rows, per_core, width)
    return (
        out_pair[None],
        grad_pair[None],
        gain_total[None, :, :piece],
        grad_query[None],
        grad_kv.reshape(depth, 2, LANES)[None],
        grad_out[None],
        jnp.transpose(router_total[:, :piece])[None],
        grad_in.astype(F32)[None],
        grad_down.astype(F32)[None],
    )


def solution(mesh):
    return jax.shard_map(
        shards,
        mesh=mesh,
        in_specs=(
            P(None, ("ctx", "wt"), None),
            P(None, ("ctx", "wt"), None),
            P(),
            P("section", None, "ctx", None),
            P("section", None, None),
            P("section", "ctx", "wt"),
            P("section", "ctx", "wt", None),
            P("section", "wt", "ctx"),
            P("section", None, None),
            P("section", "wt", "ctx", None),
            P("section", "wt", "ctx", None),
        ),
        out_specs=(
            P("section", None, ("ctx", "wt"), None),
            P("section", None, ("ctx", "wt"), None),
            P("section", None, ("ctx", "wt")),
            P("section", "ctx", "wt"),
            P("section", "ctx", "wt", None),
            P("section", "wt", "ctx"),
            P("section", ("ctx", "wt"), None),
            P("section", "wt", "ctx", None),
            P("section", "wt", "ctx", None),
        ),
        check_vma=False,
    )
```

```python
import functools

import jax
import jax.numpy as jnp
from jax import lax
from jax.experimental import pallas as pl
from jax.experimental.pallas import tpu as pltpu
from jax.sharding import PartitionSpec as P

HEAD_SIZE = 64
FF = 512
CONT_LEN = 1024
EPSILON = 1e-06
ROPE_BASE = 10000.0
MASKED = -1e30
CHUNKS = 2
LANES = 2 * HEAD_SIZE
MESH = pl.DeviceIdType.MESH
F32 = jnp.float32
BF16 = jnp.bfloat16


def dot(left, right, contract):
    return lax.dot_general(left, right, (contract, ((), ())), preferred_element_type=F32)


def norm_scale(rows):
    return lax.rsqrt(jnp.mean(rows * rows, -1, keepdims=True) + EPSILON)


def place():
    return lax.axis_index("section"), lax.axis_index("ctx"), lax.axis_index("wt")


def greet(targets):
    barrier = pltpu.get_barrier_semaphore()
    for target in targets:
        pl.semaphore_signal(barrier, inc=1, device_id=target, device_id_type=MESH)
    pl.semaphore_wait(barrier, len(targets))


def remote(source, destination, send_sem, recv_sem, target):
    return pltpu.make_async_remote_copy(
        src_ref=source,
        dst_ref=destination,
        send_sem=send_sem,
        recv_sem=recv_sem,
        device_id=target,
        device_id_type=MESH,
    )


def loaded(kernel, operands, whole, **call):
    n = len(operands)

    def body(*refs):
        held, sems = refs[-n - 1 : -1], refs[-1]
        copies = [pltpu.make_async_copy(refs[k], held[k], sems.at[k]) for k in range(n)]
        for copy in copies:
            copy.start()

        def ready():
            for copy in copies:
                copy.wait()

        kernel(ready, *held, *refs[n : -n - 1])

    call["scratch_shapes"] = (
        list(call["scratch_shapes"])
        + [pltpu.VMEM(member.shape, member.dtype) for member in operands]
        + [pltpu.SemaphoreType.DMA((n,))]
    )
    call["in_specs"] = [pl.BlockSpec(memory_space=pl.ANY)] * (n + len(whole))
    return pl.pallas_call(body, **call)(*operands, *whole)


class Near:
    def __init__(self, n_wt):
        self.section, self.ctx, self.wt = place()
        self.n_wt = n_wt
        self.sibling = (1 - self.section, self.ctx, self.wt)
        self.right = (self.section, self.ctx, jnp.minimum(self.wt + 1, n_wt - 1))
        self.left = (self.section, self.ctx, jnp.maximum(self.wt - 1, 0))
        self.has_right, self.has_left = self.wt < n_wt - 1, self.wt > 0
        self.own = self.section * n_wt + self.wt

    def greet(self, others=()):
        barrier = pltpu.get_barrier_semaphore()

        def hail(target):
            pl.semaphore_signal(barrier, inc=1, device_id=target, device_id_type=MESH)

        hail(self.sibling)
        pl.when(self.has_right)(lambda: hail(self.right))
        pl.when(self.has_left)(lambda: hail(self.left))
        for other in others:
            hail(other)
        pl.semaphore_wait(
            barrier, 1 + len(others) + self.has_right.astype(jnp.int32) + self.has_left.astype(jnp.int32)
        )


def rows_of(chunk, rows):
    return slice(chunk * rows, (chunk + 1) * rows)


def block_at(last, block, rightward):
    return last + 1 - block if rightward else block - 1


class RowSum:
    def __init__(self, near, chunks, parts, scratch):
        self.near, self.chunks, self.parts = near, chunks, parts
        self.rows = parts.shape[1] // chunks
        self.from_sibling, self.in_right, self.in_left, self.out_right, self.out_left = scratch[:5]
        self.swap_send, self.swap_recv, self.send, self.recv = scratch[5:]

    @staticmethod
    def scratch(n_wt, shape, chunks):
        dma = pltpu.SemaphoreType.DMA
        return [pltpu.VMEM((n_wt,) + shape, BF16)] * 5 + [dma((chunks * n_wt,))] * 2 + [dma((2 * chunks * n_wt,))] * 2

    def swap(self, chunk, block):
        at = rows_of(chunk, self.rows)
        number = chunk * self.near.n_wt + block
        return remote(
            self.parts.at[(1 - self.near.section) * self.near.n_wt + block, at],
            self.from_sibling.at[block, at],
            self.swap_send.at[number],
            self.swap_recv.at[number],
            self.near.sibling,
        )

    def begin(self):
        n_wt = self.near.n_wt
        order = []
        for step in range(n_wt - 1):
            order += [n_wt - 1 - step, step]
        for chunk in range(self.chunks):
            for block in dict.fromkeys(order):
                self.swap(chunk, block).start()

    def chip_sum(self, chunk, block):
        at = rows_of(chunk, self.rows)
        mine = self.parts[self.near.section * self.near.n_wt + block, at, :]
        return mine.astype(F32) + self.from_sibling[block, at, :].astype(F32)

    def toward(self, chunk, block, rightward):
        at = rows_of(chunk, self.rows)
        number = (2 * chunk + (0 if rightward else 1)) * self.near.n_wt + block
        source, target = (self.out_right, self.in_right) if rightward else (self.out_left, self.in_left)
        return remote(
            source.at[block, at],
            target.at[block, at],
            self.send.at[number],
            self.recv.at[number],
            self.near.right if rightward else self.near.left,
        )

    def send_on(self, chunk, block, rightward):
        at = rows_of(chunk, self.rows)
        self.swap(chunk, block).wait_recv()
        outward, inward = (self.out_right, self.in_right) if rightward else (self.out_left, self.in_left)
        behind = self.near.has_left if rightward else self.near.has_right

        @pl.when(jnp.logical_not(behind))
        def _():
            outward[block, at, :] = self.chip_sum(chunk, block).astype(BF16)

        @pl.when(behind)
        def _():
            self.toward(chunk, block, rightward).wait_recv()
            outward[block, at, :] = (self.chip_sum(chunk, block) + inward[block, at, :].astype(F32)).astype(BF16)

        self.toward(chunk, block, rightward).start()

    def step(self, chunk, step):
        wt, n_wt = self.near.wt, self.near.n_wt
        far, near = n_wt - 1 - step, step
        lower = 2 * wt < n_wt
        pl.when((wt < far) & lower)(lambda: self.send_on(chunk, far, True))
        pl.when(wt > near)(lambda: self.send_on(chunk, near, False))
        pl.when((wt < far) & jnp.logical_not(lower))(lambda: self.send_on(chunk, far, True))

    def point(self, chunk, number):
        wt, last = self.near.wt, self.near.n_wt - 1
        for block in range(1, last + 1):
            turn = last - block
            if number == 0:
                pl.when(wt == 0)(functools.partial(self.send_on, chunk, block_at(last, block, True), True))
                pl.when(wt == last)(functools.partial(self.send_on, chunk, block_at(last, block, False), False))
            elif 1 <= number - turn < block:
                pl.when(wt == number - turn)(functools.partial(self.send_on, chunk, block, True))
                pl.when(wt == last - (number - turn))(functools.partial(self.send_on, chunk, last - block, False))

    def collect(self, chunk, result):
        at, wt = rows_of(chunk, self.rows), self.near.wt
        self.swap(chunk, wt).wait_recv()
        result[at, :] = self.chip_sum(chunk, wt)

        @pl.when(self.near.has_left)
        def _():
            self.toward(chunk, wt, True).wait_recv()
            result[at, :] += self.in_right[wt, at, :].astype(F32)

        @pl.when(self.near.has_right)
        def _():
            self.toward(chunk, wt, False).wait_recv()
            result[at, :] += self.in_left[wt, at, :].astype(F32)

    def end(self):
        wt, n_wt = self.near.wt, self.near.n_wt
        for chunk in range(self.chunks):
            for block in range(n_wt):
                self.swap(chunk, block).wait_send()
                if block > 0:
                    pl.when(wt < block)(self.toward(chunk, block, True).wait_send)
                if block < n_wt - 1:
                    pl.when(wt > block)(self.toward(chunk, block, False).wait_send)


class RowGather:
    def __init__(self, near, chunks, all_ref, scratch):
        self.near, self.chunks, self.all = near, chunks, all_ref
        self.rows = all_ref.shape[1] // chunks
        self.send, self.recv, self.pass_send, self.pass_recv = scratch
        self.sent, self.arrivals = [], []

    @staticmethod
    def scratch(n_wt, chunks):
        return [pltpu.SemaphoreType.DMA((2 * chunks * n_wt,))] * 4

    def along(self, chunk, block, hop, rightward):
        at = rows_of(chunk, self.rows)
        number = (2 * chunk + (0 if rightward else 1)) * self.near.n_wt + hop
        return remote(
            self.all.at[block, at],
            self.all.at[block, at],
            self.send.at[number],
            self.recv.at[number],
            self.near.right if rightward else self.near.left,
        )

    def across(self, chunk, block, number):
        at = rows_of(chunk, self.rows)
        number = 2 * chunk * self.near.n_wt + number
        return remote(
            self.all.at[block, at],
            self.all.at[block, at],
            self.pass_send.at[number],
            self.pass_recv.at[number],
            self.near.sibling,
        )

    def launch(self, condition, copy):
        pl.when(condition)(copy.start)
        self.sent.append((condition, copy))

    def first(self, chunk):
        near = self.near
        always = near.wt >= 0
        self.launch(near.has_right, self.along(chunk, near.own, 1, True))
        self.launch(near.has_left, self.along(chunk, near.own, 1, False))
        self.launch(always, self.across(chunk, near.own, 0))
        self.arrivals.append((always, self.across(chunk, near.own, 0)))

    def hop(self, chunk, hop):
        near, n_wt = self.near, self.near.n_wt
        for rightward, came, more, block, number in (
            (True, near.wt >= hop, near.has_right, jnp.maximum(near.own - hop, 0), hop),
            (False, near.wt + hop < n_wt, near.has_left, jnp.minimum(near.own + hop, 2 * n_wt - 1), n_wt + hop),
        ):
            pl.when(came)(self.along(chunk, block, hop, rightward).wait_recv)
            if hop + 1 < n_wt:
                self.launch(came & more, self.along(chunk, block, hop + 1, rightward))
            self.launch(came, self.across(chunk, block, number))
            self.arrivals.append((came, self.across(chunk, block, number)))

    def arrive(self):
        for condition, copy in self.arrivals:
            pl.when(condition)(copy.wait_recv)

    def end(self):
        for condition, copy in self.sent:
            pl.when(condition)(copy.wait_send)


class CtxGather:
    def __init__(self, near, n_ctx, source, target, sems):
        self.n_ctx, self.source, self.target = n_ctx, source, target
        self.send, self.recv, self.local = sems
        self.ctx = near.ctx
        x, y = lax.rem(near.ctx, 2), near.ctx // 2
        self.at_x, self.at_y = 2 * y + 1 - x, 2 * (1 - y) + x
        self.device = lambda index: (near.section, index, near.wt)
        self.half = source.shape[0] // 2

    @staticmethod
    def scratch(n_ctx):
        dma = pltpu.SemaphoreType.DMA
        return [dma((max(4, n_ctx - 1),)), dma((max(4, n_ctx - 1),)), dma]

    def copy(self, source, target, number, index):
        return remote(source, target, self.send.at[number], self.recv.at[number], self.device(index))

    def near_copies(self):
        if self.n_ctx != 4:
            return [
                self.copy(self.source, self.target.at[self.ctx], k, lax.rem(self.ctx + 1 + k, self.n_ctx))
                for k in range(self.n_ctx - 1)
            ]
        return [
            self.copy(self.source, self.target.at[self.ctx], k, index)
            for k, index in enumerate((self.at_x, self.at_y))
        ]

    def far_copies(self):
        if self.n_ctx != 4:
            return []
        parts = []
        for number, block, at, index in (
            (2, self.at_x, slice(0, self.half), self.at_y),
            (3, self.at_y, slice(self.half, 2 * self.half), self.at_x),
        ):
            ref = self.target.at[block, at]
            parts.append(self.copy(ref, ref, number, index))
        return parts

    def start(self):
        pltpu.make_async_copy(self.source, self.target.at[self.ctx], self.local).start()
        for copy in self.near_copies():
            copy.start()

    def hand_on(self):
        for copy in self.near_copies():
            copy.wait_recv()
        for copy in self.far_copies():
            copy.start()

    def finish(self):
        pltpu.make_async_copy(self.source, self.target.at[self.ctx], self.local).wait()
        for copy in self.far_copies():
            copy.wait()
        for copy in self.near_copies():
            copy.wait_send()


class CtxSum:
    def __init__(self, near, n_ctx, parts, scratch):
        self.n_ctx, self.parts = n_ctx, parts
        *self.buffers, self.send, self.recv = scratch
        self.ctx = near.ctx
        x, y = lax.rem(near.ctx, 2), near.ctx // 2
        self.at_x, self.at_y, self.across = 2 * y + 1 - x, 2 * (1 - y) + x, 2 * (1 - y) + 1 - x
        self.device = lambda index: (near.section, index, near.wt)
        half = parts.shape[1] // 2
        self.halves = (slice(0, half), slice(half, 2 * half))

    @staticmethod
    def scratch(n_ctx, shape):
        dma = pltpu.SemaphoreType.DMA
        rows, columns = shape[1:]
        if n_ctx != 4:
            return [pltpu.VMEM((n_ctx - 1, rows, columns), BF16), dma((n_ctx - 1,)), dma((n_ctx - 1,))]
        return [
            pltpu.VMEM((2, rows // 2, columns), BF16),
            pltpu.VMEM((2, rows, columns), BF16),
            pltpu.VMEM((2, rows, columns), BF16),
            dma((4,)),
            dma((4,)),
        ]

    def copy(self, source, target, number, index):
        return remote(source, target, self.send.at[number], self.recv.at[number], self.device(index))

    def direct(self):
        blocks = [lax.rem(self.ctx + 1 + k, self.n_ctx) for k in range(self.n_ctx - 1)]
        return [self.copy(self.parts.at[block], self.buffers[0].at[k], k, block) for k, block in enumerate(blocks)]

    def far_copies(self):
        return [
            self.copy(self.parts.at[self.across, self.halves[k]], self.buffers[0].at[k], k, index)
            for k, index in enumerate((self.at_x, self.at_y))
        ]

    def near_copies(self):
        far, staged, landed = self.buffers
        return [
            self.copy(staged.at[k], landed.at[k], 2 + k, index) for k, index in enumerate((self.at_x, self.at_y))
        ]

    def start(self):
        for copy in self.far_copies() if self.n_ctx == 4 else self.direct():
            copy.start()

    def hand_on(self):
        if self.n_ctx != 4:
            return
        far, staged, landed = self.buffers
        for k, block in ((1, self.at_y), (0, self.at_x)):
            self.far_copies()[1 - k].wait_recv()
            staged[k] = self.parts[block]
            at = self.halves[1 - k]
            staged[k, at, :] = (self.parts[block, at, :].astype(F32) + far[1 - k].astype(F32)).astype(BF16)
            self.near_copies()[k].start()

    def finish(self, result):
        total = self.parts[self.ctx].astype(F32)
        if self.n_ctx == 4:
            for k, copy in enumerate(self.near_copies()):
                copy.wait_recv()
                total = total + self.buffers[2][k].astype(F32)
        else:
            for k, copy in enumerate(self.direct()):
                copy.wait_recv()
                total = total + self.buffers[0][k].astype(F32)
        result[...] = total
        for copy in self.far_copies() + self.near_copies() if self.n_ctx == 4 else self.direct():
            copy.wait_send()


def exchange_steps(
    near,
    n_ctx,
    parts,
    rows_ref,
    stream_ref,
    gain_ref,
    result_ref,
    gain_grad_ref,
    all_ref,
    spread,
    rounded,
    scratch,
    ride=None,
    ride_refs=None,
):
    n_wt = near.n_wt
    scratch = list(scratch)
    sums = RowSum(near, CHUNKS, parts, scratch[:9])
    scratch = scratch[9:]
    sum_ref = scratch.pop(0) if rounded else result_ref
    if spread:
        gathers = RowGather(near, CHUNKS, all_ref, scratch[:4])
        scratch = scratch[4:]
    chunk_rows = rows_ref.shape[0] // CHUNKS
    sums.begin()
    if ride:
        ride_ref, rode_ref = ride_refs
        if ride == "gather":
            blocks = CtxGather(near, n_ctx, ride_ref, rode_ref, scratch)
        else:
            blocks = CtxSum(near, n_ctx, ride_ref, scratch)
        blocks.start()

    def settle(chunk):
        at = rows_of(chunk, chunk_rows)
        sums.collect(chunk, sum_ref)
        total = sum_ref[at, :]
        if stream_ref is not None:
            stream = stream_ref[at, :].astype(F32)
            scale = norm_scale(stream)
            weighted = gain_ref[...] * total
            gain_part = jnp.sum(total * stream * scale, 0, keepdims=True)
            gain_grad_ref[...] = gain_part if chunk == 0 else gain_grad_ref[...] + gain_part
            total = scale * weighted - stream * (scale * scale * scale) * jnp.mean(
                weighted * stream, -1, keepdims=True
            )
        total = rows_ref[at, :].astype(F32) + total
        if rounded:
            total = total.astype(BF16)
        result_ref[at, :] = total
        total = total.astype(F32)
        if spread:
            if spread == "norm":
                total = total * norm_scale(total) * gain_ref[...]
            all_ref[near.own, at, :] = total.astype(BF16)
            gathers.first(chunk)

    stages = [functools.partial(sums.step, step=step) for step in range(n_wt - 1)]
    stages.append(settle)
    if spread:
        stages += [functools.partial(gathers.hop, hop=hop) for hop in range(1, n_wt)]
    for slot in range(CHUNKS + len(stages) - 1):
        for chunk in reversed(range(CHUNKS)):
            if 0 <= slot - chunk < len(stages):
                stages[slot - chunk](chunk)
        if ride and slot == (n_wt + 1 if spread else 1):
            blocks.hand_on()

    if spread:
        gathers.arrive()
    if ride == "gather":
        blocks.finish()
    elif ride == "sum":
        blocks.finish(rode_ref)
    if spread:
        gathers.end()
    sums.end()


def exchange_scratch(n_ctx, n_wt, shape, spread, rounded, ride=None, rider=None):
    dma = pltpu.SemaphoreType.DMA
    scratch = RowSum.scratch(n_wt, shape, CHUNKS)
    scratch += [pltpu.VMEM(shape, F32)] if rounded else []
    scratch += RowGather.scratch(n_wt, CHUNKS) if spread else []
    if ride == "gather":
        scratch += CtxGather.scratch(n_ctx)
    elif ride:
        scratch += CtxSum.scratch(n_ctx, rider)
    return scratch


def exchange_kernel(n_ctx, n_wt, back, spread, rounded, ride, ready, *refs):
    refs = list(refs)
    near = Near(n_wt)
    peers = [(near.section, lax.rem(near.ctx + k, n_ctx), near.wt) for k in range(1, n_ctx)]
    parts, rows_ref = refs.pop(0), refs.pop(0)
    stream_ref = refs.pop(0) if back else None
    gain_ref = refs.pop(0) if (back or spread) else None
    ride_ref = refs.pop(0) if ride else None
    result_ref = refs.pop(0)
    gain_grad_ref = refs.pop(0) if back else None
    all_ref = refs.pop(0) if spread else None
    rode_ref = refs.pop(0) if ride else None
    token_ref = refs.pop(0)
    token_ref[...] = jnp.zeros(token_ref.shape, F32)
    near.greet(peers if ride else ())
    if ready:
        ready()
    exchange_steps(
        near,
        n_ctx,
        parts,
        rows_ref,
        stream_ref,
        gain_ref,
        result_ref,
        gain_grad_ref,
        all_ref,
        spread,
        rounded,
        refs,
        ride,
        (ride_ref, rode_ref),
    )


VMEM = pl.BlockSpec(memory_space=pltpu.VMEM)


def exchange(number, parts, rows, stream=None, gain=None, spread=None, rounded=False, gather=None, add=None, load=False):
    n_ctx, n_wt = lax.axis_size("ctx"), lax.axis_size("wt")
    shape = rows.shape
    back = stream is not None
    ride = "gather" if gather is not None else "sum" if add is not None else None
    rider = add if gather is None else gather
    wanted = ((parts, True), (rows, True), (stream, back), (gain, back or spread), (rider, ride))
    operands = [member for member, taken in wanted if taken]
    outs = [jax.ShapeDtypeStruct(shape, BF16 if rounded else F32)]
    if back:
        outs.append(jax.ShapeDtypeStruct((1, shape[1]), F32))
    if spread:
        outs.append(jax.ShapeDtypeStruct((2 * n_wt,) + shape, BF16))
    if ride == "gather":
        outs.append(jax.ShapeDtypeStruct((n_ctx,) + gather.shape, BF16))
    elif ride == "sum":
        outs.append(jax.ShapeDtypeStruct(add.shape[1:], F32))
    outs.append(jax.ShapeDtypeStruct((8, LANES), F32))
    kernel = functools.partial(exchange_kernel, n_ctx, n_wt, back, spread, rounded, ride)
    call = dict(
        out_shape=outs,
        out_specs=[VMEM] * len(outs),
        scratch_shapes=exchange_scratch(n_ctx, n_wt, shape, spread, rounded, ride, rider.shape if ride else None),
        compiler_params=pltpu.CompilerParams(
            collective_id=number, has_side_effects=True, vmem_limit_bytes=(60 if load else 16) << 20
        ),
        cost_estimate=pl.CostEstimate(flops=0, bytes_accessed=110 << 20, transcendentals=0),
    )
    if load:
        return loaded(kernel, operands, [], **call)
    return pl.pallas_call(functools.partial(kernel, None), in_specs=[VMEM] * len(operands), **call)(*operands)


def finish_kernel(n_ctx, n_wt, *refs):
    small, attn, rows = refs[:6], refs[6:8], refs[8:12]
    gain_ref, router_ref, query_ref, pair_ref, out_ref, rows_ref, grads_ref = refs[12:19]
    parts, landed, summed, from_sibling, received, send, recv, swap_send, swap_recv = refs[19:]
    section, ctx, wt = place()
    count = n_ctx * n_wt
    own = ctx * n_wt + wt
    blocks = [lax.rem(own + k, count) for k in range(1, count)]
    peers = [(section, block // n_wt, lax.rem(block, n_wt)) for block in blocks]
    sibling = (1 - section, ctx, wt)
    greet([sibling] + peers)
    members = [(attn[0], attn[1], received)]
    members += [(rows[0], rows[1], rows_ref.at[section]), (rows[2], rows[3], grads_ref.at[section])]
    swaps = [
        [remote(member[1 - layer], member[2], swap_send.at[k], swap_recv.at[k], sibling) for k, member in enumerate(members)]
        for layer in range(2)
    ]
    for layer in range(2):

        @pl.when(section == layer)
        def _():
            for copy in swaps[layer]:
                copy.start()

    piece = small[0].shape[1] // count
    parts[...] = jnp.zeros(parts.shape, F32)
    for block in range(count):
        for layer in range(2):
            at = 0
            for ref in small[3 * layer : 3 * layer + 3]:
                end = at + ref.shape[0]
                parts[block, layer, at:end, :piece] = ref[:, block * piece : (block + 1) * piece]
                at = end
    copies = [
        remote(parts.at[blocks[k]], landed.at[k], send.at[k], recv.at[k], peers[k]) for k in range(count - 1)
    ]
    for copy in copies:
        copy.start()
    mine = section == 0
    rows_ref[section] = jnp.where(mine, rows[0][...], rows[1][...])
    grads_ref[section] = jnp.where(mine, rows[2][...], rows[3][...])
    for copy in swaps[0]:
        copy.wait_recv()
    held = jnp.where(mine, attn[0][...], attn[1][...])
    came = received[...]
    first, second = jnp.where(mine, held, came), jnp.where(mine, came, held)
    q_cols = query_ref.shape[1] // 2
    at = q_cols + LANES
    query_ref[...] = jnp.concatenate([first[:, :q_cols], second[:, :q_cols]], 1)
    pair_ref[...] = jnp.concatenate([first[:, q_cols:at], second[:, q_cols:at]], 1)
    out_ref[...] = jnp.transpose(jnp.concatenate([first[:, at:], second[:, at:]], 1))
    total = parts[own]
    for k, copy in enumerate(copies):
        copy.wait_recv()
        total = total + landed[k]
    summed[...] = total
    swap = remote(summed.at[1 - section], from_sibling, send.at[count - 1], recv.at[count - 1], sibling)
    swap.start()
    swap.wait()
    total = summed[section] + from_sibling[...]
    named = small[0].shape[0]
    gain_ref[...] = total[named : named + 2, :]
    router_ref[...] = total[:named, :]
    for copy in copies:
        copy.wait_send()
    for copy in swaps[0]:
        copy.wait_send()


def finish(number, small, attn, rows, q_cols):
    n_ctx, n_wt = lax.axis_size("ctx"), lax.axis_size("wt")
    count = n_ctx * n_wt
    named = small[0].shape[0]
    shape = (2, named + 2 + -(named + 2) % 8, LANES)
    dma = pltpu.SemaphoreType.DMA
    depth = attn[0].shape[0]
    pair = jax.ShapeDtypeStruct((2,) + rows[0].shape, BF16)
    return pl.pallas_call(
        functools.partial(finish_kernel, n_ctx, n_wt),
        out_shape=[
            jax.ShapeDtypeStruct((2, LANES), F32),
            jax.ShapeDtypeStruct((named, LANES), F32),
            jax.ShapeDtypeStruct((depth, 2 * q_cols), F32),
            jax.ShapeDtypeStruct((depth, 2 * LANES), F32),
            jax.ShapeDtypeStruct((2 * q_cols, depth), F32),
            pair,
            pair,
        ],
        in_specs=[VMEM] * 12,
        out_specs=[VMEM] * 7,
        scratch_shapes=[
            pltpu.VMEM((count,) + shape, F32),
            pltpu.VMEM((count - 1,) + shape, F32),
            pltpu.VMEM(shape, F32),
            pltpu.VMEM(shape[1:], F32),
            pltpu.VMEM(attn[0].shape, F32),
            dma((count,)),
            dma((count,)),
            dma((3,)),
            dma((3,)),
        ],
        compiler_params=pltpu.CompilerParams(
            collective_id=number, has_side_effects=True, vmem_limit_bytes=16 << 20
        ),
        cost_estimate=pl.CostEstimate(flops=0, bytes_accessed=40 << 20, transcendentals=0),
    )(*small, *attn, *rows)


def hand_over_kernel(per_core, first, second, after, inward, down, held, send, recv, load, keep):
    section, ctx, wt = place()
    sibling = (1 - section, ctx, wt)
    for layer, own in enumerate((first, second)):

        @pl.when(section == layer)
        def _():
            pltpu.make_async_copy(own, held, load).start()

    def moves(source):
        pieces = expert_halves(inward, down, source, section, per_core)
        return [remote(piece, target, send.at[k], recv.at[k], sibling) for k, (target, piece) in enumerate(pieces)]

    greet([sibling])
    for layer, other in enumerate((second, first)):

        @pl.when(section == layer)
        def _():
            for copy in moves(other):
                copy.start()

    pltpu.make_async_copy(first, held, load).wait()
    pieces = expert_halves(inward, down, held, section, per_core)
    copies = [pltpu.make_async_copy(piece, target, keep.at[k]) for k, (target, piece) in enumerate(pieces)]
    for copy in copies:
        copy.start()
    for copy in copies:
        copy.wait()
    for copy in moves(first):
        copy.wait()


def hand_over(number, first, second, after, depth, down_rows, per_core, width):
    any_place = pl.BlockSpec(memory_space=pl.ANY)
    dma = pltpu.SemaphoreType.DMA
    return pl.pallas_call(
        functools.partial(hand_over_kernel, per_core),
        out_shape=[
            jax.ShapeDtypeStruct((2 * per_core, depth, first.shape[1] // per_core), first.dtype),
            jax.ShapeDtypeStruct((2 * per_core, down_rows, width), first.dtype),
        ],
        in_specs=[any_place] * 3,
        out_specs=[any_place] * 2,
        scratch_shapes=[pltpu.VMEM(first.shape, first.dtype), dma((6,)), dma((6,)), dma, dma((6,))],
        compiler_params=pltpu.CompilerParams(
            collective_id=number, has_side_effects=True, vmem_limit_bytes=60 << 20
        ),
    )(first, second, after)


HEADS = 3


def roll(values, by):
    return pltpu.roll(values, by, 1)


def lower_half(shape):
    return lax.broadcasted_iota(jnp.int32, shape, 1) < HEAD_SIZE


def turned(values, cosine, sine):
    first = lax.rem(lax.broadcasted_iota(jnp.int32, values.shape, 1), HEAD_SIZE) < HEAD_SIZE // 2
    half = HEAD_SIZE // 2
    return values * cosine + jnp.where(first, roll(values, LANES - half), roll(values, half)) * sine


def visible(key_place, query_place, query_start):
    return (key_place <= query_place) & (key_place >= query_start)


def attend_kernel(
    n_ctx,
    n_wt,
    ride,
    x_ref,
    w_ref,
    cos_ref,
    sin_ref,
    key_place,
    query_place,
    query_start,
    *refs,
):
    refs = list(refs)
    ride_ref = refs.pop(0) if ride else None
    part_ref, q_ref, pairs_ref, out_ref, lse_ref, att_ref = [refs.pop(0) for _ in range(6)]
    all_ref = refs.pop(0) if ride else None
    top_ref, sum_ref, acc_ref, send, recv = refs[:5]
    near = Near(n_wt)
    section, ctx, wt = near.section, near.ctx, near.wt
    peers = [(section, lax.rem(ctx + k, n_ctx), wt) for k in range(1, n_ctx)]
    waiting = []
    if ride:
        gathers = RowGather(near, 1, all_ref, refs[5:])
        waiting = [functools.partial(gathers.hop, 0, hop) for hop in range(1, n_wt)]
        all_ref[near.own] = ride_ref[...]
        near.greet(peers)
        gathers.first(0)
    else:
        greet(peers)

    def ride_on():
        if waiting:
            waiting.pop(0)()

    rows = x_ref.shape[0] // 2
    low = lower_half((2 * rows, LANES))
    mixed = dot(x_ref[...], w_ref[:, : 3 * LANES], ((1,), (0,)))
    cosine, sine = cos_ref[...], sin_ref[...]
    first = turned(mixed[:, :LANES], cosine, sine)
    second = turned(mixed[:, LANES : 2 * LANES], cosine, sine)
    pairs_ref[ctx] = jnp.where(low, roll(second, HEAD_SIZE), roll(mixed[:, 2 * LANES :], HEAD_SIZE)).astype(BF16)

    def passing(k):
        return remote(
            pairs_ref.at[ctx], pairs_ref.at[ctx], send.at[k], recv.at[k], (section, lax.rem(ctx + k, n_ctx), wt)
        )

    for k in range(1, n_ctx):
        passing(k).start()
    for h, part in enumerate((first, roll(first, HEAD_SIZE), second)):
        scaled = jnp.where(low, part * (1.0 / HEAD_SIZE), 0.0).astype(BF16)
        q_ref[0, h] = scaled[:rows]
        q_ref[1, h] = scaled[rows:]
    top_ref[...] = jnp.full(top_ref.shape, MASKED, F32)
    sum_ref[...] = jnp.zeros(sum_ref.shape, F32)
    acc_ref[...] = jnp.zeros(acc_ref.shape, F32)

    def block(c, m, j):
        keys = pairs_ref[c, j * rows : (j + 1) * rows, :]
        if m == j:
            seen = visible(key_place[c, j * rows : (j + 1) * rows, :], query_place[m], query_start[m])
        for h in range(HEADS):
            logits = dot(keys, q_ref[m, h], ((1,), (1,)))
            if m == j:
                logits = jnp.where(seen, logits, MASKED)
            before = top_ref[m, h]
            top = jnp.maximum(before, jnp.max(logits, 0, keepdims=True))
            expos = jnp.exp(logits - top)
            shrink = jnp.exp(before - top)
            top_ref[m, h] = top
            sum_ref[m, h] = sum_ref[m, h] * shrink + jnp.sum(expos, 0, keepdims=True)
            acc_ref[m, h] = acc_ref[m, h] * shrink + dot(keys, expos.astype(BF16), ((0,), (0,)))

    def blocks_of(c):
        block(c, 0, 0)
        block(c, 1, 1)
        block(c, 1, 0)

    blocks_of(ctx)
    ride_on()

    def arrived(k):
        passing(k).wait_recv()
        blocks_of(lax.rem(ctx + n_ctx - k, n_ctx))

    arrived(1)
    arrived(2)
    ride_on()
    pl.loop(3, n_ctx)(arrived)
    while waiting:
        ride_on()
    low = lower_half((rows, LANES))
    for m in range(2):
        outs = []
        for h in range(HEADS):
            lse_ref[m, h] = top_ref[m, h] + jnp.log(sum_ref[m, h])
            outs.append(jnp.transpose(acc_ref[m, h] / sum_ref[m, h]))
            out_ref[m, h] = outs[h]
        att_ref[m * rows : (m + 1) * rows, :LANES] = jnp.where(low, 0.0, outs[0]).astype(BF16)
        att_ref[m * rows : (m + 1) * rows, LANES:] = jnp.where(low, roll(outs[1], HEAD_SIZE), outs[2]).astype(BF16)
    part_ref[...] = dot(att_ref[...], w_ref[:, 2 * LANES :], ((1,), (1,))).astype(BF16)
    if ride:
        gathers.arrive()
        gathers.end()
    for k in range(1, n_ctx):
        passing(k).wait_send()


def attend(number, rows_in, weights, tables, ride=None):
    n_ctx, n_wt = lax.axis_size("ctx"), lax.axis_size("wt")
    riders = [] if ride is None else [ride]
    n_rows, width = rows_in.shape
    rows = n_rows // 2
    dma = pltpu.SemaphoreType.DMA
    return pl.pallas_call(
        functools.partial(attend_kernel, n_ctx, n_wt, bool(riders)),
        out_shape=[
            jax.ShapeDtypeStruct((n_rows, width), BF16),
            jax.ShapeDtypeStruct((2, HEADS, rows, LANES), BF16),
            jax.ShapeDtypeStruct((n_ctx, n_rows, LANES), BF16),
            jax.ShapeDtypeStruct((2, HEADS, rows, LANES), F32),
            jax.ShapeDtypeStruct((2, HEADS, 1, rows), F32),
            jax.ShapeDtypeStruct((n_rows, 2 * LANES), BF16),
        ]
        + [jax.ShapeDtypeStruct((2 * n_wt,) + member.shape, BF16) for member in riders],
        in_specs=[VMEM] * (7 + len(riders)),
        out_specs=[VMEM] * (6 + len(riders)),
        scratch_shapes=[
            pltpu.VMEM((2, HEADS, 1, rows), F32),
            pltpu.VMEM((2, HEADS, 1, rows), F32),
            pltpu.VMEM((2, HEADS, LANES, rows), F32),
            dma((n_ctx,)),
            dma((n_ctx,)),
        ]
        + (RowGather.scratch(n_wt, 1) if riders else []),
        compiler_params=pltpu.CompilerParams(
            collective_id=number, has_side_effects=True, vmem_limit_bytes=20 << 20
        ),
        cost_estimate=pl.CostEstimate(flops=0, bytes_accessed=70 << 20, transcendentals=0),
    )(rows_in, weights, *tables, *riders)


def attend_back_kernel(
    n_ctx,
    n_wt,
    ride,
    ready,
    a_ref,
    w_ref,
    cos_ref,
    sin_ref,
    key_place,
    query_place,
    query_start,
    q_ref,
    pairs_ref,
    out_ref,
    lse_ref,
    *refs,
):
    refs = list(refs)
    if ride:
        rows_ref, stream_ref, gain_ref = [refs.pop(0) for _ in range(3)]
        ride_refs = [refs.pop(0), refs.pop(0)]
        raw_ref, result_ref, gain_grad_ref, all_ref, rode_ref = [refs.pop(0) for _ in range(5)]
    else:
        raw_ref, part_ref = refs.pop(0), refs.pop(0)
    do_ref, delta_ref, dq_ref, dkv_ref, own_ref, landed, send, recv = refs[:8]
    refs = refs[8:]
    near = Near(n_wt)
    section, ctx, wt = near.section, near.ctx, near.wt
    peers = [(section, lax.rem(ctx + k, n_ctx), wt) for k in range(1, n_ctx)]
    waiting = []
    if ride:
        near.greet(peers)
    else:
        greet(peers)
    if ready:
        ready()
    if ride:
        part_ref = refs.pop(0)
        sums = RowSum(near, 1, ride_refs[0], refs[:9])
        rode_sum = refs[9]
        refs = refs[10:]
        waiting = [functools.partial(sums.point, 0, number) for number in range(n_wt - 1)]
        sums.begin()

    def ride_on():
        if waiting:
            waiting.pop(0)()

    rows = a_ref.shape[0] // 2
    low = lower_half((2 * rows, LANES))
    d_att = dot(a_ref[...], w_ref[:, 2 * LANES :], ((1,), (0,)))
    for h, part in enumerate((d_att[:, :LANES], roll(d_att[:, LANES:], HEAD_SIZE), d_att[:, LANES:])):
        d_out = jnp.where(low, 0.0, part).astype(BF16)
        for m in range(2):
            do_ref[m, h] = d_out[m * rows : (m + 1) * rows]
            product = do_ref[m, h].astype(F32) * out_ref[m, h]
            delta_ref[m, h] = jnp.sum(jnp.transpose(product), 0, keepdims=True)
    dq_ref[...] = jnp.zeros(dq_ref.shape, F32)
    ride_on()

    def block(c, j):
        keys = pairs_ref[c, j * rows : (j + 1) * rows, :]
        total = jnp.zeros((rows, LANES), F32)
        for m in range(j, 2):
            if m == j:
                seen = visible(key_place[c, j * rows : (j + 1) * rows, :], query_place[m], query_start[m])
            for h in range(HEADS):
                probs = jnp.exp(dot(keys, q_ref[m, h], ((1,), (1,))) - lse_ref[m, h])
                if m == j:
                    probs = jnp.where(seen, probs, 0.0)
                d_probs = dot(keys, do_ref[m, h], ((1,), (1,)))
                d_scores = (probs * (d_probs - delta_ref[m, h])).astype(BF16)
                total = total + dot(d_scores, q_ref[m, h], ((1,), (0,)))
                total = total + dot(probs.astype(BF16), do_ref[m, h], ((1,), (0,)))
                dq_ref[m, h] += dot(keys, d_scores, ((0,), (0,)))
        return total

    def passing(k):
        target = lax.rem(ctx + k, n_ctx)
        return remote(dkv_ref.at[target], landed.at[k - 1], send.at[k], recv.at[k], (section, target, wt))

    def sent(k):
        c = lax.rem(ctx + k, n_ctx)
        for j in range(2):
            dkv_ref[c, j * rows : (j + 1) * rows, :] = block(c, j).astype(BF16)
        passing(k).start()

    sent(1)
    sent(2)
    ride_on()
    pl.loop(3, n_ctx)(sent)

    for j in range(2):
        own_ref[j * rows : (j + 1) * rows, :] = block(ctx, j)

    while waiting:
        ride_on()

    @pl.loop(1, n_ctx)
    def _(k):
        passing(k).wait_recv()
        own_ref[...] += landed[k - 1].astype(F32)

    cosine, sine = cos_ref[...], sin_ref[...]
    d_own = own_ref[...]
    over = roll(d_own, HEAD_SIZE)
    d_query = [
        jnp.concatenate([jnp.transpose(dq_ref[m, h]) for m in range(2)], 0) * (1.0 / HEAD_SIZE) for h in range(HEADS)
    ]
    first = jnp.where(low, d_query[0], roll(d_query[1], HEAD_SIZE))
    second = jnp.where(low, d_query[2], over)
    raw_ref[:, :LANES] = turned(first, cosine, -sine).astype(BF16)
    raw_ref[:, LANES : 2 * LANES] = turned(second, cosine, -sine).astype(BF16)
    raw_ref[:, 2 * LANES :] = jnp.where(low, over, 0.0).astype(BF16)
    partial = dot(raw_ref[...], w_ref[:, : 3 * LANES], ((1,), (1,))).astype(BF16)
    part_ref[...] = partial.reshape(part_ref.shape)
    if ride:
        sums.collect(0, rode_sum)
        rode_ref[...] = (rode_sum[...] + ride_refs[1][...]).astype(BF16)

    if ride:
        exchange_steps(
            near,
            n_ctx,
            part_ref,
            rows_ref,
            stream_ref,
            gain_ref,
            result_ref,
            gain_grad_ref,
            all_ref,
            "plain",
            True,
            refs,
        )
    if ride:
        sums.end()
    for k in range(1, n_ctx):
        passing(k).wait_send()


def attend_back(number, rows_a, weights, tables, kept, then=()):
    n_ctx, n_wt = lax.axis_size("ctx"), lax.axis_size("wt")
    n_rows, width = rows_a.shape
    half = n_rows // 2
    share = n_rows // (2 * n_wt)
    dma = pltpu.SemaphoreType.DMA
    shape = (share, width)
    blocks = jax.ShapeDtypeStruct((2 * n_wt,) + shape, BF16)
    outs = [jax.ShapeDtypeStruct((n_rows, 3 * LANES), BF16)]
    scratch = [
        pltpu.VMEM((2, HEADS, half, LANES), BF16),
        pltpu.VMEM((2, HEADS, 1, half), F32),
        pltpu.VMEM((2, HEADS, LANES, half), F32),
        pltpu.VMEM((n_ctx, n_rows, LANES), BF16),
        pltpu.VMEM((n_rows, LANES), F32),
        pltpu.VMEM((n_ctx - 1, n_rows, LANES), BF16),
        dma((n_ctx,)),
        dma((n_ctx,)),
    ]
    if then:
        row = jax.ShapeDtypeStruct(shape, BF16)
        outs += [row, jax.ShapeDtypeStruct((1, width), F32), blocks, row]
        scratch += [pltpu.VMEM(blocks.shape, BF16)] + RowSum.scratch(n_wt, shape, 1) + [pltpu.VMEM(shape, F32)]
        scratch += exchange_scratch(n_ctx, n_wt, shape, "plain", True)
    else:
        outs.append(blocks)
    operands = [rows_a, weights, *tables, *kept, *then]
    kernel = functools.partial(attend_back_kernel, n_ctx, n_wt, bool(then))
    call = dict(
        out_shape=outs,
        out_specs=[VMEM] * len(outs),
        scratch_shapes=scratch,
        compiler_params=pltpu.CompilerParams(
            collective_id=number, has_side_effects=True, vmem_limit_bytes=(60 if then else 24) << 20
        ),
        cost_estimate=pl.CostEstimate(flops=0, bytes_accessed=(200 if then else 100) << 20, transcendentals=0),
    )
    if then:
        return loaded(kernel, operands, [], **call)
    return pl.pallas_call(functools.partial(kernel, None), in_specs=[VMEM] * len(operands), **call)(*operands)


def expert_halves(inward, down, packed, half, per_core):
    depth, down_rows = inward.shape[1], down.shape[1]
    wide, width = packed.shape[1], down.shape[2]
    column, second = inward.shape[2], depth + down_rows
    first, middle = wide - width, down_rows // 2
    a, b = half * per_core, half * per_core + 1
    return [
        (inward.at[a], packed.at[:depth, :column]),
        (inward.at[b], packed.at[:depth, column:]),
        (down.at[a], packed.at[depth:second, :width]),
        (down.at[b, :, :first], packed.at[depth:second, width:]),
        (down.at[b, :middle, first:], packed.at[second:, : wide // 2]),
        (down.at[b, middle:, first:], packed.at[second:, wide // 2 :]),
    ]


def prepare_kernel(inward, down, first, second, halves, load, send, recv, keep):
    packed = (first, second)
    section, ctx, wt = place()
    sibling = (1 - section, ctx, wt)
    per_core = inward.shape[0] // 2
    loads = []
    for half in range(2):
        for source, target in expert_halves(inward, down, halves.at[half], half, per_core):
            loads.append(pltpu.make_async_copy(source, target, load.at[len(loads)]))
    for copy in loads:
        copy.start()
    greet([sibling])
    for copy in loads:
        copy.wait()
    for layer in range(2):

        @pl.when(section == layer)
        def _():
            move = remote(halves.at[1 - layer], packed[layer], send, recv, sibling)
            move.start()
            own = pltpu.make_async_copy(halves.at[layer], packed[layer], keep)
            own.start()
            own.wait()
            move.wait_send()
            remote(halves.at[layer], packed[1 - layer], send, recv, sibling).wait_recv()


def prepare(number, inward, down):
    depth, down_rows = inward.shape[1], down.shape[1]
    in_place = pl.BlockSpec(memory_space=pltpu.HBM)
    shape = (depth + down_rows + down_rows // 2, inward.shape[0] // 2 * inward.shape[2])
    packed = jax.ShapeDtypeStruct(shape, BF16)
    dma = pltpu.SemaphoreType.DMA
    return pl.pallas_call(
        prepare_kernel,
        out_shape=[packed, packed],
        in_specs=[in_place] * 2,
        out_specs=[in_place] * 2,
        scratch_shapes=[pltpu.VMEM((2,) + shape, BF16), dma((12,)), dma, dma, dma],
        compiler_params=pltpu.CompilerParams(
            collective_id=number, has_side_effects=True, vmem_limit_bytes=60 << 20
        ),
    )(inward, down)


def begin_kernel(n_ctx, n_wt, *refs):
    given = refs[:7]
    all_ref, rode_ref, pack, all_gains, all_router, all_routes = refs[7:13]
    tokens, query, pair, out, gains, router, routes = refs[13:20]
    halves, first_pack, load, send, recv = refs[20:25]
    near = Near(n_wt)
    loads = [
        pltpu.make_async_copy(source.at[near.section] if k == 0 else source, target, load.at[k])
        for k, (source, target) in enumerate(zip(given, refs[13:20]))
    ]
    for copy in loads:
        copy.start()
    section, ctx, wt = near.section, near.ctx, near.wt
    peers = [(section, lax.rem(ctx + k, n_ctx), wt) for k in range(1, n_ctx)]
    blocks = CtxGather(near, n_ctx, first_pack, rode_ref, refs[25:28])
    gathers = RowGather(near, CHUNKS, all_ref, refs[28:])
    near.greet(peers)
    for copy in loads:
        copy.wait()
    named = router.shape[0]
    all_gains[section] = gains[...]
    all_routes[section] = routes[...]
    all_router[section] = jnp.zeros(all_router.shape[1:], BF16)
    all_router[section, :named, :] = router[...]
    shared = [
        remote(ref.at[section], ref.at[section], send.at[k], recv.at[k], near.sibling)
        for k, ref in enumerate((all_gains, all_router, all_routes))
    ]
    for copy in shared:
        copy.start()
    q_cols = query.shape[1] // 2
    outward = jnp.transpose(out[...].astype(F32))
    for half in range(2):
        halves[half] = jnp.concatenate(
            [
                query[:, half * q_cols : (half + 1) * q_cols].astype(F32),
                pair[:, half * LANES : (half + 1) * LANES].astype(F32),
                outward[:, half * q_cols : (half + 1) * q_cols],
            ],
            1,
        ).astype(BF16)
    packs = (first_pack, pack)
    for layer in range(2):

        @pl.when(section == layer)
        def _():
            remote(halves.at[1 - layer], packs[layer], send.at[3], recv.at[3], near.sibling).start()
            packs[layer][...] = halves[layer]

    rows = tokens[...].astype(F32)
    scaled = rows * norm_scale(rows)
    shared[0].wait_recv()
    all_ref[near.own] = (scaled * all_gains[0, 0:1, :]).astype(BF16)
    for chunk in range(CHUNKS):
        gathers.first(chunk)
    for layer in range(2):

        @pl.when(section == layer)
        def _():
            remote(halves.at[layer], packs[1 - layer], send.at[3], recv.at[3], near.sibling).wait_recv()

    blocks.start()
    for hop in range(1, n_wt):
        for chunk in range(CHUNKS):
            gathers.hop(chunk, hop)
    blocks.hand_on()
    gathers.arrive()
    blocks.finish()
    gathers.end()
    shared[0].wait_send()
    for copy in shared[1:]:
        copy.wait()
    remote(halves.at[0], first_pack, send.at[3], recv.at[3], near.sibling).wait_send()


def begin(number, tokens, query, pair, out, gains, router, routes):
    n_ctx, n_wt = lax.axis_size("ctx"), lax.axis_size("wt")
    depth, columns = query.shape[0], query.shape[1] + LANES
    dma = pltpu.SemaphoreType.DMA
    pack = (depth, columns)
    return pl.pallas_call(
        functools.partial(begin_kernel, n_ctx, n_wt),
        out_shape=[
            jax.ShapeDtypeStruct((2 * n_wt,) + tokens.shape[1:], BF16),
            jax.ShapeDtypeStruct((n_ctx,) + pack, BF16),
            jax.ShapeDtypeStruct(pack, BF16),
            jax.ShapeDtypeStruct((2,) + gains.shape, gains.dtype),
            jax.ShapeDtypeStruct((2, LANES, router.shape[1]), BF16),
            jax.ShapeDtypeStruct((2,) + routes.shape, routes.dtype),
        ],
        in_specs=[pl.BlockSpec(memory_space=pltpu.HBM)] * 7,
        out_specs=[VMEM] * 6,
        scratch_shapes=[pltpu.VMEM(tokens.shape[1:], BF16)]
        + [pltpu.VMEM(member.shape, member.dtype) for member in (query, pair, out, gains, router, routes)]
        + [
            pltpu.VMEM((2,) + pack, BF16),
            pltpu.VMEM(pack, BF16),
            dma((7,)),
            dma((4,)),
            dma((4,)),
        ]
        + CtxGather.scratch(n_ctx)
        + RowGather.scratch(n_wt, CHUNKS),
        compiler_params=pltpu.CompilerParams(
            collective_id=number, has_side_effects=True, vmem_limit_bytes=16 << 20
        ),
        cost_estimate=pl.CostEstimate(flops=0, bytes_accessed=90 << 20, transcendentals=0),
    )(tokens, query, pair, out, gains, router, routes)


TILE = 256


def expert_pieces(packed, inward, down, depth, down_rows):
    n, wide, width = packed.shape[0], packed.shape[2], down.shape[2]
    half = down_rows // 2
    first = wide - width
    pairs = []
    for c in range(n):
        at = c * down_rows
        second = depth + down_rows
        pairs += [
            (packed.at[c, depth:second, :width], down.at[0, at : at + down_rows, :]),
            (packed.at[c, depth:second, width:], down.at[1, at : at + down_rows, :first]),
            (packed.at[c, second:, : wide // 2], down.at[1, at : at + half, first:]),
            (packed.at[c, second:, wide // 2 :], down.at[1, at + half : at + down_rows, first:]),
        ]
    for c in range(n):
        pairs.append((packed.at[c, :depth, :], inward.at[c * depth : (c + 1) * depth, :]))
    return pairs


def gate_rows(x, router, routes):
    lane = lax.broadcasted_iota(jnp.int32, (x.shape[0], LANES), 1)
    named = routes[:, 0:1] == lane
    for t in range(1, routes.shape[1]):
        named = named | (routes[:, t : t + 1] == lane)
    logits = jnp.where(named, dot(x, router, ((1,), (1,))), MASKED)
    expos = jnp.where(named, jnp.exp(logits - jnp.max(logits, 1, keepdims=True)), 0.0)
    return expos / jnp.sum(expos, 1, keepdims=True)


def experts_kernel(n_ctx, layer, forward, backward, depth, down_rows, ride, ready, *refs):
    refs = list(refs)
    x_ref, router_ref, pick_ref = [refs.pop(0) for _ in range(3)]
    if forward:
        hit_ref = refs.pop(0)
    else:
        gates_ref, gate_up_ref = refs.pop(0), refs.pop(0)
    d_ref = refs.pop(0) if backward else None
    ride_ref = refs.pop(0) if ride else None
    packed_ref = refs.pop(0)
    part_ref = refs.pop(0) if forward else None
    if forward and not backward:
        gates_ref, gate_up_ref = refs.pop(0), refs.pop(0)
    if backward:
        back_out, grads_ref, router_grad_ref = [refs.pop(0) for _ in range(3)]
    rode_ref = refs.pop(0) if ride else None
    inward, down, weighted, load = [refs.pop(0) for _ in range(4)]
    if forward and backward:
        gates_ref, gate_up_ref = refs.pop(0), refs.pop(0)
    if backward:
        d_gate_up, x_turned, in_grad, down_grad, store, back_ref, leave = refs[:7]
        refs = refs[7:]
        if forward:
            part_out, part_ref = part_ref, refs.pop(0)
            part_leave = pltpu.make_async_copy(part_ref, part_out, leave.at[1])
        back_leave = pltpu.make_async_copy(back_ref, back_out, leave.at[0])

    pieces = expert_pieces(packed_ref, inward, down, depth, down_rows)
    loads = [pltpu.make_async_copy(source, target, load.at[k]) for k, (source, target) in enumerate(pieces)]
    n_down = 4 * packed_ref.shape[0]
    for copy in (loads[n_down:] + loads[:n_down]) if forward else loads:
        copy.start()
    if ride:
        near = Near(1)
        greet([(near.section, lax.rem(near.ctx + k, n_ctx), near.wt) for k in range(1, n_ctx)])
        blocks = CtxSum(near, n_ctx, ride_ref, refs)
        blocks.start()
    if ready:
        ready()
    columns = [slice(t * TILE, (t + 1) * TILE) for t in range(2 * FF // TILE)]
    per_expert = FF // TILE
    width = x_ref.shape[1]

    def gate_at(t):
        return slice(2 * FF * (t // per_expert) + TILE * (t % per_expert), 2 * FF * (t // per_expert) + TILE * (t % per_expert + 1))

    def up_at(t):
        return slice(gate_at(t).start + FF, gate_at(t).stop + FF)

    def weight_of(e):
        return jnp.sum(gates_ref[...] * pick_ref[e : e + 1, :], 1, keepdims=True)

    if forward:
        routes = hit_ref[layer]
        routes = routes.reshape(routes.shape[0] * routes.shape[1], routes.shape[2])
        gates_ref[...] = gate_rows(x_ref[...], router_ref[layer], routes)
        for copy in loads[n_down:]:
            copy.wait()
        for t, place_of in enumerate(columns):
            gate = dot(x_ref[...], inward[:, gate_at(t)], ((1,), (0,)))
            up = dot(x_ref[...], inward[:, up_at(t)], ((1,), (0,)))
            gate_up_ref[:, gate_at(t)] = gate.astype(BF16)
            gate_up_ref[:, up_at(t)] = up.astype(BF16)
            weighted[:, place_of] = (gate / (1.0 + jnp.exp(-gate)) * up * weight_of(t // per_expert)).astype(BF16)
        for copy in loads[:n_down]:
            copy.wait()
        for n in range(width // TILE):
            at = slice(n * TILE, (n + 1) * TILE)
            part_ref[:, at] = (
                dot(weighted[:, :FF], down[0, :, at], ((1,), (0,)))
                + dot(weighted[:, FF:], down[1, :, at], ((1,), (0,)))
            ).astype(BF16)
        if backward:
            part_leave.start()
    else:
        for copy in loads[:n_down]:
            copy.wait()
    if backward:
        d_weight = [0.0, 0.0]
        for t, place_of in enumerate(columns):
            e = t // per_expert
            rows_of = slice(TILE * (t % per_expert), TILE * (t % per_expert + 1))
            weight = weight_of(e)
            d_weighted = dot(d_ref[...], down[e, rows_of, :], ((1,), (1,)))
            gate = gate_up_ref[:, gate_at(t)].astype(F32)
            up = gate_up_ref[:, up_at(t)].astype(F32)
            sigmoid = 1.0 / (1.0 + jnp.exp(-gate))
            activated = gate * sigmoid
            hidden = activated * up
            d_weight[e] = d_weight[e] + jnp.sum(hidden * d_weighted, 1, keepdims=True)
            weighted[:, place_of] = (hidden * weight).astype(BF16)
            d_hidden = d_weighted * weight
            d_gate_up[:, gate_at(t)] = (d_hidden * up * (sigmoid * (1.0 + gate * (1.0 - sigmoid)))).astype(BF16)
            d_gate_up[:, up_at(t)] = (d_hidden * activated).astype(BF16)
        if ride:
            blocks.hand_on()
        gates = gates_ref[...]
        terms = gates * (pick_ref[0:1, :] * d_weight[0] + pick_ref[1:2, :] * d_weight[1])
        d_logits = terms - gates * jnp.sum(terms, 1, keepdims=True)
        high = d_logits.astype(BF16)
        low = (d_logits - high.astype(F32)).astype(BF16)
        both = jnp.concatenate([high, low], 1)
        if not forward:
            for copy in loads[n_down:]:
                copy.wait()
        for n in range(width // TILE):
            at = slice(n * TILE, (n + 1) * TILE)
            table = router_ref[layer, :, at]
            back_ref[:, at] = (
                dot(d_gate_up[...], inward[at, :], ((1,), (1,)))
                + dot(both, jnp.concatenate([table, table], 0), ((1,), (0,)))
            ).astype(BF16)
        back_leave.start()
        x_turned[...] = jnp.transpose(x_ref[...])
        router_grad = dot(both, x_ref[...], ((0,), (0,)))
        named = router_grad_ref.shape[0]
        router_grad_ref[...] = router_grad[:named] + router_grad[LANES : LANES + named]
        pieces = expert_pieces(grads_ref, in_grad, down_grad, depth, down_rows)
        stores = [
            pltpu.make_async_copy(source, target, store.at[k]) for k, (target, source) in enumerate(pieces)
        ]
        for e in range(2):
            turned_hidden = jnp.transpose(weighted[:, e * FF : (e + 1) * FF])
            for n in range(width // TILE):
                at = slice(n * TILE, (n + 1) * TILE)
                down_grad[e, :, at] = dot(turned_hidden, d_ref[:, at], ((1,), (0,))).astype(BF16)
        for copy in stores[:n_down]:
            copy.start()
        for c in range(n_ctx):
            at = slice(c * depth, (c + 1) * depth)
            for n in range(2):
                wide = slice(n * 2 * FF, (n + 1) * 2 * FF)
                in_grad[at, wide] = dot(x_turned[at, :], d_gate_up[:, wide], ((1,), (0,))).astype(BF16)
            stores[n_down + c].start()
        for copy in stores:
            copy.wait()
        back_leave.wait()
        if forward:
            part_leave.wait()
    if ride:
        blocks.finish(rode_ref)


def experts(
    layer, x, packed, router, pick, n_experts, depth, down_rows, hit=None, kept=None, d_rows=None, number=None, add=None
):
    n_ctx = lax.axis_size("ctx")
    forward, backward = hit is not None, d_rows is not None
    n_rows, width = x.shape
    any_place = pl.BlockSpec(memory_space=pl.ANY)
    operands = [x, router, pick]
    operands += [hit] if forward else list(kept)
    operands += [d_rows] if backward else []
    operands += [add] if add is not None else []
    rows_out = jax.ShapeDtypeStruct((n_rows, width), BF16)
    inner = [jax.ShapeDtypeStruct((n_rows, LANES), F32), jax.ShapeDtypeStruct((n_rows, 4 * FF), BF16)]
    n_pieces = 5 * packed.shape[0]
    scratch = [
        pltpu.VMEM((width, 4 * FF), BF16),
        pltpu.VMEM((2, FF, width), BF16),
        pltpu.VMEM((n_rows, 2 * FF), BF16),
        pltpu.SemaphoreType.DMA((n_pieces,)),
    ]
    outs = []
    out_specs = []
    if forward:
        outs += [rows_out]
        out_specs += [any_place if backward else VMEM]
    if forward and not backward:
        outs += inner
        out_specs += [VMEM] * 2
    if backward:
        outs += [rows_out, jax.ShapeDtypeStruct(packed.shape, BF16), jax.ShapeDtypeStruct((n_experts, width), F32)]
        out_specs += [any_place, any_place, VMEM]
        if forward:
            scratch += [pltpu.VMEM(member.shape, member.dtype) for member in inner]
        scratch += [
            pltpu.VMEM((n_rows, 4 * FF), BF16),
            pltpu.VMEM((width, n_rows), BF16),
            pltpu.VMEM((width, 4 * FF), BF16),
            pltpu.VMEM((2, FF, width), BF16),
            pltpu.SemaphoreType.DMA((n_pieces,)),
            pltpu.VMEM((n_rows, width), BF16),
            pltpu.SemaphoreType.DMA((2,)),
        ]
        scratch += [pltpu.VMEM((n_rows, width), BF16)] if forward else []
    params = {}
    if add is not None:
        outs.append(jax.ShapeDtypeStruct(add.shape[1:], F32))
        out_specs.append(VMEM)
        scratch += CtxSum.scratch(n_ctx, add.shape)
        params = dict(collective_id=number, has_side_effects=True)
    work = n_rows * 6 * width * FF * 2 * ((1 if forward else 0) + (2 if backward else 0))
    load = forward and backward
    kernel = functools.partial(experts_kernel, n_ctx, layer, forward, backward, depth, down_rows, add is not None)
    call = dict(
        out_shape=outs,
        out_specs=out_specs,
        scratch_shapes=scratch,
        compiler_params=pltpu.CompilerParams(vmem_limit_bytes=(60 if load else 44 if backward else 28) << 20, **params),
        cost_estimate=pl.CostEstimate(flops=2 * work, bytes_accessed=40 << 20, transcendentals=0),
    )
    if load:
        return loaded(kernel, operands, [packed], **call)
    in_specs = [VMEM] * len(operands) + [any_place]
    return pl.pallas_call(functools.partial(kernel, None), in_specs=in_specs, **call)(*operands, packed)


def shards(tokens, cotangent, blocks, routes, norm_gain, w_query, key_value_weight, w_attn_out, router, w_in, w_down):
    section, ctx, wt = place()
    n_ctx, n_wt, layers = lax.axis_size("ctx"), lax.axis_size("wt"), lax.axis_size("section")
    micro_count, share, width = tokens.shape
    per_ctx = routes.shape[2]
    seq_len = per_ctx * n_ctx
    per_core = w_in.shape[1] // 2
    n_experts = router.shape[2]
    q_cols = w_query.shape[2] // 2
    depth = w_query.shape[1]

    block_len = seq_len // blocks.shape[1]
    placed = (blocks[:, :, None] * block_len + jnp.arange(block_len, dtype=jnp.int32)[None, None, :]).reshape(
        micro_count, seq_len
    )
    query_place = lax.dynamic_slice_in_dim(placed, ctx * per_ctx, per_ctx, 1)
    later = (jnp.arange(micro_count) > 0)[:, None]
    query_start = jnp.where(later, query_place - query_place % CONT_LEN, 0)
    query_pos = jnp.where(later, seq_len + query_place % CONT_LEN, query_place)
    half = HEAD_SIZE // 2
    inverse = jnp.power(ROPE_BASE, -(jnp.arange(LANES, dtype=jnp.int32) % half).astype(F32) * 2.0 / HEAD_SIZE)
    angles = query_pos.reshape(-1).astype(F32)[:, None] * inverse[None, :]
    sign = jnp.where(jnp.arange(LANES) % HEAD_SIZE < half, -1.0, 1.0)
    tables = (
        jnp.cos(angles),
        jnp.sin(angles) * sign[None, :],
        jnp.transpose(placed.reshape(micro_count, n_ctx, per_ctx), (1, 0, 2)).reshape(n_ctx, -1, 1),
        query_place[:, None, :],
        query_start[:, None, :],
    )

    moe_pack = prepare(15, w_in[0], w_down[0])
    normed_in, full, attn_pack, gain_pack, router_pack, route_pack = begin(
        0,
        tokens,
        w_query[0],
        key_value_weight[0].reshape(depth, -1),
        w_attn_out[0],
        norm_gain[0],
        jnp.transpose(router[0]),
        routes[0],
    )

    in_rows, down_rows = w_in.shape[2], w_down.shape[2]

    def gather_experts(pack):
        return lax.all_gather(pack, "ctx", axis=0, tiled=True).reshape((n_ctx,) + pack.shape)

    attn_full = [None, None]

    my_first = wt * 2 * per_core + section * per_core
    n_rows = micro_count * per_ctx

    pick = (jnp.arange(LANES)[None, :] == my_first + jnp.arange(8)[:, None]).astype(F32)
    def full_rows(values):
        return values.reshape(n_rows, width)

    def blocked(values):
        return values.reshape(2 * n_wt, share, width).astype(BF16)

    stream = lax.dynamic_index_in_dim(tokens, section, 0, False)
    top = lax.dynamic_index_in_dim(cotangent, section, 0, False)

    attn_full[0] = full.reshape(-1, full.shape[2])
    moe_full = [gather_experts(member) for member in moe_pack]
    saved = []
    outputs = []
    for layer in range(2):
        rows_in = full_rows(normed_in)
        weights = attn_full[layer]
        if layer == 0:
            partial, *heads, attended, d_mixed = attend(2, rows_in, weights, tables, top)
        else:
            partial, *heads, attended = attend(3, rows_in, weights, tables)
        middle, normed_mid, token = exchange(
            4 + layer, blocked(partial), stream, gain=gain_pack[layer, 1:2], spread="norm"
        )
        token, moe_full[layer] = lax.optimization_barrier((token, moe_full[layer]))
        pick_now = pick + token
        rows_mid = full_rows(normed_mid)
        if layer == 0:
            partial, gates, gate_up = experts(
                0, rows_mid, moe_full[0], router_pack, pick_now, n_experts, in_rows, down_rows, hit=route_pack
            )
            inner = (gates, gate_up)
        else:
            partial, *back_parts = experts(
                1,
                rows_mid,
                moe_full[1],
                router_pack,
                pick_now,
                n_experts,
                in_rows,
                down_rows,
                hit=route_pack,
                d_rows=full_rows(d_mixed),
            )
            inner = None
        saved.append(
            dict(
                stream=stream,
                middle=middle,
                rows_in=rows_in,
                rows_mid=rows_mid,
                heads=heads,
                attended=attended,
                inner=inner,
            )
        )
        if layer == 0:
            stream, normed_in, full, token = exchange(
                6, blocked(partial), middle, gain=gain_pack[1, 0:1], spread="norm", rounded=True, gather=attn_pack
            )
            attn_full[1] = full.reshape(-1, full.shape[2])
            outputs.append(stream)
        else:
            last_rows = (blocked(partial), middle)
    upstream = top
    grads_in = [None, None]
    attn_grads = [None, None]
    moe_grads = [None, None]
    small = [None, None]
    for layer in (1, 0):
        kept = saved[layer]
        if layer == 0:
            back_parts = experts(
                0,
                kept["rows_mid"],
                moe_full[0],
                router_pack,
                pick,
                n_experts,
                in_rows,
                down_rows,
                kept=kept["inner"],
                d_rows=full_rows(d_mixed),
                number=7,
                add=attn_parts,
            )
            *back_parts, attn_grads[1] = back_parts
        partial, packed_grad, router_grad = back_parts
        gain = gain_pack[layer, 1:2]
        if layer == 0:
            gain, moe_grads[1] = lax.optimization_barrier((gain, moe_grads[1]))
        moe_grads[layer] = lax.psum_scatter(packed_grad, "ctx", scatter_dimension=0, tiled=False)
        d_middle, gain_grad_mid, d_attn, token = exchange(
            8 + layer, blocked(partial), upstream, kept["middle"], gain, spread="plain", load=True
        )
        rows_a = full_rows(d_attn)
        weights = attn_full[layer]
        if layer == 1:
            then = (d_middle, kept["stream"], gain_pack[1, 0:1], *last_rows)
            raw, upstream, gain_grad_in, d_mixed, last = attend_back(11, rows_a, weights, tables, kept["heads"], then)
            outputs.append(last)
        else:
            raw, partial = attend_back(10, rows_a, weights, tables, kept["heads"])
        attn_parts = dot(kept["rows_in"], jnp.pad(raw, ((0, 0), (0, LANES))), ((0,), (0,)))
        attn_parts = attn_parts + dot(rows_a, jnp.pad(kept["attended"], ((0, 0), (2 * LANES, 0))), ((0,), (0,)))
        attn_parts = attn_parts.astype(BF16).reshape(n_ctx, depth, -1)
        if layer == 0:
            upstream, gain_grad_in, attn_grads[0], token = exchange(
                1, partial, d_middle, kept["stream"], gain_pack[0, 0:1], rounded=True, add=attn_parts
            )
        grads_in[layer] = upstream
        small[layer] = [router_grad, gain_grad_in, gain_grad_mid]

    gain_total, router_total, grad_query, grad_kv, grad_out, out_pair, grad_pair = finish(
        14, small[0] + small[1], attn_grads, outputs + grads_in, q_cols
    )
    piece = width // (n_ctx * n_wt)
    moe_grads = [member.reshape(member.shape[-2:]) for member in moe_grads]
    grad_in, grad_down = hand_over(13, moe_grads[0], moe_grads[1], gain_total, in_rows, down_rows, per_core, width)
    return (
        out_pair[None],
        grad_pair[None],
        gain_total[None, :, :piece],
        grad_query[None],
        grad_kv.reshape(depth, 2, LANES)[None],
        grad_out[None],
        jnp.transpose(router_total[:, :piece])[None],
        grad_in.astype(F32)[None],
        grad_down.astype(F32)[None],
    )


def solution(mesh):
    return jax.shard_map(
        shards,
        mesh=mesh,
        in_specs=(
            P(None, ("ctx", "wt"), None),
            P(None, ("ctx", "wt"), None),
            P(),
            P("section", None, "ctx", None),
            P("section", None, None),
            P("section", "ctx", "wt"),
            P("section", "ctx", "wt", None),
            P("section", "wt", "ctx"),
            P("section", None, None),
            P("section", "wt", "ctx", None),
            P("section", "wt", "ctx", None),
        ),
        out_specs=(
            P("section", None, ("ctx", "wt"), None),
            P("section", None, ("ctx", "wt"), None),
            P("section", None, ("ctx", "wt")),
            P("section", "ctx", "wt"),
            P("section", "ctx", "wt", None),
            P("section", "wt", "ctx"),
            P("section", ("ctx", "wt"), None),
            P("section", "wt", "ctx", None),
            P("section", "wt", "ctx", None),
        ),
        check_vma=False,
    )
```

```python
import functools

import jax
import jax.numpy as jnp
from jax import lax
from jax.experimental import pallas as pl
from jax.experimental.pallas import tpu as pltpu
from jax.sharding import PartitionSpec as P

HEAD_SIZE = 64
FF = 512
CONT_LEN = 1024
EPSILON = 1e-06
ROPE_BASE = 10000.0
MASKED = -1e30
CHUNKS = 2
LANES = 2 * HEAD_SIZE
MESH = pl.DeviceIdType.MESH
F32 = jnp.float32
BF16 = jnp.bfloat16


def dot(left, right, contract):
    return lax.dot_general(left, right, (contract, ((), ())), preferred_element_type=F32)


def norm_scale(rows):
    return lax.rsqrt(jnp.mean(rows * rows, -1, keepdims=True) + EPSILON)


def place():
    return lax.axis_index("section"), lax.axis_index("ctx"), lax.axis_index("wt")


def greet(targets):
    barrier = pltpu.get_barrier_semaphore()
    for target in targets:
        pl.semaphore_signal(barrier, inc=1, device_id=target, device_id_type=MESH)
    pl.semaphore_wait(barrier, len(targets))


def remote(source, destination, send_sem, recv_sem, target):
    return pltpu.make_async_remote_copy(
        src_ref=source,
        dst_ref=destination,
        send_sem=send_sem,
        recv_sem=recv_sem,
        device_id=target,
        device_id_type=MESH,
    )


def loaded(kernel, operands, whole, **call):
    n = len(operands)

    def body(*refs):
        held, sems = refs[-n - 1 : -1], refs[-1]
        copies = [pltpu.make_async_copy(refs[k], held[k], sems.at[k]) for k in range(n)]
        for copy in copies:
            copy.start()

        def ready():
            for copy in copies:
                copy.wait()

        kernel(ready, *held, *refs[n : -n - 1])

    call["scratch_shapes"] = (
        list(call["scratch_shapes"])
        + [pltpu.VMEM(member.shape, member.dtype) for member in operands]
        + [pltpu.SemaphoreType.DMA((n,))]
    )
    call["in_specs"] = [pl.BlockSpec(memory_space=pl.ANY)] * (n + len(whole))
    return pl.pallas_call(body, **call)(*operands, *whole)


class Near:
    def __init__(self, n_wt):
        self.section, self.ctx, self.wt = place()
        self.n_wt = n_wt
        self.sibling = (1 - self.section, self.ctx, self.wt)
        self.right = (self.section, self.ctx, jnp.minimum(self.wt + 1, n_wt - 1))
        self.left = (self.section, self.ctx, jnp.maximum(self.wt - 1, 0))
        self.has_right, self.has_left = self.wt < n_wt - 1, self.wt > 0
        self.own = self.section * n_wt + self.wt

    def greet(self, others=()):
        barrier = pltpu.get_barrier_semaphore()

        def hail(target):
            pl.semaphore_signal(barrier, inc=1, device_id=target, device_id_type=MESH)

        hail(self.sibling)
        pl.when(self.has_right)(lambda: hail(self.right))
        pl.when(self.has_left)(lambda: hail(self.left))
        for other in others:
            hail(other)
        pl.semaphore_wait(
            barrier, 1 + len(others) + self.has_right.astype(jnp.int32) + self.has_left.astype(jnp.int32)
        )


def rows_of(chunk, rows):
    return slice(chunk * rows, (chunk + 1) * rows)


def block_at(last, block, rightward):
    return last + 1 - block if rightward else block - 1


class RowSum:
    def __init__(self, near, chunks, parts, scratch):
        self.near, self.chunks, self.parts = near, chunks, parts
        self.rows = parts.shape[1] // chunks
        self.from_sibling, self.in_right, self.in_left, self.out_right, self.out_left = scratch[:5]
        self.swap_send, self.swap_recv, self.send, self.recv = scratch[5:]

    @staticmethod
    def scratch(n_wt, shape, chunks):
        dma = pltpu.SemaphoreType.DMA
        return [pltpu.VMEM((n_wt,) + shape, BF16)] * 5 + [dma((chunks * n_wt,))] * 2 + [dma((2 * chunks * n_wt,))] * 2

    def swap(self, chunk, block):
        at = rows_of(chunk, self.rows)
        number = chunk * self.near.n_wt + block
        return remote(
            self.parts.at[(1 - self.near.section) * self.near.n_wt + block, at],
            self.from_sibling.at[block, at],
            self.swap_send.at[number],
            self.swap_recv.at[number],
            self.near.sibling,
        )

    def begin(self):
        n_wt = self.near.n_wt
        order = []
        for step in range(n_wt - 1):
            order += [n_wt - 1 - step, step]
        for chunk in range(self.chunks):
            for block in dict.fromkeys(order):
                self.swap(chunk, block).start()

    def chip_sum(self, chunk, block):
        at = rows_of(chunk, self.rows)
        mine = self.parts[self.near.section * self.near.n_wt + block, at, :]
        return mine.astype(F32) + self.from_sibling[block, at, :].astype(F32)

    def toward(self, chunk, block, rightward):
        at = rows_of(chunk, self.rows)
        number = (2 * chunk + (0 if rightward else 1)) * self.near.n_wt + block
        source, target = (self.out_right, self.in_right) if rightward else (self.out_left, self.in_left)
        return remote(
            source.at[block, at],
            target.at[block, at],
            self.send.at[number],
            self.recv.at[number],
            self.near.right if rightward else self.near.left,
        )

    def send_on(self, chunk, block, rightward):
        at = rows_of(chunk, self.rows)
        self.swap(chunk, block).wait_recv()
        outward, inward = (self.out_right, self.in_right) if rightward else (self.out_left, self.in_left)
        behind = self.near.has_left if rightward else self.near.has_right

        @pl.when(jnp.logical_not(behind))
        def _():
            outward[block, at, :] = self.chip_sum(chunk, block).astype(BF16)

        @pl.when(behind)
        def _():
            self.toward(chunk, block, rightward).wait_recv()
            outward[block, at, :] = (self.chip_sum(chunk, block) + inward[block, at, :].astype(F32)).astype(BF16)

        self.toward(chunk, block, rightward).start()

    def step(self, chunk, step):
        wt, n_wt = self.near.wt, self.near.n_wt
        far, near = n_wt - 1 - step, step
        lower = 2 * wt < n_wt
        pl.when((wt < far) & lower)(lambda: self.send_on(chunk, far, True))
        pl.when(wt > near)(lambda: self.send_on(chunk, near, False))
        pl.when((wt < far) & jnp.logical_not(lower))(lambda: self.send_on(chunk, far, True))

    def point(self, chunk, number):
        wt, last = self.near.wt, self.near.n_wt - 1
        for block in range(1, last + 1):
            turn = last - block
            if number == 0:
                pl.when(wt == 0)(functools.partial(self.send_on, chunk, block_at(last, block, True), True))
                pl.when(wt == last)(functools.partial(self.send_on, chunk, block_at(last, block, False), False))
            elif 1 <= number - turn < block:
                pl.when(wt == number - turn)(functools.partial(self.send_on, chunk, block, True))
                pl.when(wt == last - (number - turn))(functools.partial(self.send_on, chunk, last - block, False))

    def collect(self, chunk, result):
        at, wt = rows_of(chunk, self.rows), self.near.wt
        self.swap(chunk, wt).wait_recv()
        result[at, :] = self.chip_sum(chunk, wt)

        @pl.when(self.near.has_left)
        def _():
            self.toward(chunk, wt, True).wait_recv()
            result[at, :] += self.in_right[wt, at, :].astype(F32)

        @pl.when(self.near.has_right)
        def _():
            self.toward(chunk, wt, False).wait_recv()
            result[at, :] += self.in_left[wt, at, :].astype(F32)

    def end(self):
        wt, n_wt = self.near.wt, self.near.n_wt
        for chunk in range(self.chunks):
            for block in range(n_wt):
                self.swap(chunk, block).wait_send()
                if block > 0:
                    pl.when(wt < block)(self.toward(chunk, block, True).wait_send)
                if block < n_wt - 1:
                    pl.when(wt > block)(self.toward(chunk, block, False).wait_send)


class RowGather:
    def __init__(self, near, chunks, all_ref, scratch):
        self.near, self.chunks, self.all = near, chunks, all_ref
        self.rows = all_ref.shape[1] // chunks
        self.send, self.recv, self.pass_send, self.pass_recv = scratch
        self.sent, self.arrivals = [], []

    @staticmethod
    def scratch(n_wt, chunks):
        return [pltpu.SemaphoreType.DMA((2 * chunks * n_wt,))] * 4

    def along(self, chunk, block, hop, rightward):
        at = rows_of(chunk, self.rows)
        number = (2 * chunk + (0 if rightward else 1)) * self.near.n_wt + hop
        return remote(
            self.all.at[block, at],
            self.all.at[block, at],
            self.send.at[number],
            self.recv.at[number],
            self.near.right if rightward else self.near.left,
        )

    def across(self, chunk, block, number):
        at = rows_of(chunk, self.rows)
        number = 2 * chunk * self.near.n_wt + number
        return remote(
            self.all.at[block, at],
            self.all.at[block, at],
            self.pass_send.at[number],
            self.pass_recv.at[number],
            self.near.sibling,
        )

    def launch(self, condition, copy):
        pl.when(condition)(copy.start)
        self.sent.append((condition, copy))

    def first(self, chunk):
        near = self.near
        always = near.wt >= 0
        self.launch(near.has_right, self.along(chunk, near.own, 1, True))
        self.launch(near.has_left, self.along(chunk, near.own, 1, False))
        self.launch(always, self.across(chunk, near.own, 0))
        self.arrivals.append((always, self.across(chunk, near.own, 0)))

    def hop(self, chunk, hop):
        near, n_wt = self.near, self.near.n_wt
        for rightward, came, more, block, number in (
            (True, near.wt >= hop, near.has_right, jnp.maximum(near.own - hop, 0), hop),
            (False, near.wt + hop < n_wt, near.has_left, jnp.minimum(near.own + hop, 2 * n_wt - 1), n_wt + hop),
        ):
            pl.when(came)(self.along(chunk, block, hop, rightward).wait_recv)
            if hop + 1 < n_wt:
                self.launch(came & more, self.along(chunk, block, hop + 1, rightward))
            self.launch(came, self.across(chunk, block, number))
            self.arrivals.append((came, self.across(chunk, block, number)))

    def arrive(self):
        for condition, copy in self.arrivals:
            pl.when(condition)(copy.wait_recv)

    def end(self):
        for condition, copy in self.sent:
            pl.when(condition)(copy.wait_send)


class CtxGather:
    def __init__(self, near, n_ctx, source, target, sems):
        self.n_ctx, self.source, self.target = n_ctx, source, target
        self.send, self.recv, self.local = sems
        self.ctx = near.ctx
        x, y = lax.rem(near.ctx, 2), near.ctx // 2
        self.at_x, self.at_y = 2 * y + 1 - x, 2 * (1 - y) + x
        self.device = lambda index: (near.section, index, near.wt)
        self.half = source.shape[0] // 2

    @staticmethod
    def scratch(n_ctx):
        dma = pltpu.SemaphoreType.DMA
        return [dma((max(4, n_ctx - 1),)), dma((max(4, n_ctx - 1),)), dma]

    def copy(self, source, target, number, index):
        return remote(source, target, self.send.at[number], self.recv.at[number], self.device(index))

    def near_copies(self):
        if self.n_ctx != 4:
            return [
                self.copy(self.source, self.target.at[self.ctx], k, lax.rem(self.ctx + 1 + k, self.n_ctx))
                for k in range(self.n_ctx - 1)
            ]
        return [
            self.copy(self.source, self.target.at[self.ctx], k, index)
            for k, index in enumerate((self.at_x, self.at_y))
        ]

    def far_copies(self):
        if self.n_ctx != 4:
            return []
        parts = []
        for number, block, at, index in (
            (2, self.at_x, slice(0, self.half), self.at_y),
            (3, self.at_y, slice(self.half, 2 * self.half), self.at_x),
        ):
            ref = self.target.at[block, at]
            parts.append(self.copy(ref, ref, number, index))
        return parts

    def start(self):
        pltpu.make_async_copy(self.source, self.target.at[self.ctx], self.local).start()
        for copy in self.near_copies():
            copy.start()

    def hand_on(self):
        for copy in self.near_copies():
            copy.wait_recv()
        for copy in self.far_copies():
            copy.start()

    def finish(self):
        pltpu.make_async_copy(self.source, self.target.at[self.ctx], self.local).wait()
        for copy in self.far_copies():
            copy.wait()
        for copy in self.near_copies():
            copy.wait_send()


class CtxSum:
    def __init__(self, near, n_ctx, parts, scratch):
        self.n_ctx, self.parts = n_ctx, parts
        *self.buffers, self.send, self.recv = scratch
        self.ctx = near.ctx
        x, y = lax.rem(near.ctx, 2), near.ctx // 2
        self.at_x, self.at_y, self.across = 2 * y + 1 - x, 2 * (1 - y) + x, 2 * (1 - y) + 1 - x
        self.device = lambda index: (near.section, index, near.wt)
        half = parts.shape[1] // 2
        self.halves = (slice(0, half), slice(half, 2 * half))

    @staticmethod
    def scratch(n_ctx, shape):
        dma = pltpu.SemaphoreType.DMA
        rows, columns = shape[1:]
        if n_ctx != 4:
            return [pltpu.VMEM((n_ctx - 1, rows, columns), BF16), dma((n_ctx - 1,)), dma((n_ctx - 1,))]
        return [
            pltpu.VMEM((2, rows // 2, columns), BF16),
            pltpu.VMEM((2, rows, columns), BF16),
            pltpu.VMEM((2, rows, columns), BF16),
            dma((4,)),
            dma((4,)),
        ]

    def copy(self, source, target, number, index):
        return remote(source, target, self.send.at[number], self.recv.at[number], self.device(index))

    def direct(self):
        blocks = [lax.rem(self.ctx + 1 + k, self.n_ctx) for k in range(self.n_ctx - 1)]
        return [self.copy(self.parts.at[block], self.buffers[0].at[k], k, block) for k, block in enumerate(blocks)]

    def far_copies(self):
        return [
            self.copy(self.parts.at[self.across, self.halves[k]], self.buffers[0].at[k], k, index)
            for k, index in enumerate((self.at_x, self.at_y))
        ]

    def near_copies(self):
        far, staged, landed = self.buffers
        return [
            self.copy(staged.at[k], landed.at[k], 2 + k, index) for k, index in enumerate((self.at_x, self.at_y))
        ]

    def start(self):
        for copy in self.far_copies() if self.n_ctx == 4 else self.direct():
            copy.start()

    def hand_on(self):
        if self.n_ctx != 4:
            return
        far, staged, landed = self.buffers
        for k, block in ((1, self.at_y), (0, self.at_x)):
            self.far_copies()[1 - k].wait_recv()
            staged[k] = self.parts[block]
            at = self.halves[1 - k]
            staged[k, at, :] = (self.parts[block, at, :].astype(F32) + far[1 - k].astype(F32)).astype(BF16)
            self.near_copies()[k].start()

    def finish(self, result):
        total = self.parts[self.ctx].astype(F32)
        if self.n_ctx == 4:
            for k, copy in enumerate(self.near_copies()):
                copy.wait_recv()
                total = total + self.buffers[2][k].astype(F32)
        else:
            for k, copy in enumerate(self.direct()):
                copy.wait_recv()
                total = total + self.buffers[0][k].astype(F32)
        result[...] = total
        for copy in self.far_copies() + self.near_copies() if self.n_ctx == 4 else self.direct():
            copy.wait_send()


def exchange_steps(
    near,
    n_ctx,
    parts,
    rows_ref,
    stream_ref,
    gain_ref,
    result_ref,
    gain_grad_ref,
    all_ref,
    spread,
    rounded,
    scratch,
    ride=None,
    ride_refs=None,
):
    n_wt = near.n_wt
    scratch = list(scratch)
    sums = RowSum(near, CHUNKS, parts, scratch[:9])
    scratch = scratch[9:]
    sum_ref = scratch.pop(0) if rounded else result_ref
    if spread:
        gathers = RowGather(near, CHUNKS, all_ref, scratch[:4])
        scratch = scratch[4:]
    chunk_rows = rows_ref.shape[0] // CHUNKS
    sums.begin()
    if ride:
        ride_ref, rode_ref = ride_refs
        if ride == "gather":
            blocks = CtxGather(near, n_ctx, ride_ref, rode_ref, scratch)
        else:
            blocks = CtxSum(near, n_ctx, ride_ref, scratch)
        blocks.start()

    def settle(chunk):
        at = rows_of(chunk, chunk_rows)
        sums.collect(chunk, sum_ref)
        total = sum_ref[at, :]
        if stream_ref is not None:
            stream = stream_ref[at, :].astype(F32)
            scale = norm_scale(stream)
            weighted = gain_ref[...] * total
            gain_part = jnp.sum(total * stream * scale, 0, keepdims=True)
            gain_grad_ref[...] = gain_part if chunk == 0 else gain_grad_ref[...] + gain_part
            total = scale * weighted - stream * (scale * scale * scale) * jnp.mean(
                weighted * stream, -1, keepdims=True
            )
        total = rows_ref[at, :].astype(F32) + total
        if rounded:
            total = total.astype(BF16)
        result_ref[at, :] = total
        total = total.astype(F32)
        if spread:
            if spread == "norm":
                total = total * norm_scale(total) * gain_ref[...]
            all_ref[near.own, at, :] = total.astype(BF16)
            gathers.first(chunk)

    stages = [functools.partial(sums.step, step=step) for step in range(n_wt - 1)]
    stages.append(settle)
    if spread:
        stages += [functools.partial(gathers.hop, hop=hop) for hop in range(1, n_wt)]
    for slot in range(CHUNKS + len(stages) - 1):
        for chunk in reversed(range(CHUNKS)):
            if 0 <= slot - chunk < len(stages):
                stages[slot - chunk](chunk)
        if ride and slot == (n_wt + 1 if spread else 1):
            blocks.hand_on()

    if spread:
        gathers.arrive()
    if ride == "gather":
        blocks.finish()
    elif ride == "sum":
        blocks.finish(rode_ref)
    if spread:
        gathers.end()
    sums.end()


def exchange_scratch(n_ctx, n_wt, shape, spread, rounded, ride=None, rider=None):
    dma = pltpu.SemaphoreType.DMA
    scratch = RowSum.scratch(n_wt, shape, CHUNKS)
    scratch += [pltpu.VMEM(shape, F32)] if rounded else []
    scratch += RowGather.scratch(n_wt, CHUNKS) if spread else []
    if ride == "gather":
        scratch += CtxGather.scratch(n_ctx)
    elif ride:
        scratch += CtxSum.scratch(n_ctx, rider)
    return scratch


def exchange_kernel(n_ctx, n_wt, back, spread, rounded, ride, ready, *refs):
    refs = list(refs)
    near = Near(n_wt)
    peers = [(near.section, lax.rem(near.ctx + k, n_ctx), near.wt) for k in range(1, n_ctx)]
    parts, rows_ref = refs.pop(0), refs.pop(0)
    stream_ref = refs.pop(0) if back else None
    gain_ref = refs.pop(0) if (back or spread) else None
    ride_ref = refs.pop(0) if ride else None
    result_ref = refs.pop(0)
    gain_grad_ref = refs.pop(0) if back else None
    all_ref = refs.pop(0) if spread else None
    rode_ref = refs.pop(0) if ride else None
    token_ref = refs.pop(0)
    token_ref[...] = jnp.zeros(token_ref.shape, F32)
    near.greet(peers if ride else ())
    if ready:
        ready()
    exchange_steps(
        near,
        n_ctx,
        parts,
        rows_ref,
        stream_ref,
        gain_ref,
        result_ref,
        gain_grad_ref,
        all_ref,
        spread,
        rounded,
        refs,
        ride,
        (ride_ref, rode_ref),
    )


VMEM = pl.BlockSpec(memory_space=pltpu.VMEM)


def exchange(number, parts, rows, stream=None, gain=None, spread=None, rounded=False, gather=None, add=None, load=False):
    n_ctx, n_wt = lax.axis_size("ctx"), lax.axis_size("wt")
    shape = rows.shape
    back = stream is not None
    ride = "gather" if gather is not None else "sum" if add is not None else None
    rider = add if gather is None else gather
    wanted = ((parts, True), (rows, True), (stream, back), (gain, back or spread), (rider, ride))
    operands = [member for member, taken in wanted if taken]
    outs = [jax.ShapeDtypeStruct(shape, BF16 if rounded else F32)]
    if back:
        outs.append(jax.ShapeDtypeStruct((1, shape[1]), F32))
    if spread:
        outs.append(jax.ShapeDtypeStruct((2 * n_wt,) + shape, BF16))
    if ride == "gather":
        outs.append(jax.ShapeDtypeStruct((n_ctx,) + gather.shape, BF16))
    elif ride == "sum":
        outs.append(jax.ShapeDtypeStruct(add.shape[1:], F32))
    outs.append(jax.ShapeDtypeStruct((8, LANES), F32))
    kernel = functools.partial(exchange_kernel, n_ctx, n_wt, back, spread, rounded, ride)
    call = dict(
        out_shape=outs,
        out_specs=[VMEM] * len(outs),
        scratch_shapes=exchange_scratch(n_ctx, n_wt, shape, spread, rounded, ride, rider.shape if ride else None),
        compiler_params=pltpu.CompilerParams(
            collective_id=number, has_side_effects=True, vmem_limit_bytes=(60 if load else 16) << 20
        ),
        cost_estimate=pl.CostEstimate(flops=0, bytes_accessed=110 << 20, transcendentals=0),
    )
    if load:
        return loaded(kernel, operands, [], **call)
    return pl.pallas_call(functools.partial(kernel, None), in_specs=[VMEM] * len(operands), **call)(*operands)


def finish_kernel(n_ctx, n_wt, *refs):
    small, attn, rows = refs[:6], refs[6:8], refs[8:12]
    gain_ref, router_ref, query_ref, pair_ref, out_ref, rows_ref, grads_ref = refs[12:19]
    parts, landed, summed, from_sibling, received, send, recv, swap_send, swap_recv = refs[19:]
    section, ctx, wt = place()
    count = n_ctx * n_wt
    own = ctx * n_wt + wt
    blocks = [lax.rem(own + k, count) for k in range(1, count)]
    peers = [(section, block // n_wt, lax.rem(block, n_wt)) for block in blocks]
    sibling = (1 - section, ctx, wt)
    greet([sibling] + peers)
    members = [(attn[0], attn[1], received)]
    members += [(rows[0], rows[1], rows_ref.at[section]), (rows[2], rows[3], grads_ref.at[section])]
    swaps = [
        [remote(member[1 - layer], member[2], swap_send.at[k], swap_recv.at[k], sibling) for k, member in enumerate(members)]
        for layer in range(2)
    ]
    for layer in range(2):

        @pl.when(section == layer)
        def _():
            for copy in swaps[layer]:
                copy.start()

    piece = small[0].shape[1] // count
    parts[...] = jnp.zeros(parts.shape, F32)
    for block in range(count):
        for layer in range(2):
            at = 0
            for ref in small[3 * layer : 3 * layer + 3]:
                end = at + ref.shape[0]
                parts[block, layer, at:end, :piece] = ref[:, block * piece : (block + 1) * piece]
                at = end
    copies = [
        remote(parts.at[blocks[k]], landed.at[k], send.at[k], recv.at[k], peers[k]) for k in range(count - 1)
    ]
    for copy in copies:
        copy.start()
    mine = section == 0
    rows_ref[section] = jnp.where(mine, rows[0][...], rows[1][...])
    grads_ref[section] = jnp.where(mine, rows[2][...], rows[3][...])
    for copy in swaps[0]:
        copy.wait_recv()
    held = jnp.where(mine, attn[0][...], attn[1][...])
    came = received[...]
    first, second = jnp.where(mine, held, came), jnp.where(mine, came, held)
    q_cols = query_ref.shape[1] // 2
    at = q_cols + LANES
    query_ref[...] = jnp.concatenate([first[:, :q_cols], second[:, :q_cols]], 1)
    pair_ref[...] = jnp.concatenate([first[:, q_cols:at], second[:, q_cols:at]], 1)
    out_ref[...] = jnp.transpose(jnp.concatenate([first[:, at:], second[:, at:]], 1))
    total = parts[own]
    for k, copy in enumerate(copies):
        copy.wait_recv()
        total = total + landed[k]
    summed[...] = total
    swap = remote(summed.at[1 - section], from_sibling, send.at[count - 1], recv.at[count - 1], sibling)
    swap.start()
    swap.wait()
    total = summed[section] + from_sibling[...]
    named = small[0].shape[0]
    gain_ref[...] = total[named : named + 2, :]
    router_ref[...] = total[:named, :]
    for copy in copies:
        copy.wait_send()
    for copy in swaps[0]:
        copy.wait_send()


def finish(number, small, attn, rows, q_cols):
    n_ctx, n_wt = lax.axis_size("ctx"), lax.axis_size("wt")
    count = n_ctx * n_wt
    named = small[0].shape[0]
    shape = (2, named + 2 + -(named + 2) % 8, LANES)
    dma = pltpu.SemaphoreType.DMA
    depth = attn[0].shape[0]
    pair = jax.ShapeDtypeStruct((2,) + rows[0].shape, BF16)
    return pl.pallas_call(
        functools.partial(finish_kernel, n_ctx, n_wt),
        out_shape=[
            jax.ShapeDtypeStruct((2, LANES), F32),
            jax.ShapeDtypeStruct((named, LANES), F32),
            jax.ShapeDtypeStruct((depth, 2 * q_cols), F32),
            jax.ShapeDtypeStruct((depth, 2 * LANES), F32),
            jax.ShapeDtypeStruct((2 * q_cols, depth), F32),
            pair,
            pair,
        ],
        in_specs=[VMEM] * 12,
        out_specs=[VMEM] * 7,
        scratch_shapes=[
            pltpu.VMEM((count,) + shape, F32),
            pltpu.VMEM((count - 1,) + shape, F32),
            pltpu.VMEM(shape, F32),
            pltpu.VMEM(shape[1:], F32),
            pltpu.VMEM(attn[0].shape, F32),
            dma((count,)),
            dma((count,)),
            dma((3,)),
            dma((3,)),
        ],
        compiler_params=pltpu.CompilerParams(
            collective_id=number, has_side_effects=True, vmem_limit_bytes=16 << 20
        ),
        cost_estimate=pl.CostEstimate(flops=0, bytes_accessed=40 << 20, transcendentals=0),
    )(*small, *attn, *rows)


def hand_over_kernel(per_core, first, second, after, inward, down, held, send, recv, load, keep):
    section, ctx, wt = place()
    sibling = (1 - section, ctx, wt)
    for layer, own in enumerate((first, second)):

        @pl.when(section == layer)
        def _():
            pltpu.make_async_copy(own, held, load).start()

    def moves(source):
        pieces = expert_halves(inward, down, source, section, per_core)
        return [remote(piece, target, send.at[k], recv.at[k], sibling) for k, (target, piece) in enumerate(pieces)]

    greet([sibling])
    for layer, other in enumerate((second, first)):

        @pl.when(section == layer)
        def _():
            for copy in moves(other):
                copy.start()

    pltpu.make_async_copy(first, held, load).wait()
    pieces = expert_halves(inward, down, held, section, per_core)
    copies = [pltpu.make_async_copy(piece, target, keep.at[k]) for k, (target, piece) in enumerate(pieces)]
    for copy in copies:
        copy.start()
    for copy in copies:
        copy.wait()
    for copy in moves(first):
        copy.wait()


def hand_over(number, first, second, after, depth, down_rows, per_core, width):
    any_place = pl.BlockSpec(memory_space=pl.ANY)
    dma = pltpu.SemaphoreType.DMA
    return pl.pallas_call(
        functools.partial(hand_over_kernel, per_core),
        out_shape=[
            jax.ShapeDtypeStruct((2 * per_core, depth, first.shape[1] // per_core), first.dtype),
            jax.ShapeDtypeStruct((2 * per_core, down_rows, width), first.dtype),
        ],
        in_specs=[any_place] * 3,
        out_specs=[any_place] * 2,
        scratch_shapes=[pltpu.VMEM(first.shape, first.dtype), dma((6,)), dma((6,)), dma, dma((6,))],
        compiler_params=pltpu.CompilerParams(
            collective_id=number, has_side_effects=True, vmem_limit_bytes=60 << 20
        ),
    )(first, second, after)


HEADS = 3


def roll(values, by):
    return pltpu.roll(values, by, 1)


def lower_half(shape):
    return lax.broadcasted_iota(jnp.int32, shape, 1) < HEAD_SIZE


def turned(values, cosine, sine):
    first = lax.rem(lax.broadcasted_iota(jnp.int32, values.shape, 1), HEAD_SIZE) < HEAD_SIZE // 2
    half = HEAD_SIZE // 2
    return values * cosine + jnp.where(first, roll(values, LANES - half), roll(values, half)) * sine


def visible(key_place, query_place, query_start):
    return (key_place <= query_place) & (key_place >= query_start)


def attend_kernel(
    n_ctx,
    n_wt,
    ride,
    x_ref,
    w_ref,
    cos_ref,
    sin_ref,
    key_place,
    query_place,
    query_start,
    *refs,
):
    refs = list(refs)
    ride_ref = refs.pop(0) if ride else None
    part_ref, q_ref, pairs_ref, out_ref, lse_ref, att_ref = [refs.pop(0) for _ in range(6)]
    all_ref = refs.pop(0) if ride else None
    top_ref, sum_ref, acc_ref, send, recv = refs[:5]
    near = Near(n_wt)
    section, ctx, wt = near.section, near.ctx, near.wt
    peers = [(section, lax.rem(ctx + k, n_ctx), wt) for k in range(1, n_ctx)]
    waiting = []
    if ride:
        gathers = RowGather(near, 1, all_ref, refs[5:])
        waiting = [functools.partial(gathers.hop, 0, hop) for hop in range(1, n_wt)]
        all_ref[near.own] = ride_ref[...]
        near.greet(peers)
        gathers.first(0)
    else:
        greet(peers)

    def ride_on():
        if waiting:
            waiting.pop(0)()

    rows = x_ref.shape[0] // 2
    low = lower_half((2 * rows, LANES))
    mixed = dot(x_ref[...], w_ref[:, : 3 * LANES], ((1,), (0,)))
    cosine, sine = cos_ref[...], sin_ref[...]
    first = turned(mixed[:, :LANES], cosine, sine)
    second = turned(mixed[:, LANES : 2 * LANES], cosine, sine)
    pairs_ref[ctx] = jnp.where(low, roll(second, HEAD_SIZE), roll(mixed[:, 2 * LANES :], HEAD_SIZE)).astype(BF16)

    def passing(k):
        return remote(
            pairs_ref.at[ctx], pairs_ref.at[ctx], send.at[k], recv.at[k], (section, lax.rem(ctx + k, n_ctx), wt)
        )

    for k in range(1, n_ctx):
        passing(k).start()
    for h, part in enumerate((first, roll(first, HEAD_SIZE), second)):
        scaled = jnp.where(low, part * (1.0 / HEAD_SIZE), 0.0).astype(BF16)
        q_ref[0, h] = scaled[:rows]
        q_ref[1, h] = scaled[rows:]
    top_ref[...] = jnp.full(top_ref.shape, MASKED, F32)
    sum_ref[...] = jnp.zeros(sum_ref.shape, F32)
    acc_ref[...] = jnp.zeros(acc_ref.shape, F32)

    def block(c, m, j):
        keys = pairs_ref[c, j * rows : (j + 1) * rows, :]
        if m == j:
            seen = visible(key_place[c, j * rows : (j + 1) * rows, :], query_place[m], query_start[m])
        for h in range(HEADS):
            logits = dot(keys, q_ref[m, h], ((1,), (1,)))
            if m == j:
                logits = jnp.where(seen, logits, MASKED)
            before = top_ref[m, h]
            top = jnp.maximum(before, jnp.max(logits, 0, keepdims=True))
            expos = jnp.exp(logits - top)
            shrink = jnp.exp(before - top)
            top_ref[m, h] = top
            sum_ref[m, h] = sum_ref[m, h] * shrink + jnp.sum(expos, 0, keepdims=True)
            acc_ref[m, h] = acc_ref[m, h] * shrink + dot(keys, expos.astype(BF16), ((0,), (0,)))

    def blocks_of(c):
        block(c, 0, 0)
        block(c, 1, 1)
        block(c, 1, 0)

    blocks_of(ctx)
    ride_on()

    def arrived(k):
        passing(k).wait_recv()
        blocks_of(lax.rem(ctx + n_ctx - k, n_ctx))

    arrived(1)
    arrived(2)
    ride_on()
    pl.loop(3, n_ctx)(arrived)
    while waiting:
        ride_on()
    low = lower_half((rows, LANES))
    for m in range(2):
        outs = []
        for h in range(HEADS):
            lse_ref[m, h] = top_ref[m, h] + jnp.log(sum_ref[m, h])
            outs.append(jnp.transpose(acc_ref[m, h] / sum_ref[m, h]))
            out_ref[m, h] = outs[h]
        att_ref[m * rows : (m + 1) * rows, :LANES] = jnp.where(low, 0.0, outs[0]).astype(BF16)
        att_ref[m * rows : (m + 1) * rows, LANES:] = jnp.where(low, roll(outs[1], HEAD_SIZE), outs[2]).astype(BF16)
    part_ref[...] = dot(att_ref[...], w_ref[:, 2 * LANES :], ((1,), (1,))).astype(BF16)
    if ride:
        gathers.arrive()
        gathers.end()
    for k in range(1, n_ctx):
        passing(k).wait_send()


def attend(number, rows_in, weights, tables, ride=None):
    n_ctx, n_wt = lax.axis_size("ctx"), lax.axis_size("wt")
    riders = [] if ride is None else [ride]
    n_rows, width = rows_in.shape
    rows = n_rows // 2
    dma = pltpu.SemaphoreType.DMA
    return pl.pallas_call(
        functools.partial(attend_kernel, n_ctx, n_wt, bool(riders)),
        out_shape=[
            jax.ShapeDtypeStruct((n_rows, width), BF16),
            jax.ShapeDtypeStruct((2, HEADS, rows, LANES), BF16),
            jax.ShapeDtypeStruct((n_ctx, n_rows, LANES), BF16),
            jax.ShapeDtypeStruct((2, HEADS, rows, LANES), F32),
            jax.ShapeDtypeStruct((2, HEADS, 1, rows), F32),
            jax.ShapeDtypeStruct((n_rows, 2 * LANES), BF16),
        ]
        + [jax.ShapeDtypeStruct((2 * n_wt,) + member.shape, BF16) for member in riders],
        in_specs=[VMEM] * (7 + len(riders)),
        out_specs=[VMEM] * (6 + len(riders)),
        scratch_shapes=[
            pltpu.VMEM((2, HEADS, 1, rows), F32),
            pltpu.VMEM((2, HEADS, 1, rows), F32),
            pltpu.VMEM((2, HEADS, LANES, rows), F32),
            dma((n_ctx,)),
            dma((n_ctx,)),
        ]
        + (RowGather.scratch(n_wt, 1) if riders else []),
        compiler_params=pltpu.CompilerParams(
            collective_id=number, has_side_effects=True, vmem_limit_bytes=20 << 20
        ),
        cost_estimate=pl.CostEstimate(flops=0, bytes_accessed=70 << 20, transcendentals=0),
    )(rows_in, weights, *tables, *riders)


def attend_back_kernel(
    n_ctx,
    n_wt,
    ride,
    ready,
    a_ref,
    w_ref,
    cos_ref,
    sin_ref,
    key_place,
    query_place,
    query_start,
    q_ref,
    pairs_ref,
    out_ref,
    lse_ref,
    *refs,
):
    refs = list(refs)
    if ride:
        rows_ref, stream_ref, gain_ref = [refs.pop(0) for _ in range(3)]
        ride_refs = [refs.pop(0), refs.pop(0)]
        raw_ref, result_ref, gain_grad_ref, all_ref, rode_ref = [refs.pop(0) for _ in range(5)]
    else:
        raw_ref, part_ref = refs.pop(0), refs.pop(0)
    do_ref, delta_ref, dq_ref, dkv_ref, own_ref, landed, send, recv = refs[:8]
    refs = refs[8:]
    near = Near(n_wt)
    section, ctx, wt = near.section, near.ctx, near.wt
    peers = [(section, lax.rem(ctx + k, n_ctx), wt) for k in range(1, n_ctx)]
    waiting = []
    if ride:
        near.greet(peers)
    else:
        greet(peers)
    if ready:
        ready()
    if ride:
        part_ref = refs.pop(0)
        sums = RowSum(near, 1, ride_refs[0], refs[:9])
        rode_sum = refs[9]
        refs = refs[10:]
        waiting = [functools.partial(sums.point, 0, number) for number in range(n_wt - 1)]
        sums.begin()

    def ride_on():
        if waiting:
            waiting.pop(0)()

    rows = a_ref.shape[0] // 2
    low = lower_half((2 * rows, LANES))
    d_att = dot(a_ref[...], w_ref[:, 2 * LANES :], ((1,), (0,)))
    for h, part in enumerate((d_att[:, :LANES], roll(d_att[:, LANES:], HEAD_SIZE), d_att[:, LANES:])):
        d_out = jnp.where(low, 0.0, part).astype(BF16)
        for m in range(2):
            do_ref[m, h] = d_out[m * rows : (m + 1) * rows]
            product = do_ref[m, h].astype(F32) * out_ref[m, h]
            delta_ref[m, h] = jnp.sum(jnp.transpose(product), 0, keepdims=True)
    dq_ref[...] = jnp.zeros(dq_ref.shape, F32)
    ride_on()

    def block(c, j):
        keys = pairs_ref[c, j * rows : (j + 1) * rows, :]
        total = jnp.zeros((rows, LANES), F32)
        for m in range(j, 2):
            if m == j:
                seen = visible(key_place[c, j * rows : (j + 1) * rows, :], query_place[m], query_start[m])
            for h in range(HEADS):
                probs = jnp.exp(dot(keys, q_ref[m, h], ((1,), (1,))) - lse_ref[m, h])
                if m == j:
                    probs = jnp.where(seen, probs, 0.0)
                d_probs = dot(keys, do_ref[m, h], ((1,), (1,)))
                d_scores = (probs * (d_probs - delta_ref[m, h])).astype(BF16)
                total = total + dot(d_scores, q_ref[m, h], ((1,), (0,)))
                total = total + dot(probs.astype(BF16), do_ref[m, h], ((1,), (0,)))
                dq_ref[m, h] += dot(keys, d_scores, ((0,), (0,)))
        return total

    def passing(k):
        target = lax.rem(ctx + k, n_ctx)
        return remote(dkv_ref.at[target], landed.at[k - 1], send.at[k], recv.at[k], (section, target, wt))

    def sent(k):
        c = lax.rem(ctx + k, n_ctx)
        for j in range(2):
            dkv_ref[c, j * rows : (j + 1) * rows, :] = block(c, j).astype(BF16)
        passing(k).start()

    sent(1)
    sent(2)
    ride_on()
    pl.loop(3, n_ctx)(sent)

    for j in range(2):
        own_ref[j * rows : (j + 1) * rows, :] = block(ctx, j)

    while waiting:
        ride_on()

    @pl.loop(1, n_ctx)
    def _(k):
        passing(k).wait_recv()
        own_ref[...] += landed[k - 1].astype(F32)

    cosine, sine = cos_ref[...], sin_ref[...]
    d_own = own_ref[...]
    over = roll(d_own, HEAD_SIZE)
    d_query = [
        jnp.concatenate([jnp.transpose(dq_ref[m, h]) for m in range(2)], 0) * (1.0 / HEAD_SIZE) for h in range(HEADS)
    ]
    first = jnp.where(low, d_query[0], roll(d_query[1], HEAD_SIZE))
    second = jnp.where(low, d_query[2], over)
    raw_ref[:, :LANES] = turned(first, cosine, -sine).astype(BF16)
    raw_ref[:, LANES : 2 * LANES] = turned(second, cosine, -sine).astype(BF16)
    raw_ref[:, 2 * LANES :] = jnp.where(low, over, 0.0).astype(BF16)
    partial = dot(raw_ref[...], w_ref[:, : 3 * LANES], ((1,), (1,))).astype(BF16)
    part_ref[...] = partial.reshape(part_ref.shape)
    if ride:
        sums.collect(0, rode_sum)
        rode_ref[...] = (rode_sum[...] + ride_refs[1][...]).astype(BF16)

    if ride:
        exchange_steps(
            near,
            n_ctx,
            part_ref,
            rows_ref,
            stream_ref,
            gain_ref,
            result_ref,
            gain_grad_ref,
            all_ref,
            "plain",
            True,
            refs,
        )
    if ride:
        sums.end()
    for k in range(1, n_ctx):
        passing(k).wait_send()


def attend_back(number, rows_a, weights, tables, kept, then=()):
    n_ctx, n_wt = lax.axis_size("ctx"), lax.axis_size("wt")
    n_rows, width = rows_a.shape
    half = n_rows // 2
    share = n_rows // (2 * n_wt)
    dma = pltpu.SemaphoreType.DMA
    shape = (share, width)
    blocks = jax.ShapeDtypeStruct((2 * n_wt,) + shape, BF16)
    outs = [jax.ShapeDtypeStruct((n_rows, 3 * LANES), BF16)]
    scratch = [
        pltpu.VMEM((2, HEADS, half, LANES), BF16),
        pltpu.VMEM((2, HEADS, 1, half), F32),
        pltpu.VMEM((2, HEADS, LANES, half), F32),
        pltpu.VMEM((n_ctx, n_rows, LANES), BF16),
        pltpu.VMEM((n_rows, LANES), F32),
        pltpu.VMEM((n_ctx - 1, n_rows, LANES), BF16),
        dma((n_ctx,)),
        dma((n_ctx,)),
    ]
    if then:
        row = jax.ShapeDtypeStruct(shape, BF16)
        outs += [row, jax.ShapeDtypeStruct((1, width), F32), blocks, row]
        scratch += [pltpu.VMEM(blocks.shape, BF16)] + RowSum.scratch(n_wt, shape, 1) + [pltpu.VMEM(shape, F32)]
        scratch += exchange_scratch(n_ctx, n_wt, shape, "plain", True)
    else:
        outs.append(blocks)
    operands = [rows_a, weights, *tables, *kept, *then]
    kernel = functools.partial(attend_back_kernel, n_ctx, n_wt, bool(then))
    call = dict(
        out_shape=outs,
        out_specs=[VMEM] * len(outs),
        scratch_shapes=scratch,
        compiler_params=pltpu.CompilerParams(
            collective_id=number, has_side_effects=True, vmem_limit_bytes=60 << 20
        ),
        cost_estimate=pl.CostEstimate(flops=0, bytes_accessed=(200 if then else 100) << 20, transcendentals=0),
    )
    return loaded(kernel, operands, [], **call)


def expert_halves(inward, down, packed, half, per_core):
    depth, down_rows = inward.shape[1], down.shape[1]
    wide, width = packed.shape[1], down.shape[2]
    column, second = inward.shape[2], depth + down_rows
    first, middle = wide - width, down_rows // 2
    a, b = half * per_core, half * per_core + 1
    return [
        (inward.at[a], packed.at[:depth, :column]),
        (inward.at[b], packed.at[:depth, column:]),
        (down.at[a], packed.at[depth:second, :width]),
        (down.at[b, :, :first], packed.at[depth:second, width:]),
        (down.at[b, :middle, first:], packed.at[second:, : wide // 2]),
        (down.at[b, middle:, first:], packed.at[second:, wide // 2 :]),
    ]


def prepare_kernel(inward, down, first, second, halves, load, send, recv, keep):
    packed = (first, second)
    section, ctx, wt = place()
    sibling = (1 - section, ctx, wt)
    per_core = inward.shape[0] // 2
    loads = []
    for half in range(2):
        for source, target in expert_halves(inward, down, halves.at[half], half, per_core):
            loads.append(pltpu.make_async_copy(source, target, load.at[len(loads)]))
    for copy in loads:
        copy.start()
    greet([sibling])
    for copy in loads:
        copy.wait()
    for layer in range(2):

        @pl.when(section == layer)
        def _():
            move = remote(halves.at[1 - layer], packed[layer], send, recv, sibling)
            move.start()
            own = pltpu.make_async_copy(halves.at[layer], packed[layer], keep)
            own.start()
            own.wait()
            move.wait_send()
            remote(halves.at[layer], packed[1 - layer], send, recv, sibling).wait_recv()


def prepare(number, inward, down):
    depth, down_rows = inward.shape[1], down.shape[1]
    in_place = pl.BlockSpec(memory_space=pltpu.HBM)
    shape = (depth + down_rows + down_rows // 2, inward.shape[0] // 2 * inward.shape[2])
    packed = jax.ShapeDtypeStruct(shape, BF16)
    dma = pltpu.SemaphoreType.DMA
    return pl.pallas_call(
        prepare_kernel,
        out_shape=[packed, packed],
        in_specs=[in_place] * 2,
        out_specs=[in_place] * 2,
        scratch_shapes=[pltpu.VMEM((2,) + shape, BF16), dma((12,)), dma, dma, dma],
        compiler_params=pltpu.CompilerParams(
            collective_id=number, has_side_effects=True, vmem_limit_bytes=60 << 20
        ),
    )(inward, down)


def begin_kernel(n_ctx, n_wt, *refs):
    given = refs[:7]
    all_ref, rode_ref, pack, all_gains, all_router, all_routes = refs[7:13]
    tokens, query, pair, out, gains, router, routes = refs[13:20]
    halves, first_pack, load, send, recv = refs[20:25]
    near = Near(n_wt)
    loads = [
        pltpu.make_async_copy(source.at[near.section] if k == 0 else source, target, load.at[k])
        for k, (source, target) in enumerate(zip(given, refs[13:20]))
    ]
    for copy in loads:
        copy.start()
    section, ctx, wt = near.section, near.ctx, near.wt
    peers = [(section, lax.rem(ctx + k, n_ctx), wt) for k in range(1, n_ctx)]
    blocks = CtxGather(near, n_ctx, first_pack, rode_ref, refs[25:28])
    gathers = RowGather(near, CHUNKS, all_ref, refs[28:])
    near.greet(peers)
    for copy in loads:
        copy.wait()
    named = router.shape[0]
    all_gains[section] = gains[...]
    all_routes[section] = routes[...]
    all_router[section] = jnp.zeros(all_router.shape[1:], BF16)
    all_router[section, :named, :] = router[...]
    shared = [
        remote(ref.at[section], ref.at[section], send.at[k], recv.at[k], near.sibling)
        for k, ref in enumerate((all_gains, all_router, all_routes))
    ]
    for copy in shared:
        copy.start()
    q_cols = query.shape[1] // 2
    outward = jnp.transpose(out[...].astype(F32))
    for half in range(2):
        halves[half] = jnp.concatenate(
            [
                query[:, half * q_cols : (half + 1) * q_cols].astype(F32),
                pair[:, half * LANES : (half + 1) * LANES].astype(F32),
                outward[:, half * q_cols : (half + 1) * q_cols],
            ],
            1,
        ).astype(BF16)
    packs = (first_pack, pack)
    for layer in range(2):

        @pl.when(section == layer)
        def _():
            remote(halves.at[1 - layer], packs[layer], send.at[3], recv.at[3], near.sibling).start()
            packs[layer][...] = halves[layer]

    rows = tokens[...].astype(F32)
    scaled = rows * norm_scale(rows)
    shared[0].wait_recv()
    all_ref[near.own] = (scaled * all_gains[0, 0:1, :]).astype(BF16)
    for chunk in range(CHUNKS):
        gathers.first(chunk)
    for layer in range(2):

        @pl.when(section == layer)
        def _():
            remote(halves.at[layer], packs[1 - layer], send.at[3], recv.at[3], near.sibling).wait_recv()

    blocks.start()
    for hop in range(1, n_wt):
        for chunk in range(CHUNKS):
            gathers.hop(chunk, hop)
    blocks.hand_on()
    gathers.arrive()
    blocks.finish()
    gathers.end()
    shared[0].wait_send()
    for copy in shared[1:]:
        copy.wait()
    remote(halves.at[0], first_pack, send.at[3], recv.at[3], near.sibling).wait_send()


def begin(number, tokens, query, pair, out, gains, router, routes):
    n_ctx, n_wt = lax.axis_size("ctx"), lax.axis_size("wt")
    depth, columns = query.shape[0], query.shape[1] + LANES
    dma = pltpu.SemaphoreType.DMA
    pack = (depth, columns)
    return pl.pallas_call(
        functools.partial(begin_kernel, n_ctx, n_wt),
        out_shape=[
            jax.ShapeDtypeStruct((2 * n_wt,) + tokens.shape[1:], BF16),
            jax.ShapeDtypeStruct((n_ctx,) + pack, BF16),
            jax.ShapeDtypeStruct(pack, BF16),
            jax.ShapeDtypeStruct((2,) + gains.shape, gains.dtype),
            jax.ShapeDtypeStruct((2, LANES, router.shape[1]), BF16),
            jax.ShapeDtypeStruct((2,) + routes.shape, routes.dtype),
        ],
        in_specs=[pl.BlockSpec(memory_space=pltpu.HBM)] * 7,
        out_specs=[VMEM] * 6,
        scratch_shapes=[pltpu.VMEM(tokens.shape[1:], BF16)]
        + [pltpu.VMEM(member.shape, member.dtype) for member in (query, pair, out, gains, router, routes)]
        + [
            pltpu.VMEM((2,) + pack, BF16),
            pltpu.VMEM(pack, BF16),
            dma((7,)),
            dma((4,)),
            dma((4,)),
        ]
        + CtxGather.scratch(n_ctx)
        + RowGather.scratch(n_wt, CHUNKS),
        compiler_params=pltpu.CompilerParams(
            collective_id=number, has_side_effects=True, vmem_limit_bytes=16 << 20
        ),
        cost_estimate=pl.CostEstimate(flops=0, bytes_accessed=90 << 20, transcendentals=0),
    )(tokens, query, pair, out, gains, router, routes)


TILE = 256


def expert_pieces(packed, inward, down, depth, down_rows):
    n, wide, width = packed.shape[0], packed.shape[2], down.shape[2]
    half = down_rows // 2
    first = wide - width
    pairs = []
    for c in range(n):
        at = c * down_rows
        second = depth + down_rows
        pairs += [
            (packed.at[c, depth:second, :width], down.at[0, at : at + down_rows, :]),
            (packed.at[c, depth:second, width:], down.at[1, at : at + down_rows, :first]),
            (packed.at[c, second:, : wide // 2], down.at[1, at : at + half, first:]),
            (packed.at[c, second:, wide // 2 :], down.at[1, at + half : at + down_rows, first:]),
        ]
    for c in range(n):
        pairs.append((packed.at[c, :depth, :], inward.at[c * depth : (c + 1) * depth, :]))
    return pairs


def gate_rows(x, router, routes):
    lane = lax.broadcasted_iota(jnp.int32, (x.shape[0], LANES), 1)
    named = routes[:, 0:1] == lane
    for t in range(1, routes.shape[1]):
        named = named | (routes[:, t : t + 1] == lane)
    logits = jnp.where(named, dot(x, router, ((1,), (1,))), MASKED)
    expos = jnp.where(named, jnp.exp(logits - jnp.max(logits, 1, keepdims=True)), 0.0)
    return expos / jnp.sum(expos, 1, keepdims=True)


def experts_kernel(n_ctx, layer, forward, backward, depth, down_rows, ride, ready, *refs):
    refs = list(refs)
    x_ref, router_ref, pick_ref = [refs.pop(0) for _ in range(3)]
    if forward:
        hit_ref = refs.pop(0)
    else:
        gates_ref, gate_up_ref = refs.pop(0), refs.pop(0)
    d_ref = refs.pop(0) if backward else None
    ride_ref = refs.pop(0) if ride else None
    packed_ref = refs.pop(0)
    part_ref = refs.pop(0) if forward else None
    if forward and not backward:
        gates_ref, gate_up_ref = refs.pop(0), refs.pop(0)
    if backward:
        back_out, grads_ref, router_grad_ref = [refs.pop(0) for _ in range(3)]
    rode_ref = refs.pop(0) if ride else None
    inward, down, weighted, load = [refs.pop(0) for _ in range(4)]
    if forward and backward:
        gates_ref, gate_up_ref = refs.pop(0), refs.pop(0)
    if backward:
        d_gate_up, x_turned, in_grad, down_grad, store, back_ref, leave = refs[:7]
        refs = refs[7:]
        if forward:
            part_out, part_ref = part_ref, refs.pop(0)
            part_leave = pltpu.make_async_copy(part_ref, part_out, leave.at[1])
        back_leave = pltpu.make_async_copy(back_ref, back_out, leave.at[0])

    pieces = expert_pieces(packed_ref, inward, down, depth, down_rows)
    loads = [pltpu.make_async_copy(source, target, load.at[k]) for k, (source, target) in enumerate(pieces)]
    n_down = 4 * packed_ref.shape[0]
    for copy in (loads[n_down:] + loads[:n_down]) if forward else loads:
        copy.start()
    if ride:
        near = Near(1)
        greet([(near.section, lax.rem(near.ctx + k, n_ctx), near.wt) for k in range(1, n_ctx)])
        blocks = CtxSum(near, n_ctx, ride_ref, refs)
        blocks.start()
    if ready:
        ready()
    columns = [slice(t * TILE, (t + 1) * TILE) for t in range(2 * FF // TILE)]
    per_expert = FF // TILE
    width = x_ref.shape[1]

    def gate_at(t):
        return slice(2 * FF * (t // per_expert) + TILE * (t % per_expert), 2 * FF * (t // per_expert) + TILE * (t % per_expert + 1))

    def up_at(t):
        return slice(gate_at(t).start + FF, gate_at(t).stop + FF)

    def weight_of(e):
        return jnp.sum(gates_ref[...] * pick_ref[e : e + 1, :], 1, keepdims=True)

    if forward:
        routes = hit_ref[layer]
        routes = routes.reshape(routes.shape[0] * routes.shape[1], routes.shape[2])
        gates_ref[...] = gate_rows(x_ref[...], router_ref[layer], routes)
        for copy in loads[n_down:]:
            copy.wait()
        for t, place_of in enumerate(columns):
            gate = dot(x_ref[...], inward[:, gate_at(t)], ((1,), (0,)))
            up = dot(x_ref[...], inward[:, up_at(t)], ((1,), (0,)))
            gate_up_ref[:, gate_at(t)] = gate.astype(BF16)
            gate_up_ref[:, up_at(t)] = up.astype(BF16)
            weighted[:, place_of] = (gate / (1.0 + jnp.exp(-gate)) * up * weight_of(t // per_expert)).astype(BF16)
        for copy in loads[:n_down]:
            copy.wait()
        for n in range(width // TILE):
            at = slice(n * TILE, (n + 1) * TILE)
            part_ref[:, at] = (
                dot(weighted[:, :FF], down[0, :, at], ((1,), (0,)))
                + dot(weighted[:, FF:], down[1, :, at], ((1,), (0,)))
            ).astype(BF16)
        if backward:
            part_leave.start()
    else:
        for copy in loads[:n_down]:
            copy.wait()
    if backward:
        d_weight = [0.0, 0.0]
        for t, place_of in enumerate(columns):
            e = t // per_expert
            rows_of = slice(TILE * (t % per_expert), TILE * (t % per_expert + 1))
            weight = weight_of(e)
            d_weighted = dot(d_ref[...], down[e, rows_of, :], ((1,), (1,)))
            gate = gate_up_ref[:, gate_at(t)].astype(F32)
            up = gate_up_ref[:, up_at(t)].astype(F32)
            sigmoid = 1.0 / (1.0 + jnp.exp(-gate))
            activated = gate * sigmoid
            hidden = activated * up
            d_weight[e] = d_weight[e] + jnp.sum(hidden * d_weighted, 1, keepdims=True)
            weighted[:, place_of] = (hidden * weight).astype(BF16)
            d_hidden = d_weighted * weight
            d_gate_up[:, gate_at(t)] = (d_hidden * up * (sigmoid * (1.0 + gate * (1.0 - sigmoid)))).astype(BF16)
            d_gate_up[:, up_at(t)] = (d_hidden * activated).astype(BF16)
        if ride:
            blocks.hand_on()
        gates = gates_ref[...]
        terms = gates * (pick_ref[0:1, :] * d_weight[0] + pick_ref[1:2, :] * d_weight[1])
        d_logits = terms - gates * jnp.sum(terms, 1, keepdims=True)
        high = d_logits.astype(BF16)
        low = (d_logits - high.astype(F32)).astype(BF16)
        both = jnp.concatenate([high, low], 1)
        if not forward:
            for copy in loads[n_down:]:
                copy.wait()
        for n in range(width // TILE):
            at = slice(n * TILE, (n + 1) * TILE)
            table = router_ref[layer, :, at]
            back_ref[:, at] = (
                dot(d_gate_up[...], inward[at, :], ((1,), (1,)))
                + dot(both, jnp.concatenate([table, table], 0), ((1,), (0,)))
            ).astype(BF16)
        back_leave.start()
        x_turned[...] = jnp.transpose(x_ref[...])
        router_grad = dot(both, x_ref[...], ((0,), (0,)))
        named = router_grad_ref.shape[0]
        router_grad_ref[...] = router_grad[:named] + router_grad[LANES : LANES + named]
        pieces = expert_pieces(grads_ref, in_grad, down_grad, depth, down_rows)
        stores = [
            pltpu.make_async_copy(source, target, store.at[k]) for k, (target, source) in enumerate(pieces)
        ]
        for e in range(2):
            turned_hidden = jnp.transpose(weighted[:, e * FF : (e + 1) * FF])
            for n in range(width // TILE):
                at = slice(n * TILE, (n + 1) * TILE)
                down_grad[e, :, at] = dot(turned_hidden, d_ref[:, at], ((1,), (0,))).astype(BF16)
        for copy in stores[:n_down]:
            copy.start()
        for c in range(n_ctx):
            at = slice(c * depth, (c + 1) * depth)
            for n in range(2):
                wide = slice(n * 2 * FF, (n + 1) * 2 * FF)
                in_grad[at, wide] = dot(x_turned[at, :], d_gate_up[:, wide], ((1,), (0,))).astype(BF16)
            stores[n_down + c].start()
        for copy in stores:
            copy.wait()
        back_leave.wait()
        if forward:
            part_leave.wait()
    if ride:
        blocks.finish(rode_ref)


def experts(
    layer, x, packed, router, pick, n_experts, depth, down_rows, hit=None, kept=None, d_rows=None, number=None, add=None
):
    n_ctx = lax.axis_size("ctx")
    forward, backward = hit is not None, d_rows is not None
    n_rows, width = x.shape
    any_place = pl.BlockSpec(memory_space=pl.ANY)
    operands = [x, router, pick]
    operands += [hit] if forward else list(kept)
    operands += [d_rows] if backward else []
    operands += [add] if add is not None else []
    rows_out = jax.ShapeDtypeStruct((n_rows, width), BF16)
    inner = [jax.ShapeDtypeStruct((n_rows, LANES), F32), jax.ShapeDtypeStruct((n_rows, 4 * FF), BF16)]
    n_pieces = 5 * packed.shape[0]
    scratch = [
        pltpu.VMEM((width, 4 * FF), BF16),
        pltpu.VMEM((2, FF, width), BF16),
        pltpu.VMEM((n_rows, 2 * FF), BF16),
        pltpu.SemaphoreType.DMA((n_pieces,)),
    ]
    outs = []
    out_specs = []
    if forward:
        outs += [rows_out]
        out_specs += [any_place if backward else VMEM]
    if forward and not backward:
        outs += inner
        out_specs += [VMEM] * 2
    if backward:
        outs += [rows_out, jax.ShapeDtypeStruct(packed.shape, BF16), jax.ShapeDtypeStruct((n_experts, width), F32)]
        out_specs += [any_place, any_place, VMEM]
        if forward:
            scratch += [pltpu.VMEM(member.shape, member.dtype) for member in inner]
        scratch += [
            pltpu.VMEM((n_rows, 4 * FF), BF16),
            pltpu.VMEM((width, n_rows), BF16),
            pltpu.VMEM((width, 4 * FF), BF16),
            pltpu.VMEM((2, FF, width), BF16),
            pltpu.SemaphoreType.DMA((n_pieces,)),
            pltpu.VMEM((n_rows, width), BF16),
            pltpu.SemaphoreType.DMA((2,)),
        ]
        scratch += [pltpu.VMEM((n_rows, width), BF16)] if forward else []
    params = {}
    if add is not None:
        outs.append(jax.ShapeDtypeStruct(add.shape[1:], F32))
        out_specs.append(VMEM)
        scratch += CtxSum.scratch(n_ctx, add.shape)
        params = dict(collective_id=number, has_side_effects=True)
    work = n_rows * 6 * width * FF * 2 * ((1 if forward else 0) + (2 if backward else 0))
    load = forward
    kernel = functools.partial(experts_kernel, n_ctx, layer, forward, backward, depth, down_rows, add is not None)
    call = dict(
        out_shape=outs,
        out_specs=out_specs,
        scratch_shapes=scratch,
        compiler_params=pltpu.CompilerParams(vmem_limit_bytes=(60 if load else 44 if backward else 28) << 20, **params),
        cost_estimate=pl.CostEstimate(flops=2 * work, bytes_accessed=40 << 20, transcendentals=0),
    )
    if load:
        return loaded(kernel, operands, [packed], **call)
    in_specs = [VMEM] * len(operands) + [any_place]
    return pl.pallas_call(functools.partial(kernel, None), in_specs=in_specs, **call)(*operands, packed)


def shards(tokens, cotangent, blocks, routes, norm_gain, w_query, key_value_weight, w_attn_out, router, w_in, w_down):
    section, ctx, wt = place()
    n_ctx, n_wt, layers = lax.axis_size("ctx"), lax.axis_size("wt"), lax.axis_size("section")
    micro_count, share, width = tokens.shape
    per_ctx = routes.shape[2]
    seq_len = per_ctx * n_ctx
    per_core = w_in.shape[1] // 2
    n_experts = router.shape[2]
    q_cols = w_query.shape[2] // 2
    depth = w_query.shape[1]

    block_len = seq_len // blocks.shape[1]
    placed = (blocks[:, :, None] * block_len + jnp.arange(block_len, dtype=jnp.int32)[None, None, :]).reshape(
        micro_count, seq_len
    )
    query_place = lax.dynamic_slice_in_dim(placed, ctx * per_ctx, per_ctx, 1)
    later = (jnp.arange(micro_count) > 0)[:, None]
    query_start = jnp.where(later, query_place - query_place % CONT_LEN, 0)
    query_pos = jnp.where(later, seq_len + query_place % CONT_LEN, query_place)
    half = HEAD_SIZE // 2
    inverse = jnp.power(ROPE_BASE, -(jnp.arange(LANES, dtype=jnp.int32) % half).astype(F32) * 2.0 / HEAD_SIZE)
    angles = query_pos.reshape(-1).astype(F32)[:, None] * inverse[None, :]
    sign = jnp.where(jnp.arange(LANES) % HEAD_SIZE < half, -1.0, 1.0)
    tables = (
        jnp.cos(angles),
        jnp.sin(angles) * sign[None, :],
        jnp.transpose(placed.reshape(micro_count, n_ctx, per_ctx), (1, 0, 2)).reshape(n_ctx, -1, 1),
        query_place[:, None, :],
        query_start[:, None, :],
    )

    moe_pack = prepare(15, w_in[0], w_down[0])
    normed_in, full, attn_pack, gain_pack, router_pack, route_pack = begin(
        0,
        tokens,
        w_query[0],
        key_value_weight[0].reshape(depth, -1),
        w_attn_out[0],
        norm_gain[0],
        jnp.transpose(router[0]),
        routes[0],
    )

    in_rows, down_rows = w_in.shape[2], w_down.shape[2]

    def gather_experts(pack):
        return lax.all_gather(pack, "ctx", axis=0, tiled=True).reshape((n_ctx,) + pack.shape)

    attn_full = [None, None]

    my_first = wt * 2 * per_core + section * per_core
    n_rows = micro_count * per_ctx

    pick = (jnp.arange(LANES)[None, :] == my_first + jnp.arange(8)[:, None]).astype(F32)
    def full_rows(values):
        return values.reshape(n_rows, width)

    def blocked(values):
        return values.reshape(2 * n_wt, share, width).astype(BF16)

    stream = lax.dynamic_index_in_dim(tokens, section, 0, False)
    top = lax.dynamic_index_in_dim(cotangent, section, 0, False)

    attn_full[0] = full.reshape(-1, full.shape[2])
    moe_full = [gather_experts(member) for member in moe_pack]
    saved = []
    outputs = []
    for layer in range(2):
        rows_in = full_rows(normed_in)
        weights = attn_full[layer]
        if layer == 0:
            partial, *heads, attended, d_mixed = attend(2, rows_in, weights, tables, top)
        else:
            partial, *heads, attended = attend(3, rows_in, weights, tables)
        middle, normed_mid, token = exchange(
            4 + layer, blocked(partial), stream, gain=gain_pack[layer, 1:2], spread="norm"
        )
        token, moe_full[layer] = lax.optimization_barrier((token, moe_full[layer]))
        pick_now = pick + token
        rows_mid = full_rows(normed_mid)
        if layer == 0:
            partial, gates, gate_up = experts(
                0, rows_mid, moe_full[0], router_pack, pick_now, n_experts, in_rows, down_rows, hit=route_pack
            )
            inner = (gates, gate_up)
        else:
            partial, *back_parts = experts(
                1,
                rows_mid,
                moe_full[1],
                router_pack,
                pick_now,
                n_experts,
                in_rows,
                down_rows,
                hit=route_pack,
                d_rows=full_rows(d_mixed),
            )
            inner = None
        saved.append(
            dict(
                stream=stream,
                middle=middle,
                rows_in=rows_in,
                rows_mid=rows_mid,
                heads=heads,
                attended=attended,
                inner=inner,
            )
        )
        if layer == 0:
            stream, normed_in, full, token = exchange(
                6, blocked(partial), middle, gain=gain_pack[1, 0:1], spread="norm", rounded=True, gather=attn_pack
            )
            attn_full[1] = full.reshape(-1, full.shape[2])
            outputs.append(stream)
        else:
            last_rows = (blocked(partial), middle)
    upstream = top
    grads_in = [None, None]
    attn_grads = [None, None]
    moe_grads = [None, None]
    small = [None, None]
    for layer in (1, 0):
        kept = saved[layer]
        if layer == 0:
            back_parts = experts(
                0,
                kept["rows_mid"],
                moe_full[0],
                router_pack,
                pick,
                n_experts,
                in_rows,
                down_rows,
                kept=kept["inner"],
                d_rows=full_rows(d_mixed),
                number=7,
                add=attn_parts,
            )
            *back_parts, attn_grads[1] = back_parts
        partial, packed_grad, router_grad = back_parts
        gain = gain_pack[layer, 1:2]
        if layer == 0:
            gain, moe_grads[1] = lax.optimization_barrier((gain, moe_grads[1]))
        moe_grads[layer] = lax.psum_scatter(packed_grad, "ctx", scatter_dimension=0, tiled=False)
        d_middle, gain_grad_mid, d_attn, token = exchange(
            8 + layer, blocked(partial), upstream, kept["middle"], gain, spread="plain", load=True
        )
        rows_a = full_rows(d_attn)
        weights = attn_full[layer]
        if layer == 1:
            then = (d_middle, kept["stream"], gain_pack[1, 0:1], *last_rows)
            raw, upstream, gain_grad_in, d_mixed, last = attend_back(11, rows_a, weights, tables, kept["heads"], then)
            outputs.append(last)
        else:
            raw, partial = attend_back(10, rows_a, weights, tables, kept["heads"])
        attn_parts = dot(kept["rows_in"], jnp.pad(raw, ((0, 0), (0, LANES))), ((0,), (0,)))
        attn_parts = attn_parts + dot(rows_a, jnp.pad(kept["attended"], ((0, 0), (2 * LANES, 0))), ((0,), (0,)))
        attn_parts = attn_parts.astype(BF16).reshape(n_ctx, depth, -1)
        if layer == 0:
            upstream, gain_grad_in, attn_grads[0], token = exchange(
                1, partial, d_middle, kept["stream"], gain_pack[0, 0:1], rounded=True, add=attn_parts
            )
        grads_in[layer] = upstream
        small[layer] = [router_grad, gain_grad_in, gain_grad_mid]

    gain_total, router_total, grad_query, grad_kv, grad_out, out_pair, grad_pair = finish(
        14, small[0] + small[1], attn_grads, outputs + grads_in, q_cols
    )
    piece = width // (n_ctx * n_wt)
    moe_grads = [member.reshape(member.shape[-2:]) for member in moe_grads]
    grad_in, grad_down = hand_over(13, moe_grads[0], moe_grads[1], gain_total, in_rows, down_rows, per_core, width)
    return (
        out_pair[None],
        grad_pair[None],
        gain_total[None, :, :piece],
        grad_query[None],
        grad_kv.reshape(depth, 2, LANES)[None],
        grad_out[None],
        jnp.transpose(router_total[:, :piece])[None],
        grad_in.astype(F32)[None],
        grad_down.astype(F32)[None],
    )


def solution(mesh):
    return jax.shard_map(
        shards,
        mesh=mesh,
        in_specs=(
            P(None, ("ctx", "wt"), None),
            P(None, ("ctx", "wt"), None),
            P(),
            P("section", None, "ctx", None),
            P("section", None, None),
            P("section", "ctx", "wt"),
            P("section", "ctx", "wt", None),
            P("section", "wt", "ctx"),
            P("section", None, None),
            P("section", "wt", "ctx", None),
            P("section", "wt", "ctx", None),
        ),
        out_specs=(
            P("section", None, ("ctx", "wt"), None),
            P("section", None, ("ctx", "wt"), None),
            P("section", None, ("ctx", "wt")),
            P("section", "ctx", "wt"),
            P("section", "ctx", "wt", None),
            P("section", "wt", "ctx"),
            P("section", ("ctx", "wt"), None),
            P("section", "wt", "ctx", None),
            P("section", "wt", "ctx", None),
        ),
        check_vma=False,
    )
```
